128 devices in a mesh: seq: 32 (over z_lo, x, y), head: 4 (over z_hi, core).
Axes of the slice: x: 4, y: 4, z: 4 (z_hi: 2, z_lo: 2; z = z_hi * 2 + z_lo), core: 2. Of those that a mesh axis runs over, the one named last changes fastest.
Arguments:
- tokens: bfloat16 [8192, 2048], P('seq'), may hold values from -6 to 6
- segment_ids: int32 [8192], P('seq'), may hold values from 0 to 2, as said below
- cotangent: bfloat16 [8192, 2048], P('seq'), may hold values from -6 to 6
- norm1_gain: float32 [2048], replicated, may hold values from 0.5 to 1.5
- x_weight: bfloat16 [2048, 3072], P(None, 'head'), may hold values from -0.125 to 0.125
- z_weight: bfloat16 [2048, 3072], P(None, 'head'), may hold values from -0.125 to 0.125
- bc_weight: bfloat16 [2048, 512], replicated, may hold values from -0.125 to 0.125
- dt_weight: bfloat16 [2048, 48], P(None, 'head'), may hold values from -0.125 to 0.125
- x_conv: float32 [4, 3072], P(None, 'head'), may hold values from -3 to 3
- bc_conv: float32 [4, 512], replicated, may hold values from -0.6 to 0.6
- dt_bias: float32 [48], P('head'), may hold values from -1 to 1
- decay_rate: float32 [48], P('head'), may hold values from 0.00012207031 to 0.2
- skip_gain: float32 [48], P('head'), may hold values from 0.5 to 1.5
- out_weight: bfloat16 [3072, 2048], P('head'), may hold values from -0.0546875 to 0.0546875
- query_weight: bfloat16 [2048, 1024], P(None, 'head'), may hold values from -0.125 to 0.125
- kv_weight: bfloat16 [2048, 512], replicated, may hold values from -0.125 to 0.125
- attn_weight: bfloat16 [1024, 2048], P('head'), may hold values from -1.5 to 1.5
- norm2_gain: float32 [2048], replicated, may hold values from 0.5 to 1.5
- gate_weight: bfloat16 [2048, 4096], P(None, 'head'), may hold values from -0.125 to 0.125
- up_weight: bfloat16 [2048, 4096], P(None, 'head'), may hold values from -0.125 to 0.125
- down_weight: bfloat16 [4096, 2048], P('head'), may hold values from -0.09375 to 0.09375
Outputs:
- output: bfloat16 [8192, 2048], P('seq')
- grad_tokens: float32 [8192, 2048], P('seq')
- grad_norm1_gain: float32 [2048], replicated
- grad_x_weight: float32 [2048, 3072], P('seq', 'head')
- grad_z_weight: float32 [2048, 3072], P('seq', 'head')
- grad_bc_weight: float32 [2048, 512], replicated
- grad_dt_weight: float32 [2048, 48], P('seq', 'head')
- grad_x_conv: float32 [4, 3072], replicated
- grad_bc_conv: float32 [4, 512], replicated
- grad_dt_bias: float32 [48], replicated
- grad_decay_rate: float32 [48], replicated
- grad_skip_gain: float32 [48], replicated
- grad_out_weight: float32 [3072, 2048], P('head', 'seq')
- grad_query_weight: float32 [2048, 1024], P('seq', 'head')
- grad_kv_weight: float32 [2048, 512], replicated
- grad_attn_weight: float32 [1024, 2048], P('head', 'seq')
- grad_norm2_gain: float32 [2048], replicated
- grad_gate_weight: float32 [2048, 4096], P('seq', 'head')
- grad_up_weight: float32 [2048, 4096], P('seq', 'head')
- grad_down_weight: float32 [4096, 2048], P('head', 'seq')
The draws below stay inside these ranges and needn't reach their ends.
Inputs may be any that keep to these rules, and one draw needn't show every extreme that they name: `segment_ids`: never decreasing; document 1 begins within the first 256 tokens and document 2 within the last 256.
All inputs are finite; a program needn't handle non-finite values.
Results may differ from the reference program's by a relative error of at most 0.03.
Values may be sent and summed in bfloat16 or wider, within the bound.
A program may use at most 256 MiB of HBM per device.

```python
import math
import jax
import jax.numpy as jnp
from jax import lax

D = 2048
SSM_HEADS = 48
SSM_DIM = 64
STATE = 256
CONV = 4
QHEADS = 8
KVHEADS = 2
HEAD_DIM = 128
FF = 4096
TOK_DEV = 256
TOKENS = 8192
DI = 3072


def draw_segment_ids(key, part):
    key = jax.random.fold_in(key, 11)
    first_key, second_key = jax.random.split(key)
    first_start = jax.random.randint(first_key, (), 1, TOK_DEV)
    last_start = jax.random.randint(second_key, (), TOKENS - TOK_DEV + 1, TOKENS)
    positions = jnp.arange(TOKENS)
    return (positions >= first_start).astype(jnp.int32) + (positions >= last_start).astype(jnp.int32)


def shard_levels(own_key, shape, cuts, low, high):
    loudness, own = 1.0, jax.random.fold_in(own_key, 6)
    for axis_at, shards_of in cuts:
        draws = jnp.exp(jax.random.uniform(jax.random.fold_in(own, axis_at), (shards_of,), jnp.float32, low / len(cuts), high / len(cuts)))
        loudness = loudness * jnp.repeat(draws, shape[axis_at] // shards_of).reshape([-1 if axis == axis_at else 1 for axis in range(len(shape))])
    return loudness


def noise(key, extent, deviation, bound, cuts=(), kind=jnp.bfloat16):
    loudness = shard_levels(key, extent, cuts, -0.22, 0.18) if cuts else 1.0
    drawn = jax.random.normal(key, extent, jnp.float32) * deviation * loudness
    return jnp.minimum(jnp.maximum(drawn, -bound), bound).astype(kind)


def setup_inputs(seed: int = 0) -> dict:
    key_of = jax.random.split(jax.random.key(seed), 22)
    return {
        "tokens": noise(key_of[0], (TOKENS, D), 1.0, 6.0, ((0, 32),)),
        "segment_ids": draw_segment_ids(jax.random.fold_in(key_of[21], 71), 0),
        "cotangent": noise(key_of[2], (TOKENS, D), 1.0, 6.0, ((0, 32),)),
        "norm1_gain": jnp.clip(1.0 + 0.1 * jax.random.normal(key_of[3], (D,), jnp.float32), 0.5, 1.5),
        "x_weight": noise(key_of[4], (D, DI), D ** -0.5, 0.125, ((1, 4),)),
        "z_weight": noise(key_of[5], (D, DI), D ** -0.5, 0.125, ((1, 4),)),
        "bc_weight": noise(key_of[6], (D, 2 * STATE), D ** -0.5, 0.125),
        "dt_weight": noise(key_of[7], (D, SSM_HEADS), D ** -0.5, 0.125, ((1, 4),)),
        "x_conv": noise(key_of[8], (CONV, DI), 0.5, 3.0, ((1, 4),), jnp.float32),
        "bc_conv": noise(key_of[9], (CONV, 2 * STATE), 0.1, 0.6, (), jnp.float32),
        "dt_bias": jnp.clip(jax.random.uniform(key_of[10], (SSM_HEADS,), jnp.float32, -1.0, 1.0) * shard_levels(key_of[10], (SSM_HEADS,), ((0, 4),), -0.4, 0.0), -1.0, 1.0),
        "decay_rate": jnp.clip(jnp.exp(math.log(0.2) - 7.4014754 * jax.random.uniform(key_of[11], (SSM_HEADS,), jnp.float32) ** shard_levels(key_of[11], (SSM_HEADS,), ((0, 4),), -0.2, 0.2)), 0.00012207031, 0.2),
        "skip_gain": jnp.clip(1.0 + 0.1 * jax.random.normal(key_of[12], (SSM_HEADS,), jnp.float32), 0.5, 1.5),
        "out_weight": noise(key_of[13], (DI, D), (DI * 4) ** -0.5, 0.0546875, ((0, 4),)),
        "query_weight": noise(key_of[14], (D, QHEADS * HEAD_DIM), D ** -0.5, 0.125, ((1, 4),)),
        "kv_weight": noise(key_of[15], (D, 2 * KVHEADS * HEAD_DIM), D ** -0.5, 0.125),
        "attn_weight": noise(key_of[16], (QHEADS * HEAD_DIM, D), (QHEADS * HEAD_DIM // 64) ** -0.5, 1.5, ((0, 4),)),
        "norm2_gain": jnp.clip(1.0 + 0.1 * jax.random.normal(key_of[17], (D,), jnp.float32), 0.5, 1.5),
        "gate_weight": noise(key_of[18], (D, FF), D ** -0.5, 0.125, ((1, 4),)),
        "up_weight": noise(key_of[19], (D, FF), D ** -0.5, 0.125, ((1, 4),)),
        "down_weight": noise(key_of[20], (FF, D), FF ** -0.5, 0.09375, ((0, 4),)),
    }


EPSILON = 1e-05
ROPE_BASE = 100000000000.0
HIGHEST = lax.Precision.HIGHEST

@jax.custom_vjp
def low(v):
    return lax.optimization_barrier(v.astype(jnp.bfloat16)).astype(jnp.float32)

@jax.custom_vjp
def low_back(v):
    return v

def low_keep(v):
    return (low(v), None)

def low_pass(kept, grad):
    return (grad,)

def back_keep(v):
    return (v, None)

def back_low(kept, grad):
    return (low(grad),)
low.defvjp(low_keep, low_pass)
low_back.defvjp(back_keep, back_low)

def exact_dot(left_side, right_side):
    return jnp.dot(left_side, right_side, precision=HIGHEST)

def rms_norm(values, scales):
    return values * lax.rsqrt(lax.optimization_barrier(jnp.mean(values * values, -1, keepdims=True)) + EPSILON) * scales

def rope_turn(values, positions, direction):
    half_dim = values.shape[-1] // 2
    frequency = ROPE_BASE ** (-(jnp.arange(half_dim).astype(jnp.float32) * 2.0 / values.shape[-1]))
    angles = positions.astype(jnp.float32)[:, None] * frequency[None, :]
    cosine = jnp.cos(angles)[:, None, :]
    sine_part = direction * jnp.sin(angles)[:, None, :]
    first_half = values[..., :half_dim]
    second_half = values[..., half_dim:]
    return jnp.concatenate([first_half * cosine - second_half * sine_part, second_half * cosine + first_half * sine_part], -1)

def conv_taps(extended, seg_extended, kernel):
    tap_count = kernel.shape[0]
    row_count = extended.shape[0] - tap_count + 1
    own_segment = seg_extended[tap_count - 1:]
    running_sum = jnp.zeros((row_count, extended.shape[1]), jnp.float32)
    for tap_index in range(tap_count):
        same_doc = seg_extended[tap_index:tap_index + row_count] == own_segment
        running_sum = running_sum + kernel[tap_index] * jnp.where(same_doc[:, None], extended[tap_index:tap_index + row_count], 0.0)
    return running_sum

def state_part(x_values, step_sizes, b_matrix, rates, segment, seg_before):
    cumulative = jnp.cumsum(-step_sizes * rates, 0)
    carry_weight = jnp.exp(cumulative[-1][None, :] - cumulative) * (segment == segment[-1]).astype(jnp.float32)[:, None]
    moved = x_values * (step_sizes * carry_weight)[:, :, None]
    local_state = jnp.einsum('jhp,jn->hpn', moved, b_matrix, precision=HIGHEST)
    through = jnp.exp(cumulative[-1]) * (segment[-1] == seg_before).astype(jnp.float32)
    return (local_state, through)

def output_part(x_values, step_sizes, b_matrix, c_matrix, rates, segment, seg_before, state_in):
    cumulative = jnp.cumsum(-step_sizes * rates, 0)
    row_index = jnp.arange(segment.shape[0])
    causal = (row_index[None, :] <= row_index[:, None]) & (segment[None, :] == segment[:, None])
    gaps = jnp.where(causal[:, :, None], cumulative[:, None, :] - cumulative[None, :, :], -jnp.inf)
    mixing = jnp.exp(gaps) * jnp.dot(c_matrix, b_matrix.T, precision=HIGHEST)[:, :, None]
    moved = x_values * step_sizes[:, :, None]
    inner = jnp.einsum('ijh,jhp->ihp', mixing, moved, precision=HIGHEST)
    entry = jnp.exp(cumulative) * (segment == seg_before).astype(jnp.float32)[:, None]
    outer = jnp.einsum('in,hpn->ihp', c_matrix, state_in, precision=HIGHEST) * entry[:, :, None]
    return inner + outer

def ssm_scan(x_heads, step_sizes, b_matrix, c_matrix, rates, segment):
    blocks = TOKENS // TOK_DEV

    def one_step(carry, piece):
        state_now, seg_before = carry
        part_x, part_dt, part_b, part_c, part_seg = piece
        block_out = output_part(part_x, part_dt, part_b, part_c, rates, part_seg, seg_before, state_now)
        local_state, through = state_part(part_x, part_dt, part_b, rates, part_seg, seg_before)
        return ((through[:, None, None] * state_now + local_state, part_seg[-1]), block_out)
    start_state = (jnp.zeros((SSM_HEADS, SSM_DIM, STATE), jnp.float32), jnp.array(-1, jnp.int32))
    pieces = (x_heads.reshape(blocks, TOK_DEV, SSM_HEADS, SSM_DIM), step_sizes.reshape(blocks, TOK_DEV, SSM_HEADS), b_matrix.reshape(blocks, TOK_DEV, STATE), c_matrix.reshape(blocks, TOK_DEV, STATE), segment.reshape(blocks, TOK_DEV))
    _, outputs = lax.scan(jax.checkpoint(one_step), start_state, pieces)
    return outputs.reshape(TOKENS, SSM_HEADS, SSM_DIM)

def attention(queries, key_rows, value_rows, segment):
    group_size = QHEADS // KVHEADS
    key_all = jnp.repeat(key_rows, group_size, axis=1)
    value_all = jnp.repeat(value_rows, group_size, axis=1)
    block_rows = math.gcd(512, TOKENS)
    block_count = TOKENS // block_rows
    positions = jnp.arange(TOKENS)
    score_scale = HEAD_DIM ** (-0.5)

    def one_block(piece):
        query_part, pos_part, seg_part = piece
        scores = low_back(jnp.einsum('ihd,jhd->hij', query_part, key_all, precision=HIGHEST) * score_scale)
        visible = (positions[None, :] <= pos_part[:, None]) & (segment[None, :] == seg_part[:, None])
        scores = jnp.where(visible[None], scores, -1e+30)
        row_max = lax.optimization_barrier(jnp.max(scores, -1, keepdims=True))
        exp_scores = jnp.exp(scores - row_max)
        attn_probs = low(exp_scores / lax.optimization_barrier(jnp.sum(exp_scores, -1, keepdims=True)))
        return jnp.einsum('hij,jhd->ihd', attn_probs, value_all, precision=HIGHEST)
    pieces = (queries.reshape(block_count, block_rows, QHEADS, HEAD_DIM), positions.reshape(block_count, block_rows), segment.reshape(block_count, block_rows))
    results = lax.map(jax.checkpoint(one_block), pieces)
    return results.reshape(TOKENS, QHEADS * HEAD_DIM)

def reference(tokens, segment_ids, cotangent, norm1_gain, x_weight, z_weight, bc_weight, dt_weight, x_conv, bc_conv, dt_bias, decay_rate, skip_gain, out_weight, query_weight, kv_weight, attn_weight, norm2_gain, gate_weight, up_weight, down_weight):

    def layer(x_input, gain_one, x_proj, z_proj, bc_proj, dt_proj, x_kernel, bc_kernel, bias_dt, rates, skips, out_proj, query_proj, kv_proj, attn_proj, gain_two, gate_proj, up_proj, down_proj):
        positions = jnp.arange(TOKENS)
        normed = low(rms_norm(x_input, gain_one))
        x_pre = low(low_back(exact_dot(normed, x_proj)))
        z_val = low_back(exact_dot(normed, z_proj))
        bc_pre = low(low_back(exact_dot(normed, bc_proj)))
        dt_raw = low_back(exact_dot(normed, dt_proj))
        pad_seg = jnp.concatenate([jnp.full((CONV - 1,), -1, jnp.int32), segment_ids])
        x_act = low(jax.nn.silu(conv_taps(jnp.pad(x_pre, ((CONV - 1, 0), (0, 0))), pad_seg, x_kernel)))
        bc_act = low(jax.nn.silu(conv_taps(jnp.pad(bc_pre, ((CONV - 1, 0), (0, 0))), pad_seg, bc_kernel)))
        step_sizes = jax.nn.softplus(dt_raw + bias_dt)
        x_heads = x_act.reshape(TOKENS, SSM_HEADS, SSM_DIM)
        ssm_out = ssm_scan(x_heads, step_sizes, bc_act[:, :STATE], bc_act[:, STATE:], rates, segment_ids)
        ssm_out = ssm_out + skips[None, :, None] * x_heads
        gated_out = low(ssm_out.reshape(TOKENS, DI) * jax.nn.silu(z_val))
        query_raw = low_back(exact_dot(normed, query_proj)).reshape(TOKENS, QHEADS, HEAD_DIM)
        kv_raw = low_back(exact_dot(normed, kv_proj))
        queries = low(rope_turn(query_raw, positions, 1.0))
        key_rows = low(rope_turn(kv_raw[:, :KVHEADS * HEAD_DIM].reshape(TOKENS, KVHEADS, HEAD_DIM), positions, 1.0))
        value_rows = low(kv_raw[:, KVHEADS * HEAD_DIM:].reshape(TOKENS, KVHEADS, HEAD_DIM))
        attended = low(low_back(attention(queries, key_rows, value_rows, segment_ids)))
        mixer_sum = low_back(exact_dot(gated_out, out_proj) + exact_dot(attended, attn_proj))
        hidden_in = x_input + mixer_sum
        normed_two = low(rms_norm(hidden_in, gain_two))
        gate_val = low_back(exact_dot(normed_two, gate_proj))
        up_val = low_back(exact_dot(normed_two, up_proj))
        hidden = low(jax.nn.silu(gate_val) * up_val)
        return hidden_in + low_back(exact_dot(hidden, down_proj))
    floats = [item.astype(jnp.float32) for item in (tokens, norm1_gain, x_weight, z_weight, bc_weight, dt_weight, x_conv, bc_conv, dt_bias, decay_rate, skip_gain, out_weight, query_weight, kv_weight, attn_weight, norm2_gain, gate_weight, up_weight, down_weight)]
    result, back_fn = jax.vjp(layer, *floats)
    grads = back_fn(cotangent.astype(jnp.float32))
    return (result.astype(jnp.bfloat16), grads[0], grads[1], grads[2], grads[3], grads[4], grads[5], grads[6], grads[7], grads[8], grads[9], grads[10], grads[11], grads[12], grads[13], grads[14], grads[15], grads[16], grads[17], grads[18])
```

```python
import functools

import jax
import jax.numpy as jnp
from jax import lax
from jax.experimental import pallas as pl
from jax.experimental.pallas import tpu as pltpu
from jax.sharding import Mesh
from jax.sharding import PartitionSpec as P

SSM_DIM = 64
STATE = 256
CONV = 4
KVHEADS = 2
HEAD_DIM = 128
NZ, NX, NY = 2, 4, 4
BLOCKS = NZ * NX * NY
CHIPS = 2 * BLOCKS
ROWS = 256
MODEL = 2048
SEQ = ("zl", "x", "y")
EPSILON = 1e-05
ROPE_BASE = 100000000000.0
HIGHEST = lax.Precision.HIGHEST
MESH = pl.DeviceIdType.MESH
BF16, F32 = jnp.bfloat16, jnp.float32
MASKED = -1e30
LOG2E = 1.4426950408889634
VMEM_LIMIT = 56 * 2**20


def block_index():
    return (lax.axis_index("zl") * NX + lax.axis_index("x")) * NY + lax.axis_index("y")


def block_at(s):
    return {"zl": s // (NX * NY), "x": (s // NY) % NX, "y": s % NY}


def signal(sem, where):
    pl.semaphore_signal(sem, inc=1, device_id=where, device_id_type=MESH)


def remote(src, dst, send, recv, where):
    return pltpu.make_async_remote_copy(src, dst, send, recv, device_id=where, device_id_type=MESH)


def over(start, stop, body):
    def step(i, carry):
        body(i)
        return carry

    lax.fori_loop(start, stop, step, 0)


def dot(a, b, left=1, right=0):
    return lax.dot_general(
        a, b, (((left,), (right,)), ((), ())), preferred_element_type=F32
    )


def vmem(n):
    return [pl.BlockSpec(memory_space=pltpu.VMEM)] * n


def params(collective_id):
    return pltpu.CompilerParams(
        collective_id=collective_id, has_side_effects=True, vmem_limit_bytes=VMEM_LIMIT
    )


def key_segments(block):
    turned = jnp.transpose(block.astype(F32))
    return jnp.concatenate([turned[:, 0:1], turned[:, 1:2]], 0)


def attention_forward_kernel(
    q_ref, own_ref, qseg_ref, edge_ref, out_ref, lse_ref, kv_ref, edge_out,
    m_ref, l_ref, acc_ref, send_sem, recv_sem, sib_send, sib_recv, edge_sem,
):
    me, c = block_index(), lax.axis_index("c")
    sibling = {"c": 1 - c}
    barrier = pltpu.get_barrier_semaphore()
    over(1, BLOCKS, lambda o: signal(barrier, block_at((me + o) % BLOCKS)))
    signal(barrier, sibling)
    pl.semaphore_wait(barrier, BLOCKS)

    kv_ref[c, 0] = own_ref[...]
    to_sibling = lambda t, src: remote(
        src, kv_ref.at[c, t], sib_send.at[t], sib_recv.at[t], sibling
    )
    from_sibling = lambda t: remote(
        kv_ref.at[1 - c, t], kv_ref.at[1 - c, t], sib_send.at[t], sib_recv.at[t], sibling
    )
    to_block = lambda t: remote(
        own_ref, kv_ref.at[c, t], send_sem.at[t], recv_sem.at[t], block_at((me + t) % BLOCKS)
    )
    edge_copy = remote(
        edge_ref, edge_out, edge_sem.at[0], edge_sem.at[1], block_at((me + 1) % BLOCKS)
    )

    @pl.when(me < BLOCKS - 1)
    def _():
        edge_copy.start()

    to_sibling(0, own_ref).start()
    over(1, BLOCKS - me, lambda t: to_block(t).start())

    scale = LOG2E * HEAD_DIM**-0.5
    queries = q_ref[...]
    qseg = qseg_ref[0:1, :]

    def scores_of(t):
        s = dot(kv_ref[0, t, :ROWS], queries, 1, 1) * scale
        return jnp.where(key_segments(kv_ref[0, t, ROWS:]) == qseg, s, MASKED)

    from_sibling(0).wait_recv()
    row = lax.broadcasted_iota(jnp.int32, (ROWS, 2 * ROWS), 0)
    col = lax.broadcasted_iota(jnp.int32, (ROWS, 2 * ROWS), 1) % ROWS
    s = jnp.where(row <= col, scores_of(0), MASKED)
    m = jnp.max(s, 0, keepdims=True)
    p = jnp.exp2(s - m)
    m_ref[...] = m
    l_ref[...] = jnp.sum(p, 0, keepdims=True)
    acc_ref[...] = dot(kv_ref[1, 0, :ROWS], p.astype(BF16), 0, 0)

    def forward(t):
        to_block(t).wait_recv()
        to_sibling(t, kv_ref.at[c, t]).start()

    @pl.when(me >= 1)
    def _():
        forward(1)

    def step(t):
        @pl.when(t + 1 <= me)
        def _():
            forward(t + 1)

        from_sibling(t).wait_recv()
        s = scores_of(t)
        m_old = m_ref[...]
        m = jnp.maximum(m_old, jnp.max(s, 0, keepdims=True))
        p = jnp.exp2(s - m)
        alpha = jnp.exp2(m_old - m)
        m_ref[...] = m
        l_ref[...] = l_ref[...] * alpha + jnp.sum(p, 0, keepdims=True)
        acc_ref[...] = acc_ref[...] * alpha + dot(kv_ref[1, t, :ROWS], p.astype(BF16), 0, 0)

    over(1, me + 1, step)
    out_ref[...] = jnp.transpose(acc_ref[...] / l_ref[...])
    lse_ref[...] = jnp.broadcast_to(m_ref[...] + jnp.log2(l_ref[...]), lse_ref.shape)

    over(0, me + 1, lambda t: to_sibling(t, own_ref).wait_send())
    over(1, BLOCKS - me, lambda t: to_block(t).wait_send())

    @pl.when(me < BLOCKS - 1)
    def _():
        edge_copy.wait_send()

    @pl.when(me > 0)
    def _():
        edge_copy.wait_recv()

    @pl.when(me == 0)
    def _():
        edge_out[...] = jnp.zeros_like(edge_out)


def attention_forward(queries, own, qseg, edge):
    wide = 2 * ROWS
    return pl.pallas_call(
        attention_forward_kernel,
        name="attention_forward",
        out_shape=(
            jax.ShapeDtypeStruct((wide, HEAD_DIM), F32),
            jax.ShapeDtypeStruct((8, wide), F32),
            jax.ShapeDtypeStruct((2, BLOCKS, *own.shape), BF16),
            jax.ShapeDtypeStruct(edge.shape, edge.dtype),
        ),
        in_specs=vmem(4),
        out_specs=tuple(vmem(4)),
        scratch_shapes=[
            pltpu.VMEM((1, wide), F32),
            pltpu.VMEM((1, wide), F32),
            pltpu.VMEM((HEAD_DIM, wide), F32),
            pltpu.SemaphoreType.DMA((BLOCKS,)),
            pltpu.SemaphoreType.DMA((BLOCKS,)),
            pltpu.SemaphoreType.DMA((BLOCKS,)),
            pltpu.SemaphoreType.DMA((BLOCKS,)),
            pltpu.SemaphoreType.DMA((2,)),
        ],
        compiler_params=params(1),
    )(queries, own, qseg, edge)


def attention_backward_kernel(
    q_ref, do_ref, lse_ref, delta_ref, qseg_ref, kv_ref, edge_ref, dq_ref, own_ref, edge_out,
    dqt_ref, mine, theirs, sib, summed, got, send_sem, recv_sem, sib_send, sib_recv, edge_sem,
):
    me, c = block_index(), lax.axis_index("c")
    sibling = {"c": 1 - c}
    barrier = pltpu.get_barrier_semaphore()
    over(1, BLOCKS, lambda o: signal(barrier, block_at((me + o) % BLOCKS)))
    signal(barrier, sibling)
    pl.semaphore_wait(barrier, BLOCKS)

    to_sibling = lambda t: remote(
        theirs.at[t], sib.at[t], sib_send.at[t], sib_recv.at[t], sibling
    )
    to_owner = lambda t: remote(
        summed.at[t], got.at[t], send_sem.at[t], recv_sem.at[t],
        block_at((me + BLOCKS - t) % BLOCKS),
    )
    edge_copy = remote(
        edge_ref, edge_out, edge_sem.at[0], edge_sem.at[1],
        block_at((me + BLOCKS - 1) % BLOCKS),
    )

    @pl.when(me > 0)
    def _():
        edge_copy.start()

    scale = LOG2E * HEAD_DIM**-0.5
    queries, grads = q_ref[...], do_ref[...]
    lse, delta, qseg = lse_ref[0:1, :], delta_ref[0:1, :], qseg_ref[0:1, :]

    def block(t, own):
        keys = kv_ref[0, t, :ROWS]
        s = dot(keys, queries, 1, 1) * scale
        s = jnp.where(key_segments(kv_ref[0, t, ROWS:]) == qseg, s, MASKED)
        if own:
            row = lax.broadcasted_iota(jnp.int32, (ROWS, 2 * ROWS), 0)
            col = lax.broadcasted_iota(jnp.int32, (ROWS, 2 * ROWS), 1) % ROWS
            s = jnp.where(row <= col, s, MASKED)
        p = jnp.exp2(s - lse)
        ds = (p * (dot(kv_ref[1, t, :ROWS], grads, 1, 1) - delta)).astype(BF16)
        dk = dot(ds, queries)
        dv = dot(p.astype(BF16), grads)
        change = dot(keys, ds, 0, 0)
        dqt_ref[...] = change if own else dqt_ref[...] + change
        mine[t] = jnp.where(c == 0, dk, dv).astype(BF16)
        theirs[t] = jnp.where(c == 0, dv, dk).astype(BF16)
        to_sibling(t).start()

    def pair(t):
        to_sibling(t).wait_recv()
        return mine[t].astype(F32) + sib[t].astype(F32)

    block(0, True)

    def step(t):
        block(t, False)

        @pl.when(t >= 2)
        def _():
            summed[t - 1] = pair(t - 1).astype(BF16)
            to_owner(t - 1).start()

    over(1, me + 1, step)

    @pl.when(me >= 1)
    def _():
        summed[me] = pair(me).astype(BF16)
        to_owner(me).start()

    own_ref[...] = pair(0)
    dq_ref[...] = jnp.transpose(dqt_ref[...])

    def collect(t):
        to_owner(t).wait_recv()
        own_ref[...] += got[t].astype(F32)

    over(1, BLOCKS - me, collect)
    over(0, me + 1, lambda t: to_sibling(t).wait_send())
    over(1, me + 1, lambda t: to_owner(t).wait_send())

    @pl.when(me > 0)
    def _():
        edge_copy.wait_send()

    @pl.when(me < BLOCKS - 1)
    def _():
        edge_copy.wait_recv()

    @pl.when(me == BLOCKS - 1)
    def _():
        edge_out[...] = jnp.zeros_like(edge_out)


def attention_backward(queries, grads, lse, delta, qseg, kv, edge):
    wide = 2 * ROWS
    piece = (BLOCKS, ROWS, HEAD_DIM)
    return pl.pallas_call(
        attention_backward_kernel,
        name="attention_backward",
        out_shape=(
            jax.ShapeDtypeStruct((wide, HEAD_DIM), F32),
            jax.ShapeDtypeStruct((ROWS, HEAD_DIM), F32),
            jax.ShapeDtypeStruct(edge.shape, edge.dtype),
        ),
        in_specs=vmem(7),
        out_specs=tuple(vmem(3)),
        scratch_shapes=[
            pltpu.VMEM((HEAD_DIM, wide), F32),
            *[pltpu.VMEM(piece, BF16)] * 5,
            *[pltpu.SemaphoreType.DMA((BLOCKS,))] * 4,
            pltpu.SemaphoreType.DMA((2,)),
        ],
        compiler_params=params(2),
    )(queries, grads, lse, delta, qseg, kv, edge)


SCAN_ROWS = 24


def scan_kernel(reverse, part_ref, out_ref, got, back, send_sem, recv_sem):
    me = block_index()
    barrier = pltpu.get_barrier_semaphore()
    over(1, BLOCKS, lambda o: signal(barrier, block_at((me + o) % BLOCKS)))
    pl.semaphore_wait(barrier, BLOCKS - 1)

    def there(o):
        d = (me + o) % BLOCKS
        return remote(
            part_ref.at[d], got.at[me], send_sem.at[0, o], recv_sem.at[0, o], block_at(d)
        )

    def arrived(phase, dst, o):
        s = (me + BLOCKS - o) % BLOCKS
        return remote(
            dst.at[s], dst.at[s], send_sem.at[phase, o], recv_sem.at[phase, o], block_at(s)
        )

    over(1, BLOCKS, lambda o: there(o).start())
    got[me] = part_ref[me]
    over(1, BLOCKS, lambda o: arrived(0, got, o).wait_recv())

    at_lane = lax.broadcasted_iota(jnp.int32, (SCAN_ROWS, 128), 1)
    at_row = lax.broadcasted_iota(jnp.int32, (SCAN_ROWS, 128), 0)

    def scan(i, state):
        k = BLOCKS - 1 - i if reverse else i
        message = got[k].astype(F32)
        back[k] = jnp.concatenate([state, jnp.zeros((8, STATE), F32)], 0).astype(BF16)

        @pl.when(k != me)
        def _():
            o = (k + BLOCKS - me) % BLOCKS
            remote(
                back.at[k], out_ref.at[me], send_sem.at[1, o], recv_sem.at[1, o], block_at(k)
            ).start()

        factors = message[SCAN_ROWS : SCAN_ROWS + 1, :128]
        factors += message[SCAN_ROWS + 1 : SCAN_ROWS + 2, :128]
        factors += message[SCAN_ROWS + 2 : SCAN_ROWS + 3, :128]
        through = jnp.sum(jnp.where(at_lane == at_row, factors, 0.0), 1, keepdims=True)
        return through * state + message[:SCAN_ROWS]

    lax.fori_loop(0, BLOCKS, scan, jnp.zeros((SCAN_ROWS, STATE), F32))
    out_ref[me] = back[me]
    over(1, BLOCKS, lambda o: arrived(1, out_ref, o).wait_recv())

    def sent(o):
        there(o).wait_send()
        d = (me + o) % BLOCKS
        remote(
            back.at[d], out_ref.at[me], send_sem.at[1, o], recv_sem.at[1, o], block_at(d)
        ).wait_send()

    over(1, BLOCKS, sent)


def scan_states(state, through, reverse, collective_id):
    heads = state.shape[0]
    per = heads * SSM_DIM // BLOCKS
    rows = state.reshape(BLOCKS, per, STATE).astype(BF16)
    factor = jnp.repeat(through, SSM_DIM).reshape(BLOCKS, per)
    high = factor.astype(BF16)
    rest = factor - high.astype(F32)
    middle = rest.astype(BF16)
    low = (rest - middle.astype(F32)).astype(BF16)
    extra = jnp.stack([high, middle, low], 1)
    extra = jnp.pad(extra, ((0, 0), (0, 5), (0, STATE - per)))
    message = jnp.concatenate([rows, extra], 1)
    out = pl.pallas_call(
        functools.partial(scan_kernel, reverse),
        name="scan_back" if reverse else "scan_ahead",
        out_shape=jax.ShapeDtypeStruct(message.shape, BF16),
        in_specs=vmem(1),
        out_specs=vmem(1)[0],
        scratch_shapes=[
            pltpu.VMEM(message.shape, BF16),
            pltpu.VMEM(message.shape, BF16),
            pltpu.SemaphoreType.DMA((2, BLOCKS)),
            pltpu.SemaphoreType.DMA((2, BLOCKS)),
        ],
        compiler_params=params(collective_id),
    )(message)
    return out[:, :per].reshape(heads, SSM_DIM, STATE).astype(F32)


HEAD_CHUNKS = 4


def head_sum_kernel(x_ref, out_ref, near, pair, far, near_send, near_recv, far_send, far_recv, last_send, last_recv):
    c, zh = lax.axis_index("c"), lax.axis_index("zh")
    sibling, opposite = {"c": 1 - c}, {"zh": 1 - zh}
    barrier = pltpu.get_barrier_semaphore()
    signal(barrier, sibling)
    signal(barrier, opposite)
    pl.semaphore_wait(barrier, 2)
    half = x_ref.shape[0] // 2
    n = half // HEAD_CHUNKS

    def rows(core, k):
        return pl.ds(pl.multiple_of(core * half + k * n, 16), n)

    def local(k):
        return pl.ds(k * n, n)

    first = lambda k: remote(
        x_ref.at[rows(1 - c, k)], near.at[local(k)], near_send.at[k], near_recv.at[k], sibling
    )
    second = lambda k: remote(
        pair.at[local(k)], far.at[local(k)], far_send.at[k], far_recv.at[k], opposite
    )
    third = lambda k, core: remote(
        out_ref.at[rows(core, k)], out_ref.at[rows(core, k)],
        last_send.at[k], last_recv.at[k], sibling,
    )
    for k in range(HEAD_CHUNKS):
        first(k).start()
    for k in range(HEAD_CHUNKS):
        first(k).wait_recv()
        pair[local(k)] = (x_ref[rows(c, k)].astype(F32) + near[local(k)].astype(F32)).astype(BF16)
        second(k).start()
    for k in range(HEAD_CHUNKS):
        second(k).wait_recv()
        out_ref[rows(c, k)] = (pair[local(k)].astype(F32) + far[local(k)].astype(F32)).astype(BF16)
        third(k, c).start()
    for k in range(HEAD_CHUNKS):
        third(k, 1 - c).wait_recv()
    for k in range(HEAD_CHUNKS):
        first(k).wait_send()
        second(k).wait_send()
        third(k, c).wait_send()


def head_sum(x, collective_id):
    half = (x.shape[0] // 2, x.shape[1])
    return pl.pallas_call(
        head_sum_kernel,
        name=f"head_sum_{collective_id}",
        out_shape=jax.ShapeDtypeStruct(x.shape, BF16),
        in_specs=vmem(1),
        out_specs=vmem(1)[0],
        scratch_shapes=[
            *[pltpu.VMEM(half, BF16)] * 3,
            *[pltpu.SemaphoreType.DMA((HEAD_CHUNKS,))] * 6,
        ],
        compiler_params=params(collective_id),
    )(x)


def head_share_kernel(x_ref, out_ref, got, send_sem, recv_sem):
    me = lax.axis_index("zh") * 2 + lax.axis_index("c")
    at = lambda d: {"zh": d // 2, "c": d % 2}
    barrier = pltpu.get_barrier_semaphore()
    for o in range(1, 4):
        signal(barrier, at((me + o) % 4))
    pl.semaphore_wait(barrier, 3)
    copy = lambda o: remote(
        x_ref.at[(me + o) % 4], got.at[o], send_sem.at[o], recv_sem.at[o], at((me + o) % 4)
    )
    for o in range(1, 4):
        copy(o).start()
    total = x_ref[me].astype(F32)
    for o in range(1, 4):
        copy(o).wait_recv()
        total += got[o].astype(F32)
    out_ref[...] = total
    for o in range(1, 4):
        copy(o).wait_send()


def head_share(x, collective_id):
    return pl.pallas_call(
        head_share_kernel,
        name="head_share",
        out_shape=jax.ShapeDtypeStruct(x.shape[1:], F32),
        in_specs=vmem(1),
        out_specs=vmem(1)[0],
        scratch_shapes=[
            pltpu.VMEM(x.shape, BF16),
            pltpu.SemaphoreType.DMA((4,)),
            pltpu.SemaphoreType.DMA((4,)),
        ],
        compiler_params=params(collective_id),
    )(x)


WIDE = 256
LAG = 3


def weight_kernel(
    first_of, l_ref, r_ref, out_ref, lz, rz, part, gx, half, gy,
    lz_send, lz_recv, rz_send, rz_recv, gx_send, gx_recv, gy_send, gy_recv,
):
    n = r_ref.shape[1] // WIDE
    n_left = l_ref.shape[0]
    own = MODEL // NZ
    zl, x, y = (lax.axis_index(a) for a in SEQ)
    other = {"zl": 1 - zl}
    barrier = pltpu.get_barrier_semaphore()
    signal(barrier, other)
    for o in range(1, 4):
        signal(barrier, {"x": (x + o) % NX})
        signal(barrier, {"y": (y + o) % NY})
    pl.semaphore_wait(barrier, 7)

    def columns(c):
        return pl.ds(pl.multiple_of(c * WIDE, WIDE), WIDE)

    def left(g):
        return remote(
            l_ref.at[g, pl.ds(pl.multiple_of((1 - zl) * own, own), own)], lz.at[g],
            lz_send.at[g], lz_recv.at[g], other,
        )

    def right(c):
        return remote(r_ref.at[:, columns(c)], rz.at[c], rz_send.at[c], rz_recv.at[c], other)

    for g in range(n_left):
        left(g).start()
        over(first_of[g], first_of[g + 1], lambda c: right(c).start())

    def spread(c, phase, o):
        along_x = c % 2 == phase
        x_to = jnp.where(along_x, (x + o) % NX, x)
        y_to = jnp.where(along_x, y, (y + o) % NY)
        return {"x": x_to, "y": y_to}, jnp.where(along_x, x_to, y_to)

    def send_first(c, o):
        where, d = spread(c, 0, o)
        return remote(part.at[c, d], gx.at[c, o - 1], gx_send.at[c], gx_recv.at[c], where)

    def send_second(c, o):
        where, d = spread(c, 1, o)
        return remote(half.at[c, d], gy.at[c, o - 1], gy_send.at[c], gy_recv.at[c], where)

    def whole(got, send, recv, c):
        return remote(got.at[c], got.at[c], send.at[c], recv.at[c], other)

    def product(c):
        for g in range(n_left):
            @pl.when(c == first_of[g])
            def _():
                left(g).wait_recv()
        right(c).wait_recv()
        g = sum((c >= first_of[k]).astype(jnp.int32) for k in range(1, n_left)) if n_left > 1 else 0
        mine, theirs = r_ref[:, columns(c)], rz[c]
        even = c % 2 == 0
        for i in range(NX):
            a = l_ref[g, pl.ds(pl.multiple_of(zl * own + i * 256, 256), 256), :]
            b = lz[g, pl.ds(i * 256, 256), :]
            tile = (dot(a, mine) + dot(b, theirs)).astype(BF16)
            for j in range(NY):
                part[c, jnp.where(even, i, j), jnp.where(even, j, i)] = tile[j * 64 : (j + 1) * 64]
        for o in range(1, 4):
            send_first(c, o).start()

    def middle(c):
        whole(gx, gx_send, gx_recv, c).wait_recv()
        mine = jnp.where(c % 2 == 0, x, y)
        for j in range(4):
            total = part[c, mine, j].astype(F32)
            for o in range(3):
                total += gx[c, o, j].astype(F32)
            half[c, j] = total.astype(BF16)
        for o in range(1, 4):
            send_second(c, o).start()

    def last(c):
        whole(gy, gy_send, gy_recv, c).wait_recv()
        mine = jnp.where(c % 2 == 0, y, x)
        total = half[c, mine].astype(F32)
        for o in range(3):
            total += gy[c, o].astype(F32)
        out_ref[:, columns(c)] = total

    def step(i):
        @pl.when(i < n)
        def _():
            product(i)

        @pl.when((i >= LAG) & (i < n + LAG))
        def _():
            middle(i - LAG)

        @pl.when(i >= 2 * LAG)
        def _():
            last(i - 2 * LAG)

    over(0, n + 2 * LAG, step)

    for g in range(n_left):
        left(g).wait_send()

    def sent(c):
        right(c).wait_send()
        whole(gx, gx_send, gx_recv, c).wait_send()
        whole(gy, gy_send, gy_recv, c).wait_send()

    over(0, n, sent)


def weight_gradients(lefts, groups, collective_id, name):
    first_of, at = [0], 0
    flat = []
    for arrays in groups:
        for a in arrays:
            flat.append(a)
            at += a.shape[1]
        first_of.append(at // WIDE)
    left = jnp.stack(lefts)
    right = jnp.concatenate(flat, 1)
    n, n_left = at // WIDE, len(lefts)
    own = MODEL // NZ
    dma = pltpu.SemaphoreType.DMA
    return pl.pallas_call(
        functools.partial(weight_kernel, tuple(first_of)),
        name=name,
        out_shape=jax.ShapeDtypeStruct((own // (NX * NY), at), F32),
        in_specs=vmem(2),
        out_specs=vmem(1)[0],
        scratch_shapes=[
            pltpu.VMEM((n_left, own, ROWS), BF16),
            pltpu.VMEM((n, ROWS, WIDE), BF16),
            pltpu.VMEM((n, 4, 4, 64, WIDE), BF16),
            pltpu.VMEM((n, 3, 4, 64, WIDE), BF16),
            pltpu.VMEM((n, 4, 64, WIDE), BF16),
            pltpu.VMEM((n, 3, 64, WIDE), BF16),
            dma((n_left,)), dma((n_left,)),
            *[dma((n,))] * 6,
        ],
        compiler_params=params(collective_id),
    )(left, right)


SMALL = 8 * 128
TAIL = 80


def gather_kernel(
    w_ref, e_ref, out_ref, got, mine, e_send, e_recv, w_send, w_recv, sib_send, sib_recv
):
    me, c, zh = block_index(), lax.axis_index("c"), lax.axis_index("zh")
    chip = zh * BLOCKS + me
    sibling = {"c": 1 - c}

    def chip_at(p):
        return {"zh": p // BLOCKS, **block_at(p % BLOCKS)}

    barrier = pltpu.get_barrier_semaphore()
    over(1, CHIPS, lambda o: signal(barrier, chip_at((chip + o) % CHIPS)))
    signal(barrier, sibling)
    pl.semaphore_wait(barrier, CHIPS)

    def share(o):
        d = (me + o) % BLOCKS
        return remote(e_ref.at[d], got.at[o], e_send.at[o], e_recv.at[o], block_at(d))

    over(1, BLOCKS, lambda o: share(o).start())
    got[0] = e_ref[me]

    def add(o, total):
        share(o).wait_recv()
        return total + got[o]

    total = lax.fori_loop(1, BLOCKS, add, got[0])
    mine[:64] = w_ref[...].astype(BF16)
    mine[64:] = jnp.zeros((TAIL - 64, 2 * 128), BF16)
    mine[64:, :128] = jnp.concatenate([total, jnp.zeros_like(total)], 0).astype(BF16)
    out_ref[c, chip] = mine[...]

    def spread(o):
        d = (chip + o) % CHIPS
        return remote(mine, out_ref.at[c, chip], w_send.at[o], w_recv.at[o], chip_at(d))

    def arrived(o):
        s = (chip + CHIPS - o) % CHIPS
        return s, remote(mine, out_ref.at[c, s], w_send.at[o], w_recv.at[o], chip_at(s))

    def to_sibling(s, core):
        return remote(
            out_ref.at[core, s], out_ref.at[core, s], sib_send.at[s], sib_recv.at[s], sibling
        )

    over(1, CHIPS, lambda o: spread(o).start())
    to_sibling(chip, c).start()

    def pass_on(o):
        s, copy = arrived(o)
        copy.wait_recv()
        to_sibling(s, c).start()

    over(1, CHIPS, pass_on)
    over(0, CHIPS, lambda s: to_sibling(s, 1 - c).wait_recv())
    over(0, CHIPS, lambda s: to_sibling(s, c).wait_send())
    over(1, CHIPS, lambda o: spread(o).wait_send())
    over(1, BLOCKS, lambda o: share(o).wait_send())


def gather_replicated(weights, small, collective_id):
    dma = pltpu.SemaphoreType.DMA
    return pl.pallas_call(
        gather_kernel,
        name="gather_replicated",
        out_shape=jax.ShapeDtypeStruct((2, CHIPS, TAIL, 256), BF16),
        in_specs=vmem(2),
        out_specs=vmem(1)[0],
        scratch_shapes=[
            pltpu.VMEM((BLOCKS, 8, 128), F32),
            pltpu.VMEM((TAIL, 256), BF16),
            dma((BLOCKS,)), dma((BLOCKS,)),
            *[dma((CHIPS,))] * 4,
        ],
        compiler_params=params(collective_id),
    )(weights, small)


def rms_norm(values, scales):
    return values * lax.rsqrt(jnp.mean(values * values, -1, keepdims=True) + EPSILON) * scales


def rope_turn(values, cosine, sine):
    half = values.shape[-1] // 2
    first, second = values[..., :half], values[..., half:]
    return jnp.concatenate([first * cosine - second * sine, second * cosine + first * sine], -1)


def conv_taps(extended, seg_extended, kernel):
    tap_count = kernel.shape[0]
    row_count = extended.shape[0] - tap_count + 1
    own_segment = seg_extended[tap_count - 1 :]
    running_sum = jnp.zeros((row_count, extended.shape[1]), F32)
    for tap_index in range(tap_count):
        same_doc = seg_extended[tap_index : tap_index + row_count] == own_segment
        running_sum = running_sum + kernel[tap_index] * jnp.where(
            same_doc[:, None], extended[tap_index : tap_index + row_count], 0.0
        )
    return running_sum


def state_part(x_values, step_sizes, b_matrix, rates, segment, seg_before):
    cumulative = jnp.cumsum(-step_sizes * rates, 0)
    carry_weight = (
        jnp.exp(cumulative[-1][None, :] - cumulative)
        * (segment == segment[-1]).astype(F32)[:, None]
    )
    moved = x_values * (step_sizes * carry_weight)[:, :, None]
    local_state = jnp.einsum("jhp,jn->hpn", moved, b_matrix, precision=HIGHEST)
    through = jnp.exp(cumulative[-1]) * (segment[-1] == seg_before).astype(F32)
    return (local_state, through)


def output_part(x_values, step_sizes, cb_product, c_matrix, rates, segment, seg_before, state_in):
    cumulative = jnp.cumsum(-step_sizes * rates, 0)
    row_index = jnp.arange(segment.shape[0])
    causal = (row_index[None, :] <= row_index[:, None]) & (segment[None, :] == segment[:, None])
    gaps = jnp.where(causal[:, :, None], cumulative[:, None, :] - cumulative[None, :, :], -jnp.inf)
    mixing = jnp.exp(gaps) * cb_product[:, :, None]
    moved = x_values * step_sizes[:, :, None]
    inner = jnp.einsum("ijh,jhp->ihp", mixing, moved, precision=HIGHEST)
    entry = jnp.exp(cumulative) * (segment == seg_before).astype(F32)[:, None]
    outer = jnp.einsum("in,hpn->ihp", c_matrix, state_in, precision=HIGHEST) * entry[:, :, None]
    return inner + outer


def on_device(
    tokens, segment_ids, cotangent, norm1_gain, x_weight, z_weight, bc_weight, dt_weight,
    x_conv, bc_conv, dt_bias, decay_rate, skip_gain, out_weight, query_weight, kv_weight,
    attn_weight, norm2_gain, gate_weight, up_weight, down_weight,
):
    edge_rows = CONV - 1
    zh, c = lax.axis_index("zh"), lax.axis_index("c")
    head_index = zh * 2 + c
    heads = decay_rate.shape[0]
    inner = x_weight.shape[1]
    q_heads = query_weight.shape[1] // HEAD_DIM
    positions = block_index() * ROWS + jnp.arange(ROWS)
    half_dim = HEAD_DIM // 2
    frequency = ROPE_BASE ** (-(jnp.arange(half_dim).astype(F32) * 2.0 / HEAD_DIM))
    angles = positions.astype(F32)[:, None] * frequency[None, :]
    cosine, sine = jnp.cos(angles), jnp.sin(angles)

    x_input = tokens.astype(F32)
    normed_f, norm_back = jax.vjp(rms_norm, x_input, norm1_gain)
    normed = normed_f.astype(BF16)
    kv_at = c * (KVHEADS * HEAD_DIM) + zh * HEAD_DIM
    kv_columns = lax.dynamic_slice_in_dim(kv_weight, kv_at, HEAD_DIM, 1)
    kv_raw = dot(normed, kv_columns)
    kv_own = jnp.where(c == 0, rope_turn(kv_raw, cosine, sine), kv_raw).astype(BF16)
    query_raw = dot(normed, query_weight).reshape(ROWS, q_heads, HEAD_DIM)
    queries = rope_turn(query_raw, cosine[:, None, :], sine[:, None, :]).astype(BF16)
    queries = queries.transpose(1, 0, 2).reshape(q_heads * ROWS, HEAD_DIM)
    x_pre = dot(normed, x_weight).astype(BF16)
    bc_pre = dot(normed, bc_weight).astype(BF16)
    z_val = dot(normed, z_weight)
    dt_raw = dot(normed, dt_weight)

    seg_low = segment_ids.astype(BF16)
    own_block = jnp.concatenate(
        [kv_own, jnp.pad(seg_low.reshape(2, HEAD_DIM), ((0, 14), (0, 0)))], 0
    )
    seg_row = jnp.broadcast_to(jnp.tile(segment_ids.astype(F32), q_heads), (8, q_heads * ROWS))
    edge = jnp.concatenate(
        [x_pre[-16:], bc_pre[-16:], jnp.broadcast_to(seg_low[-16:, None], (16, 128))], 1
    )
    attended, lse, kv_all, edge_in = attention_forward(queries, own_block, seg_row, edge)
    edge_in = edge_in[-edge_rows:]
    seg_extended = jnp.concatenate([edge_in[:, inner + 2 * STATE].astype(jnp.int32), segment_ids])
    seg_before = seg_extended[edge_rows - 1]
    x_extended = jnp.concatenate([edge_in[:, :inner], x_pre]).astype(F32)
    bc_extended = jnp.concatenate([edge_in[:, inner : inner + 2 * STATE], bc_pre]).astype(F32)

    def conv_silu(extended, kernel):
        return jax.nn.silu(conv_taps(extended, seg_extended, kernel))

    x_act_f, x_conv_back = jax.vjp(conv_silu, x_extended, x_conv)
    bc_act_f = conv_silu(bc_extended, bc_conv)
    bc_at = head_index * 128
    _, bc_conv_back = jax.vjp(
        conv_silu,
        lax.dynamic_slice_in_dim(bc_extended, bc_at, 128, 1),
        lax.dynamic_slice_in_dim(bc_conv, bc_at, 128, 1),
    )
    x_heads = x_act_f.astype(BF16).astype(F32).reshape(ROWS, heads, SSM_DIM)
    bc_low = bc_act_f.astype(BF16)
    bc_act = bc_low.astype(F32)
    b_matrix, c_matrix = bc_act[:, :STATE], bc_act[:, STATE:]
    cb_product = dot(bc_low[:, STATE:], bc_low[:, :STATE], 1, 1)
    dt_pre = dt_raw + dt_bias
    step_sizes = jax.nn.softplus(dt_pre)

    def state_fn(x_values, step_vals, b_vals, rate_vals):
        return state_part(x_values, step_vals, b_vals, rate_vals, segment_ids, seg_before)

    (local_state, through), state_part_back = jax.vjp(
        state_fn, x_heads, step_sizes, b_matrix, decay_rate
    )
    state_in = scan_states(local_state, through, False, 3)

    def output_fn(x_values, step_vals, cb_vals, c_vals, rate_vals, entry_state):
        return output_part(
            x_values, step_vals, cb_vals, c_vals, rate_vals, segment_ids, seg_before, entry_state
        )

    ssm_core, output_back = jax.vjp(
        output_fn, x_heads, step_sizes, cb_product, c_matrix, decay_rate, state_in
    )
    ssm_out = (ssm_core + skip_gain[None, :, None] * x_heads).reshape(ROWS, inner)
    z_gate = jax.nn.silu(z_val)
    gated = (ssm_out * z_gate).astype(BF16)
    attended_low = (
        attended.astype(BF16).reshape(q_heads, ROWS, HEAD_DIM).transpose(1, 0, 2)
        .reshape(ROWS, q_heads * HEAD_DIM)
    )
    mixer_part = dot(gated, out_weight) + dot(attended_low, attn_weight)
    hidden_in = x_input + head_sum(mixer_part.astype(BF16), 4).astype(F32)

    normed_two_f, norm_two_back = jax.vjp(rms_norm, hidden_in, norm2_gain)
    normed_two = normed_two_f.astype(BF16)
    gate_val = dot(normed_two, gate_weight)
    up_val = dot(normed_two, up_weight)
    gate_sig = jax.nn.sigmoid(gate_val)
    gate_act = gate_val * gate_sig
    hidden = (gate_act * up_val).astype(BF16)
    grad_hidden = dot(cotangent, down_weight, 1, 1)
    grad_gate = (grad_hidden * up_val * gate_sig * (1.0 + gate_val * (1.0 - gate_sig))).astype(BF16)
    grad_up = (grad_hidden * gate_act).astype(BF16)
    ffn_part = dot(hidden, down_weight).astype(BF16)
    back_part = (dot(grad_gate, gate_weight, 1, 1) + dot(grad_up, up_weight, 1, 1)).astype(BF16)
    sums = head_sum(jnp.concatenate([back_part, ffn_part], 0), 5).astype(F32)
    output = (hidden_in + sums[ROWS:]).astype(BF16)
    grad_from_two, grad_gain_two = norm_two_back(sums[:ROWS])
    grad_hidden_in = grad_from_two + cotangent.astype(F32)
    grad_mix = grad_hidden_in.astype(BF16)
    ffn_w = weight_gradients(
        [normed_two.T, cotangent.T], [[grad_gate, grad_up], [hidden]], 6, "ffn_weights"
    )

    grad_gated = dot(grad_mix, out_weight, 1, 1)
    grad_attended = (
        dot(grad_mix, attn_weight, 1, 1).astype(BF16).reshape(ROWS, q_heads, HEAD_DIM)
        .transpose(1, 0, 2).reshape(q_heads * ROWS, HEAD_DIM)
    )
    z_sig = jax.nn.sigmoid(z_val)
    grad_z = (grad_gated * ssm_out * z_sig * (1.0 + z_val * (1.0 - z_sig))).astype(BF16)
    grad_ssm = (grad_gated * z_gate).reshape(ROWS, heads, SSM_DIM)
    grad_skip = jnp.sum(grad_ssm * x_heads, (0, 2))
    out_grads = output_back(grad_ssm)
    state_grad = scan_states(out_grads[5], through, True, 7)
    grad_through = jnp.sum(state_grad * state_in, (1, 2))
    state_grads = state_part_back((state_grad, grad_through))
    grad_cb = out_grads[2]
    grad_b = state_grads[2] + jnp.dot(grad_cb.T, c_matrix, precision=HIGHEST)
    grad_c = out_grads[3] + jnp.dot(grad_cb, b_matrix, precision=HIGHEST)
    grad_x_heads = out_grads[0] + state_grads[0] + skip_gain[None, :, None] * grad_ssm
    grad_rate = out_grads[4] + state_grads[3]
    grad_dt_pre = (out_grads[1] + state_grads[1]) * jax.nn.sigmoid(dt_pre)
    grad_dt_raw = grad_dt_pre.astype(BF16)
    grad_bias = jnp.sum(grad_dt_pre, 0)
    shares = jnp.concatenate([grad_b, grad_c], -1).astype(BF16)
    shares = shares.reshape(ROWS, 4, 128).transpose(1, 0, 2)
    grad_bc_act = head_share(shares, 8)
    grad_x_ext, grad_x_conv = x_conv_back(grad_x_heads.reshape(ROWS, inner))
    grad_bc_ext, grad_bc_conv = bc_conv_back(grad_bc_act)
    edge_back = jnp.pad(
        jnp.concatenate([grad_x_ext[:edge_rows], grad_bc_ext[:edge_rows]], 1),
        ((0, 8 - edge_rows), (0, 0)),
    )
    delta = jnp.sum(grad_attended.astype(F32) * attended, 1)
    delta = jnp.broadcast_to(delta, (8, q_heads * ROWS))
    grad_query, grad_kv, edge_next = attention_backward(
        queries, grad_attended, lse, delta, seg_row, kv_all, edge_back
    )
    edge_next = edge_next[:edge_rows]
    grad_x_pre = grad_x_ext[edge_rows:].at[-edge_rows:].add(edge_next[:, :inner]).astype(BF16)
    grad_bc_low = grad_bc_ext[edge_rows:].at[-edge_rows:].add(edge_next[:, inner:]).astype(BF16)
    score_scale = HEAD_DIM**-0.5
    grad_query = (grad_query * score_scale).reshape(q_heads, ROWS, HEAD_DIM).transpose(1, 0, 2)
    grad_query_raw = (
        rope_turn(grad_query, cosine[:, None, :], -sine[:, None, :]).astype(BF16)
        .reshape(ROWS, q_heads * HEAD_DIM)
    )
    grad_kv_low = jnp.where(
        c == 0, rope_turn(grad_kv * score_scale, cosine, -sine), grad_kv
    ).astype(BF16)
    bc_columns = lax.dynamic_slice_in_dim(bc_weight, bc_at, 128, 1)
    back_part = (
        dot(grad_x_pre, x_weight, 1, 1)
        + dot(grad_z, z_weight, 1, 1)
        + dot(grad_dt_raw, dt_weight, 1, 1)
        + dot(grad_query_raw, query_weight, 1, 1)
        + dot(grad_bc_low, bc_columns, 1, 1)
        + dot(grad_kv_low, kv_columns, 1, 1)
    )
    grad_normed = head_sum(back_part.astype(BF16), 9).astype(F32)
    grad_from_one, grad_gain_one = norm_back(grad_normed)
    grad_tokens = grad_hidden_in + grad_from_one
    dt_wide = jnp.pad(grad_dt_raw, ((0, 0), (0, WIDE - heads)))
    mixer_w = weight_gradients(
        [normed.T, grad_mix.T],
        [
            [grad_x_pre, grad_z, grad_query_raw, grad_bc_low, grad_kv_low, dt_wide],
            [gated, attended_low],
        ],
        10,
        "mixer_weights",
    )
    quarter = MODEL // 4
    small = [
        grad_x_conv, grad_bc_conv, grad_bias, grad_rate, grad_skip,
        lax.dynamic_slice_in_dim(grad_gain_one, head_index * quarter, quarter),
        lax.dynamic_slice_in_dim(grad_gain_two, head_index * quarter, quarter),
    ]
    flat = jnp.concatenate([a.reshape(-1) for a in small])
    flat = jnp.pad(flat, (0, BLOCKS * SMALL - flat.size)).reshape(BLOCKS, 8, 128)
    at = [0, inner, 2 * inner, 2 * inner + 256, 2 * inner + 512, 2 * inner + 768]
    gathered = gather_replicated(mixer_w[:, at[3] : at[4]], flat, 11)
    gathered = gathered.reshape(2, 2, BLOCKS, TAIL, 256).astype(F32)
    bc_w = gathered[:, :, :, :64, :128].transpose(2, 3, 1, 0, 4).reshape(MODEL, 512)
    kv_w = gathered[:, :, :, :64, 128:].transpose(2, 3, 0, 1, 4).reshape(MODEL, 512)
    total = gathered[:, :, :, 64:72, :128].transpose(1, 0, 2, 3, 4).reshape(4, BLOCKS * SMALL)
    pieces, start = [], 0
    for a in small:
        pieces.append(total[:, start : start + a.size].reshape(4, *a.shape))
        start += a.size
    x_conv_sum = pieces[0].transpose(1, 0, 2).reshape(CONV, 4 * inner)
    bc_conv_sum = pieces[1].transpose(1, 0, 2).reshape(CONV, 512)
    bias_sum, rate_sum, skip_sum, gain_one_sum, gain_two_sum = (p.reshape(-1) for p in pieces[2:])
    ff = gate_weight.shape[1]
    return (
        output,
        grad_tokens,
        gain_one_sum,
        mixer_w[:, : at[1]],
        mixer_w[:, at[1] : at[2]],
        bc_w,
        mixer_w[:, at[4] : at[4] + heads],
        x_conv_sum,
        bc_conv_sum,
        bias_sum,
        rate_sum,
        skip_sum,
        mixer_w[:, at[5] : at[5] + inner].T,
        mixer_w[:, at[2] : at[3]],
        kv_w,
        mixer_w[:, at[5] + inner :].T,
        gain_two_sum,
        ffn_w[:, :ff],
        ffn_w[:, ff : 2 * ff],
        ffn_w[:, 2 * ff :].T,
    )


def solution(mesh):
    split = Mesh(mesh.devices.reshape(NZ, NX, NY, 2, 2), (*SEQ, "zh", "c"))
    head = ("zh", "c")
    rows, columns, both, turned = P(SEQ, None), P(None, head), P(SEQ, head), P(head, SEQ)
    return jax.shard_map(
        on_device,
        mesh=split,
        in_specs=(
            rows, P(SEQ), rows, P(), columns, columns, P(), columns, columns, P(), P(head),
            P(head), P(head), P(head, None), columns, P(), P(head, None), P(), columns, columns,
            P(head, None),
        ),
        out_specs=(
            rows, rows, P(), both, both, P(), both, P(), P(), P(), P(), P(), turned, both, P(),
            turned, P(), both, both, turned,
        ),
        check_vma=False,
    )
```

```python
import functools

import jax
import jax.numpy as jnp
from jax import lax
from jax.experimental import pallas as pl
from jax.experimental.pallas import tpu as pltpu
from jax.sharding import Mesh
from jax.sharding import PartitionSpec as P

SSM_DIM = 64
STATE = 256
CONV = 4
KVHEADS = 2
HEAD_DIM = 128
NZ, NX, NY = 2, 4, 4
BLOCKS = NZ * NX * NY
CHIPS = 2 * BLOCKS
ROWS = 256
MODEL = 2048
SEQ = ("zl", "x", "y")
EPSILON = 1e-05
ROPE_BASE = 100000000000.0
HIGHEST = lax.Precision.HIGHEST
MESH = pl.DeviceIdType.MESH
BF16, F32 = jnp.bfloat16, jnp.float32
MASKED = -1e30
LOG2E = 1.4426950408889634
VMEM_LIMIT = 56 * 2**20


def block_index():
    return (lax.axis_index("zl") * NX + lax.axis_index("x")) * NY + lax.axis_index("y")


def block_at(s):
    return {"zl": s // (NX * NY), "x": (s // NY) % NX, "y": s % NY}


PLANE = NX * NY


def plane_shift(k):
    o = 1 + (k * 7) % (PLANE - 1)
    return o // NY, o % NY


def plane_peer(k, sign):
    dx, dy = plane_shift(k)
    x, y = lax.axis_index("x"), lax.axis_index("y")
    if sign < 0:
        dx, dy = NX - dx, NY - dy
    x, y = (x + dx) % NX, (y + dy) % NY
    return x * NY + y, {"x": x, "y": y}


def signal(sem, where):
    pl.semaphore_signal(sem, inc=1, device_id=where, device_id_type=MESH)


def remote(src, dst, send, recv, where):
    return pltpu.make_async_remote_copy(src, dst, send, recv, device_id=where, device_id_type=MESH)


def over(start, stop, body):
    def step(i, carry):
        body(i)
        return carry

    lax.fori_loop(start, stop, step, 0)


def dot(a, b, left=1, right=0):
    return lax.dot_general(
        a, b, (((left,), (right,)), ((), ())), preferred_element_type=F32
    )


def vmem(n):
    return [pl.BlockSpec(memory_space=pltpu.VMEM)] * n


def params(collective_id):
    return pltpu.CompilerParams(
        collective_id=collective_id, has_side_effects=True, vmem_limit_bytes=VMEM_LIMIT
    )


HEADS = 12
INNER = HEADS * SSM_DIM
GROUPS = INNER // 128
BC = 2 * STATE
SCAN_ROWS = INNER // BLOCKS
EDGE_WIDE = INNER + BC + 128
GRAD_EDGE = INNER + 128


def two_parts(v):
    high = v.astype(BF16)
    return high, (v - high.astype(F32)).astype(BF16)


def low_lanes(rows):
    return lax.broadcasted_iota(jnp.int32, (rows, 128), 1) < SSM_DIM


def widen(v, g):
    low = low_lanes(v.shape[0])
    return jnp.where(low, v[:, 2 * g : 2 * g + 1], v[:, 2 * g + 1 : 2 * g + 2])


def per_head(v, g):
    lane = lax.broadcasted_iota(jnp.int32, v.shape, 1)
    first = jnp.sum(jnp.where(lane < SSM_DIM, v, 0.0), 1, keepdims=True)
    second = jnp.sum(jnp.where(lane < SSM_DIM, 0.0, v), 1, keepdims=True)
    return jnp.where(lane == 2 * g, first, jnp.where(lane == 2 * g + 1, second, 0.0))


def triangle():
    row = lax.broadcasted_iota(jnp.int32, (ROWS, ROWS), 0)
    col = lax.broadcasted_iota(jnp.int32, (ROWS, ROWS), 1)
    return (col <= row).astype(F32).astype(BF16)


def running(v, lower, side):
    high, low = two_parts(v)
    middle, lowest = two_parts(v - high.astype(F32))
    return (
        dot(lower, high, side, 0) + dot(lower, middle, side, 0) + dot(lower, lowest, side, 0)
    )


def sigmoid(v):
    return 1.0 / (1.0 + jnp.exp(-v))


def softplus(v):
    return jnp.maximum(v, 0.0) + jnp.log(1.0 + jnp.exp(-jnp.abs(v)))


def lane_block(g):
    return pl.ds(pl.multiple_of(g * 128, 128), 128)


def decays(dt_ref, vec_ref, seg_ref, segx_ref, lower):
    pre = dt_ref[...] + vec_ref[0:1, :]
    step = softplus(pre)
    total = running(-step * vec_ref[1:2, :] * LOG2E, lower, 1)
    last = total[ROWS - 1 : ROWS, :]
    seg = seg_ref[...]
    seg_last, before = seg[ROWS - 1 : ROWS, :], segx_ref[7:8, :]
    carry = jnp.where(seg == seg_last, jnp.exp2(last - total), 0.0)
    entry = jnp.where(seg == before, jnp.exp2(total), 0.0)
    through = jnp.where(seg_last == before, jnp.exp2(last), 0.0)
    return pre, step, total, carry, entry, through


def conv_group(ext_ref, segx_ref, seg_ref, taps_ref, cols):
    total, inputs = None, []
    for k in range(CONV):
        same = segx_ref[pl.ds(5 + k, ROWS), :] == seg_ref[...]
        v = jnp.where(same, ext_ref[pl.ds(5 + k, ROWS), cols], 0.0)
        inputs.append(v)
        term = taps_ref[k : k + 1, cols] * v
        total = term if total is None else total + term
    return total, inputs


def scan_message(msg_ref, state_ref, through):
    high = through.astype(BF16)
    rest = through - high.astype(F32)
    middle = rest.astype(BF16)
    low = rest - middle.astype(F32)
    extra = jnp.concatenate([high.astype(F32), middle.astype(F32), low, jnp.zeros((5, 128), F32)], 0)
    extra = jnp.concatenate([extra, jnp.zeros((8, STATE - 128), F32)], 1)

    def fill(b):
        rows = state_ref[pl.ds(pl.multiple_of(b * SCAN_ROWS, 8), SCAN_ROWS), :]
        msg_ref[b] = jnp.concatenate([rows, extra], 0).astype(BF16)

    over(0, BLOCKS, fill)


class Scan:
    def __init__(self, reverse, me, msg, got, back, out, send, recv):
        self.reverse, self.me = reverse, me
        self.msg, self.got, self.back, self.out = msg, got, back, out
        self.send, self.recv = send, recv

    def there(self, o):
        d = (self.me + o) % BLOCKS
        return remote(
            self.msg.at[d], self.got.at[self.me], self.send.at[0, o], self.recv.at[0, o],
            block_at(d),
        )

    def arrived(self, phase, dst, o):
        s = (self.me + BLOCKS - o) % BLOCKS
        return remote(
            dst.at[s], dst.at[s], self.send.at[phase, o], self.recv.at[phase, o], block_at(s)
        )

    def start(self):
        over(1, BLOCKS, lambda o: self.there(o).start())
        self.got[self.me] = self.msg[self.me]

    def turn(self):
        me = self.me
        over(1, BLOCKS, lambda o: self.arrived(0, self.got, o).wait_recv())
        lane = lax.broadcasted_iota(jnp.int32, (SCAN_ROWS, 128), 1)
        row = lax.broadcasted_iota(jnp.int32, (SCAN_ROWS, 128), 0) + me * SCAN_ROWS
        at_head = (row >= lane * SSM_DIM) & (row < lane * SSM_DIM + SSM_DIM)

        def scan(i, state):
            k = BLOCKS - 1 - i if self.reverse else i
            message = self.got[k].astype(F32)
            self.back[k] = jnp.concatenate([state, jnp.zeros((8, STATE), F32)], 0).astype(BF16)

            @pl.when(k != me)
            def _():
                self.returned(k).start()

            factors = message[SCAN_ROWS : SCAN_ROWS + 1, :128]
            factors += message[SCAN_ROWS + 1 : SCAN_ROWS + 2, :128]
            factors += message[SCAN_ROWS + 2 : SCAN_ROWS + 3, :128]
            through = jnp.sum(jnp.where(at_head, factors, 0.0), 1, keepdims=True)
            return through * state + message[:SCAN_ROWS]

        lax.fori_loop(0, BLOCKS, scan, jnp.zeros((SCAN_ROWS, STATE), F32))
        self.out[me] = self.back[me]

    def returned(self, k):
        o = (k + BLOCKS - self.me) % BLOCKS
        return remote(
            self.back.at[k], self.out.at[self.me], self.send.at[1, o], self.recv.at[1, o],
            block_at(k),
        )

    def finish(self, state_ref):
        over(1, BLOCKS, lambda o: self.arrived(1, self.out, o).wait_recv())

        def fill(b):
            rows = self.out[b].astype(F32)
            state_ref[pl.ds(pl.multiple_of(b * SCAN_ROWS, 8), SCAN_ROWS), :] = rows[:SCAN_ROWS]

        over(0, BLOCKS, fill)

    def close(self):
        def sent(o):
            self.there(o).wait_send()
            self.returned((self.me + o) % BLOCKS).wait_send()

        over(1, BLOCKS, sent)


def key_segments(block):
    turned = jnp.transpose(block.astype(F32))
    return jnp.concatenate([turned[:, 0:1], turned[:, 1:2]], 0)


def causal_mask(s):
    row = lax.broadcasted_iota(jnp.int32, (ROWS, 2 * ROWS), 0)
    col = lax.broadcasted_iota(jnp.int32, (ROWS, 2 * ROWS), 1) % ROWS
    return jnp.where(row <= col, s, MASKED)


def mixing_bias(seg_ref, segrow_ref):
    row = lax.broadcasted_iota(jnp.int32, (ROWS, ROWS), 0)
    col = lax.broadcasted_iota(jnp.int32, (ROWS, ROWS), 1)
    same = segrow_ref[0:1, :ROWS] == seg_ref[:, 0:1]
    return jnp.where((col <= row) & same, 0.0, MASKED)


WIDE = 256
LAG = 3
OWN = MODEL // NZ


class Reduce:
    def __init__(self, lefts, n, r_ref, rz, part, gx, half, gy, out_ref, sems):
        self.lefts, self.n = lefts, n
        self.r, self.rz, self.part, self.gx, self.half, self.gy = r_ref, rz, part, gx, half, gy
        self.out = out_ref
        (self.rz_send, self.rz_recv, self.gx_send, self.gx_recv, self.gy_send, self.gy_recv) = sems
        self.zl, self.x, self.y = (lax.axis_index(a) for a in SEQ)
        self.other = {"zl": 1 - self.zl}

    @staticmethod
    def scratch(n):
        v, dma = pltpu.VMEM, pltpu.SemaphoreType.DMA
        return [
            v((n, ROWS, WIDE), BF16),
            v((n, ROWS, WIDE), BF16),
            v((n, 4, 4, 64, WIDE), BF16),
            v((n, 3, 4, 64, WIDE), BF16),
            v((n, 4, 64, WIDE), BF16),
            v((n, 3, 64, WIDE), BF16),
            *[dma((n,))] * 6,
        ]

    def fill(self, arrays):
        c = 0
        for ref in arrays:
            for k in range(ref.shape[1] // WIDE):
                self.r[c] = ref[:, k * WIDE : (k + 1) * WIDE]
                c += 1

    def right(self, c):
        return remote(
            self.r.at[c], self.rz.at[c], self.rz_send.at[c], self.rz_recv.at[c], self.other
        )

    def start(self):
        over(0, self.n, lambda c: self.right(c).start())

    def spread(self, c, phase, o):
        along_x = c % 2 == phase
        x_to = jnp.where(along_x, (self.x + o) % NX, self.x)
        y_to = jnp.where(along_x, self.y, (self.y + o) % NY)
        return {"x": x_to, "y": y_to}, jnp.where(along_x, x_to, y_to)

    def send_first(self, c, o):
        where, d = self.spread(c, 0, o)
        return remote(
            self.part.at[c, d], self.gx.at[c, o - 1], self.gx_send.at[c], self.gx_recv.at[c], where
        )

    def send_second(self, c, o):
        where, d = self.spread(c, 1, o)
        return remote(
            self.half.at[c, d], self.gy.at[c, o - 1], self.gy_send.at[c], self.gy_recv.at[c], where
        )

    def whole(self, got, send, recv, c):
        return remote(got.at[c], got.at[c], send.at[c], recv.at[c], self.other)

    def product(self, c):
        self.right(c).wait_recv()
        mine, theirs = self.r[c], self.rz[c]
        even = c % 2 == 0
        ends = [first for _, _, first in self.lefts[1:]] + [self.n]
        for (own, near, first), end in zip(self.lefts, ends):
            @pl.when((c >= first) & (c < end))
            def _():
                for i in range(NX):
                    a = own[pl.ds(pl.multiple_of(self.zl * OWN + i * 256, 256), 256), :]
                    b = near[pl.ds(i * 256, 256), :]
                    tile = (dot(a, mine) + dot(b, theirs)).astype(BF16)
                    for j in range(NY):
                        self.part[c, jnp.where(even, i, j), jnp.where(even, j, i)] = (
                            tile[j * 64 : (j + 1) * 64]
                        )
        for o in range(1, 4):
            self.send_first(c, o).start()

    def middle(self, c):
        self.whole(self.gx, self.gx_send, self.gx_recv, c).wait_recv()
        mine = jnp.where(c % 2 == 0, self.x, self.y)
        for j in range(4):
            total = self.part[c, mine, j].astype(F32)
            for o in range(3):
                total += self.gx[c, o, j].astype(F32)
            self.half[c, j] = total.astype(BF16)
        for o in range(1, 4):
            self.send_second(c, o).start()

    def last(self, c):
        self.whole(self.gy, self.gy_send, self.gy_recv, c).wait_recv()
        mine = jnp.where(c % 2 == 0, self.y, self.x)
        total = self.half[c, mine].astype(F32)
        for o in range(3):
            total += self.gy[c, o].astype(F32)
        self.out[:, pl.ds(pl.multiple_of(c * WIDE, WIDE), WIDE)] = total

    @property
    def steps(self):
        return self.n + 2 * LAG

    def step(self, i):
        @pl.when(i < self.n)
        def _():
            self.product(i)

        @pl.when((i >= LAG) & (i < self.n + LAG))
        def _():
            self.middle(i - LAG)

        @pl.when(i >= 2 * LAG)
        def _():
            self.last(i - 2 * LAG)

    def close(self):
        def sent(c):
            self.right(c).wait_send()
            self.whole(self.gx, self.gx_send, self.gx_recv, c).wait_send()
            self.whole(self.gy, self.gy_send, self.gy_recv, c).wait_send()

        over(0, self.n, sent)


class Left:
    def __init__(self, l_ref, lz, sems):
        zl, c = lax.axis_index("zl"), lax.axis_index("c")
        half = OWN // 2
        there = pl.ds(pl.multiple_of((1 - zl) * OWN + c * half, half), half)
        near, other = (pl.ds(pl.multiple_of(k * half, half), half) for k in (c, 1 - c))
        sem = [sems.at[k] for k in range(4)]
        self.out = remote(l_ref.at[there], lz.at[near], sem[0], sem[1], {"zl": 1 - zl})
        self.on = remote(lz.at[near], lz.at[near], sem[2], sem[3], {"c": 1 - c})
        self.back = remote(lz.at[other], lz.at[other], sem[2], sem[3], {"c": 1 - c})

    def start(self):
        self.out.start()

    def pass_on(self):
        self.out.wait_recv()
        self.on.start()

    def finish(self):
        self.back.wait_recv()

    def close(self):
        self.out.wait_send()
        self.on.wait_send()


HEAD_CHUNKS = 4


class HeadSum:
    def __init__(self, x, out, near, pair, far, sems):
        self.x, self.out, self.near, self.pair, self.far = x, out, near, pair, far
        self.near_send, self.near_recv, self.far_send, self.far_recv, self.end_send, self.end_recv = sems
        self.c, zh = lax.axis_index("c"), lax.axis_index("zh")
        self.sibling, self.opposite = {"c": 1 - self.c}, {"zh": 1 - zh}
        self.half = x.shape[0] // 2
        self.rows_each = self.half // HEAD_CHUNKS

    @staticmethod
    def scratch():
        v, dma = pltpu.VMEM, pltpu.SemaphoreType.DMA
        return [*[v((ROWS // 2, MODEL), BF16)] * 3, *[dma((HEAD_CHUNKS,))] * 6]

    def rows(self, core, k):
        return pl.ds(pl.multiple_of(core * self.half + k * self.rows_each, 16), self.rows_each)

    def local(self, k):
        return pl.ds(k * self.rows_each, self.rows_each)

    def first(self, k):
        return remote(
            self.x.at[self.rows(1 - self.c, k)], self.near.at[self.local(k)],
            self.near_send.at[k], self.near_recv.at[k], self.sibling,
        )

    def second(self, k):
        return remote(
            self.pair.at[self.local(k)], self.far.at[self.local(k)],
            self.far_send.at[k], self.far_recv.at[k], self.opposite,
        )

    def third(self, k, core):
        rows = self.rows(core, k)
        return remote(
            self.out.at[rows], self.out.at[rows], self.end_send.at[k], self.end_recv.at[k],
            self.sibling,
        )

    def start(self):
        for k in range(HEAD_CHUNKS):
            self.first(k).start()

    def across(self):
        for k in range(HEAD_CHUNKS):
            self.first(k).wait_recv()
            own = self.x[self.rows(self.c, k)].astype(F32)
            self.pair[self.local(k)] = (own + self.near[self.local(k)].astype(F32)).astype(BF16)
            self.second(k).start()

    def join(self):
        for k in range(HEAD_CHUNKS):
            self.second(k).wait_recv()
            total = self.pair[self.local(k)].astype(F32) + self.far[self.local(k)].astype(F32)
            self.out[self.rows(self.c, k)] = total.astype(BF16)
            self.third(k, self.c).start()

    def finish(self):
        for k in range(HEAD_CHUNKS):
            self.third(k, 1 - self.c).wait_recv()

    def close(self):
        for k in range(HEAD_CHUNKS):
            self.first(k).wait_send()
            self.second(k).wait_send()
            self.third(k, self.c).wait_send()


def head_sum_kernel(x_ref, out_ref, *scratch):
    total = HeadSum(x_ref, out_ref, *scratch[:3], scratch[3:])
    barrier = pltpu.get_barrier_semaphore()
    signal(barrier, total.sibling)
    signal(barrier, total.opposite)
    pl.semaphore_wait(barrier, 2)
    total.start()
    total.across()
    total.join()
    total.finish()
    total.close()


def head_sum(x, collective_id):
    return pl.pallas_call(
        head_sum_kernel,
        name=f"head_sum_{collective_id}",
        out_shape=jax.ShapeDtypeStruct(x.shape, BF16),
        in_specs=vmem(1),
        out_specs=vmem(1)[0],
        scratch_shapes=HeadSum.scratch(),
        compiler_params=params(collective_id),
    )(x)


EARLY = 6


def mixer_forward_kernel(
    q_ref, own_ref, edge_ref, x_ref, bc_ref, dt_ref, z_ref, seg_ref, segrow_ref, xtaps_ref,
    bctaps_ref, vec_ref, skip_ref, nt_ref, ct_ref,
    att_ref, lse_ref, kv_ref, edge_out, gated_ref, core_ref, xact_ref, bcact_ref, state_ref,
    ntz_ref, ctz_ref,
    m_ref, l_ref, acc_ref, xext, bcext, segx, local, msg, got, back, result, bias_ref, cb_ref,
    cumt_ref,
    send_sem, recv_sem, sib_send, sib_recv, edge_sem, scan_send, scan_recv, left_sem,
):
    me, c, zl = block_index(), lax.axis_index("c"), lax.axis_index("zl")
    at = me % PLANE
    sibling = {"c": 1 - c}
    barrier = pltpu.get_barrier_semaphore()
    over(1, BLOCKS, lambda o: signal(barrier, block_at((me + o) % BLOCKS)))
    signal(barrier, sibling)
    pl.semaphore_wait(barrier, BLOCKS)

    def block_copy(src, j, send, where):
        return remote(src, kv_ref.at[c, j], send_sem.at[send], recv_sem.at[j], where)

    def arrival(j):
        return block_copy(own_ref, j, 0, sibling)

    to_sibling = lambda j, src: remote(
        src, kv_ref.at[c, j], sib_send.at[j], sib_recv.at[j], sibling
    )
    from_sibling = lambda j: remote(
        kv_ref.at[1 - c, j], kv_ref.at[1 - c, j], sib_send.at[j], sib_recv.at[j], sibling
    )
    across = block_copy(own_ref, me, PLANE - 1, {"zl": 1 - zl})

    def own_copy(k, wait):
        d, where = plane_peer(k, 1)

        @pl.when(d > at)
        def _():
            copy = block_copy(own_ref, me, k, where)
            copy.wait_send() if wait else copy.start()

    def relay_copy(k, wait):
        copy = block_copy(kv_ref.at[c, at], at, PLANE + k, plane_peer(k, 1)[1])
        copy.wait_send() if wait else copy.start()

    edge_copy = remote(
        edge_ref, edge_out, edge_sem.at[0], edge_sem.at[1], block_at((me + 1) % BLOCKS)
    )
    states = Scan(False, me, msg, got, back, result, scan_send, scan_recv)

    @pl.when(me < BLOCKS - 1)
    def _():
        edge_copy.start()

    @pl.when(zl == 0)
    def _():
        across.start()

    to_sibling(me, own_ref).start()
    over(0, EARLY, lambda k: own_copy(k, False))
    lefts = [Left(ct_ref, ctz_ref, left_sem.at[0]), Left(nt_ref, ntz_ref, left_sem.at[1])]

    kv_ref[c, me] = own_ref[...]
    xext[8:, :] = x_ref[...].astype(F32)
    bcext[8:, :] = bc_ref[...].astype(F32)
    segx[8:, :] = seg_ref[...]
    lower = triangle()
    bias_ref[...] = mixing_bias(seg_ref, segrow_ref)

    @pl.when(me > 0)
    def _():
        edge_copy.wait_recv()

    @pl.when(me == 0)
    def _():
        edge_out[...] = jnp.zeros_like(edge_out)

    edge = edge_out[...].astype(F32)[8:]
    xext[:8, :] = edge[:, :INNER]
    bcext[:8, :] = edge[:, INNER : INNER + BC]
    segx[:8, :] = edge[:, INNER + BC :]

    def activate(ext, taps, out):
        def group(g):
            pre, _ = conv_group(ext, segx, seg_ref, taps, lane_block(g))
            out[:, lane_block(g)] = (pre * sigmoid(pre)).astype(BF16)

        over(0, out.shape[1] // 128, group)

    activate(bcext, bctaps_ref, bcact_ref)
    activate(xext, xtaps_ref, xact_ref)

    _, step, total, carry, entry, through = decays(dt_ref, vec_ref, seg_ref, segx, lower)
    cumt_ref[...] = jnp.transpose(total)
    weight = step * carry
    b_low, c_low = bcact_ref[:, :STATE], bcact_ref[:, STATE:]
    for g in range(GROUPS):
        moved = xact_ref[:, g * 128 : (g + 1) * 128].astype(F32) * widen(weight, g)
        local[g * 128 : (g + 1) * 128, :] = dot(moved.astype(BF16), b_low, 0, 0)
    scan_message(msg, local, through)
    states.start()
    over(EARLY, PLANE - 1, lambda k: own_copy(k, False))

    @pl.when(zl == 1)
    def _():
        arrival(at).wait_recv()
        to_sibling(at, kv_ref.at[c, at]).start()
        over(0, PLANE - 1, lambda k: relay_copy(k, False))

    cb_ref[...] = dot(c_low, b_low, 1, 1)
    low_lane = lax.broadcasted_iota(jnp.int32, (ROWS, 128), 1) < SSM_DIM
    for g in range(GROUPS):
        cols = slice(g * 128, (g + 1) * 128)
        u = (xact_ref[:, cols].astype(F32) * widen(step, g)).astype(BF16)
        made = []
        for h in (2 * g, 2 * g + 1):
            gap = total[:, h : h + 1] - cumt_ref[h : h + 1, :] + bias_ref[...]
            made.append(dot((jnp.exp2(gap) * cb_ref[...]).astype(BF16), u))
        core_ref[:, cols] = jnp.where(low_lane, made[0], made[1])

    scale = LOG2E * HEAD_DIM**-0.5
    queries = q_ref[...]
    qseg = segrow_ref[0:1, :]

    def scores_of(j):
        s = dot(kv_ref[0, j, :ROWS], queries, 1, 1) * scale
        return jnp.where(key_segments(kv_ref[0, j, ROWS:]) == qseg, s, MASKED)

    from_sibling(me).wait_recv()
    s = causal_mask(scores_of(me))
    m = jnp.max(s, 0, keepdims=True)
    p = jnp.exp2(s - m)
    m_ref[...] = m
    l_ref[...] = jnp.sum(p, 0, keepdims=True)
    acc_ref[...] = dot(kv_ref[1, me, :ROWS], p.astype(BF16), 0, 0)

    states.turn()
    for left in lefts:
        left.start()

    def forward(k):
        q, _ = plane_peer(k, -1)

        def one(j):
            arrival(j).wait_recv()
            to_sibling(j, kv_ref.at[c, j]).start()

        pl.when(q < at)(lambda: one(zl * PLANE + q))
        pl.when(zl == 1)(lambda: one(q))

    def attend(j):
        from_sibling(j).wait_recv()
        s = scores_of(j)
        m_old = m_ref[...]
        m = jnp.maximum(m_old, jnp.max(s, 0, keepdims=True))
        p = jnp.exp2(s - m)
        alpha = jnp.exp2(m_old - m)
        m_ref[...] = m
        l_ref[...] = l_ref[...] * alpha + jnp.sum(p, 0, keepdims=True)
        acc_ref[...] = acc_ref[...] * alpha + dot(kv_ref[1, j, :ROWS], p.astype(BF16), 0, 0)

    forward(0)

    @pl.when(zl == 1)
    def _():
        attend(at)

    def step_over(k):
        @pl.when(k + 1 < PLANE - 1)
        def _():
            forward(k + 1)

        q, _ = plane_peer(k, -1)
        pl.when(q < at)(lambda: attend(zl * PLANE + q))
        pl.when(zl == 1)(lambda: attend(q))

    over(0, PLANE - 1, step_over)
    for left in lefts:
        left.pass_on()
    att_ref[...] = jnp.transpose(acc_ref[...] / l_ref[...])
    lse_ref[...] = jnp.broadcast_to(m_ref[...] + jnp.log2(l_ref[...]), lse_ref.shape)

    states.finish(state_ref)
    for g in range(GROUPS):
        cols = slice(g * 128, (g + 1) * 128)
        outer = dot(c_low, state_ref[cols, :].astype(BF16), 1, 1) * widen(entry, g)
        core = core_ref[:, cols] + outer
        core_ref[:, cols] = core
        out = core + skip_ref[0:1, cols] * xact_ref[:, cols].astype(F32)
        z = z_ref[:, cols]
        gated_ref[:, cols] = (out * z * sigmoid(z)).astype(BF16)

    states.close()
    for left in lefts:
        left.finish()
        left.close()
    to_sibling(me, own_ref).wait_send()
    over(0, PLANE - 1, lambda k: own_copy(k, True))

    @pl.when(zl == 0)
    def _():
        across.wait_send()

    @pl.when(zl == 1)
    def _():
        over(0, PLANE - 1, lambda k: relay_copy(k, True))
        over(0, PLANE, lambda j: to_sibling(j, own_ref).wait_send())

    over(0, at, lambda q: to_sibling(zl * PLANE + q, own_ref).wait_send())

    @pl.when(me < BLOCKS - 1)
    def _():
        edge_copy.wait_send()


def mixer_forward(*args):
    wide = 2 * ROWS
    s = jax.ShapeDtypeStruct
    dma = pltpu.SemaphoreType.DMA
    return pl.pallas_call(
        mixer_forward_kernel,
        name="mixer_forward",
        out_shape=(
            s((wide, HEAD_DIM), F32),
            s((8, wide), F32),
            s((2, BLOCKS, ROWS + 16, HEAD_DIM), BF16),
            s((16, EDGE_WIDE), BF16),
            s((ROWS, INNER), BF16),
            s((ROWS, INNER), F32),
            s((ROWS, INNER), BF16),
            s((ROWS, BC), BF16),
            s((INNER, STATE), F32),
            s((OWN, ROWS), BF16),
            s((OWN, ROWS), BF16),
        ),
        in_specs=vmem(len(args)),
        out_specs=tuple(vmem(11)),
        scratch_shapes=[
            pltpu.VMEM((1, wide), F32),
            pltpu.VMEM((1, wide), F32),
            pltpu.VMEM((HEAD_DIM, wide), F32),
            pltpu.VMEM((ROWS + 8, INNER), F32),
            pltpu.VMEM((ROWS + 8, BC), F32),
            pltpu.VMEM((ROWS + 8, 128), F32),
            pltpu.VMEM((INNER, STATE), F32),
            *[pltpu.VMEM((BLOCKS, SCAN_ROWS + 8, STATE), BF16)] * 4,
            pltpu.VMEM((ROWS, ROWS), F32),
            pltpu.VMEM((ROWS, ROWS), F32),
            pltpu.VMEM((128, ROWS), F32),
            *[dma((BLOCKS,))] * 4,
            dma((2,)),
            dma((2, BLOCKS)),
            dma((2, BLOCKS)),
            dma((2, 4)),
        ],
        compiler_params=params(1),
    )(*args)


def mixer_backward_kernel(
    q_ref, do_ref, att_ref, lse_ref, segrow_ref, kv_ref, gg_ref, z_ref, core_ref, xact_ref,
    bcact_ref, x_ref, bcown_ref, edge_in, dt_ref, state_ref, seg_ref, xtaps_ref, bctaps_ref,
    vec_ref, skip_ref, dgate_ref, dup_ref, hidden_ref, ft_ref, ct_ref, ctz_ref, mt_ref,
    dq_ref, dkv_ref, dz_ref, dx_ref, dbc_ref, ddt_ref, dxtaps_ref, dbctaps_ref, dvec_ref,
    w_ref, mtz_ref,
    dqt_ref, mine, theirs, sib, kvgot, relay_ref, total_ref, xext, bcext, segx, local, msg, got, back, result,
    bias_ref, cb_ref, cumt_ref, g_ref, du_ref, dbc_all, shares, share_got, edge_ref,
    edge_out, enter_ref, gext, dcum_ref, ddtx_ref,
    send_sem, recv_sem, sib_send, sib_recv, edge_sem, scan_send, scan_recv, share_send, share_recv,
    ftz_ref, left_sem, *reduce,
):
    me, c, zh, zl = block_index(), *(lax.axis_index(a) for a in ("c", "zh", "zl"))
    head_at = zh * 2 + c
    sibling = {"c": 1 - c}
    at_head = lambda d: {"zh": d // 2, "c": d % 2}
    barrier = pltpu.get_barrier_semaphore()
    over(1, BLOCKS, lambda o: signal(barrier, block_at((me + o) % BLOCKS)))
    for o in range(1, 4):
        signal(barrier, at_head((head_at + o) % 4))
    pl.semaphore_wait(barrier, BLOCKS + 2)

    at = me % PLANE
    to_sibling = lambda j: remote(
        theirs.at[j], sib.at[j], sib_send.at[j], sib_recv.at[j], sibling
    )

    def to_owner(k, kind):
        q, where = plane_peer(k, -1)
        j = q if kind else zl * PLANE + q
        return remote(
            mine.at[j], kvgot.at[kind, at], send_sem.at[kind, k], recv_sem.at[kind, at], where
        )

    def from_plane(kind, q):
        return remote(
            kvgot.at[kind, q], kvgot.at[kind, q], send_sem.at[kind, 0], recv_sem.at[kind, q],
            sibling,
        )

    across = remote(
        relay_ref, kvgot.at[1, 0], send_sem.at[0, PLANE - 1], recv_sem.at[1, 0], {"zl": 1 - zl}
    )
    states = Scan(True, me, msg, got, back, result, scan_send, scan_recv)
    rs = Reduce(
        [(ft_ref, ftz_ref, 0), (ct_ref, ctz_ref, 8)], 12, *reduce[:6], w_ref, reduce[6:]
    )
    lefts = [Left(ft_ref, ftz_ref, left_sem.at[0]), Left(mt_ref, mtz_ref, left_sem.at[1])]
    rs.fill([dgate_ref, dup_ref, hidden_ref])

    lower = triangle()
    edge = edge_in[...].astype(F32)[8:]
    xext[:8, :] = edge[:, :INNER]
    segx[:8, :] = edge[:, INNER + BC :]
    xext[8:, :] = x_ref[...].astype(F32)
    segx[8:, :] = seg_ref[...]
    bcext[...] = bcown_ref[...].astype(F32)[8:]
    bias_ref[...] = mixing_bias(seg_ref, segrow_ref)
    pre_dt, step, total, carry, entry, through = decays(dt_ref, vec_ref, seg_ref, segx, lower)
    cumt_ref[...] = jnp.transpose(total)
    b_low, c_low = bcact_ref[:, :STATE], bcact_ref[:, STATE:]
    dcum = jnp.zeros((ROWS, 128), F32)
    dskip = jnp.zeros((8, 128), F32)
    dc = jnp.zeros((ROWS, STATE), F32)
    for g in range(GROUPS):
        cols = slice(g * 128, (g + 1) * 128)
        z, core, x = z_ref[:, cols], core_ref[:, cols], xact_ref[:, cols].astype(F32)
        sig = sigmoid(z)
        gg = gg_ref[:, cols]
        out = core + skip_ref[0:1, cols] * x
        dz_ref[:, cols] = (gg * out * sig * (1.0 + z * (1.0 - sig))).astype(BF16)
        grad = gg * z * sig
        g_ref[:, cols] = grad
        dcum += per_head(grad * core, g)
        dskip += per_head(jnp.broadcast_to(jnp.sum(grad * x, 0, keepdims=True), (8, 128)), g)
        entered = (grad * widen(entry, g)).astype(BF16)
        local[cols, :] = dot(entered, c_low, 0, 0)
        dc += dot(entered, state_ref[cols, :].astype(BF16))
    scan_message(msg, local, through)
    states.start()
    lefts[0].start()
    rs.start()
    lefts[1].start()
    dbc_all[:, STATE:] = dc

    cb_ref[...] = dot(c_low, b_low, 1, 1)
    low_lane = lax.broadcasted_iota(jnp.int32, (ROWS, 128), 1) < SSM_DIM
    dcb = jnp.zeros((ROWS, ROWS), F32)
    for g in range(GROUPS):
        cols = slice(g * 128, (g + 1) * 128)
        u = xact_ref[:, cols].astype(F32) * widen(step, g)
        u_low, grad = u.astype(BF16), g_ref[:, cols]
        grad_low = grad.astype(BF16)
        made = []
        for i in range(2):
            h = 2 * g + i
            decay = jnp.exp2(total[:, h : h + 1] - cumt_ref[h : h + 1, :] + bias_ref[...])
            mixing = (decay * cb_ref[...]).astype(BF16)
            made.append(dot(mixing, grad_low, 0, 0))
            half = jnp.where(low_lane if i == 0 else ~low_lane, grad, 0.0).astype(BF16)
            dcb += decay * dot(half, u_low, 1, 1)
        du = jnp.where(low_lane, made[0], made[1])
        du_ref[:, cols] = du
        dcum -= per_head(u * du, g)
    dcum_ref[...] = dcum
    dcb_low = dcb.astype(BF16)
    dbc_all[:, :STATE] = dot(dcb_low, c_low, 0, 0)
    dbc_all[:, STATE:] += dot(dcb_low, b_low)

    scale = LOG2E * HEAD_DIM**-0.5
    queries, grads = q_ref[...], do_ref[...]
    lse, qseg = lse_ref[0:1, :], segrow_ref[0:1, :]
    high, low = two_parts(grads.astype(F32) * att_ref[...])
    ones = jnp.ones((8, HEAD_DIM), BF16)
    delta = (dot(ones, high, 1, 1) + dot(ones, low, 1, 1))[0:1, :]

    def block(t, own):
        keys = kv_ref[0, t, :ROWS]
        s = dot(keys, queries, 1, 1) * scale
        s = jnp.where(key_segments(kv_ref[0, t, ROWS:]) == qseg, s, MASKED)
        if own:
            s = causal_mask(s)
        p = jnp.exp2(s - lse)
        ds = (p * (dot(kv_ref[1, t, :ROWS], grads, 1, 1) - delta)).astype(BF16)
        dk = dot(ds, queries)
        dv = dot(p.astype(BF16), grads)
        change = dot(keys, ds, 0, 0)
        dqt_ref[...] = change if own else dqt_ref[...] + change
        mine[t] = jnp.where(c == 0, dk, dv).astype(BF16)
        theirs[t] = jnp.where(c == 0, dv, dk).astype(BF16)
        to_sibling(t).start()

    def pair(t):
        to_sibling(t).wait_recv()
        return mine[t].astype(F32) + sib[t].astype(F32)

    block(me, True)
    lefts[0].pass_on()
    states.turn()
    lefts[0].finish()

    @pl.when(zl == 1)
    def _():
        block(at, False)

    def give(k):
        q, _ = plane_peer(k, -1)

        @pl.when(q < at)
        def _():
            j = zl * PLANE + q
            mine[j] = pair(j).astype(BF16)
            to_owner(k, 0).start()

        @pl.when(zl == 1)
        def _():
            mine[q] = pair(q).astype(BF16)
            to_owner(k, 1).start()

    def step_over(k):
        q, _ = plane_peer(k, -1)
        pl.when(q < at)(lambda: block(zl * PLANE + q, False))
        pl.when(zl == 1)(lambda: block(q, False))

        @pl.when(k >= 1)
        def _():
            give(k - 1)

        rs.step(k)

    over(0, PLANE - 1, step_over)
    give(PLANE - 2)
    over(PLANE - 1, rs.steps, rs.step)
    lefts[1].pass_on()
    dkv_ref[...] = pair(me)

    @pl.when(zl == 1)
    def _():
        total_ref[...] = pair(at)

    dq_ref[...] = jnp.transpose(dqt_ref[...])

    states.finish(enter_ref)
    dcum = dcum_ref[...]
    dstep = jnp.zeros((ROWS, 128), F32)
    dlast = jnp.zeros((8, 128), F32)
    db = jnp.zeros((ROWS, STATE), F32)
    for g in range(GROUPS):
        cols = slice(g * 128, (g + 1) * 128)
        entering = enter_ref[cols, :]
        entering_low = entering.astype(BF16)
        x = xact_ref[:, cols].astype(F32)
        steps, carries = widen(step, g), widen(carry, g)
        v = x * steps * carries
        dv = dot(b_low, entering_low, 1, 1)
        db += dot(v.astype(BF16), entering_low)
        dcarry = per_head(v * dv, g)
        dcum -= dcarry
        dlast += jnp.broadcast_to(jnp.sum(dcarry, 0, keepdims=True), (8, 128))
        du = du_ref[:, cols] + carries * dv
        dstep += per_head(x * du, g)
        pieces = jnp.sum(entering * state_ref[cols, :], 1, keepdims=True)
        both = jnp.sum(jnp.broadcast_to(pieces, (128, 128)) * head_of_lane_f32(g), 0, keepdims=True)
        dlast += through * both
        g_ref[:, cols] = steps * du + skip_ref[0:1, cols] * g_ref[:, cols]
    dbc_all[:, :STATE] += db
    last_row = lax.broadcasted_iota(jnp.int32, (ROWS, 128), 0) == ROWS - 1
    dcum += jnp.where(last_row, dlast[0:1, :], 0.0)
    da = running(dcum, lower, 0)
    rate = vec_ref[1:2, :]
    drate = -jnp.sum(step * da, 0, keepdims=True)
    ddt = (dstep - rate * da) * sigmoid(pre_dt)
    ddt_ref[...] = ddt.astype(BF16)
    dbias = jnp.sum(ddt, 0, keepdims=True)
    dvec_ref[...] = jnp.concatenate([dbias, drate, dskip[0:1, :], jnp.zeros((5, 128), F32)], 0)

    for d in range(4):
        shares[d] = dbc_all[:, d * 128 : (d + 1) * 128].astype(BF16)
    share = lambda o: remote(
        shares.at[(head_at + o) % 4], share_got.at[o], share_send.at[o], share_recv.at[o],
        at_head((head_at + o) % 4),
    )
    for o in range(1, 4):
        share(o).start()

    def conv_back(ext, taps, grad, cols, out_taps, out_grad):
        pre, inputs = conv_group(ext, segx, seg_ref, taps, cols)
        sig = sigmoid(pre)
        dpre = grad * sig * (1.0 + pre * (1.0 - sig))
        gext[...] = jnp.zeros_like(gext)
        rows = []
        for k in range(CONV):
            rows.append(jnp.sum(dpre * inputs[k], 0, keepdims=True))
            same = segx[pl.ds(5 + k, ROWS), :] == seg_ref[...]
            gext[pl.ds(5 + k, ROWS), :] += jnp.where(same, taps[k : k + 1, cols] * dpre, 0.0)
        out_taps[:, cols] = jnp.concatenate([*rows, jnp.zeros((4, 128), F32)], 0)
        out_grad[...] = gext[...]

    def x_group(g):
        cols = lane_block(g)
        conv_back(xext, xtaps_ref, g_ref[:, cols], cols, dxtaps_ref, ddtx_ref)
        edge_ref[:, cols] = ddtx_ref[:8, :]
        g_ref[:, cols] = ddtx_ref[8:, :]

    over(0, GROUPS, x_group)
    grad_bc = shares[head_at].astype(F32)
    for o in range(1, 4):
        share(o).wait_recv()
        grad_bc += share_got[o].astype(F32)
    conv_back(bcext, bctaps_ref, grad_bc, slice(0, 128), dbctaps_ref, ddtx_ref)
    edge_ref[:, INNER:] = ddtx_ref[:8, :]
    edge_copy = remote(
        edge_ref, edge_out, edge_sem.at[0], edge_sem.at[1], block_at((me + BLOCKS - 1) % BLOCKS)
    )

    @pl.when(me > 0)
    def _():
        edge_copy.start()

    def collect(q):
        @pl.when((zl == 1) & (q != at))
        def _():
            from_plane(1, q).wait_recv()
            total_ref[...] += kvgot[1, q].astype(F32)

    over(0, PLANE, collect)

    @pl.when(zl == 1)
    def _():
        relay_ref[...] = total_ref[...].astype(BF16)
        across.start()

    def collect_own(q):
        from_plane(0, q).wait_recv()
        dkv_ref[...] += kvgot[0, q].astype(F32)

    over(at + 1, PLANE, collect_own)

    @pl.when(zl == 0)
    def _():
        from_plane(1, 0).wait_recv()
        dkv_ref[...] += kvgot[1, 0].astype(F32)

    @pl.when(me < BLOCKS - 1)
    def _():
        edge_copy.wait_recv()

    @pl.when(me == BLOCKS - 1)
    def _():
        edge_out[...] = jnp.zeros_like(edge_out)

    tail = pl.ds(ROWS - 8, 8)
    g_ref[tail, :] += edge_out[:, :INNER]
    ddtx_ref[pl.ds(ROWS, 8), :] += edge_out[:, INNER:]
    dx_ref[...] = g_ref[...].astype(BF16)
    dbc_ref[...] = ddtx_ref[8:, :].astype(BF16)

    @pl.when(me > 0)
    def _():
        edge_copy.wait_send()

    states.close()
    rs.close()
    lefts[0].close()
    lefts[1].finish()
    lefts[1].close()
    for o in range(1, 4):
        share(o).wait_send()
    to_sibling(me).wait_send()

    def given(k):
        q, _ = plane_peer(k, -1)

        @pl.when(q < at)
        def _():
            to_sibling(zl * PLANE + q).wait_send()
            to_owner(k, 0).wait_send()

        @pl.when(zl == 1)
        def _():
            to_sibling(q).wait_send()
            to_owner(k, 1).wait_send()

    over(0, PLANE - 1, given)

    @pl.when(zl == 1)
    def _():
        to_sibling(at).wait_send()
        across.wait_send()


def head_of_lane_f32(g):
    row = lax.broadcasted_iota(jnp.int32, (128, 128), 0)
    lane = lax.broadcasted_iota(jnp.int32, (128, 128), 1)
    return (lane == 2 * g + (row >= SSM_DIM).astype(jnp.int32)).astype(F32)


def mixer_backward(*args):
    wide = 2 * ROWS
    s = jax.ShapeDtypeStruct
    dma = pltpu.SemaphoreType.DMA
    v = pltpu.VMEM
    piece = (BLOCKS, ROWS, HEAD_DIM)
    return pl.pallas_call(
        mixer_backward_kernel,
        name="mixer_backward",
        out_shape=(
            s((wide, HEAD_DIM), F32),
            s((ROWS, HEAD_DIM), F32),
            s((ROWS, INNER), BF16),
            s((ROWS, INNER), BF16),
            s((ROWS, 128), BF16),
            s((ROWS, 128), BF16),
            s((8, INNER), F32),
            s((8, 128), F32),
            s((8, 128), F32),
            s((64, 12 * WIDE), F32),
            s((OWN, ROWS), BF16),
        ),
        in_specs=vmem(len(args)),
        out_specs=tuple(vmem(11)),
        scratch_shapes=[
            v((HEAD_DIM, wide), F32),
            *[v(piece, BF16)] * 3,
            v((2, PLANE, ROWS, HEAD_DIM), BF16),
            v((ROWS, HEAD_DIM), BF16),
            v((ROWS, HEAD_DIM), F32),
            v((ROWS + 8, INNER), F32),
            v((ROWS + 8, 128), F32),
            v((ROWS + 8, 128), F32),
            v((INNER, STATE), F32),
            *[v((BLOCKS, SCAN_ROWS + 8, STATE), BF16)] * 4,
            v((ROWS, ROWS), F32),
            v((ROWS, ROWS), F32),
            v((128, ROWS), F32),
            v((ROWS, INNER), F32),
            v((ROWS, INNER), F32),
            v((ROWS, BC), F32),
            v((4, ROWS, 128), BF16),
            v((4, ROWS, 128), BF16),
            v((8, GRAD_EDGE), F32),
            v((8, GRAD_EDGE), F32),
            v((INNER, STATE), F32),
            v((ROWS + 8, 128), F32),
            v((ROWS, 128), F32),
            v((ROWS + 8, 128), F32),
            dma((2, PLANE)),
            dma((2, PLANE)),
            dma((BLOCKS,)),
            dma((BLOCKS,)),
            dma((2,)),
            dma((2, BLOCKS)),
            dma((2, BLOCKS)),
            dma((4,)),
            dma((4,)),
            v((OWN, ROWS), BF16),
            dma((2, 4)),
            *Reduce.scratch(12),
        ],
        compiler_params=params(2),
    )(*args)


SMALL = 8 * 128
SMALL_AT = 5
CHUNKS = 13
GATHER_FROM = CHUNKS


def finish_kernel(
    misc_ref, dx_ref, dz_ref, dq_ref, ddt_ref, gated_ref, att_ref, nt_ref, ntz_ref, mt_ref,
    mtz_ref, back_ref, ffn_ref, tok_ref, gain_ref, ghid_ref, hid_ref, small_ref,
    out_ref, dtok_ref, w_ref, all_ref, alls_ref,
    own_small, back_sum, ffn_sum, mine, esum, egot, e_send, e_recv, z_send, z_recv, w_send, w_recv, sib_send, sib_recv,
    s_send, s_recv, t_send, t_recv, part_ref, *rest,
):
    me, c, zh = block_index(), lax.axis_index("c"), lax.axis_index("zh")
    chip = zh * BLOCKS + me
    sibling = {"c": 1 - c}

    def chip_at(p):
        return {"zh": p // BLOCKS, **block_at(p % BLOCKS)}

    n_rs = len(Reduce.scratch(CHUNKS))
    rs = Reduce(
        [(nt_ref, ntz_ref, 0), (mt_ref, mtz_ref, 9)], CHUNKS, *rest[:6], w_ref, rest[6:n_rs]
    )
    rest = rest[n_rs:]
    n_sum = len(HeadSum.scratch())
    back = HeadSum(back_ref, back_sum, *rest[:3], rest[3:n_sum])
    rest = rest[n_sum:]
    ffn = HeadSum(ffn_ref, ffn_sum, *rest[:3], rest[3:])

    barrier = pltpu.get_barrier_semaphore()
    over(1, CHIPS, lambda o: signal(barrier, chip_at((chip + o) % CHIPS)))
    signal(barrier, sibling)
    pl.semaphore_wait(barrier, CHIPS)

    back.start()
    rs.fill([misc_ref, dx_ref, dz_ref, dq_ref, ddt_ref, gated_ref, att_ref])
    rs.right(0).start()
    back.across()
    over(1, CHUNKS, lambda k: rs.right(k).start())
    ffn.start()

    at, level = me % PLANE, zh * NZ + lax.axis_index("zl")

    def along_z(o):
        d = (level + o) % 4
        where = {"zh": d // NZ, "zl": d % NZ}
        return remote(mine, all_ref.at[c, at, level], z_send.at[o], z_recv.at[o], where)

    def column(k):
        return remote(
            all_ref.at[c, at], all_ref.at[c, at], w_send.at[k], w_recv.at[at], plane_peer(k, 1)[1]
        )

    def to_sibling(q, core):
        return remote(
            all_ref.at[core, q], all_ref.at[core, q], sib_send.at[q], sib_recv.at[q], sibling
        )

    def pass_on(k):
        q, where = plane_peer(k, -1)
        remote(
            all_ref.at[c, q], all_ref.at[c, q], w_send.at[k], w_recv.at[q], where
        ).wait_recv()
        to_sibling(q, c).start()

    def columns_out():
        for o in range(1, 4):
            along_z(o).wait_recv()
        over(0, PLANE - 1, lambda k: column(k).start())
        to_sibling(at, c).start()

    def share(d):
        return remote(own_small.at[d], egot.at[me], e_send.at[d], e_recv.at[me], block_at(d))

    def shared(s):
        return remote(egot.at[s], egot.at[s], e_send.at[0], e_recv.at[s], block_at(s))

    def small_spread(o):
        d = (chip + o) % CHIPS
        slot = zh * SMALL_AT + me
        return remote(esum, alls_ref.at[c, slot], s_send.at[o], s_recv.at[slot], chip_at(d))

    def small_sibling(slot, core):
        return remote(
            alls_ref.at[core, slot], alls_ref.at[core, slot], t_send.at[slot], t_recv.at[slot],
            sibling,
        )

    def gradient():
        for r in range(0, ROWS, 32):
            rows = pl.ds(r, 32)
            x = tok_ref[rows, :].astype(F32)
            scale = lax.rsqrt(jnp.mean(x * x, 1, keepdims=True) + EPSILON)
            n = x * scale
            grad = back_sum[rows, :].astype(F32)
            scaled = grad * gain_ref[0:1, :]
            along = jnp.mean(n * scaled, 1, keepdims=True)
            dtok_ref[rows, :] = ghid_ref[rows, :] + scale * (scaled - n * along)
            gains = jnp.sum(grad * n, 0, keepdims=True)
            for k in range(MODEL // 128):
                piece = gains[:, k * 128 : (k + 1) * 128]
                part_ref[k : k + 1, :] = piece if r == 0 else part_ref[k : k + 1, :] + piece
        quarter = MODEL // 4 // 128
        own_small[...] = small_ref[...]
        own_small[0, :quarter] = part_ref[pl.ds((zh * 2 + c) * quarter, quarter), :]

        def give(d):
            @pl.when(d != me)
            def _():
                share(d).start()

        over(0, SMALL_AT, give)

    def small_sums():
        @pl.when(me < SMALL_AT)
        def _():
            egot[me] = own_small[me]

            def take(s):
                @pl.when(s != me)
                def _():
                    shared(s).wait_recv()

            over(0, BLOCKS, take)
            total = lax.fori_loop(0, BLOCKS, lambda s, t: t + egot[s], jnp.zeros((8, 128), F32))
            esum[...] = jnp.concatenate([total, jnp.zeros_like(total)], 0).astype(BF16)
            slot = zh * SMALL_AT + me
            alls_ref[c, slot] = esum[...]
            over(1, CHIPS, lambda o: small_spread(o).start())
            small_sibling(slot, c).start()

    def small_pass():
        def one(slot):
            @pl.when(slot != zh * SMALL_AT + me + jnp.where(me < SMALL_AT, 0, CHIPS))
            def _():
                remote(
                    esum, alls_ref.at[c, slot], s_send.at[0], s_recv.at[slot], sibling
                ).wait_recv()
                small_sibling(slot, c).start()

        over(0, 2 * SMALL_AT, one)

    def weights_out():
        mine[...] = w_ref[:, :WIDE].astype(BF16)
        all_ref[c, at, level] = mine[...]
        for o in range(1, 4):
            along_z(o).start()

    batch, first_pass = 3, rs.steps - 5

    def step(i):
        rs.step(i)

        @pl.when(i == 2)
        def _():
            ffn.across()

        @pl.when(i == 4)
        def _():
            back.join()

        @pl.when(i == 2 * LAG)
        def _():
            weights_out()
            back.finish()
            gradient()

        @pl.when(i == 9)
        def _():
            columns_out()
            ffn.join()

        @pl.when(i == 11)
        def _():
            small_sums()

        @pl.when(i == 12)
        def _():
            ffn.finish()
            out_ref[...] = (hid_ref[...] + ffn_sum[...].astype(F32)).astype(BF16)

        @pl.when(i >= first_pass)
        def _():
            k = i - first_pass
            over(k * batch, (k + 1) * batch, pass_on)

    over(0, rs.steps, step)
    small_pass()

    over(0, PLANE, lambda q: to_sibling(q, 1 - c).wait_recv())
    over(0, 2 * SMALL_AT, lambda s: small_sibling(s, 1 - c).wait_recv())
    rs.close()
    back.close()
    ffn.close()
    over(0, PLANE, lambda q: to_sibling(q, c).wait_send())
    over(0, 2 * SMALL_AT, lambda s: small_sibling(s, c).wait_send())
    over(0, PLANE - 1, lambda k: column(k).wait_send())
    for o in range(1, 4):
        along_z(o).wait_send()

    @pl.when(me < SMALL_AT)
    def _():
        over(1, CHIPS, lambda o: small_spread(o).wait_send())

    def given(d):
        @pl.when(d != me)
        def _():
            share(d).wait_send()

    over(0, SMALL_AT, given)


def finish(*args):
    s = jax.ShapeDtypeStruct
    v, dma = pltpu.VMEM, pltpu.SemaphoreType.DMA
    return pl.pallas_call(
        finish_kernel,
        name="finish",
        out_shape=(
            s((ROWS, MODEL), BF16),
            s((ROWS, MODEL), F32),
            s((64, CHUNKS * WIDE), F32),
            s((2, PLANE, 4, 64, WIDE), BF16),
            s((2, 2 * SMALL_AT, 16, 128), BF16),
        ),
        in_specs=vmem(len(args)),
        out_specs=tuple(vmem(5)),
        scratch_shapes=[
            v((SMALL_AT, 8, 128), F32),
            v((ROWS, MODEL), BF16),
            v((ROWS, MODEL), BF16),
            v((64, WIDE), BF16),
            v((16, 128), BF16),
            v((BLOCKS, 8, 128), F32),
            dma((SMALL_AT,)), dma((BLOCKS,)),
            dma((4,)), dma((4,)),
            *[dma((PLANE,))] * 4,
            dma((CHIPS,)), dma((2 * SMALL_AT,)),
            dma((2 * SMALL_AT,)), dma((2 * SMALL_AT,)),
            v((16, 128), F32),
            *Reduce.scratch(CHUNKS),
            *HeadSum.scratch(),
            *HeadSum.scratch(),
        ],
        compiler_params=params(3),
    )(*args)


def format_kernel(all_ref, bc_ref, kv_ref):
    for c in range(2):
        for p in range(all_ref.shape[1]):
            for zh in range(2):
                rows = slice(p * 64, (p + 1) * 64)
                at, turned = (zh * 2 + c) * 128, (c * 2 + zh) * 128
                bc_ref[rows, at : at + 128] = all_ref[c, p, zh, 0, :, :128].astype(F32)
                kv_ref[rows, turned : turned + 128] = all_ref[c, p, zh, 0, :, 128:].astype(F32)


def format_replicated(gathered):
    step = 8
    steps = PLANE // step
    block = pl.BlockSpec((64 * step, 512), lambda i: (i, 0))
    return pl.pallas_call(
        format_kernel,
        name="format_replicated",
        out_shape=(jax.ShapeDtypeStruct((MODEL, 512), F32),) * 2,
        grid=(NZ * steps,),
        in_specs=[
            pl.BlockSpec(
                (2, step, 2, 1, 64, WIDE), lambda i: (0, i % steps, 0, i // steps, 0, 0)
            )
        ],
        out_specs=(block, block),
    )(gathered.reshape(2, PLANE, 2, NZ, 64, WIDE))


def rms_norm(values, scales):
    return values * lax.rsqrt(jnp.mean(values * values, -1, keepdims=True) + EPSILON) * scales


def rope_turn(values, cosine, sine):
    half = values.shape[-1] // 2
    first, second = values[..., :half], values[..., half:]
    return jnp.concatenate([first * cosine - second * sine, second * cosine + first * sine], -1)


def on_device(
    tokens, segment_ids, cotangent, norm1_gain, x_weight, z_weight, bc_weight, dt_weight,
    x_conv, bc_conv, dt_bias, decay_rate, skip_gain, out_weight, query_weight, kv_weight,
    attn_weight, norm2_gain, gate_weight, up_weight, down_weight,
):
    zh, c = lax.axis_index("zh"), lax.axis_index("c")
    head_index = zh * 2 + c
    heads = decay_rate.shape[0]
    inner = x_weight.shape[1]
    q_heads = query_weight.shape[1] // HEAD_DIM
    positions = block_index() * ROWS + jnp.arange(ROWS)
    half_dim = HEAD_DIM // 2
    frequency = ROPE_BASE ** (-(jnp.arange(half_dim).astype(F32) * 2.0 / HEAD_DIM))
    angles = positions.astype(F32)[:, None] * frequency[None, :]
    cosine, sine = jnp.cos(angles), jnp.sin(angles)

    x_input = tokens.astype(F32)
    normed_f, norm_back = jax.vjp(rms_norm, x_input, norm1_gain)
    normed = normed_f.astype(BF16)
    kv_at = c * (KVHEADS * HEAD_DIM) + zh * HEAD_DIM
    kv_columns = lax.dynamic_slice_in_dim(kv_weight, kv_at, HEAD_DIM, 1)
    kv_raw = dot(normed, kv_columns)
    kv_own = jnp.where(c == 0, rope_turn(kv_raw, cosine, sine), kv_raw).astype(BF16)
    query_raw = dot(normed, query_weight).reshape(ROWS, q_heads, HEAD_DIM)
    queries = rope_turn(query_raw, cosine[:, None, :], sine[:, None, :]).astype(BF16)
    queries = queries.transpose(1, 0, 2).reshape(q_heads * ROWS, HEAD_DIM)
    x_pre = dot(normed, x_weight).astype(BF16)
    bc_pre = dot(normed, bc_weight).astype(BF16)
    z_val = dot(normed, z_weight)
    dt_wide = jnp.pad(dt_weight, ((0, 0), (0, 128 - heads)))
    dt_raw = dot(normed, dt_wide)

    seg_low = segment_ids.astype(BF16)
    own_block = jnp.concatenate(
        [kv_own, jnp.pad(seg_low.reshape(2, HEAD_DIM), ((0, 14), (0, 0)))], 0
    )
    seg = segment_ids.astype(F32)
    seg_row = jnp.broadcast_to(jnp.tile(seg, q_heads), (8, q_heads * ROWS))
    seg_column = jnp.broadcast_to(seg[:, None], (ROWS, 128))
    edge = jnp.concatenate(
        [x_pre[-16:], bc_pre[-16:], jnp.broadcast_to(seg_low[-16:, None], (16, 128))], 1
    )
    vectors = jnp.pad(jnp.stack([dt_bias, decay_rate]), ((0, 6), (0, 128 - heads)))
    skip = jnp.broadcast_to(jnp.repeat(skip_gain, SSM_DIM), (8, inner))
    attended, lse, kv_all, edge_in, gated, core, x_act, bc_act, state_in, normed_near, cot_near = mixer_forward(
        queries, own_block, edge, x_pre, bc_pre, dt_raw, z_val, seg_column, seg_row, x_conv,
        bc_conv, vectors, skip, normed.T, cotangent.T,
    )
    attended_low = (
        attended.astype(BF16).reshape(q_heads, ROWS, HEAD_DIM).transpose(1, 0, 2)
        .reshape(ROWS, q_heads * HEAD_DIM)
    )
    mixer_part = dot(gated, out_weight) + dot(attended_low, attn_weight)
    hidden_in = x_input + head_sum(mixer_part.astype(BF16), 4).astype(F32)

    normed_two_f, norm_two_back = jax.vjp(rms_norm, hidden_in, norm2_gain)
    normed_two = normed_two_f.astype(BF16)
    gate_val = dot(normed_two, gate_weight)
    up_val = dot(normed_two, up_weight)
    gate_sig = jax.nn.sigmoid(gate_val)
    gate_act = gate_val * gate_sig
    hidden = (gate_act * up_val).astype(BF16)
    grad_hidden = dot(cotangent, down_weight, 1, 1)
    grad_gate = (grad_hidden * up_val * gate_sig * (1.0 + gate_val * (1.0 - gate_sig))).astype(BF16)
    grad_up = (grad_hidden * gate_act).astype(BF16)
    ffn_part = dot(hidden, down_weight).astype(BF16)
    back_part = (dot(grad_gate, gate_weight, 1, 1) + dot(grad_up, up_weight, 1, 1)).astype(BF16)
    grad_from_two, grad_gain_two = norm_two_back(head_sum(back_part, 5).astype(F32))
    grad_hidden_in = grad_from_two + cotangent.astype(F32)
    grad_mix = grad_hidden_in.astype(BF16)
    grad_gated = dot(grad_mix, out_weight, 1, 1)
    grad_attended = (
        dot(grad_mix, attn_weight, 1, 1).astype(BF16).reshape(ROWS, q_heads, HEAD_DIM)
        .transpose(1, 0, 2).reshape(q_heads * ROWS, HEAD_DIM)
    )
    bc_at = head_index * 128
    bc_own = jnp.concatenate(
        [
            lax.dynamic_slice_in_dim(edge_in, inner + bc_at, 128, 1),
            lax.dynamic_slice_in_dim(bc_pre, bc_at, 128, 1),
        ]
    )
    (
        grad_query, grad_kv, grad_z, grad_x_pre, grad_bc_low, grad_dt_raw, grad_x_conv,
        grad_bc_conv, grad_vectors, ffn_w, mix_near,
    ) = mixer_backward(
        queries, grad_attended, attended, lse, seg_row, kv_all, grad_gated, z_val, core, x_act,
        bc_act, x_pre, bc_own, edge_in, dt_raw, state_in, seg_column, x_conv,
        lax.dynamic_slice_in_dim(bc_conv, bc_at, 128, 1), vectors, skip, grad_gate, grad_up,
        hidden, normed_two.T, cotangent.T, cot_near, grad_mix.T,
    )
    score_scale = HEAD_DIM**-0.5
    grad_query = (grad_query * score_scale).reshape(q_heads, ROWS, HEAD_DIM).transpose(1, 0, 2)
    grad_query_raw = (
        rope_turn(grad_query, cosine[:, None, :], -sine[:, None, :]).astype(BF16)
        .reshape(ROWS, q_heads * HEAD_DIM)
    )
    grad_kv_low = jnp.where(
        c == 0, rope_turn(grad_kv * score_scale, cosine, -sine), grad_kv
    ).astype(BF16)
    bc_columns = lax.dynamic_slice_in_dim(bc_weight, bc_at, 128, 1)
    back_part = (
        dot(grad_x_pre, x_weight, 1, 1)
        + dot(grad_z, z_weight, 1, 1)
        + dot(grad_dt_raw, dt_wide, 1, 1)
        + dot(grad_query_raw, query_weight, 1, 1)
        + dot(grad_bc_low, bc_columns, 1, 1)
        + dot(grad_kv_low, kv_columns, 1, 1)
    )
    quarter = MODEL // 4
    small = [
        jnp.zeros((quarter,), F32), grad_x_conv[:CONV], grad_bc_conv[:CONV],
        grad_vectors[0, :heads], grad_vectors[1, :heads], grad_vectors[2, :heads],
        lax.dynamic_slice_in_dim(grad_gain_two, head_index * quarter, quarter),
    ]
    flat = jnp.concatenate([a.reshape(-1) for a in small])
    flat = jnp.pad(flat, (0, SMALL_AT * SMALL - flat.size)).reshape(SMALL_AT, 8, 128)
    output, grad_tokens, mixer_w, gathered, small_sums = finish(
        jnp.concatenate([grad_bc_low, grad_kv_low], 1), grad_x_pre, grad_z, grad_query_raw,
        jnp.pad(grad_dt_raw, ((0, 0), (0, 128))), gated, attended_low, normed.T, normed_near,
        grad_mix.T, mix_near, back_part.astype(BF16), ffn_part, tokens,
        jnp.broadcast_to(norm1_gain, (8, MODEL)), grad_hidden_in, hidden_in, flat,
    )
    bc_w, kv_w = format_replicated(gathered)
    total = small_sums.reshape(2, 2, SMALL_AT, 16, 128)[:, :, :, :8].astype(F32)
    total = total.transpose(1, 0, 2, 3, 4).reshape(4, SMALL_AT * SMALL)
    at = [WIDE, WIDE + inner, WIDE + 2 * inner, 2 * WIDE + 2 * inner, 3 * WIDE + 2 * inner]
    pieces, start = [], 0
    for a in small:
        pieces.append(total[:, start : start + a.size].reshape(4, *a.shape))
        start += a.size
    x_conv_sum = pieces[1].transpose(1, 0, 2).reshape(CONV, 4 * inner)
    bc_conv_sum = pieces[2].transpose(1, 0, 2).reshape(CONV, 512)
    bias_sum, rate_sum, skip_sum, gain_two_sum = (p.reshape(-1) for p in pieces[3:])
    gain_one_sum = pieces[0].reshape(-1)
    ff = gate_weight.shape[1]
    return (
        output,
        grad_tokens,
        gain_one_sum,
        mixer_w[:, at[0] : at[1]],
        mixer_w[:, at[1] : at[2]],
        bc_w,
        mixer_w[:, at[3] : at[3] + heads],
        x_conv_sum,
        bc_conv_sum,
        bias_sum,
        rate_sum,
        skip_sum,
        mixer_w[:, at[4] : at[4] + inner].T,
        mixer_w[:, at[2] : at[3]],
        kv_w,
        mixer_w[:, at[4] + inner :].T,
        gain_two_sum,
        ffn_w[:, :ff],
        ffn_w[:, ff : 2 * ff],
        ffn_w[:, 2 * ff :].T,
    )


def solution(mesh):
    split = Mesh(mesh.devices.reshape(NZ, NX, NY, 2, 2), (*SEQ, "zh", "c"))
    head = ("zh", "c")
    rows, columns, both, turned = P(SEQ, None), P(None, head), P(SEQ, head), P(head, SEQ)
    return jax.shard_map(
        on_device,
        mesh=split,
        in_specs=(
            rows, P(SEQ), rows, P(), columns, columns, P(), columns, columns, P(), P(head),
            P(head), P(head), P(head, None), columns, P(), P(head, None), P(), columns, columns,
            P(head, None),
        ),
        out_specs=(
            rows, rows, P(), both, both, P(), both, P(), P(), P(), P(), P(), turned, both, P(),
            turned, P(), both, both, turned,
        ),
        check_vma=False,
    )
```

```python
import functools

import jax
import jax.numpy as jnp
from jax import lax
from jax.experimental import pallas as pl
from jax.experimental.pallas import tpu as pltpu
from jax.sharding import Mesh
from jax.sharding import PartitionSpec as P

SSM_DIM = 64
STATE = 256
CONV = 4
KVHEADS = 2
HEAD_DIM = 128
NZ, NX, NY = 2, 4, 4
BLOCKS = NZ * NX * NY
CHIPS = 2 * BLOCKS
ROWS = 256
MODEL = 2048
SEQ = ("zl", "x", "y")
EPSILON = 1e-05
ROPE_BASE = 100000000000.0
HIGHEST = lax.Precision.HIGHEST
MESH = pl.DeviceIdType.MESH
BF16, F32 = jnp.bfloat16, jnp.float32
MASKED = -1e30
LOG2E = 1.4426950408889634
VMEM_LIMIT = 56 * 2**20


def block_index():
    return (lax.axis_index("zl") * NX + lax.axis_index("x")) * NY + lax.axis_index("y")


def block_at(s):
    return {"zl": s // (NX * NY), "x": (s // NY) % NX, "y": s % NY}


PLANE = NX * NY


def plane_shift(k):
    o = 1 + (k * 7) % (PLANE - 1)
    return o // NY, o % NY


def plane_peer(k, sign):
    dx, dy = plane_shift(k)
    x, y = lax.axis_index("x"), lax.axis_index("y")
    if sign < 0:
        dx, dy = NX - dx, NY - dy
    x, y = (x + dx) % NX, (y + dy) % NY
    return x * NY + y, {"x": x, "y": y}


def signal(sem, where):
    pl.semaphore_signal(sem, inc=1, device_id=where, device_id_type=MESH)


def remote(src, dst, send, recv, where):
    return pltpu.make_async_remote_copy(src, dst, send, recv, device_id=where, device_id_type=MESH)


def over(start, stop, body):
    def step(i, carry):
        body(i)
        return carry

    lax.fori_loop(start, stop, step, 0)


def dot(a, b, left=1, right=0):
    return lax.dot_general(
        a, b, (((left,), (right,)), ((), ())), preferred_element_type=F32
    )


def vmem(n):
    return [pl.BlockSpec(memory_space=pltpu.VMEM)] * n


def params(collective_id):
    return pltpu.CompilerParams(
        collective_id=collective_id, has_side_effects=True, vmem_limit_bytes=VMEM_LIMIT
    )


HEADS = 12
INNER = HEADS * SSM_DIM
GROUPS = INNER // 128
BC = 2 * STATE
SCAN_ROWS = INNER // BLOCKS
EDGE_WIDE = INNER + BC + 128
GRAD_EDGE = INNER + 128


def two_parts(v):
    high = v.astype(BF16)
    return high, (v - high.astype(F32)).astype(BF16)


def low_lanes(rows):
    return lax.broadcasted_iota(jnp.int32, (rows, 128), 1) < SSM_DIM


def widen(v, g):
    low = low_lanes(v.shape[0])
    return jnp.where(low, v[:, 2 * g : 2 * g + 1], v[:, 2 * g + 1 : 2 * g + 2])


def per_head(v, g):
    lane = lax.broadcasted_iota(jnp.int32, v.shape, 1)
    first = jnp.sum(jnp.where(lane < SSM_DIM, v, 0.0), 1, keepdims=True)
    second = jnp.sum(jnp.where(lane < SSM_DIM, 0.0, v), 1, keepdims=True)
    return jnp.where(lane == 2 * g, first, jnp.where(lane == 2 * g + 1, second, 0.0))


def triangle():
    row = lax.broadcasted_iota(jnp.int32, (ROWS, ROWS), 0)
    col = lax.broadcasted_iota(jnp.int32, (ROWS, ROWS), 1)
    return (col <= row).astype(F32).astype(BF16)


def running(v, lower, side):
    high, low = two_parts(v)
    middle, lowest = two_parts(v - high.astype(F32))
    return (
        dot(lower, high, side, 0) + dot(lower, middle, side, 0) + dot(lower, lowest, side, 0)
    )


def sigmoid(v):
    return 1.0 / (1.0 + jnp.exp(-v))


def softplus(v):
    return jnp.maximum(v, 0.0) + jnp.log(1.0 + jnp.exp(-jnp.abs(v)))


def lane_block(g):
    return pl.ds(pl.multiple_of(g * 128, 128), 128)


def decays(dt_ref, vec_ref, seg_ref, segx_ref, lower):
    pre = dt_ref[...] + vec_ref[0:1, :]
    step = softplus(pre)
    total = running(-step * vec_ref[1:2, :] * LOG2E, lower, 1)
    last = total[ROWS - 1 : ROWS, :]
    seg = seg_ref[...]
    seg_last, before = seg[ROWS - 1 : ROWS, :], segx_ref[7:8, :]
    carry = jnp.where(seg == seg_last, jnp.exp2(last - total), 0.0)
    entry = jnp.where(seg == before, jnp.exp2(total), 0.0)
    through = jnp.where(seg_last == before, jnp.exp2(last), 0.0)
    return pre, step, total, carry, entry, through


def conv_group(ext_ref, segx_ref, seg_ref, taps_ref, cols):
    total, inputs = None, []
    for k in range(CONV):
        same = segx_ref[pl.ds(5 + k, ROWS), :] == seg_ref[...]
        v = jnp.where(same, ext_ref[pl.ds(5 + k, ROWS), cols], 0.0)
        inputs.append(v)
        term = taps_ref[k : k + 1, cols] * v
        total = term if total is None else total + term
    return total, inputs


def scan_message(msg_ref, state_ref, through):
    high = through.astype(BF16)
    rest = through - high.astype(F32)
    middle = rest.astype(BF16)
    low = rest - middle.astype(F32)
    extra = jnp.concatenate([high.astype(F32), middle.astype(F32), low, jnp.zeros((5, 128), F32)], 0)
    extra = jnp.concatenate([extra, jnp.zeros((8, STATE - 128), F32)], 1)

    def fill(b):
        rows = state_ref[pl.ds(pl.multiple_of(b * SCAN_ROWS, 8), SCAN_ROWS), :]
        msg_ref[b] = jnp.concatenate([rows, extra], 0).astype(BF16)

    over(0, BLOCKS, fill)


class Scan:
    def __init__(self, reverse, me, msg, got, back, out, send, recv):
        self.reverse, self.me = reverse, me
        self.msg, self.got, self.back, self.out = msg, got, back, out
        self.send, self.recv = send, recv

    def there(self, o):
        d = (self.me + o) % BLOCKS
        return remote(
            self.msg.at[d], self.got.at[self.me], self.send.at[0, o], self.recv.at[0, o],
            block_at(d),
        )

    def arrived(self, phase, dst, o):
        s = (self.me + BLOCKS - o) % BLOCKS
        return remote(
            dst.at[s], dst.at[s], self.send.at[phase, o], self.recv.at[phase, o], block_at(s)
        )

    def start(self):
        over(1, BLOCKS, lambda o: self.there(o).start())
        self.got[self.me] = self.msg[self.me]

    def turn(self):
        me = self.me
        over(1, BLOCKS, lambda o: self.arrived(0, self.got, o).wait_recv())
        lane = lax.broadcasted_iota(jnp.int32, (SCAN_ROWS, 128), 1)
        row = lax.broadcasted_iota(jnp.int32, (SCAN_ROWS, 128), 0) + me * SCAN_ROWS
        at_head = (row >= lane * SSM_DIM) & (row < lane * SSM_DIM + SSM_DIM)

        def scan(i, state):
            k = BLOCKS - 1 - i if self.reverse else i
            message = self.got[k].astype(F32)
            self.back[k] = jnp.concatenate([state, jnp.zeros((8, STATE), F32)], 0).astype(BF16)

            @pl.when(k != me)
            def _():
                self.returned(k).start()

            factors = message[SCAN_ROWS : SCAN_ROWS + 1, :128]
            factors += message[SCAN_ROWS + 1 : SCAN_ROWS + 2, :128]
            factors += message[SCAN_ROWS + 2 : SCAN_ROWS + 3, :128]
            through = jnp.sum(jnp.where(at_head, factors, 0.0), 1, keepdims=True)
            return through * state + message[:SCAN_ROWS]

        lax.fori_loop(0, BLOCKS, scan, jnp.zeros((SCAN_ROWS, STATE), F32))
        self.out[me] = self.back[me]

    def returned(self, k):
        o = (k + BLOCKS - self.me) % BLOCKS
        return remote(
            self.back.at[k], self.out.at[self.me], self.send.at[1, o], self.recv.at[1, o],
            block_at(k),
        )

    def finish(self, state_ref):
        over(1, BLOCKS, lambda o: self.arrived(1, self.out, o).wait_recv())

        def fill(b):
            rows = self.out[b].astype(F32)
            state_ref[pl.ds(pl.multiple_of(b * SCAN_ROWS, 8), SCAN_ROWS), :] = rows[:SCAN_ROWS]

        over(0, BLOCKS, fill)

    def close(self):
        def sent(o):
            self.there(o).wait_send()
            self.returned((self.me + o) % BLOCKS).wait_send()

        over(1, BLOCKS, sent)


def key_segments(block):
    turned = jnp.transpose(block.astype(F32))
    return jnp.concatenate([turned[:, 0:1], turned[:, 1:2]], 0)


def causal_mask(s):
    row = lax.broadcasted_iota(jnp.int32, (ROWS, 2 * ROWS), 0)
    col = lax.broadcasted_iota(jnp.int32, (ROWS, 2 * ROWS), 1) % ROWS
    return jnp.where(row <= col, s, MASKED)


def mixing_bias(seg_ref, segrow_ref):
    row = lax.broadcasted_iota(jnp.int32, (ROWS, ROWS), 0)
    col = lax.broadcasted_iota(jnp.int32, (ROWS, ROWS), 1)
    same = segrow_ref[0:1, :ROWS] == seg_ref[:, 0:1]
    return jnp.where((col <= row) & same, 0.0, MASKED)


WIDE = 256
LAG = 3
AHEAD = 4
OWN = MODEL // NZ


class Reduce:
    def __init__(self, lefts, n, r_ref, rz, part, gx, half, gy, out_ref, sems):
        self.lefts, self.n = lefts, n
        self.r, self.rz, self.part, self.gx, self.half, self.gy = r_ref, rz, part, gx, half, gy
        self.out = out_ref
        (self.rz_send, self.rz_recv, self.gx_send, self.gx_recv, self.gy_send, self.gy_recv) = sems
        self.zl, self.x, self.y = (lax.axis_index(a) for a in SEQ)
        self.other = {"zl": 1 - self.zl}

    @staticmethod
    def scratch(n):
        v, dma = pltpu.VMEM, pltpu.SemaphoreType.DMA
        return [
            v((n, ROWS, WIDE), BF16),
            v((n, ROWS, WIDE), BF16),
            v((n, 4, 4, 64, WIDE), BF16),
            v((n, 3, 4, 64, WIDE), BF16),
            v((n, 4, 64, WIDE), BF16),
            v((n, 3, 64, WIDE), BF16),
            *[dma((n,))] * 6,
        ]

    def fill(self, arrays, c=0):
        for ref in arrays:
            for k in range(ref.shape[1] // WIDE):
                self.r[c] = ref[:, k * WIDE : (k + 1) * WIDE]
                c += 1

    def right(self, c):
        return remote(
            self.r.at[c], self.rz.at[c], self.rz_send.at[c], self.rz_recv.at[c], self.other
        )

    def start(self):
        over(0, AHEAD, lambda c: self.right(c).start())

    def spread(self, c, phase, o):
        along_x = c % 2 == phase
        x_to = jnp.where(along_x, (self.x + o) % NX, self.x)
        y_to = jnp.where(along_x, self.y, (self.y + o) % NY)
        return {"x": x_to, "y": y_to}, jnp.where(along_x, x_to, y_to)

    def send_first(self, c, o):
        where, d = self.spread(c, 0, o)
        return remote(
            self.part.at[c, d], self.gx.at[c, o - 1], self.gx_send.at[c], self.gx_recv.at[c], where
        )

    def send_second(self, c, o):
        where, d = self.spread(c, 1, o)
        return remote(
            self.half.at[c, d], self.gy.at[c, o - 1], self.gy_send.at[c], self.gy_recv.at[c], where
        )

    def whole(self, got, send, recv, c):
        return remote(got.at[c], got.at[c], send.at[c], recv.at[c], self.other)

    def product(self, c):
        @pl.when(c + AHEAD < self.n)
        def _():
            self.right(c + AHEAD).start()

        self.right(c).wait_recv()
        mine, theirs = self.r[c], self.rz[c]
        even = c % 2 == 0
        ends = [first for _, _, first in self.lefts[1:]] + [self.n]
        for (own, near, first), end in zip(self.lefts, ends):
            @pl.when((c >= first) & (c < end))
            def _():
                for i in range(NX):
                    a = own[pl.ds(pl.multiple_of(self.zl * OWN + i * 256, 256), 256), :]
                    b = near[pl.ds(i * 256, 256), :]
                    tile = (dot(a, mine) + dot(b, theirs)).astype(BF16)
                    for j in range(NY):
                        self.part[c, jnp.where(even, i, j), jnp.where(even, j, i)] = (
                            tile[j * 64 : (j + 1) * 64]
                        )
        for o in range(1, 4):
            self.send_first(c, o).start()

    def middle(self, c):
        self.whole(self.gx, self.gx_send, self.gx_recv, c).wait_recv()
        mine = jnp.where(c % 2 == 0, self.x, self.y)
        for j in range(4):
            total = self.part[c, mine, j].astype(F32)
            for o in range(3):
                total += self.gx[c, o, j].astype(F32)
            self.half[c, j] = total.astype(BF16)
        for o in range(1, 4):
            self.send_second(c, o).start()

    def last(self, c):
        self.whole(self.gy, self.gy_send, self.gy_recv, c).wait_recv()
        mine = jnp.where(c % 2 == 0, self.y, self.x)
        total = self.half[c, mine].astype(F32)
        for o in range(3):
            total += self.gy[c, o].astype(F32)
        self.out[:, pl.ds(pl.multiple_of(c * WIDE, WIDE), WIDE)] = total

    @property
    def steps(self):
        return self.n + 2 * LAG

    def step(self, i):
        @pl.when(i < self.n)
        def _():
            self.product(i)

        @pl.when((i >= LAG) & (i < self.n + LAG))
        def _():
            self.middle(i - LAG)

        @pl.when(i >= 2 * LAG)
        def _():
            self.last(i - 2 * LAG)

    def close(self):
        def sent(c):
            self.right(c).wait_send()
            self.whole(self.gx, self.gx_send, self.gx_recv, c).wait_send()
            self.whole(self.gy, self.gy_send, self.gy_recv, c).wait_send()

        over(0, self.n, sent)


class Left:
    def __init__(self, l_ref, lz, sems):
        zl, c = lax.axis_index("zl"), lax.axis_index("c")
        half = OWN // 2
        there = pl.ds(pl.multiple_of((1 - zl) * OWN + c * half, half), half)
        near, other = (pl.ds(pl.multiple_of(k * half, half), half) for k in (c, 1 - c))
        sem = [sems.at[k] for k in range(4)]
        self.out = remote(l_ref.at[there], lz.at[near], sem[0], sem[1], {"zl": 1 - zl})
        self.on = remote(lz.at[near], lz.at[near], sem[2], sem[3], {"c": 1 - c})
        self.back = remote(lz.at[other], lz.at[other], sem[2], sem[3], {"c": 1 - c})

    def start(self):
        self.out.start()

    def pass_on(self):
        self.out.wait_recv()
        self.on.start()

    def finish(self):
        self.back.wait_recv()

    def close(self):
        self.out.wait_send()
        self.on.wait_send()


HEAD_CHUNKS = 4


class HeadSum:
    def __init__(self, x, out, near, pair, far, sems):
        self.x, self.out, self.near, self.pair, self.far = x, out, near, pair, far
        self.near_send, self.near_recv, self.far_send, self.far_recv, self.end_send, self.end_recv = sems
        self.c, zh = lax.axis_index("c"), lax.axis_index("zh")
        self.sibling, self.opposite = {"c": 1 - self.c}, {"zh": 1 - zh}
        self.half = x.shape[0] // 2
        self.rows_each = self.half // HEAD_CHUNKS

    @staticmethod
    def scratch():
        v, dma = pltpu.VMEM, pltpu.SemaphoreType.DMA
        return [*[v((ROWS // 2, MODEL), BF16)] * 3, *[dma((HEAD_CHUNKS,))] * 6]

    def rows(self, core, k):
        return pl.ds(pl.multiple_of(core * self.half + k * self.rows_each, 16), self.rows_each)

    def local(self, k):
        return pl.ds(k * self.rows_each, self.rows_each)

    def first(self, k):
        return remote(
            self.x.at[self.rows(1 - self.c, k)], self.near.at[self.local(k)],
            self.near_send.at[k], self.near_recv.at[k], self.sibling,
        )

    def second(self, k):
        return remote(
            self.pair.at[self.local(k)], self.far.at[self.local(k)],
            self.far_send.at[k], self.far_recv.at[k], self.opposite,
        )

    def third(self, k, core):
        rows = self.rows(core, k)
        return remote(
            self.out.at[rows], self.out.at[rows], self.end_send.at[k], self.end_recv.at[k],
            self.sibling,
        )

    def start(self):
        for k in range(HEAD_CHUNKS):
            self.first(k).start()

    def across(self):
        for k in range(HEAD_CHUNKS):
            self.first(k).wait_recv()
            own = self.x[self.rows(self.c, k)].astype(F32)
            self.pair[self.local(k)] = (own + self.near[self.local(k)].astype(F32)).astype(BF16)
            self.second(k).start()

    def join(self):
        for k in range(HEAD_CHUNKS):
            self.second(k).wait_recv()
            total = self.pair[self.local(k)].astype(F32) + self.far[self.local(k)].astype(F32)
            self.out[self.rows(self.c, k)] = total.astype(BF16)
            self.third(k, self.c).start()

    def finish(self):
        for k in range(HEAD_CHUNKS):
            self.third(k, 1 - self.c).wait_recv()

    def close(self):
        for k in range(HEAD_CHUNKS):
            self.first(k).wait_send()
            self.second(k).wait_send()
            self.third(k, self.c).wait_send()


class Loads:
    def __init__(self, pairs, sems):
        self.copies = {
            id(there): pltpu.make_async_copy(here, there, sems.at[i])
            for i, (here, there) in enumerate(pairs)
        }

    def start(self):
        for copy in self.copies.values():
            copy.start()

    def need(self, *refs):
        for ref in refs:
            copy = self.copies.pop(id(ref), None)
            if copy is not None:
                copy.wait()


def fetching(kernel, n_in, late):
    def wrapped(*refs):
        count = len(late)
        ins, rest = list(refs[:n_in]), refs[n_in:]
        buffers, sems = rest[-1 - count : -1], rest[-1]
        pairs = []
        for buffer, i in zip(buffers, late):
            pairs.append((ins[i], buffer))
            ins[i] = buffer
        kernel(Loads(pairs, sems), *ins, *rest[: -1 - count])

    return wrapped


def call(kernel, name, args, late, outs, scratch, collective_id):
    spec = [
        pl.BlockSpec(memory_space=pl.ANY if i in late else pltpu.VMEM) for i in range(len(args))
    ]
    compiler = (
        pltpu.CompilerParams(vmem_limit_bytes=VMEM_LIMIT)
        if collective_id is None
        else params(collective_id)
    )
    return pl.pallas_call(
        fetching(kernel, len(args), late),
        name=name,
        out_shape=tuple(jax.ShapeDtypeStruct(*o) for o in outs),
        in_specs=spec,
        out_specs=tuple(vmem(len(outs))),
        scratch_shapes=[
            *scratch,
            *[pltpu.VMEM(args[i].shape, args[i].dtype) for i in late],
            pltpu.SemaphoreType.DMA((max(len(late), 1),)),
        ],
        compiler_params=compiler,
    )(*args)


def turn_pairs(v, cosine, sine, direction):
    return v * cosine + pltpu.roll(v, HEAD_DIM // 2, 1) * (sine * direction)


def transpose_to(out_ref, ref):
    for k in range(ref.shape[1] // 256):
        out_ref[k * 256 : (k + 1) * 256, :] = jnp.transpose(ref[:, k * 256 : (k + 1) * 256])


def project_kernel(
    loads, tok_ref, cot_ref, gain_ref, q_ref, kv_ref, x_ref, bc_ref, dt_ref, z_ref, cos_ref,
    sin_ref, seg_ref, segrow_ref,
    nt_ref, ct_ref, queries_ref, own_ref, x_out, bc_out, dt_out, z_out, edge_out, normed,
):
    loads.start()
    for r in range(0, ROWS, 32):
        rows = slice(r, r + 32)
        x = tok_ref[rows, :].astype(F32)
        scale = lax.rsqrt(jnp.mean(x * x, 1, keepdims=True) + EPSILON)
        normed[rows, :] = (x * scale * gain_ref[0:1, :]).astype(BF16)
    n = normed[...]
    cosine, sine = cos_ref[...], sin_ref[...]
    loads.need(q_ref, kv_ref)
    for h in range(q_ref.shape[1] // HEAD_DIM):
        raw = dot(n, q_ref[:, h * HEAD_DIM : (h + 1) * HEAD_DIM])
        queries_ref[h * ROWS : (h + 1) * ROWS, :] = turn_pairs(raw, cosine, sine, 1.0).astype(BF16)
    raw = dot(n, kv_ref[...])
    turned = turn_pairs(raw, cosine, sine, 1.0)
    own_ref[:ROWS, :] = jnp.where(lax.axis_index("c") == 0, turned, raw).astype(BF16)
    rows = [segrow_ref[0:1, :HEAD_DIM], segrow_ref[0:1, HEAD_DIM : 2 * HEAD_DIM]]
    own_ref[ROWS:, :] = jnp.concatenate([*rows, jnp.zeros((14, HEAD_DIM), F32)], 0).astype(BF16)
    loads.need(x_ref, bc_ref, dt_ref)
    x_out[...] = dot(n, x_ref[...]).astype(BF16)
    bc_out[...] = dot(n, bc_ref[...]).astype(BF16)
    dt_out[...] = dot(n, dt_ref[...])
    edge_out[:, :INNER] = x_out[ROWS - 16 :, :]
    edge_out[:, INNER : INNER + BC] = bc_out[ROWS - 16 :, :]
    edge_out[:, INNER + BC :] = seg_ref[ROWS - 16 :, :].astype(BF16)
    loads.need(z_ref)
    z_out[...] = dot(n, z_ref[...])
    transpose_to(nt_ref, normed)
    loads.need(cot_ref)
    transpose_to(ct_ref, cot_ref)


def project(*args):
    return call(
        project_kernel, "project", args, (1, 3, 4, 5, 6, 7, 8),
        [
            ((MODEL, ROWS), BF16),
            ((MODEL, ROWS), BF16),
            ((2 * ROWS, HEAD_DIM), BF16),
            ((ROWS + 16, HEAD_DIM), BF16),
            ((ROWS, INNER), BF16),
            ((ROWS, BC), BF16),
            ((ROWS, 128), F32),
            ((ROWS, INNER), F32),
            ((16, EDGE_WIDE), BF16),
        ],
        [pltpu.VMEM((ROWS, MODEL), BF16)],
        None,
    )


def feed_forward_kernel(
    loads, gated_ref, att_ref, tok_ref, cot_ref, gain_ref, out_w, attn_w, gate_w, up_w, down_w,
    hid_ref, ft_ref, dgate_ref, dup_ref, hidden_ref, ffn_ref, ghid_ref, mt_ref, gain_out,
    gg_ref, do_ref,
    x_ref, sum_ref, normed, mix_ref, *sums,
):
    loads.start()
    n_sum = len(HeadSum.scratch())
    first = HeadSum(x_ref, sum_ref, *sums[:3], sums[3:n_sum])
    second = HeadSum(x_ref, sum_ref, *sums[n_sum : n_sum + 3], sums[n_sum + 3 :])
    barrier = pltpu.get_barrier_semaphore()
    signal(barrier, first.sibling)
    signal(barrier, first.opposite)
    pl.semaphore_wait(barrier, 2)
    loads.need(out_w, attn_w)

    def mixed(rows):
        x_ref[rows, :] = (
            dot(gated_ref[rows, :], out_w[...]) + dot(att_ref[rows, :], attn_w[...])
        ).astype(BF16)

    c = lax.axis_index("c")
    other = pl.ds(pl.multiple_of((1 - c) * (ROWS // 2), ROWS // 2), ROWS // 2)
    own = pl.ds(pl.multiple_of(c * (ROWS // 2), ROWS // 2), ROWS // 2)
    mixed(other)
    first.start()
    mixed(own)
    first.across()

    wide = 256
    loads.need(cot_ref, down_w)
    for k in range(0, hidden_ref.shape[1], wide):
        ghid_ref[:, k : k + wide] = dot(cot_ref[...], down_w[k : k + wide, :], 1, 1)
    first.join()
    loads.need(tok_ref)
    first.finish()
    for r in range(0, ROWS, 32):
        rows = slice(r, r + 32)
        x = tok_ref[rows, :].astype(F32) + sum_ref[rows, :].astype(F32)
        hid_ref[rows, :] = x
        scale = lax.rsqrt(jnp.mean(x * x, 1, keepdims=True) + EPSILON)
        normed[rows, :] = (x * scale * gain_ref[0:1, :]).astype(BF16)
    loads.need(gate_w, up_w)
    for k in range(0, hidden_ref.shape[1], wide):
        cols = slice(k, k + wide)
        gate, up = dot(normed[...], gate_w[:, cols]), dot(normed[...], up_w[:, cols])
        grad = ghid_ref[:, cols]
        sig = sigmoid(gate)
        act = gate * sig
        hidden_ref[:, cols] = (act * up).astype(BF16)
        dgate_ref[:, cols] = (grad * up * sig * (1.0 + gate * (1.0 - sig))).astype(BF16)
        dup_ref[:, cols] = (grad * act).astype(BF16)
    first.close()

    def back(rows):
        x_ref[rows, :] = (
            dot(dgate_ref[rows, :], gate_w[...], 1, 1) + dot(dup_ref[rows, :], up_w[...], 1, 1)
        ).astype(BF16)

    back(other)
    second.start()
    back(own)
    second.across()
    ffn_ref[...] = dot(hidden_ref[...], down_w[...]).astype(BF16)
    transpose_to(ft_ref, normed)
    second.join()
    second.finish()
    for r in range(0, ROWS, 32):
        rows = slice(r, r + 32)
        x = hid_ref[rows, :]
        scale = lax.rsqrt(jnp.mean(x * x, 1, keepdims=True) + EPSILON)
        n = x * scale
        grad = sum_ref[rows, :].astype(F32)
        scaled = grad * gain_ref[0:1, :]
        along = jnp.mean(n * scaled, 1, keepdims=True)
        total = cot_ref[rows, :].astype(F32) + scale * (scaled - n * along)
        ghid_ref[rows, :] = total
        mix_ref[rows, :] = total.astype(BF16)
        gains = jnp.sum(grad * n, 0, keepdims=True)
        gain_out[0:1, :] = gains if r == 0 else gain_out[0:1, :] + gains
    grad_att = dot(mix_ref[...], attn_w[...], 1, 1).astype(BF16)
    for h in range(2):
        do_ref[h * ROWS : (h + 1) * ROWS, :] = grad_att[:, h * HEAD_DIM : (h + 1) * HEAD_DIM]
    gg_ref[...] = dot(mix_ref[...], out_w[...], 1, 1)
    transpose_to(mt_ref, mix_ref)
    second.close()


def feed_forward(*args):
    v = pltpu.VMEM
    ff = args[7].shape[1]
    return call(
        feed_forward_kernel, "feed_forward", args, (2, 3, 5, 6, 7, 8, 9),
        [
            ((ROWS, MODEL), F32),
            ((MODEL, ROWS), BF16),
            ((ROWS, ff), BF16),
            ((ROWS, ff), BF16),
            ((ROWS, ff), BF16),
            ((ROWS, MODEL), BF16),
            ((ROWS, MODEL), F32),
            ((MODEL, ROWS), BF16),
            ((8, MODEL), F32),
            ((ROWS, INNER), F32),
            ((2 * ROWS, HEAD_DIM), BF16),
        ],
        [
            v((ROWS, MODEL), BF16),
            v((ROWS, MODEL), BF16),
            v((ROWS, MODEL), BF16),
            v((ROWS, MODEL), BF16),
            *HeadSum.scratch(),
            *HeadSum.scratch(),
        ],
        4,
    )


EARLY = 6


def mixer_forward_kernel(
    loads, q_ref, own_ref, edge_ref, x_ref, bc_ref, dt_ref, z_ref, seg_ref, segrow_ref, xtaps_ref,
    bctaps_ref, vec_ref, skip_ref, nt_ref, ct_ref,
    att_ref, lse_ref, kv_ref, edge_out, gated_ref, core_ref, xact_ref, bcact_ref, state_ref,
    ntz_ref, ctz_ref, attlow_ref,
    m_ref, l_ref, acc_ref, xext, bcext, segx, local, msg, got, back, result, bias_ref, cb_ref,
    cumt_ref,
    send_sem, recv_sem, sib_send, sib_recv, edge_sem, scan_send, scan_recv, left_sem,
):
    me, c, zl = block_index(), lax.axis_index("c"), lax.axis_index("zl")
    at = me % PLANE
    sibling = {"c": 1 - c}
    loads.start()
    barrier = pltpu.get_barrier_semaphore()
    over(1, BLOCKS, lambda o: signal(barrier, block_at((me + o) % BLOCKS)))
    signal(barrier, sibling)
    pl.semaphore_wait(barrier, BLOCKS)

    def block_copy(src, j, send, where):
        return remote(src, kv_ref.at[c, j], send_sem.at[send], recv_sem.at[j], where)

    def arrival(j):
        return block_copy(own_ref, j, 0, sibling)

    to_sibling = lambda j, src: remote(
        src, kv_ref.at[c, j], sib_send.at[j], sib_recv.at[j], sibling
    )
    from_sibling = lambda j: remote(
        kv_ref.at[1 - c, j], kv_ref.at[1 - c, j], sib_send.at[j], sib_recv.at[j], sibling
    )
    across = block_copy(own_ref, me, PLANE - 1, {"zl": 1 - zl})

    def own_copy(k, wait):
        d, where = plane_peer(k, 1)

        @pl.when(d > at)
        def _():
            copy = block_copy(own_ref, me, k, where)
            copy.wait_send() if wait else copy.start()

    def relay_copy(k, wait):
        copy = block_copy(kv_ref.at[c, at], at, PLANE + k, plane_peer(k, 1)[1])
        copy.wait_send() if wait else copy.start()

    edge_copy = remote(
        edge_ref, edge_out, edge_sem.at[0], edge_sem.at[1], block_at((me + 1) % BLOCKS)
    )
    states = Scan(False, me, msg, got, back, result, scan_send, scan_recv)

    @pl.when(me < BLOCKS - 1)
    def _():
        edge_copy.start()

    @pl.when(zl == 0)
    def _():
        across.start()

    to_sibling(me, own_ref).start()
    over(0, EARLY, lambda k: own_copy(k, False))
    lefts = [Left(ct_ref, ctz_ref, left_sem.at[0]), Left(nt_ref, ntz_ref, left_sem.at[1])]

    kv_ref[c, me] = own_ref[...]
    xext[8:, :] = x_ref[...].astype(F32)
    bcext[8:, :] = bc_ref[...].astype(F32)
    segx[8:, :] = seg_ref[...]
    lower = triangle()
    bias_ref[...] = mixing_bias(seg_ref, segrow_ref)

    @pl.when(me > 0)
    def _():
        edge_copy.wait_recv()

    @pl.when(me == 0)
    def _():
        edge_out[...] = jnp.zeros_like(edge_out)

    edge = edge_out[...].astype(F32)[8:]
    xext[:8, :] = edge[:, :INNER]
    bcext[:8, :] = edge[:, INNER : INNER + BC]
    segx[:8, :] = edge[:, INNER + BC :]

    def activate(ext, taps, out):
        def group(g):
            pre, _ = conv_group(ext, segx, seg_ref, taps, lane_block(g))
            out[:, lane_block(g)] = (pre * sigmoid(pre)).astype(BF16)

        over(0, out.shape[1] // 128, group)

    activate(bcext, bctaps_ref, bcact_ref)
    activate(xext, xtaps_ref, xact_ref)

    _, step, total, carry, entry, through = decays(dt_ref, vec_ref, seg_ref, segx, lower)
    cumt_ref[...] = jnp.transpose(total)
    weight = step * carry
    b_low, c_low = bcact_ref[:, :STATE], bcact_ref[:, STATE:]
    for g in range(GROUPS):
        moved = xact_ref[:, g * 128 : (g + 1) * 128].astype(F32) * widen(weight, g)
        local[g * 128 : (g + 1) * 128, :] = dot(moved.astype(BF16), b_low, 0, 0)
    scan_message(msg, local, through)
    states.start()
    over(EARLY, PLANE - 1, lambda k: own_copy(k, False))

    @pl.when(zl == 1)
    def _():
        arrival(at).wait_recv()
        to_sibling(at, kv_ref.at[c, at]).start()
        over(0, PLANE - 1, lambda k: relay_copy(k, False))

    cb_ref[...] = dot(c_low, b_low, 1, 1)
    low_lane = lax.broadcasted_iota(jnp.int32, (ROWS, 128), 1) < SSM_DIM
    for g in range(GROUPS):
        cols = slice(g * 128, (g + 1) * 128)
        u = (xact_ref[:, cols].astype(F32) * widen(step, g)).astype(BF16)
        made = []
        for h in (2 * g, 2 * g + 1):
            gap = total[:, h : h + 1] - cumt_ref[h : h + 1, :] + bias_ref[...]
            made.append(dot((jnp.exp2(gap) * cb_ref[...]).astype(BF16), u))
        core_ref[:, cols] = jnp.where(low_lane, made[0], made[1])

    scale = LOG2E * HEAD_DIM**-0.5
    queries = q_ref[...]
    qseg = segrow_ref[0:1, :]

    def scores_of(j):
        s = dot(kv_ref[0, j, :ROWS], queries, 1, 1) * scale
        return jnp.where(key_segments(kv_ref[0, j, ROWS:]) == qseg, s, MASKED)

    from_sibling(me).wait_recv()
    s = causal_mask(scores_of(me))
    m = jnp.max(s, 0, keepdims=True)
    p = jnp.exp2(s - m)
    m_ref[...] = m
    l_ref[...] = jnp.sum(p, 0, keepdims=True)
    acc_ref[...] = dot(kv_ref[1, me, :ROWS], p.astype(BF16), 0, 0)

    states.turn()
    loads.need(nt_ref, ct_ref)
    for left in lefts:
        left.start()

    def forward(k):
        q, _ = plane_peer(k, -1)

        def one(j):
            arrival(j).wait_recv()
            to_sibling(j, kv_ref.at[c, j]).start()

        pl.when(q < at)(lambda: one(zl * PLANE + q))
        pl.when(zl == 1)(lambda: one(q))

    def attend(j):
        from_sibling(j).wait_recv()
        s = scores_of(j)
        m_old = m_ref[...]
        m = jnp.maximum(m_old, jnp.max(s, 0, keepdims=True))
        p = jnp.exp2(s - m)
        alpha = jnp.exp2(m_old - m)
        m_ref[...] = m
        l_ref[...] = l_ref[...] * alpha + jnp.sum(p, 0, keepdims=True)
        acc_ref[...] = acc_ref[...] * alpha + dot(kv_ref[1, j, :ROWS], p.astype(BF16), 0, 0)

    forward(0)

    @pl.when(zl == 1)
    def _():
        attend(at)

    def step_over(k):
        @pl.when(k + 1 < PLANE - 1)
        def _():
            forward(k + 1)

        q, _ = plane_peer(k, -1)
        pl.when(q < at)(lambda: attend(zl * PLANE + q))
        pl.when(zl == 1)(lambda: attend(q))

    over(0, PLANE - 1, step_over)
    for left in lefts:
        left.pass_on()
    attended = jnp.transpose(acc_ref[...] / l_ref[...])
    att_ref[...] = attended
    for h in range(2):
        attlow_ref[:, h * HEAD_DIM : (h + 1) * HEAD_DIM] = (
            attended[h * ROWS : (h + 1) * ROWS].astype(BF16)
        )
    lse_ref[...] = jnp.broadcast_to(m_ref[...] + jnp.log2(l_ref[...]), lse_ref.shape)

    states.finish(state_ref)
    loads.need(z_ref)
    for g in range(GROUPS):
        cols = slice(g * 128, (g + 1) * 128)
        outer = dot(c_low, state_ref[cols, :].astype(BF16), 1, 1) * widen(entry, g)
        core = core_ref[:, cols] + outer
        core_ref[:, cols] = core
        out = core + skip_ref[0:1, cols] * xact_ref[:, cols].astype(F32)
        z = z_ref[:, cols]
        gated_ref[:, cols] = (out * z * sigmoid(z)).astype(BF16)

    states.close()
    for left in lefts:
        left.finish()
        left.close()
    to_sibling(me, own_ref).wait_send()
    over(0, PLANE - 1, lambda k: own_copy(k, True))

    @pl.when(zl == 0)
    def _():
        across.wait_send()

    @pl.when(zl == 1)
    def _():
        over(0, PLANE - 1, lambda k: relay_copy(k, True))
        over(0, PLANE, lambda j: to_sibling(j, own_ref).wait_send())

    over(0, at, lambda q: to_sibling(zl * PLANE + q, own_ref).wait_send())

    @pl.when(me < BLOCKS - 1)
    def _():
        edge_copy.wait_send()


def mixer_forward(*args):
    wide = 2 * ROWS
    dma = pltpu.SemaphoreType.DMA
    return call(
        mixer_forward_kernel, "mixer_forward", args, (6, 13, 14),
        [
            ((wide, HEAD_DIM), F32),
            ((8, wide), F32),
            ((2, BLOCKS, ROWS + 16, HEAD_DIM), BF16),
            ((16, EDGE_WIDE), BF16),
            ((ROWS, INNER), BF16),
            ((ROWS, INNER), F32),
            ((ROWS, INNER), BF16),
            ((ROWS, BC), BF16),
            ((INNER, STATE), F32),
            ((OWN, ROWS), BF16),
            ((OWN, ROWS), BF16),
            ((ROWS, 2 * HEAD_DIM), BF16),
        ],
        [
            pltpu.VMEM((1, wide), F32),
            pltpu.VMEM((1, wide), F32),
            pltpu.VMEM((HEAD_DIM, wide), F32),
            pltpu.VMEM((ROWS + 8, INNER), F32),
            pltpu.VMEM((ROWS + 8, BC), F32),
            pltpu.VMEM((ROWS + 8, 128), F32),
            pltpu.VMEM((INNER, STATE), F32),
            *[pltpu.VMEM((BLOCKS, SCAN_ROWS + 8, STATE), BF16)] * 4,
            pltpu.VMEM((ROWS, ROWS), F32),
            pltpu.VMEM((ROWS, ROWS), F32),
            pltpu.VMEM((128, ROWS), F32),
            *[dma((BLOCKS,))] * 4,
            dma((2,)),
            dma((2, BLOCKS)),
            dma((2, BLOCKS)),
            dma((2, 4)),
        ],
        1,
    )


def mixer_backward_kernel(
    loads, q_ref, do_ref, att_ref, lse_ref, segrow_ref, kv_ref, gg_ref, z_ref, core_ref, xact_ref,
    bcact_ref, x_ref, bcown_ref, edge_in, dt_ref, state_ref, seg_ref, xtaps_ref, bctaps_ref,
    vec_ref, skip_ref, dgate_ref, dup_ref, hidden_ref, ft_ref, ct_ref, ctz_ref, mt_ref, cos_ref,
    sin_ref,
    dqraw_ref, misc_ref, dz_ref, dx_ref, ddt_ref, dxtaps_ref, dbctaps_ref, dvec_ref,
    w_ref, mtz_ref,
    dkv_ref, dqt_ref, mine, theirs, sib, kvgot, relay_ref, total_ref, xext, bcext, segx, local, msg, got, back, result,
    bias_ref, cb_ref, cumt_ref, g_ref, du_ref, dbc_all, shares, share_got, edge_ref,
    edge_out, enter_ref, gext, dcum_ref, ddtx_ref,
    send_sem, recv_sem, sib_send, sib_recv, edge_sem, scan_send, scan_recv, share_send, share_recv,
    ftz_ref, left_sem, *reduce,
):
    me, c, zh, zl = block_index(), *(lax.axis_index(a) for a in ("c", "zh", "zl"))
    head_at = zh * 2 + c
    sibling = {"c": 1 - c}
    at_head = lambda d: {"zh": d // 2, "c": d % 2}
    loads.start()
    barrier = pltpu.get_barrier_semaphore()
    over(1, BLOCKS, lambda o: signal(barrier, block_at((me + o) % BLOCKS)))
    for o in range(1, 4):
        signal(barrier, at_head((head_at + o) % 4))
    pl.semaphore_wait(barrier, BLOCKS + 2)

    at = me % PLANE
    to_sibling = lambda j: remote(
        theirs.at[j], sib.at[j], sib_send.at[j], sib_recv.at[j], sibling
    )

    def to_owner(k, kind):
        q, where = plane_peer(k, -1)
        j = q if kind else zl * PLANE + q
        return remote(
            mine.at[j], kvgot.at[kind, at], send_sem.at[kind, k], recv_sem.at[kind, at], where
        )

    def from_plane(kind, q):
        return remote(
            kvgot.at[kind, q], kvgot.at[kind, q], send_sem.at[kind, 0], recv_sem.at[kind, q],
            sibling,
        )

    across = remote(
        relay_ref, kvgot.at[1, 0], send_sem.at[0, PLANE - 1], recv_sem.at[1, 0], {"zl": 1 - zl}
    )
    states = Scan(True, me, msg, got, back, result, scan_send, scan_recv)
    rs = Reduce(
        [(ft_ref, ftz_ref, 0), (ct_ref, ctz_ref, 8)], 12, *reduce[:6], w_ref, reduce[6:]
    )
    lefts = [Left(ft_ref, ftz_ref, left_sem.at[0]), Left(mt_ref, mtz_ref, left_sem.at[1])]
    loads.need(ft_ref, dgate_ref, dup_ref, hidden_ref)
    lefts[0].start()
    rs.fill([dgate_ref, dup_ref, hidden_ref])
    rs.start()

    lower = triangle()
    edge = edge_in[...].astype(F32)[8:]
    xext[:8, :] = edge[:, :INNER]
    segx[:8, :] = edge[:, INNER + BC :]
    xext[8:, :] = x_ref[...].astype(F32)
    segx[8:, :] = seg_ref[...]
    bcext[...] = bcown_ref[...].astype(F32)[8:]
    bias_ref[...] = mixing_bias(seg_ref, segrow_ref)
    pre_dt, step, total, carry, entry, through = decays(dt_ref, vec_ref, seg_ref, segx, lower)
    cumt_ref[...] = jnp.transpose(total)
    b_low, c_low = bcact_ref[:, :STATE], bcact_ref[:, STATE:]
    dcum = jnp.zeros((ROWS, 128), F32)
    dskip = jnp.zeros((8, 128), F32)
    dc = jnp.zeros((ROWS, STATE), F32)
    for g in range(GROUPS):
        cols = slice(g * 128, (g + 1) * 128)
        z, core, x = z_ref[:, cols], core_ref[:, cols], xact_ref[:, cols].astype(F32)
        sig = sigmoid(z)
        gg = gg_ref[:, cols]
        out = core + skip_ref[0:1, cols] * x
        dz_ref[:, cols] = (gg * out * sig * (1.0 + z * (1.0 - sig))).astype(BF16)
        grad = gg * z * sig
        g_ref[:, cols] = grad
        dcum += per_head(grad * core, g)
        dskip += per_head(jnp.broadcast_to(jnp.sum(grad * x, 0, keepdims=True), (8, 128)), g)
        entered = (grad * widen(entry, g)).astype(BF16)
        local[cols, :] = dot(entered, c_low, 0, 0)
        dc += dot(entered, state_ref[cols, :].astype(BF16))
    scan_message(msg, local, through)
    states.start()
    dbc_all[:, STATE:] = dc

    cb_ref[...] = dot(c_low, b_low, 1, 1)
    low_lane = lax.broadcasted_iota(jnp.int32, (ROWS, 128), 1) < SSM_DIM
    dcb = jnp.zeros((ROWS, ROWS), F32)
    for g in range(GROUPS):
        cols = slice(g * 128, (g + 1) * 128)
        u = xact_ref[:, cols].astype(F32) * widen(step, g)
        u_low, grad = u.astype(BF16), g_ref[:, cols]
        grad_low = grad.astype(BF16)
        made = []
        for i in range(2):
            h = 2 * g + i
            decay = jnp.exp2(total[:, h : h + 1] - cumt_ref[h : h + 1, :] + bias_ref[...])
            mixing = (decay * cb_ref[...]).astype(BF16)
            made.append(dot(mixing, grad_low, 0, 0))
            half = jnp.where(low_lane if i == 0 else ~low_lane, grad, 0.0).astype(BF16)
            dcb += decay * dot(half, u_low, 1, 1)
        du = jnp.where(low_lane, made[0], made[1])
        du_ref[:, cols] = du
        dcum -= per_head(u * du, g)
    dcum_ref[...] = dcum
    dcb_low = dcb.astype(BF16)
    dbc_all[:, :STATE] = dot(dcb_low, c_low, 0, 0)
    dbc_all[:, STATE:] += dot(dcb_low, b_low)

    loads.need(q_ref, do_ref, att_ref, kv_ref)
    scale = LOG2E * HEAD_DIM**-0.5
    queries, grads = q_ref[...], do_ref[...]
    lse, qseg = lse_ref[0:1, :], segrow_ref[0:1, :]
    high, low = two_parts(grads.astype(F32) * att_ref[...])
    ones = jnp.ones((8, HEAD_DIM), BF16)
    delta = (dot(ones, high, 1, 1) + dot(ones, low, 1, 1))[0:1, :]

    def block(t, own):
        keys = kv_ref[0, t, :ROWS]
        s = dot(keys, queries, 1, 1) * scale
        s = jnp.where(key_segments(kv_ref[0, t, ROWS:]) == qseg, s, MASKED)
        if own:
            s = causal_mask(s)
        p = jnp.exp2(s - lse)
        ds = (p * (dot(kv_ref[1, t, :ROWS], grads, 1, 1) - delta)).astype(BF16)
        dk = dot(ds, queries)
        dv = dot(p.astype(BF16), grads)
        change = dot(keys, ds, 0, 0)
        dqt_ref[...] = change if own else dqt_ref[...] + change
        mine[t] = jnp.where(c == 0, dk, dv).astype(BF16)
        theirs[t] = jnp.where(c == 0, dv, dk).astype(BF16)
        to_sibling(t).start()

    def pair(t):
        to_sibling(t).wait_recv()
        return mine[t].astype(F32) + sib[t].astype(F32)

    block(me, True)
    lefts[0].pass_on()
    states.turn()
    loads.need(mt_ref, ct_ref, ctz_ref)
    lefts[1].start()
    lefts[0].finish()

    @pl.when(zl == 1)
    def _():
        block(at, False)

    def give(k):
        q, _ = plane_peer(k, -1)

        @pl.when(q < at)
        def _():
            j = zl * PLANE + q
            mine[j] = pair(j).astype(BF16)
            to_owner(k, 0).start()

        @pl.when(zl == 1)
        def _():
            mine[q] = pair(q).astype(BF16)
            to_owner(k, 1).start()

    def step_over(k):
        q, _ = plane_peer(k, -1)
        pl.when(q < at)(lambda: block(zl * PLANE + q, False))
        pl.when(zl == 1)(lambda: block(q, False))

        @pl.when(k >= 1)
        def _():
            give(k - 1)

        @pl.when(k % 2 == 1)
        def _():
            rs.step(k // 2)

    over(0, PLANE - 1, step_over)
    give(PLANE - 2)
    done = (PLANE - 1) // 2

    def reduce_some(n):
        nonlocal done
        over(done, done + n, rs.step)
        done += n

    reduce_some(1)
    lefts[1].pass_on()
    dkv_ref[...] = pair(me)

    @pl.when(zl == 1)
    def _():
        total_ref[...] = pair(at)

    score_scale = HEAD_DIM**-0.5
    dq = jnp.transpose(dqt_ref[...]) * score_scale
    cosine, sine = cos_ref[...], sin_ref[...]
    for h in range(2):
        raw = turn_pairs(dq[h * ROWS : (h + 1) * ROWS], cosine, sine, -1.0)
        dqraw_ref[:, h * HEAD_DIM : (h + 1) * HEAD_DIM] = raw.astype(BF16)

    states.finish(enter_ref)
    dcum = dcum_ref[...]
    dstep = jnp.zeros((ROWS, 128), F32)
    dlast = jnp.zeros((8, 128), F32)
    db = jnp.zeros((ROWS, STATE), F32)
    for g in range(GROUPS):
        cols = slice(g * 128, (g + 1) * 128)
        entering = enter_ref[cols, :]
        entering_low = entering.astype(BF16)
        x = xact_ref[:, cols].astype(F32)
        steps, carries = widen(step, g), widen(carry, g)
        v = x * steps * carries
        dv = dot(b_low, entering_low, 1, 1)
        db += dot(v.astype(BF16), entering_low)
        dcarry = per_head(v * dv, g)
        dcum -= dcarry
        dlast += jnp.broadcast_to(jnp.sum(dcarry, 0, keepdims=True), (8, 128))
        du = du_ref[:, cols] + carries * dv
        dstep += per_head(x * du, g)
        pieces = jnp.sum(entering * state_ref[cols, :], 1, keepdims=True)
        both = jnp.sum(jnp.broadcast_to(pieces, (128, 128)) * head_of_lane_f32(g), 0, keepdims=True)
        dlast += through * both
        g_ref[:, cols] = steps * du + skip_ref[0:1, cols] * g_ref[:, cols]
    dbc_all[:, :STATE] += db
    last_row = lax.broadcasted_iota(jnp.int32, (ROWS, 128), 0) == ROWS - 1
    dcum += jnp.where(last_row, dlast[0:1, :], 0.0)
    da = running(dcum, lower, 0)
    rate = vec_ref[1:2, :]
    drate = -jnp.sum(step * da, 0, keepdims=True)
    ddt = (dstep - rate * da) * sigmoid(pre_dt)
    ddt_ref[...] = ddt.astype(BF16)
    dbias = jnp.sum(ddt, 0, keepdims=True)
    dvec_ref[...] = jnp.concatenate([dbias, drate, dskip[0:1, :], jnp.zeros((5, 128), F32)], 0)

    reduce_some(1)

    for d in range(4):
        shares[d] = dbc_all[:, d * 128 : (d + 1) * 128].astype(BF16)
    share = lambda o: remote(
        shares.at[(head_at + o) % 4], share_got.at[o], share_send.at[o], share_recv.at[o],
        at_head((head_at + o) % 4),
    )
    for o in range(1, 4):
        share(o).start()

    def conv_back(ext, taps, grad, cols, out_taps, out_grad):
        pre, inputs = conv_group(ext, segx, seg_ref, taps, cols)
        sig = sigmoid(pre)
        dpre = grad * sig * (1.0 + pre * (1.0 - sig))
        gext[...] = jnp.zeros_like(gext)
        rows = []
        for k in range(CONV):
            rows.append(jnp.sum(dpre * inputs[k], 0, keepdims=True))
            same = segx[pl.ds(5 + k, ROWS), :] == seg_ref[...]
            gext[pl.ds(5 + k, ROWS), :] += jnp.where(same, taps[k : k + 1, cols] * dpre, 0.0)
        out_taps[:, cols] = jnp.concatenate([*rows, jnp.zeros((4, 128), F32)], 0)
        out_grad[...] = gext[...]

    def x_group(g):
        cols = lane_block(g)
        conv_back(xext, xtaps_ref, g_ref[:, cols], cols, dxtaps_ref, ddtx_ref)
        edge_ref[:, cols] = ddtx_ref[:8, :]
        g_ref[:, cols] = ddtx_ref[8:, :]

    over(0, GROUPS, x_group)
    reduce_some(2)
    grad_bc = shares[head_at].astype(F32)
    for o in range(1, 4):
        share(o).wait_recv()
        grad_bc += share_got[o].astype(F32)
    conv_back(bcext, bctaps_ref, grad_bc, slice(0, 128), dbctaps_ref, ddtx_ref)
    edge_ref[:, INNER:] = ddtx_ref[:8, :]
    edge_copy = remote(
        edge_ref, edge_out, edge_sem.at[0], edge_sem.at[1], block_at((me + BLOCKS - 1) % BLOCKS)
    )

    @pl.when(me > 0)
    def _():
        edge_copy.start()

    reduce_some(2)

    def collect(q):
        @pl.when((zl == 1) & (q != at))
        def _():
            from_plane(1, q).wait_recv()
            total_ref[...] += kvgot[1, q].astype(F32)

    over(0, PLANE, collect)

    @pl.when(zl == 1)
    def _():
        relay_ref[...] = total_ref[...].astype(BF16)
        across.start()

    reduce_some(1)

    def collect_own(q):
        from_plane(0, q).wait_recv()
        dkv_ref[...] += kvgot[0, q].astype(F32)

    over(at + 1, PLANE, collect_own)

    @pl.when(zl == 0)
    def _():
        from_plane(1, 0).wait_recv()
        dkv_ref[...] += kvgot[1, 0].astype(F32)

    @pl.when(me < BLOCKS - 1)
    def _():
        edge_copy.wait_recv()

    @pl.when(me == BLOCKS - 1)
    def _():
        edge_out[...] = jnp.zeros_like(edge_out)

    tail = pl.ds(ROWS - 8, 8)
    g_ref[tail, :] += edge_out[:, :INNER]
    ddtx_ref[pl.ds(ROWS, 8), :] += edge_out[:, INNER:]
    dx_ref[...] = g_ref[...].astype(BF16)
    misc_ref[:, :128] = ddtx_ref[8:, :].astype(BF16)
    dkv = dkv_ref[...]
    turned = turn_pairs(dkv * score_scale, cosine, sine, -1.0)
    misc_ref[:, 128:] = jnp.where(c == 0, turned, dkv).astype(BF16)

    reduce_some(rs.steps - done)

    @pl.when(me > 0)
    def _():
        edge_copy.wait_send()

    states.close()
    rs.close()
    lefts[0].close()
    lefts[1].finish()
    lefts[1].close()
    for o in range(1, 4):
        share(o).wait_send()
    to_sibling(me).wait_send()

    def given(k):
        q, _ = plane_peer(k, -1)

        @pl.when(q < at)
        def _():
            to_sibling(zl * PLANE + q).wait_send()
            to_owner(k, 0).wait_send()

        @pl.when(zl == 1)
        def _():
            to_sibling(q).wait_send()
            to_owner(k, 1).wait_send()

    over(0, PLANE - 1, given)

    @pl.when(zl == 1)
    def _():
        to_sibling(at).wait_send()
        across.wait_send()


def head_of_lane_f32(g):
    row = lax.broadcasted_iota(jnp.int32, (128, 128), 0)
    lane = lax.broadcasted_iota(jnp.int32, (128, 128), 1)
    return (lane == 2 * g + (row >= SSM_DIM).astype(jnp.int32)).astype(F32)


def mixer_backward(*args):
    wide = 2 * ROWS
    dma = pltpu.SemaphoreType.DMA
    v = pltpu.VMEM
    piece = (BLOCKS, ROWS, HEAD_DIM)
    return call(
        mixer_backward_kernel, "mixer_backward", args, (0, 1, 2, 5, 21, 22, 23, 24, 25, 26, 27),
        [
            ((ROWS, 2 * HEAD_DIM), BF16),
            ((ROWS, 256), BF16),
            ((ROWS, INNER), BF16),
            ((ROWS, INNER), BF16),
            ((ROWS, 128), BF16),
            ((8, INNER), F32),
            ((8, 128), F32),
            ((8, 128), F32),
            ((64, 12 * WIDE), F32),
            ((OWN, ROWS), BF16),
        ],
        [
            v((ROWS, HEAD_DIM), F32),
            v((HEAD_DIM, wide), F32),
            *[v(piece, BF16)] * 3,
            v((2, PLANE, ROWS, HEAD_DIM), BF16),
            v((ROWS, HEAD_DIM), BF16),
            v((ROWS, HEAD_DIM), F32),
            v((ROWS + 8, INNER), F32),
            v((ROWS + 8, 128), F32),
            v((ROWS + 8, 128), F32),
            v((INNER, STATE), F32),
            *[v((BLOCKS, SCAN_ROWS + 8, STATE), BF16)] * 4,
            v((ROWS, ROWS), F32),
            v((ROWS, ROWS), F32),
            v((128, ROWS), F32),
            v((ROWS, INNER), F32),
            v((ROWS, INNER), F32),
            v((ROWS, BC), F32),
            v((4, ROWS, 128), BF16),
            v((4, ROWS, 128), BF16),
            v((8, GRAD_EDGE), F32),
            v((8, GRAD_EDGE), F32),
            v((INNER, STATE), F32),
            v((ROWS + 8, 128), F32),
            v((ROWS, 128), F32),
            v((ROWS + 8, 128), F32),
            dma((2, PLANE)),
            dma((2, PLANE)),
            dma((BLOCKS,)),
            dma((BLOCKS,)),
            dma((2,)),
            dma((2, BLOCKS)),
            dma((2, BLOCKS)),
            dma((4,)),
            dma((4,)),
            v((OWN, ROWS), BF16),
            dma((2, 4)),
            *Reduce.scratch(12),
        ],
        2,
    )


SMALL = 8 * 128
SMALL_AT = 5
CHUNKS = 13
GATHER_FROM = CHUNKS


def finish_kernel(
    loads, misc_ref, dx_ref, dz_ref, dq_ref, ddt_ref, gated_ref, att_ref, nt_ref, ntz_ref, mt_ref,
    mtz_ref, ffn_ref, tok_ref, small_ref, x_w, z_w, q_w, dt_w, bc_w, kv_w,
    w_ref, all_ref, alls_ref, back_sum, ffn_sum,
    back_ref, own_small, mine, esum, egot, e_send, e_recv, z_send, z_recv, w_send, w_recv,
    sib_send, sib_recv, s_send, s_recv, t_send, t_recv, part_ref, *rest,
):
    loads.start()
    me, c, zh = block_index(), lax.axis_index("c"), lax.axis_index("zh")
    chip = zh * BLOCKS + me
    sibling = {"c": 1 - c}

    def chip_at(p):
        return {"zh": p // BLOCKS, **block_at(p % BLOCKS)}

    n_rs = len(Reduce.scratch(CHUNKS))
    rs = Reduce(
        [(nt_ref, ntz_ref, 0), (mt_ref, mtz_ref, 9)], CHUNKS, *rest[:6], w_ref, rest[6:n_rs]
    )
    rest = rest[n_rs:]
    n_sum = len(HeadSum.scratch())
    back = HeadSum(back_ref, back_sum, *rest[:3], rest[3:n_sum])
    rest = rest[n_sum:]
    ffn = HeadSum(ffn_ref, ffn_sum, *rest[:3], rest[3:])

    barrier = pltpu.get_barrier_semaphore()
    over(1, CHIPS, lambda o: signal(barrier, chip_at((chip + o) % CHIPS)))
    signal(barrier, sibling)
    pl.semaphore_wait(barrier, CHIPS)

    loads.need(gated_ref, att_ref)
    rs.fill([misc_ref, dx_ref, dz_ref, dq_ref])
    rs.r[8, :, :128] = ddt_ref[...]
    rs.r[8, :, 128:] = jnp.zeros_like(ddt_ref)
    rs.fill([gated_ref, att_ref], 9)
    over(0, 2, lambda k: rs.right(k).start())
    loads.need(x_w, z_w, q_w, dt_w, bc_w, kv_w)

    def partial(rows):
        total = dot(dx_ref[rows, :], x_w[...], 1, 1)
        total += dot(dz_ref[rows, :], z_w[...], 1, 1)
        total += dot(dq_ref[rows, :], q_w[...], 1, 1)
        total += dot(ddt_ref[rows, :], dt_w[...], 1, 1)
        total += dot(misc_ref[rows, :128], bc_w[...], 1, 1)
        back_ref[rows, :] = (total + dot(misc_ref[rows, 128:], kv_w[...], 1, 1)).astype(BF16)

    half = ROWS // 2
    partial(pl.ds(pl.multiple_of((1 - c) * half, half), half))
    back.start()
    partial(pl.ds(pl.multiple_of(c * half, half), half))
    loads.need(nt_ref, ntz_ref, mt_ref, mtz_ref, ffn_ref, tok_ref)
    back.across()
    over(2, AHEAD, lambda k: rs.right(k).start())
    ffn.start()

    at, level = me % PLANE, zh * NZ + lax.axis_index("zl")

    def along_z(o):
        d = (level + o) % 4
        where = {"zh": d // NZ, "zl": d % NZ}
        return remote(mine, all_ref.at[c, at, level], z_send.at[o], z_recv.at[o], where)

    def column(k):
        return remote(
            all_ref.at[c, at], all_ref.at[c, at], w_send.at[k], w_recv.at[at], plane_peer(k, 1)[1]
        )

    def to_sibling(q, core):
        return remote(
            all_ref.at[core, q], all_ref.at[core, q], sib_send.at[q], sib_recv.at[q], sibling
        )

    def pass_on(k):
        q, where = plane_peer(k, -1)
        remote(
            all_ref.at[c, q], all_ref.at[c, q], w_send.at[k], w_recv.at[q], where
        ).wait_recv()
        to_sibling(q, c).start()

    def columns_out():
        for o in range(1, 4):
            along_z(o).wait_recv()
        over(0, PLANE - 1, lambda k: column(k).start())
        to_sibling(at, c).start()

    def share(d):
        return remote(own_small.at[d], egot.at[me], e_send.at[d], e_recv.at[me], block_at(d))

    def shared(s):
        return remote(egot.at[s], egot.at[s], e_send.at[0], e_recv.at[s], block_at(s))

    def small_spread(o):
        d = (chip + o) % CHIPS
        slot = zh * SMALL_AT + me
        return remote(esum, alls_ref.at[c, slot], s_send.at[o], s_recv.at[slot], chip_at(d))

    def small_sibling(slot, core):
        return remote(
            alls_ref.at[core, slot], alls_ref.at[core, slot], t_send.at[slot], t_recv.at[slot],
            sibling,
        )

    def gradient():
        for r in range(0, ROWS, 32):
            rows = pl.ds(r, 32)
            x = tok_ref[rows, :].astype(F32)
            scale = lax.rsqrt(jnp.mean(x * x, 1, keepdims=True) + EPSILON)
            n = x * scale
            grad = back_sum[rows, :].astype(F32)
            gains = jnp.sum(grad * n, 0, keepdims=True)
            for k in range(MODEL // 128):
                piece = gains[:, k * 128 : (k + 1) * 128]
                part_ref[k : k + 1, :] = piece if r == 0 else part_ref[k : k + 1, :] + piece
        quarter = MODEL // 4 // 128
        own_small[...] = small_ref[...]
        own_small[0, :quarter] = part_ref[pl.ds((zh * 2 + c) * quarter, quarter), :]

        def give(d):
            @pl.when(d != me)
            def _():
                share(d).start()

        over(0, SMALL_AT, give)

    def small_sums():
        @pl.when(me < SMALL_AT)
        def _():
            egot[me] = own_small[me]

            def take(s):
                @pl.when(s != me)
                def _():
                    shared(s).wait_recv()

            over(0, BLOCKS, take)
            total = lax.fori_loop(0, BLOCKS, lambda s, t: t + egot[s], jnp.zeros((8, 128), F32))
            esum[...] = jnp.concatenate([total, jnp.zeros_like(total)], 0).astype(BF16)
            slot = zh * SMALL_AT + me
            alls_ref[c, slot] = esum[...]
            over(1, CHIPS, lambda o: small_spread(o).start())
            small_sibling(slot, c).start()

    def small_pass():
        def one(slot):
            @pl.when(slot != zh * SMALL_AT + me + jnp.where(me < SMALL_AT, 0, CHIPS))
            def _():
                remote(
                    esum, alls_ref.at[c, slot], s_send.at[0], s_recv.at[slot], sibling
                ).wait_recv()
                small_sibling(slot, c).start()

        over(0, 2 * SMALL_AT, one)

    def weights_out():
        mine[...] = w_ref[:, :WIDE].astype(BF16)
        all_ref[c, at, level] = mine[...]
        for o in range(1, 4):
            along_z(o).start()

    batch, first_pass = 3, rs.steps - 5

    def step(i):
        rs.step(i)

        @pl.when(i == 3)
        def _():
            back.join()

        @pl.when(i == 4)
        def _():
            back.finish()
            gradient()

        @pl.when(i == 2 * LAG)
        def _():
            weights_out()

        @pl.when(i == 7)
        def _():
            ffn.across()

        @pl.when(i == 8)
        def _():
            small_sums()

        @pl.when(i == 9)
        def _():
            columns_out()

        @pl.when(i >= first_pass)
        def _():
            k = i - first_pass
            over(k * batch, (k + 1) * batch, pass_on)

    over(0, rs.steps, step)
    ffn.join()
    small_pass()
    ffn.finish()

    over(0, PLANE, lambda q: to_sibling(q, 1 - c).wait_recv())
    over(0, 2 * SMALL_AT, lambda s: small_sibling(s, 1 - c).wait_recv())
    rs.close()
    back.close()
    ffn.close()
    over(0, PLANE, lambda q: to_sibling(q, c).wait_send())
    over(0, 2 * SMALL_AT, lambda s: small_sibling(s, c).wait_send())
    over(0, PLANE - 1, lambda k: column(k).wait_send())
    for o in range(1, 4):
        along_z(o).wait_send()

    @pl.when(me < SMALL_AT)
    def _():
        over(1, CHIPS, lambda o: small_spread(o).wait_send())

    def given(d):
        @pl.when(d != me)
        def _():
            share(d).wait_send()

    over(0, SMALL_AT, given)


def finish(*args):
    v, dma = pltpu.VMEM, pltpu.SemaphoreType.DMA
    return call(
        finish_kernel, "finish", args, (5, 6, 7, 8, 9, 10, 11, 12, 14, 15, 16, 17, 18, 19),
        [
            ((64, CHUNKS * WIDE), F32),
            ((2, PLANE, 4, 64, WIDE), BF16),
            ((2, 2 * SMALL_AT, 16, 128), BF16),
            ((ROWS, MODEL), BF16),
            ((ROWS, MODEL), BF16),
        ],
        [
            v((ROWS, MODEL), BF16),
            v((SMALL_AT, 8, 128), F32),
            v((64, WIDE), BF16),
            v((16, 128), BF16),
            v((BLOCKS, 8, 128), F32),
            dma((SMALL_AT,)), dma((BLOCKS,)),
            dma((4,)), dma((4,)),
            *[dma((PLANE,))] * 4,
            dma((CHIPS,)), dma((2 * SMALL_AT,)),
            dma((2 * SMALL_AT,)), dma((2 * SMALL_AT,)),
            v((16, 128), F32),
            *Reduce.scratch(CHUNKS),
            *HeadSum.scratch(),
            *HeadSum.scratch(),
        ],
        3,
    )


def format_kernel(all_ref, bc_ref, kv_ref):
    for c in range(2):
        for p in range(all_ref.shape[1]):
            for zh in range(2):
                rows = slice(p * 64, (p + 1) * 64)
                at, turned = (zh * 2 + c) * 128, (c * 2 + zh) * 128
                bc_ref[rows, at : at + 128] = all_ref[c, p, zh, 0, :, :128].astype(F32)
                kv_ref[rows, turned : turned + 128] = all_ref[c, p, zh, 0, :, 128:].astype(F32)


def format_replicated(gathered):
    step = 8
    steps = PLANE // step
    block = pl.BlockSpec((64 * step, 512), lambda i: (i, 0))
    return pl.pallas_call(
        format_kernel,
        name="format_replicated",
        out_shape=(jax.ShapeDtypeStruct((MODEL, 512), F32),) * 2,
        grid=(NZ * steps,),
        in_specs=[
            pl.BlockSpec(
                (2, step, 2, 1, 64, WIDE), lambda i: (0, i % steps, 0, i // steps, 0, 0)
            )
        ],
        out_specs=(block, block),
    )(gathered.reshape(2, PLANE, 2, NZ, 64, WIDE))


def on_device(
    tokens, segment_ids, cotangent, norm1_gain, x_weight, z_weight, bc_weight, dt_weight,
    x_conv, bc_conv, dt_bias, decay_rate, skip_gain, out_weight, query_weight, kv_weight,
    attn_weight, norm2_gain, gate_weight, up_weight, down_weight,
):
    zh, c = lax.axis_index("zh"), lax.axis_index("c")
    head_index = zh * 2 + c
    heads = decay_rate.shape[0]
    inner = x_weight.shape[1]
    positions = block_index() * ROWS + jnp.arange(ROWS)
    half_dim = HEAD_DIM // 2
    frequency = ROPE_BASE ** (-(jnp.arange(half_dim).astype(F32) * 2.0 / HEAD_DIM))
    angles = positions.astype(F32)[:, None] * frequency[None, :]
    cosine, sine = jnp.cos(angles), jnp.sin(angles)
    cosine = jnp.concatenate([cosine, cosine], 1)
    sine = jnp.concatenate([-sine, sine], 1)
    kv_at = c * (KVHEADS * HEAD_DIM) + zh * HEAD_DIM
    kv_columns = lax.dynamic_slice_in_dim(kv_weight, kv_at, HEAD_DIM, 1)
    bc_at = head_index * 128
    bc_columns = lax.dynamic_slice_in_dim(bc_weight, bc_at, 128, 1)
    dt_wide = jnp.pad(dt_weight, ((0, 0), (0, 128 - heads)))
    seg = segment_ids.astype(F32)
    seg_row = jnp.broadcast_to(jnp.tile(seg, 2), (8, 2 * ROWS))
    seg_column = jnp.broadcast_to(seg[:, None], (ROWS, 128))
    vectors = jnp.pad(jnp.stack([dt_bias, decay_rate]), ((0, 6), (0, 128 - heads)))
    skip = jnp.broadcast_to(jnp.repeat(skip_gain, SSM_DIM), (8, inner))
    gain_one = jnp.broadcast_to(norm1_gain, (8, MODEL))
    gain_two = jnp.broadcast_to(norm2_gain, (8, MODEL))

    normed_t, cot_t, queries, own_block, x_pre, bc_pre, dt_raw, z_val, edge = project(
        tokens, cotangent, gain_one, query_weight, kv_columns, x_weight, bc_weight, dt_wide,
        z_weight, cosine, sine, seg_column, seg_row,
    )
    (
        attended, lse, kv_all, edge_in, gated, core, x_act, bc_act, state_in, normed_near,
        cot_near, attended_low,
    ) = mixer_forward(
        queries, own_block, edge, x_pre, bc_pre, dt_raw, z_val, seg_column, seg_row, x_conv,
        bc_conv, vectors, skip, normed_t, cot_t,
    )
    (
        hidden_in, two_t, grad_gate, grad_up, hidden, ffn_part, grad_hidden_in, mix_t, gains_two,
        grad_gated, grad_attended,
    ) = feed_forward(
        gated, attended_low, tokens, cotangent, gain_two, out_weight, attn_weight, gate_weight,
        up_weight, down_weight,
    )
    bc_own = jnp.concatenate(
        [
            lax.dynamic_slice_in_dim(edge_in, inner + bc_at, 128, 1),
            lax.dynamic_slice_in_dim(bc_pre, bc_at, 128, 1),
        ]
    )
    (
        grad_query, misc, grad_z, grad_x_pre, grad_dt, grad_x_conv, grad_bc_conv, grad_vectors,
        ffn_w, mix_near,
    ) = mixer_backward(
        queries, grad_attended, attended, lse, seg_row, kv_all, grad_gated, z_val, core, x_act,
        bc_act, x_pre, bc_own, edge_in, dt_raw, state_in, seg_column, x_conv,
        lax.dynamic_slice_in_dim(bc_conv, bc_at, 128, 1), vectors, skip, grad_gate, grad_up,
        hidden, two_t, cot_t, cot_near, mix_t, cosine, sine,
    )
    quarter = MODEL // 4
    small = [
        jnp.zeros((quarter,), F32), grad_x_conv[:CONV], grad_bc_conv[:CONV],
        grad_vectors[0, :heads], grad_vectors[1, :heads], grad_vectors[2, :heads],
        lax.dynamic_slice_in_dim(gains_two[0], head_index * quarter, quarter),
    ]
    flat = jnp.concatenate([a.reshape(-1) for a in small])
    flat = jnp.pad(flat, (0, SMALL_AT * SMALL - flat.size)).reshape(SMALL_AT, 8, 128)
    mixer_w, gathered, small_sums, grad_normed, ffn_sum = finish(
        misc, grad_x_pre, grad_z, grad_query, grad_dt, gated, attended_low, normed_t, normed_near,
        mix_t, mix_near, ffn_part, tokens, flat, x_weight, z_weight, query_weight, dt_wide,
        bc_columns, kv_columns,
    )
    output = (hidden_in + ffn_sum.astype(F32)).astype(BF16)
    x = tokens.astype(F32)
    scale = lax.rsqrt(jnp.mean(x * x, 1, keepdims=True) + EPSILON)
    scaled, n = grad_normed.astype(F32) * norm1_gain, x * scale
    grad_tokens = grad_hidden_in + scale * (scaled - n * jnp.mean(n * scaled, 1, keepdims=True))
    bc_w, kv_w = format_replicated(gathered)
    total = small_sums.reshape(2, 2, SMALL_AT, 16, 128)[:, :, :, :8].astype(F32)
    total = total.transpose(1, 0, 2, 3, 4).reshape(4, SMALL_AT * SMALL)
    at = [WIDE, WIDE + inner, WIDE + 2 * inner, 2 * WIDE + 2 * inner, 3 * WIDE + 2 * inner]
    pieces, start = [], 0
    for a in small:
        pieces.append(total[:, start : start + a.size].reshape(4, *a.shape))
        start += a.size
    x_conv_sum = pieces[1].transpose(1, 0, 2).reshape(CONV, 4 * inner)
    bc_conv_sum = pieces[2].transpose(1, 0, 2).reshape(CONV, 512)
    bias_sum, rate_sum, skip_sum, gain_two_sum = (p.reshape(-1) for p in pieces[3:])
    gain_one_sum = pieces[0].reshape(-1)
    ff = gate_weight.shape[1]
    return (
        output,
        grad_tokens,
        gain_one_sum,
        mixer_w[:, at[0] : at[1]],
        mixer_w[:, at[1] : at[2]],
        bc_w,
        mixer_w[:, at[3] : at[3] + heads],
        x_conv_sum,
        bc_conv_sum,
        bias_sum,
        rate_sum,
        skip_sum,
        mixer_w[:, at[4] : at[4] + inner].T,
        mixer_w[:, at[2] : at[3]],
        kv_w,
        mixer_w[:, at[4] + inner :].T,
        gain_two_sum,
        ffn_w[:, :ff],
        ffn_w[:, ff : 2 * ff],
        ffn_w[:, 2 * ff :].T,
    )


def solution(mesh):
    split = Mesh(mesh.devices.reshape(NZ, NX, NY, 2, 2), (*SEQ, "zh", "c"))
    head = ("zh", "c")
    rows, columns, both, turned = P(SEQ, None), P(None, head), P(SEQ, head), P(head, SEQ)
    return jax.shard_map(
        on_device,
        mesh=split,
        in_specs=(
            rows, P(SEQ), rows, P(), columns, columns, P(), columns, columns, P(), P(head),
            P(head), P(head), P(head, None), columns, P(), P(head, None), P(), columns, columns,
            P(head, None),
        ),
        out_specs=(
            rows, rows, P(), both, both, P(), both, P(), P(), P(), P(), P(), turned, both, P(),
            turned, P(), both, both, turned,
        ),
        check_vma=False,
    )
```

```python
import functools

import jax
import jax.numpy as jnp
from jax import lax
from jax.experimental import pallas as pl
from jax.experimental.pallas import tpu as pltpu
from jax.sharding import Mesh
from jax.sharding import PartitionSpec as P

SSM_DIM = 64
STATE = 256
CONV = 4
KVHEADS = 2
HEAD_DIM = 128
NZ, NX, NY = 2, 4, 4
BLOCKS = NZ * NX * NY
CHIPS = 2 * BLOCKS
ROWS = 256
MODEL = 2048
SEQ = ("zl", "x", "y")
EPSILON = 1e-05
ROPE_BASE = 100000000000.0
HIGHEST = lax.Precision.HIGHEST
MESH = pl.DeviceIdType.MESH
BF16, F32 = jnp.bfloat16, jnp.float32
MASKED = -1e30
LOG2E = 1.4426950408889634
VMEM_LIMIT = 56 * 2**20


def block_index():
    return (lax.axis_index("zl") * NX + lax.axis_index("x")) * NY + lax.axis_index("y")


def block_at(s):
    return {"zl": s // (NX * NY), "x": (s // NY) % NX, "y": s % NY}


PLANE = NX * NY


def plane_shift(k):
    o = 1 + (k * 7) % (PLANE - 1)
    return o // NY, o % NY


def plane_peer(k, sign):
    dx, dy = plane_shift(k)
    x, y = lax.axis_index("x"), lax.axis_index("y")
    if sign < 0:
        dx, dy = NX - dx, NY - dy
    x, y = (x + dx) % NX, (y + dy) % NY
    return x * NY + y, {"x": x, "y": y}


def signal(sem, where):
    pl.semaphore_signal(sem, inc=1, device_id=where, device_id_type=MESH)


def remote(src, dst, send, recv, where):
    return pltpu.make_async_remote_copy(src, dst, send, recv, device_id=where, device_id_type=MESH)


def over(start, stop, body):
    def step(i, carry):
        body(i)
        return carry

    lax.fori_loop(start, stop, step, 0)


def dot(a, b, left=1, right=0):
    return lax.dot_general(
        a, b, (((left,), (right,)), ((), ())), preferred_element_type=F32
    )


def vmem(n):
    return [pl.BlockSpec(memory_space=pltpu.VMEM)] * n


def params(collective_id):
    return pltpu.CompilerParams(
        collective_id=collective_id, has_side_effects=True, vmem_limit_bytes=VMEM_LIMIT
    )


HEADS = 12
INNER = HEADS * SSM_DIM
GROUPS = INNER // 128
BC = 2 * STATE
SCAN_ROWS = INNER // BLOCKS
EDGE_WIDE = INNER + BC + 128
GRAD_EDGE = INNER + 128


def two_parts(v):
    high = v.astype(BF16)
    return high, (v - high.astype(F32)).astype(BF16)


def low_lanes(rows):
    return lax.broadcasted_iota(jnp.int32, (rows, 128), 1) < SSM_DIM


def widen(v, g):
    low = low_lanes(v.shape[0])
    return jnp.where(low, v[:, 2 * g : 2 * g + 1], v[:, 2 * g + 1 : 2 * g + 2])


def per_head(v, g):
    lane = lax.broadcasted_iota(jnp.int32, v.shape, 1)
    first = jnp.sum(jnp.where(lane < SSM_DIM, v, 0.0), 1, keepdims=True)
    second = jnp.sum(jnp.where(lane < SSM_DIM, 0.0, v), 1, keepdims=True)
    return jnp.where(lane == 2 * g, first, jnp.where(lane == 2 * g + 1, second, 0.0))


def triangle():
    row = lax.broadcasted_iota(jnp.int32, (ROWS, ROWS), 0)
    col = lax.broadcasted_iota(jnp.int32, (ROWS, ROWS), 1)
    return (col <= row).astype(F32).astype(BF16)


def running(v, lower, side):
    high, low = two_parts(v)
    middle, lowest = two_parts(v - high.astype(F32))
    return (
        dot(lower, high, side, 0) + dot(lower, middle, side, 0) + dot(lower, lowest, side, 0)
    )


def sigmoid(v):
    return 1.0 / (1.0 + jnp.exp(-v))


def softplus(v):
    return jnp.maximum(v, 0.0) + jnp.log(1.0 + jnp.exp(-jnp.abs(v)))


def lane_block(g):
    return pl.ds(pl.multiple_of(g * 128, 128), 128)


def decays(dt_ref, vec_ref, seg_ref, segx_ref, lower):
    pre = dt_ref[...] + vec_ref[0:1, :]
    step = softplus(pre)
    total = running(-step * vec_ref[1:2, :] * LOG2E, lower, 1)
    last = total[ROWS - 1 : ROWS, :]
    seg = seg_ref[...]
    seg_last, before = seg[ROWS - 1 : ROWS, :], segx_ref[7:8, :]
    carry = jnp.where(seg == seg_last, jnp.exp2(last - total), 0.0)
    entry = jnp.where(seg == before, jnp.exp2(total), 0.0)
    through = jnp.where(seg_last == before, jnp.exp2(last), 0.0)
    return pre, step, total, carry, entry, through


def conv_group(ext_ref, segx_ref, seg_ref, taps_ref, cols):
    total, inputs = None, []
    for k in range(CONV):
        same = segx_ref[pl.ds(5 + k, ROWS), :] == seg_ref[...]
        v = jnp.where(same, ext_ref[pl.ds(5 + k, ROWS), cols], 0.0)
        inputs.append(v)
        term = taps_ref[k : k + 1, cols] * v
        total = term if total is None else total + term
    return total, inputs


def scan_message(msg_ref, state_ref, through):
    high = through.astype(BF16)
    rest = through - high.astype(F32)
    middle = rest.astype(BF16)
    low = rest - middle.astype(F32)
    extra = jnp.concatenate([high.astype(F32), middle.astype(F32), low, jnp.zeros((5, 128), F32)], 0)
    extra = jnp.concatenate([extra, jnp.zeros((8, STATE - 128), F32)], 1)

    def fill(b):
        rows = state_ref[pl.ds(pl.multiple_of(b * SCAN_ROWS, 8), SCAN_ROWS), :]
        msg_ref[b] = jnp.concatenate([rows, extra], 0).astype(BF16)

    over(0, BLOCKS, fill)


class Scan:
    def __init__(self, reverse, me, msg, got, back, out, send, recv):
        self.reverse, self.me = reverse, me
        self.msg, self.got, self.back, self.out = msg, got, back, out
        self.send, self.recv = send, recv

    def there(self, o):
        d = (self.me + o) % BLOCKS
        return remote(
            self.msg.at[d], self.got.at[self.me], self.send.at[0, o], self.recv.at[0, o],
            block_at(d),
        )

    def arrived(self, phase, dst, o):
        s = (self.me + BLOCKS - o) % BLOCKS
        return remote(
            dst.at[s], dst.at[s], self.send.at[phase, o], self.recv.at[phase, o], block_at(s)
        )

    def start(self):
        over(1, BLOCKS, lambda o: self.there(o).start())
        self.got[self.me] = self.msg[self.me]

    def turn(self):
        me = self.me
        over(1, BLOCKS, lambda o: self.arrived(0, self.got, o).wait_recv())
        lane = lax.broadcasted_iota(jnp.int32, (SCAN_ROWS, 128), 1)
        row = lax.broadcasted_iota(jnp.int32, (SCAN_ROWS, 128), 0) + me * SCAN_ROWS
        at_head = (row >= lane * SSM_DIM) & (row < lane * SSM_DIM + SSM_DIM)

        def scan(i, state):
            k = BLOCKS - 1 - i if self.reverse else i
            message = self.got[k].astype(F32)
            self.back[k] = jnp.concatenate([state, jnp.zeros((8, STATE), F32)], 0).astype(BF16)

            @pl.when(k != me)
            def _():
                self.returned(k).start()

            factors = message[SCAN_ROWS : SCAN_ROWS + 1, :128]
            factors += message[SCAN_ROWS + 1 : SCAN_ROWS + 2, :128]
            factors += message[SCAN_ROWS + 2 : SCAN_ROWS + 3, :128]
            through = jnp.sum(jnp.where(at_head, factors, 0.0), 1, keepdims=True)
            return through * state + message[:SCAN_ROWS]

        lax.fori_loop(0, BLOCKS, scan, jnp.zeros((SCAN_ROWS, STATE), F32))
        self.out[me] = self.back[me]

    def returned(self, k):
        o = (k + BLOCKS - self.me) % BLOCKS
        return remote(
            self.back.at[k], self.out.at[self.me], self.send.at[1, o], self.recv.at[1, o],
            block_at(k),
        )

    def finish(self, state_ref):
        over(1, BLOCKS, lambda o: self.arrived(1, self.out, o).wait_recv())

        def fill(b):
            rows = self.out[b].astype(F32)
            state_ref[pl.ds(pl.multiple_of(b * SCAN_ROWS, 8), SCAN_ROWS), :] = rows[:SCAN_ROWS]

        over(0, BLOCKS, fill)

    def close(self):
        def sent(o):
            self.there(o).wait_send()
            self.returned((self.me + o) % BLOCKS).wait_send()

        over(1, BLOCKS, sent)


def key_segments(block):
    turned = jnp.transpose(block.astype(F32))
    return jnp.concatenate([turned[:, 0:1], turned[:, 1:2]], 0)


def causal_mask(s):
    row = lax.broadcasted_iota(jnp.int32, (ROWS, 2 * ROWS), 0)
    col = lax.broadcasted_iota(jnp.int32, (ROWS, 2 * ROWS), 1) % ROWS
    return jnp.where(row <= col, s, MASKED)


def mixing_bias(seg_ref, segrow_ref):
    row = lax.broadcasted_iota(jnp.int32, (ROWS, ROWS), 0)
    col = lax.broadcasted_iota(jnp.int32, (ROWS, ROWS), 1)
    same = segrow_ref[0:1, :ROWS] == seg_ref[:, 0:1]
    return jnp.where((col <= row) & same, 0.0, MASKED)


WIDE = 256
RELAY, MIDDLE, LAST = 2, 4, 6
AHEAD = 4
OWN = MODEL // NZ


class Reduce:
    def __init__(self, lefts, n, here, r_ref, rz, part, rel, gx, half, gy, out_ref, sems):
        self.lefts, self.n, self.here, self.throttled = lefts, n, here, here == n
        self.r, self.rz, self.part, self.rel = r_ref, rz, part, rel
        self.gx, self.half, self.gy, self.out = gx, half, gy, out_ref
        self.rz_sem, self.rel_sem, self.gx_sem, self.gy_sem = (
            (sems[2 * k], sems[2 * k + 1]) for k in range(4)
        )
        self.zl, self.x, self.y = (lax.axis_index(a) for a in SEQ)
        self.other = {"zl": 1 - self.zl}

    @staticmethod
    def scratch(n):
        v, dma = pltpu.VMEM, pltpu.SemaphoreType.DMA
        return [
            v((n, ROWS, WIDE), BF16),
            v((n, ROWS, WIDE), BF16),
            v((n, 4, 4, 64, WIDE), BF16),
            v((n, 2, 2, 64, WIDE), BF16),
            v((n, 2, 4, 64, WIDE), BF16),
            v((n, 4, 64, WIDE), BF16),
            v((n, 3, 64, WIDE), BF16),
            *[dma((n,))] * 8,
        ]

    def fill(self, arrays, c=0):
        for ref in arrays:
            for k in range(ref.shape[1] // WIDE):
                self.r[c] = ref[:, k * WIDE : (k + 1) * WIDE]
                c += 1

    def right(self, c):
        return remote(
            self.r.at[c], self.rz.at[c], self.rz_sem[0].at[c], self.rz_sem[1].at[c], self.other
        )

    def start(self):
        over(0, AHEAD, lambda c: self.right(c).start())

    def place(self, c, phase, o):
        along_x = c % 2 == phase
        x_to = jnp.where(along_x, (self.x + o) % NX, self.x)
        y_to = jnp.where(along_x, self.y, (self.y + o) % NY)
        return {"x": x_to, "y": y_to}, jnp.where(along_x, x_to, y_to)

    def send(self, src, dst, sem, c, where):
        return remote(src, dst, sem[0].at[c], sem[1].at[c], where)

    def send_second(self, c, o):
        where, d = self.place(c, 1, o)
        return self.send(self.half.at[c, d], self.gy.at[c, o - 1], self.gy_sem, c, where)

    def whole(self, got, sem, c):
        return self.send(got.at[c], got.at[c], sem, c, self.other)

    def product(self, c):
        @pl.when((c + AHEAD < self.here) & self.throttled)
        def _():
            self.right(c + AHEAD).start()

        @pl.when(c < self.here)
        def _():
            self.right(c).wait_recv()

        mine, theirs = self.r[c], self.rz[c]
        even = c % 2 == 0
        ends = [first for _, _, first in self.lefts[1:]] + [self.n]
        for (own, near, first), end in zip(self.lefts, ends):
            @pl.when((c >= first) & (c < end))
            def _():
                for i in range(NX):
                    a = own[pl.ds(pl.multiple_of(self.zl * OWN + i * 256, 256), 256), :]
                    b = near[pl.ds(i * 256, 256), :]
                    tile = (dot(a, mine) + dot(b, theirs)).astype(BF16)
                    for j in range(NY):
                        self.part[c, jnp.where(even, i, j), jnp.where(even, j, i)] = (
                            tile[j * 64 : (j + 1) * 64]
                        )
        _, d = self.place(c, 0, 2)
        for k, o in ((0, 1), (1, 3)):
            src = self.part.at[c, d, pl.ds(2 * k, 2)]
            self.send(src, self.rel.at[c, k], self.rel_sem, c, self.place(c, 0, o)[0]).start()

    def relay(self, c):
        self.whole(self.rel, self.rel_sem, c).wait_recv()
        for k, o in ((0, 1), (1, 3)):
            where, d = self.place(c, 0, o)
            for j in (2 * k, 2 * k + 1):
                total = self.part[c, d, j].astype(F32) + self.rel[c, k, j - 2 * k].astype(F32)
                self.part[c, d, j] = total.astype(BF16)
            self.send(self.part.at[c, d], self.gx.at[c, k], self.gx_sem, c, where).start()

    def middle(self, c):
        self.whole(self.gx, self.gx_sem, c).wait_recv()
        mine = jnp.where(c % 2 == 0, self.x, self.y)
        for j in range(4):
            total = self.part[c, mine, j].astype(F32)
            for k in range(2):
                total += self.gx[c, k, j].astype(F32)
            self.half[c, j] = total.astype(BF16)
        for o in range(1, 4):
            self.send_second(c, o).start()

    def last(self, c):
        self.whole(self.gy, self.gy_sem, c).wait_recv()
        mine = jnp.where(c % 2 == 0, self.y, self.x)
        total = self.half[c, mine].astype(F32)
        for o in range(3):
            total += self.gy[c, o].astype(F32)
        self.out[:, pl.ds(pl.multiple_of(c * WIDE, WIDE), WIDE)] = total

    @property
    def steps(self):
        return self.n + LAST

    def step(self, i):
        for late, do in ((0, self.product), (RELAY, self.relay), (MIDDLE, self.middle), (LAST, self.last)):
            @pl.when((i >= late) & (i < self.n + late))
            def _():
                do(i - late)

    def close(self):
        over(0, self.here, lambda c: self.right(c).wait_send())

        def sent(c):
            self.whole(self.rel, self.rel_sem, c).wait_send()
            self.whole(self.gx, self.gx_sem, c).wait_send()
            self.whole(self.gy, self.gy_sem, c).wait_send()

        over(0, self.n, sent)


class Left:
    def __init__(self, l_ref, lz, sems):
        zl, c = lax.axis_index("zl"), lax.axis_index("c")
        half = OWN // 2
        there = pl.ds(pl.multiple_of((1 - zl) * OWN + c * half, half), half)
        near, other = (pl.ds(pl.multiple_of(k * half, half), half) for k in (c, 1 - c))
        sem = [sems.at[k] for k in range(4)]
        self.out = remote(l_ref.at[there], lz.at[near], sem[0], sem[1], {"zl": 1 - zl})
        self.on = remote(lz.at[near], lz.at[near], sem[2], sem[3], {"c": 1 - c})
        self.back = remote(lz.at[other], lz.at[other], sem[2], sem[3], {"c": 1 - c})

    def start(self):
        self.out.start()

    def pass_on(self):
        self.out.wait_recv()
        self.on.start()

    def finish(self):
        self.back.wait_recv()

    def close(self):
        self.out.wait_send()
        self.on.wait_send()


HEAD_CHUNKS = 4


class HeadSum:
    def __init__(self, x, out, near, pair, far, sems):
        self.x, self.out, self.near, self.pair, self.far = x, out, near, pair, far
        self.near_send, self.near_recv, self.far_send, self.far_recv, self.end_send, self.end_recv = sems
        self.c, zh = lax.axis_index("c"), lax.axis_index("zh")
        self.sibling, self.opposite = {"c": 1 - self.c}, {"zh": 1 - zh}
        self.half = x.shape[0] // 2
        self.rows_each = self.half // HEAD_CHUNKS

    @staticmethod
    def scratch():
        v, dma = pltpu.VMEM, pltpu.SemaphoreType.DMA
        return [*[v((ROWS // 2, MODEL), BF16)] * 3, *[dma((HEAD_CHUNKS,))] * 6]

    def rows(self, core, k):
        return pl.ds(pl.multiple_of(core * self.half + k * self.rows_each, 16), self.rows_each)

    def local(self, k):
        return pl.ds(k * self.rows_each, self.rows_each)

    def first(self, k):
        return remote(
            self.x.at[self.rows(1 - self.c, k)], self.near.at[self.local(k)],
            self.near_send.at[k], self.near_recv.at[k], self.sibling,
        )

    def second(self, k):
        return remote(
            self.pair.at[self.local(k)], self.far.at[self.local(k)],
            self.far_send.at[k], self.far_recv.at[k], self.opposite,
        )

    def third(self, k, core):
        rows = self.rows(core, k)
        return remote(
            self.out.at[rows], self.out.at[rows], self.end_send.at[k], self.end_recv.at[k],
            self.sibling,
        )

    def start(self):
        for k in range(HEAD_CHUNKS):
            self.first(k).start()

    def across(self):
        for k in range(HEAD_CHUNKS):
            self.first(k).wait_recv()
            own = self.x[self.rows(self.c, k)].astype(F32)
            self.pair[self.local(k)] = (own + self.near[self.local(k)].astype(F32)).astype(BF16)
            self.second(k).start()

    def join(self):
        for k in range(HEAD_CHUNKS):
            self.second(k).wait_recv()
            total = self.pair[self.local(k)].astype(F32) + self.far[self.local(k)].astype(F32)
            self.out[self.rows(self.c, k)] = total.astype(BF16)
            self.third(k, self.c).start()

    def finish(self):
        for k in range(HEAD_CHUNKS):
            self.third(k, 1 - self.c).wait_recv()

    def close(self):
        for k in range(HEAD_CHUNKS):
            self.first(k).wait_send()
            self.second(k).wait_send()
            self.third(k, self.c).wait_send()


class Loads:
    def __init__(self, pairs, sems):
        self.copies = {
            id(there): pltpu.make_async_copy(here, there, sems.at[i])
            for i, (here, there) in enumerate(pairs)
        }

    def start(self):
        for copy in self.copies.values():
            copy.start()

    def need(self, *refs):
        for ref in refs:
            copy = self.copies.pop(id(ref), None)
            if copy is not None:
                copy.wait()


def fetching(kernel, n_in, late):
    def wrapped(*refs):
        count = len(late)
        ins, rest = list(refs[:n_in]), refs[n_in:]
        buffers, sems = rest[-1 - count : -1], rest[-1]
        pairs = []
        for buffer, i in zip(buffers, late):
            pairs.append((ins[i], buffer))
            ins[i] = buffer
        kernel(Loads(pairs, sems), *ins, *rest[: -1 - count])

    return wrapped


def call(kernel, name, args, late, outs, scratch, collective_id, left=()):
    spec = [
        pl.BlockSpec(memory_space=pl.ANY if i in (*late, *left) else pltpu.VMEM)
        for i in range(len(args))
    ]
    compiler = (
        pltpu.CompilerParams(vmem_limit_bytes=VMEM_LIMIT)
        if collective_id is None
        else params(collective_id)
    )
    return pl.pallas_call(
        fetching(kernel, len(args), late),
        name=name,
        out_shape=tuple(jax.ShapeDtypeStruct(*o) for o in outs),
        in_specs=spec,
        out_specs=tuple(vmem(len(outs))),
        scratch_shapes=[
            *scratch,
            *[pltpu.VMEM(args[i].shape, args[i].dtype) for i in late],
            pltpu.SemaphoreType.DMA((max(len(late), 1),)),
        ],
        compiler_params=compiler,
    )(*args)


def turn_pairs(v, cosine, sine, direction):
    return v * cosine + pltpu.roll(v, HEAD_DIM // 2, 1) * (sine * direction)


def transpose_to(out_ref, ref):
    for k in range(ref.shape[1] // 256):
        out_ref[k * 256 : (k + 1) * 256, :] = jnp.transpose(ref[:, k * 256 : (k + 1) * 256])


def feed_forward_kernel(
    loads, gated_ref, att_ref, tok_ref, cot_ref, gain_ref, out_w, attn_w, gate_w, up_w, down_w,
    hid_ref, ft_ref, dgate_ref, dup_ref, hidden_ref, ffn_ref, ghid_ref, mt_ref, gain_out,
    gg_ref, do_ref, ftz_ref, outz_ref,
    x_ref, sum_ref, normed, mix_ref, outs_ref, left_sem, outz_sem, *sums,
):
    loads.start()
    n_sum = len(HeadSum.scratch())
    first = HeadSum(x_ref, sum_ref, *sums[:3], sums[3:n_sum])
    second = HeadSum(x_ref, sum_ref, *sums[n_sum : n_sum + 3], sums[n_sum + 3 :])
    barrier = pltpu.get_barrier_semaphore()
    other_z = {"zl": 1 - lax.axis_index("zl")}
    signal(barrier, first.sibling)
    signal(barrier, first.opposite)
    signal(barrier, other_z)
    pl.semaphore_wait(barrier, 3)
    left = Left(ft_ref, ftz_ref, left_sem)
    outs = remote(outs_ref, outz_ref, outz_sem.at[0], outz_sem.at[1], other_z)
    loads.need(out_w, attn_w)

    def mixed(rows):
        x_ref[rows, :] = (
            dot(gated_ref[rows, :], out_w[...]) + dot(att_ref[rows, :], attn_w[...])
        ).astype(BF16)

    c = lax.axis_index("c")
    other = pl.ds(pl.multiple_of((1 - c) * (ROWS // 2), ROWS // 2), ROWS // 2)
    own = pl.ds(pl.multiple_of(c * (ROWS // 2), ROWS // 2), ROWS // 2)
    mixed(other)
    first.start()
    mixed(own)
    first.across()

    wide = 256
    loads.need(cot_ref, down_w)
    for k in range(0, hidden_ref.shape[1], wide):
        ghid_ref[:, k : k + wide] = dot(cot_ref[...], down_w[k : k + wide, :], 1, 1)
    first.join()
    loads.need(tok_ref)
    first.finish()
    for r in range(0, ROWS, 32):
        rows = slice(r, r + 32)
        x = tok_ref[rows, :].astype(F32) + sum_ref[rows, :].astype(F32)
        hid_ref[rows, :] = x
        scale = lax.rsqrt(jnp.mean(x * x, 1, keepdims=True) + EPSILON)
        normed[rows, :] = (x * scale * gain_ref[0:1, :]).astype(BF16)
    transpose_to(ft_ref, normed)
    left.start()
    loads.need(gate_w, up_w)
    for k in range(0, hidden_ref.shape[1], wide):
        cols = slice(k, k + wide)
        gate, up = dot(normed[...], gate_w[:, cols]), dot(normed[...], up_w[:, cols])
        grad = ghid_ref[:, cols]
        sig = sigmoid(gate)
        act = gate * sig
        hidden_ref[:, cols] = (act * up).astype(BF16)
        dgate_ref[:, cols] = (grad * up * sig * (1.0 + gate * (1.0 - sig))).astype(BF16)
        dup_ref[:, cols] = (grad * act).astype(BF16)
    first.close()

    def back(rows):
        x_ref[rows, :] = (
            dot(dgate_ref[rows, :], gate_w[...], 1, 1) + dot(dup_ref[rows, :], up_w[...], 1, 1)
        ).astype(BF16)

    back(other)
    second.start()
    back(own)
    second.across()
    for k in range(3):
        outs_ref[k] = gated_ref[:, k * WIDE : (k + 1) * WIDE]
    outs_ref[3] = att_ref[...]
    outs.start()
    left.pass_on()
    ffn_ref[...] = dot(hidden_ref[...], down_w[...]).astype(BF16)
    second.join()
    second.finish()
    for r in range(0, ROWS, 32):
        rows = slice(r, r + 32)
        x = hid_ref[rows, :]
        scale = lax.rsqrt(jnp.mean(x * x, 1, keepdims=True) + EPSILON)
        n = x * scale
        grad = sum_ref[rows, :].astype(F32)
        scaled = grad * gain_ref[0:1, :]
        along = jnp.mean(n * scaled, 1, keepdims=True)
        total = cot_ref[rows, :].astype(F32) + scale * (scaled - n * along)
        ghid_ref[rows, :] = total
        mix_ref[rows, :] = total.astype(BF16)
        gains = jnp.sum(grad * n, 0, keepdims=True)
        gain_out[0:1, :] = gains if r == 0 else gain_out[0:1, :] + gains
    grad_att = dot(mix_ref[...], attn_w[...], 1, 1).astype(BF16)
    for h in range(2):
        do_ref[h * ROWS : (h + 1) * ROWS, :] = grad_att[:, h * HEAD_DIM : (h + 1) * HEAD_DIM]
    gg_ref[...] = dot(mix_ref[...], out_w[...], 1, 1)
    transpose_to(mt_ref, mix_ref)
    second.close()
    left.finish()
    left.close()
    outs.wait()


def feed_forward(*args):
    v = pltpu.VMEM
    ff = args[7].shape[1]
    return call(
        feed_forward_kernel, "feed_forward", args, (2, 3, 5, 6, 7, 8, 9),
        [
            ((ROWS, MODEL), F32),
            ((MODEL, ROWS), BF16),
            ((ROWS, ff), BF16),
            ((ROWS, ff), BF16),
            ((ROWS, ff), BF16),
            ((ROWS, MODEL), BF16),
            ((ROWS, MODEL), F32),
            ((MODEL, ROWS), BF16),
            ((8, MODEL), F32),
            ((ROWS, INNER), F32),
            ((2 * ROWS, HEAD_DIM), BF16),
            ((OWN, ROWS), BF16),
            ((4, ROWS, WIDE), BF16),
        ],
        [
            v((ROWS, MODEL), BF16),
            v((ROWS, MODEL), BF16),
            v((ROWS, MODEL), BF16),
            v((ROWS, MODEL), BF16),
            v((4, ROWS, WIDE), BF16),
            pltpu.SemaphoreType.DMA((4,)),
            pltpu.SemaphoreType.DMA((2,)),
            *HeadSum.scratch(),
            *HeadSum.scratch(),
        ],
        4,
    )


EARLY = 6


def mixer_forward_kernel(
    loads, tok_ref, cot_ref, gain_ref, q_w, kv_w, x_w, bc_w, dt_w, z_w, cos_ref, sin_ref, seg_ref,
    segrow_ref, xtaps_ref, bctaps_ref, vec_ref, skip_ref,
    nt_ref, ct_ref, q_ref, x_ref, bc_ref, dt_ref, z_ref,
    att_ref, lse_ref, kv_ref, edge_out, gated_ref, core_ref, xact_ref, bcact_ref, state_ref,
    ntz_ref, ctz_ref, attlow_ref,
    m_ref, l_ref, acc_ref, xext, bcext, segx, local, msg, got, back, result, bias_ref, cb_ref,
    cumt_ref, normed, own_ref, edge_ref, kv_cols,
    send_sem, recv_sem, sib_send, sib_recv, edge_sem, scan_send, scan_recv, left_sem, kv_sem,
):
    me, c, zl = block_index(), lax.axis_index("c"), lax.axis_index("zl")
    at = me % PLANE
    sibling = {"c": 1 - c}
    kv_at = (c * KVHEADS + lax.axis_index("zh")) * HEAD_DIM
    kv_copy = pltpu.make_async_copy(
        kv_w.at[:, pl.ds(pl.multiple_of(kv_at, HEAD_DIM), HEAD_DIM)], kv_cols, kv_sem
    )
    loads.start()
    kv_copy.start()
    barrier = pltpu.get_barrier_semaphore()
    over(1, BLOCKS, lambda o: signal(barrier, block_at((me + o) % BLOCKS)))
    signal(barrier, sibling)

    loads.need(tok_ref)
    for r in range(0, ROWS, 32):
        rows = slice(r, r + 32)
        v = tok_ref[rows, :].astype(F32)
        scale = lax.rsqrt(jnp.mean(v * v, 1, keepdims=True) + EPSILON)
        normed[rows, :] = (v * scale * gain_ref[0:1, :]).astype(BF16)
    n = normed[...]
    loads.need(x_w, bc_w)
    x_ref[...] = dot(n, x_w[...]).astype(BF16)
    bc_ref[...] = dot(n, bc_w[...]).astype(BF16)
    edge_ref[:, :INNER] = x_ref[ROWS - 16 :, :]
    edge_ref[:, INNER : INNER + BC] = bc_ref[ROWS - 16 :, :]
    edge_ref[:, INNER + BC :] = seg_ref[ROWS - 16 :, :].astype(BF16)
    pl.semaphore_wait(barrier, BLOCKS)

    def block_copy(src, j, send, where):
        return remote(src, kv_ref.at[c, j], send_sem.at[send], recv_sem.at[j], where)

    def arrival(j):
        return block_copy(own_ref, j, 0, sibling)

    to_sibling = lambda j, src: remote(
        src, kv_ref.at[c, j], sib_send.at[j], sib_recv.at[j], sibling
    )
    from_sibling = lambda j: remote(
        kv_ref.at[1 - c, j], kv_ref.at[1 - c, j], sib_send.at[j], sib_recv.at[j], sibling
    )
    across = block_copy(own_ref, me, PLANE - 1, {"zl": 1 - zl})

    def own_copy(k, wait):
        d, where = plane_peer(k, 1)

        @pl.when(d > at)
        def _():
            copy = block_copy(own_ref, me, k, where)
            copy.wait_send() if wait else copy.start()

    def relay_copy(k, wait):
        copy = block_copy(kv_ref.at[c, at], at, PLANE + k, plane_peer(k, 1)[1])
        copy.wait_send() if wait else copy.start()

    edge_copy = remote(
        edge_ref, edge_out, edge_sem.at[0], edge_sem.at[1], block_at((me + 1) % BLOCKS)
    )
    states = Scan(False, me, msg, got, back, result, scan_send, scan_recv)

    @pl.when(me < BLOCKS - 1)
    def _():
        edge_copy.start()

    cosine, sine = cos_ref[...], sin_ref[...]
    kv_copy.wait()
    raw = dot(n, kv_cols[...])
    turned = turn_pairs(raw, cosine, sine, 1.0)
    own_ref[:ROWS, :] = jnp.where(c == 0, turned, raw).astype(BF16)
    rows = [segrow_ref[0:1, :HEAD_DIM], segrow_ref[0:1, HEAD_DIM : 2 * HEAD_DIM]]
    own_ref[ROWS:, :] = jnp.concatenate([*rows, jnp.zeros((14, HEAD_DIM), F32)], 0).astype(BF16)

    @pl.when(zl == 0)
    def _():
        across.start()

    to_sibling(me, own_ref).start()
    over(0, EARLY, lambda k: own_copy(k, False))
    lefts = [Left(ct_ref, ctz_ref, left_sem.at[0]), Left(nt_ref, ntz_ref, left_sem.at[1])]

    kv_ref[c, me] = own_ref[...]
    loads.need(dt_w)
    dt_ref[...] = dot(n, dt_w[...])
    xext[8:, :] = x_ref[...].astype(F32)
    bcext[8:, :] = bc_ref[...].astype(F32)
    segx[8:, :] = seg_ref[...]
    lower = triangle()
    bias_ref[...] = mixing_bias(seg_ref, segrow_ref)

    @pl.when(me > 0)
    def _():
        edge_copy.wait_recv()

    @pl.when(me == 0)
    def _():
        edge_out[...] = jnp.zeros_like(edge_out)

    edge = edge_out[...].astype(F32)[8:]
    xext[:8, :] = edge[:, :INNER]
    bcext[:8, :] = edge[:, INNER : INNER + BC]
    segx[:8, :] = edge[:, INNER + BC :]

    def activate(ext, taps, out):
        def group(g):
            pre, _ = conv_group(ext, segx, seg_ref, taps, lane_block(g))
            out[:, lane_block(g)] = (pre * sigmoid(pre)).astype(BF16)

        over(0, out.shape[1] // 128, group)

    activate(bcext, bctaps_ref, bcact_ref)
    activate(xext, xtaps_ref, xact_ref)

    _, step, total, carry, entry, through = decays(dt_ref, vec_ref, seg_ref, segx, lower)
    cumt_ref[...] = jnp.transpose(total)
    weight = step * carry
    b_low, c_low = bcact_ref[:, :STATE], bcact_ref[:, STATE:]
    for g in range(GROUPS):
        moved = xact_ref[:, g * 128 : (g + 1) * 128].astype(F32) * widen(weight, g)
        local[g * 128 : (g + 1) * 128, :] = dot(moved.astype(BF16), b_low, 0, 0)
    scan_message(msg, local, through)
    states.start()
    over(EARLY, PLANE - 1, lambda k: own_copy(k, False))

    @pl.when(zl == 1)
    def _():
        arrival(at).wait_recv()
        to_sibling(at, kv_ref.at[c, at]).start()
        over(0, PLANE - 1, lambda k: relay_copy(k, False))

    cb_ref[...] = dot(c_low, b_low, 1, 1)
    low_lane = lax.broadcasted_iota(jnp.int32, (ROWS, 128), 1) < SSM_DIM
    for g in range(GROUPS):
        cols = slice(g * 128, (g + 1) * 128)
        u = (xact_ref[:, cols].astype(F32) * widen(step, g)).astype(BF16)
        made = []
        for h in (2 * g, 2 * g + 1):
            gap = total[:, h : h + 1] - cumt_ref[h : h + 1, :] + bias_ref[...]
            made.append(dot((jnp.exp2(gap) * cb_ref[...]).astype(BF16), u))
        core_ref[:, cols] = jnp.where(low_lane, made[0], made[1])

    loads.need(q_w)
    for h in range(2):
        raw = dot(n, q_w[:, h * HEAD_DIM : (h + 1) * HEAD_DIM])
        q_ref[h * ROWS : (h + 1) * ROWS, :] = turn_pairs(raw, cosine, sine, 1.0).astype(BF16)
    scale = LOG2E * HEAD_DIM**-0.5
    queries = q_ref[...]
    qseg = segrow_ref[0:1, :]

    def scores_of(j):
        s = dot(kv_ref[0, j, :ROWS], queries, 1, 1) * scale
        return jnp.where(key_segments(kv_ref[0, j, ROWS:]) == qseg, s, MASKED)

    from_sibling(me).wait_recv()
    s = causal_mask(scores_of(me))
    m = jnp.max(s, 0, keepdims=True)
    p = jnp.exp2(s - m)
    m_ref[...] = m
    l_ref[...] = jnp.sum(p, 0, keepdims=True)
    acc_ref[...] = dot(kv_ref[1, me, :ROWS], p.astype(BF16), 0, 0)

    transpose_to(nt_ref, normed)
    loads.need(cot_ref)
    transpose_to(ct_ref, cot_ref)
    states.turn()
    for left in lefts:
        left.start()
    loads.need(z_w)
    z_ref[...] = dot(n, z_w[...])

    def forward(k):
        q, _ = plane_peer(k, -1)

        def one(j):
            arrival(j).wait_recv()
            to_sibling(j, kv_ref.at[c, j]).start()

        pl.when(q < at)(lambda: one(zl * PLANE + q))
        pl.when(zl == 1)(lambda: one(q))

    def attend(j):
        from_sibling(j).wait_recv()
        s = scores_of(j)
        m_old = m_ref[...]
        m = jnp.maximum(m_old, jnp.max(s, 0, keepdims=True))
        p = jnp.exp2(s - m)
        alpha = jnp.exp2(m_old - m)
        m_ref[...] = m
        l_ref[...] = l_ref[...] * alpha + jnp.sum(p, 0, keepdims=True)
        acc_ref[...] = acc_ref[...] * alpha + dot(kv_ref[1, j, :ROWS], p.astype(BF16), 0, 0)

    forward(0)

    @pl.when(zl == 1)
    def _():
        attend(at)

    def step_over(k):
        @pl.when(k + 1 < PLANE - 1)
        def _():
            forward(k + 1)

        q, _ = plane_peer(k, -1)
        pl.when(q < at)(lambda: attend(zl * PLANE + q))
        pl.when(zl == 1)(lambda: attend(q))

    over(0, PLANE - 1, step_over)
    for left in lefts:
        left.pass_on()
    attended = jnp.transpose(acc_ref[...] / l_ref[...])
    att_ref[...] = attended
    for h in range(2):
        attlow_ref[:, h * HEAD_DIM : (h + 1) * HEAD_DIM] = (
            attended[h * ROWS : (h + 1) * ROWS].astype(BF16)
        )
    lse_ref[...] = jnp.broadcast_to(m_ref[...] + jnp.log2(l_ref[...]), lse_ref.shape)

    states.finish(state_ref)
    for g in range(GROUPS):
        cols = slice(g * 128, (g + 1) * 128)
        outer = dot(c_low, state_ref[cols, :].astype(BF16), 1, 1) * widen(entry, g)
        core = core_ref[:, cols] + outer
        core_ref[:, cols] = core
        out = core + skip_ref[0:1, cols] * xact_ref[:, cols].astype(F32)
        z = z_ref[:, cols]
        gated_ref[:, cols] = (out * z * sigmoid(z)).astype(BF16)

    states.close()
    for left in lefts:
        left.finish()
        left.close()
    to_sibling(me, own_ref).wait_send()
    over(0, PLANE - 1, lambda k: own_copy(k, True))

    @pl.when(zl == 0)
    def _():
        across.wait_send()

    @pl.when(zl == 1)
    def _():
        over(0, PLANE - 1, lambda k: relay_copy(k, True))
        over(0, PLANE, lambda j: to_sibling(j, own_ref).wait_send())

    over(0, at, lambda q: to_sibling(zl * PLANE + q, own_ref).wait_send())

    @pl.when(me < BLOCKS - 1)
    def _():
        edge_copy.wait_send()


def mixer_forward(*args):
    wide = 2 * ROWS
    dma = pltpu.SemaphoreType.DMA
    return call(
        mixer_forward_kernel, "mixer_forward", args, (0, 5, 6, 7, 3, 8, 1),
        [
            ((MODEL, ROWS), BF16),
            ((MODEL, ROWS), BF16),
            ((wide, HEAD_DIM), BF16),
            ((ROWS, INNER), BF16),
            ((ROWS, BC), BF16),
            ((ROWS, 128), F32),
            ((ROWS, INNER), F32),
            ((wide, HEAD_DIM), F32),
            ((8, wide), F32),
            ((2, BLOCKS, ROWS + 16, HEAD_DIM), BF16),
            ((16, EDGE_WIDE), BF16),
            ((ROWS, INNER), BF16),
            ((ROWS, INNER), F32),
            ((ROWS, INNER), BF16),
            ((ROWS, BC), BF16),
            ((INNER, STATE), F32),
            ((OWN, ROWS), BF16),
            ((OWN, ROWS), BF16),
            ((ROWS, 2 * HEAD_DIM), BF16),
        ],
        [
            pltpu.VMEM((1, wide), F32),
            pltpu.VMEM((1, wide), F32),
            pltpu.VMEM((HEAD_DIM, wide), F32),
            pltpu.VMEM((ROWS + 8, INNER), F32),
            pltpu.VMEM((ROWS + 8, BC), F32),
            pltpu.VMEM((ROWS + 8, 128), F32),
            pltpu.VMEM((INNER, STATE), F32),
            *[pltpu.VMEM((BLOCKS, SCAN_ROWS + 8, STATE), BF16)] * 4,
            pltpu.VMEM((ROWS, ROWS), F32),
            pltpu.VMEM((ROWS, ROWS), F32),
            pltpu.VMEM((128, ROWS), F32),
            pltpu.VMEM((ROWS, MODEL), BF16),
            pltpu.VMEM((ROWS + 16, HEAD_DIM), BF16),
            pltpu.VMEM((16, EDGE_WIDE), BF16),
            pltpu.VMEM((MODEL, HEAD_DIM), BF16),
            *[dma((BLOCKS,))] * 4,
            dma((2,)),
            dma((2, BLOCKS)),
            dma((2, BLOCKS)),
            dma((2, 4)),
            dma,
        ],
        1,
        (4,),
    )


def mixer_backward_kernel(
    loads, q_ref, do_ref, att_ref, lse_ref, segrow_ref, kv_ref, gg_ref, z_ref, core_ref, xact_ref,
    bcact_ref, x_ref, bcown_ref, edge_in, dt_ref, state_ref, seg_ref, xtaps_ref, bctaps_ref,
    vec_ref, skip_ref, dgate_ref, dup_ref, hidden_ref, ft_ref, ct_ref, ctz_ref, mt_ref, cos_ref,
    sin_ref, ftz_ref,
    dqraw_ref, misc_ref, dz_ref, dx_ref, ddt_ref, dxtaps_ref, dbctaps_ref, dvec_ref,
    w_ref, mtz_ref,
    dkv_ref, dqt_ref, mine, theirs, sib, kvgot, relay_ref, total_ref, xext, bcext, segx, local, msg, got, back, result,
    bias_ref, cb_ref, cumt_ref, g_ref, du_ref, dbc_all, shares, share_got, edge_ref,
    edge_out, enter_ref, gext, dcum_ref, ddtx_ref,
    send_sem, recv_sem, sib_send, sib_recv, edge_sem, scan_send, scan_recv, share_send, share_recv,
    left_sem, owntaps_ref, *reduce,
):
    me, c, zh, zl = block_index(), *(lax.axis_index(a) for a in ("c", "zh", "zl"))
    head_at = zh * 2 + c
    sibling = {"c": 1 - c}
    at_head = lambda d: {"zh": d // 2, "c": d % 2}
    loads.start()
    barrier = pltpu.get_barrier_semaphore()
    over(1, BLOCKS, lambda o: signal(barrier, block_at((me + o) % BLOCKS)))
    for o in range(1, 4):
        signal(barrier, at_head((head_at + o) % 4))
    pl.semaphore_wait(barrier, BLOCKS + 2)

    at = me % PLANE
    to_sibling = lambda j: remote(
        theirs.at[j], sib.at[j], sib_send.at[j], sib_recv.at[j], sibling
    )

    def to_owner(k, kind):
        q, where = plane_peer(k, -1)
        j = q if kind else zl * PLANE + q
        return remote(
            mine.at[j], kvgot.at[kind, at], send_sem.at[kind, k], recv_sem.at[kind, at], where
        )

    def from_plane(kind, q):
        return remote(
            kvgot.at[kind, q], kvgot.at[kind, q], send_sem.at[kind, 0], recv_sem.at[kind, q],
            sibling,
        )

    across = remote(
        relay_ref, kvgot.at[1, 0], send_sem.at[0, PLANE - 1], recv_sem.at[1, 0], {"zl": 1 - zl}
    )
    states = Scan(True, me, msg, got, back, result, scan_send, scan_recv)
    rs = Reduce(
        [(ct_ref, ctz_ref, 0), (ft_ref, ftz_ref, 4)], 12, 12, *reduce[:7], w_ref, reduce[7:]
    )
    left = Left(mt_ref, mtz_ref, left_sem)
    loads.need(hidden_ref)
    rs.fill([hidden_ref])
    rs.start()
    loads.need(dgate_ref, dup_ref)
    rs.fill([dgate_ref, dup_ref], 4)
    done = 0

    def reduce_some(n):
        nonlocal done
        over(done, done + n, rs.step)
        done += n


    lower = triangle()
    edge = edge_in[...].astype(F32)[8:]
    xext[:8, :] = edge[:, :INNER]
    segx[:8, :] = edge[:, INNER + BC :]
    xext[8:, :] = x_ref[...].astype(F32)
    segx[8:, :] = seg_ref[...]
    bc_cols = lane_block(head_at)
    edge_cols = lane_block(head_at + INNER // 128)
    bcext[:8, :] = edge_in[:, edge_cols].astype(F32)[8:]
    bcext[8:, :] = bcown_ref[:, bc_cols].astype(F32)
    owntaps_ref[...] = bctaps_ref[:, bc_cols]
    bias_ref[...] = mixing_bias(seg_ref, segrow_ref)
    pre_dt, step, total, carry, entry, through = decays(dt_ref, vec_ref, seg_ref, segx, lower)
    cumt_ref[...] = jnp.transpose(total)
    b_low, c_low = bcact_ref[:, :STATE], bcact_ref[:, STATE:]
    for g in range(GROUPS):
        cols = slice(g * 128, (g + 1) * 128)
        z = z_ref[:, cols]
        grad = gg_ref[:, cols] * z * sigmoid(z)
        g_ref[:, cols] = grad
        entered = (grad * widen(entry, g)).astype(BF16)
        du_ref[:, cols] = entered.astype(F32)
        local[cols, :] = dot(entered, c_low, 0, 0)
    scan_message(msg, local, through)
    states.start()
    loads.need(ct_ref, ctz_ref, ft_ref, ftz_ref)
    reduce_some(1)

    dcum = jnp.zeros((ROWS, 128), F32)
    dskip = jnp.zeros((8, 128), F32)
    dc = jnp.zeros((ROWS, STATE), F32)
    for g in range(GROUPS):
        cols = slice(g * 128, (g + 1) * 128)
        z, core, x = z_ref[:, cols], core_ref[:, cols], xact_ref[:, cols].astype(F32)
        sig = sigmoid(z)
        out = core + skip_ref[0:1, cols] * x
        dz_ref[:, cols] = (gg_ref[:, cols] * out * sig * (1.0 + z * (1.0 - sig))).astype(BF16)
        grad = g_ref[:, cols]
        dcum += per_head(grad * core, g)
        dskip += per_head(jnp.broadcast_to(jnp.sum(grad * x, 0, keepdims=True), (8, 128)), g)
        dc += dot(du_ref[:, cols].astype(BF16), state_ref[cols, :].astype(BF16))
    dbc_all[:, STATE:] = dc
    reduce_some(1)

    cb_ref[...] = dot(c_low, b_low, 1, 1)
    low_lane = lax.broadcasted_iota(jnp.int32, (ROWS, 128), 1) < SSM_DIM
    dcb = jnp.zeros((ROWS, ROWS), F32)
    for g in range(GROUPS):
        cols = slice(g * 128, (g + 1) * 128)
        u = xact_ref[:, cols].astype(F32) * widen(step, g)
        u_low, grad = u.astype(BF16), g_ref[:, cols]
        grad_low = grad.astype(BF16)
        made = []
        for i in range(2):
            h = 2 * g + i
            decay = jnp.exp2(total[:, h : h + 1] - cumt_ref[h : h + 1, :] + bias_ref[...])
            mixing = (decay * cb_ref[...]).astype(BF16)
            made.append(dot(mixing, grad_low, 0, 0))
            half = jnp.where(low_lane if i == 0 else ~low_lane, grad, 0.0).astype(BF16)
            dcb += decay * dot(half, u_low, 1, 1)
        du = jnp.where(low_lane, made[0], made[1])
        du_ref[:, cols] = du
        dcum -= per_head(u * du, g)
    dcum_ref[...] = dcum
    reduce_some(1)
    dcb_low = dcb.astype(BF16)
    dbc_all[:, :STATE] = dot(dcb_low, c_low, 0, 0)
    dbc_all[:, STATE:] += dot(dcb_low, b_low)

    loads.need(q_ref, do_ref, att_ref, kv_ref)
    scale = LOG2E * HEAD_DIM**-0.5
    queries, grads = q_ref[...], do_ref[...]
    lse, qseg = lse_ref[0:1, :], segrow_ref[0:1, :]
    high, low = two_parts(grads.astype(F32) * att_ref[...])
    ones = jnp.ones((8, HEAD_DIM), BF16)
    delta = (dot(ones, high, 1, 1) + dot(ones, low, 1, 1))[0:1, :]

    def block(t, own):
        keys = kv_ref[0, t, :ROWS]
        s = dot(keys, queries, 1, 1) * scale
        s = jnp.where(key_segments(kv_ref[0, t, ROWS:]) == qseg, s, MASKED)
        if own:
            s = causal_mask(s)
        p = jnp.exp2(s - lse)
        ds = (p * (dot(kv_ref[1, t, :ROWS], grads, 1, 1) - delta)).astype(BF16)
        dk = dot(ds, queries)
        dv = dot(p.astype(BF16), grads)
        change = dot(keys, ds, 0, 0)
        dqt_ref[...] = change if own else dqt_ref[...] + change
        mine[t] = jnp.where(c == 0, dk, dv).astype(BF16)
        theirs[t] = jnp.where(c == 0, dv, dk).astype(BF16)
        to_sibling(t).start()

    def pair(t):
        to_sibling(t).wait_recv()
        return mine[t].astype(F32) + sib[t].astype(F32)

    block(me, True)
    reduce_some(1)
    states.turn()
    loads.need(mt_ref)
    left.start()
    before = done

    @pl.when(zl == 1)
    def _():
        block(at, False)

    def give(k):
        q, _ = plane_peer(k, -1)

        @pl.when(q < at)
        def _():
            j = zl * PLANE + q
            mine[j] = pair(j).astype(BF16)
            to_owner(k, 0).start()

        @pl.when(zl == 1)
        def _():
            mine[q] = pair(q).astype(BF16)
            to_owner(k, 1).start()

    def step_over(k):
        q, _ = plane_peer(k, -1)
        pl.when(q < at)(lambda: block(zl * PLANE + q, False))
        pl.when(zl == 1)(lambda: block(q, False))

        @pl.when(k >= 1)
        def _():
            give(k - 1)

        @pl.when(k % 2 == 1)
        def _():
            rs.step(before + k // 2)

    over(0, PLANE - 1, step_over)
    give(PLANE - 2)
    done += (PLANE - 1) // 2
    reduce_some(1)
    left.pass_on()
    dkv_ref[...] = pair(me)

    @pl.when(zl == 1)
    def _():
        total_ref[...] = pair(at)

    score_scale = HEAD_DIM**-0.5
    dq = jnp.transpose(dqt_ref[...]) * score_scale
    cosine, sine = cos_ref[...], sin_ref[...]
    for h in range(2):
        raw = turn_pairs(dq[h * ROWS : (h + 1) * ROWS], cosine, sine, -1.0)
        dqraw_ref[:, h * HEAD_DIM : (h + 1) * HEAD_DIM] = raw.astype(BF16)

    states.finish(enter_ref)
    dcum = dcum_ref[...]
    dstep = jnp.zeros((ROWS, 128), F32)
    dlast = jnp.zeros((8, 128), F32)
    db = jnp.zeros((ROWS, STATE), F32)
    for g in range(GROUPS):
        cols = slice(g * 128, (g + 1) * 128)
        entering = enter_ref[cols, :]
        entering_low = entering.astype(BF16)
        x = xact_ref[:, cols].astype(F32)
        steps, carries = widen(step, g), widen(carry, g)
        v = x * steps * carries
        dv = dot(b_low, entering_low, 1, 1)
        db += dot(v.astype(BF16), entering_low)
        dcarry = per_head(v * dv, g)
        dcum -= dcarry
        dlast += jnp.broadcast_to(jnp.sum(dcarry, 0, keepdims=True), (8, 128))
        du = du_ref[:, cols] + carries * dv
        dstep += per_head(x * du, g)
        pieces = jnp.sum(entering * state_ref[cols, :], 1, keepdims=True)
        both = jnp.sum(jnp.broadcast_to(pieces, (128, 128)) * head_of_lane_f32(g), 0, keepdims=True)
        dlast += through * both
        g_ref[:, cols] = steps * du + skip_ref[0:1, cols] * g_ref[:, cols]
    dbc_all[:, :STATE] += db
    last_row = lax.broadcasted_iota(jnp.int32, (ROWS, 128), 0) == ROWS - 1
    dcum += jnp.where(last_row, dlast[0:1, :], 0.0)
    da = running(dcum, lower, 0)
    rate = vec_ref[1:2, :]
    drate = -jnp.sum(step * da, 0, keepdims=True)
    ddt = (dstep - rate * da) * sigmoid(pre_dt)
    ddt_ref[...] = ddt.astype(BF16)
    dbias = jnp.sum(ddt, 0, keepdims=True)
    dvec_ref[...] = jnp.concatenate([dbias, drate, dskip[0:1, :], jnp.zeros((5, 128), F32)], 0)

    reduce_some(1)

    for d in range(4):
        shares[d] = dbc_all[:, d * 128 : (d + 1) * 128].astype(BF16)
    share = lambda o: remote(
        shares.at[(head_at + o) % 4], share_got.at[o], share_send.at[o], share_recv.at[o],
        at_head((head_at + o) % 4),
    )
    for o in range(1, 4):
        share(o).start()

    def conv_back(ext, taps, grad, cols, out_taps, out_grad):
        pre, inputs = conv_group(ext, segx, seg_ref, taps, cols)
        sig = sigmoid(pre)
        dpre = grad * sig * (1.0 + pre * (1.0 - sig))
        gext[...] = jnp.zeros_like(gext)
        rows = []
        for k in range(CONV):
            rows.append(jnp.sum(dpre * inputs[k], 0, keepdims=True))
            same = segx[pl.ds(5 + k, ROWS), :] == seg_ref[...]
            gext[pl.ds(5 + k, ROWS), :] += jnp.where(same, taps[k : k + 1, cols] * dpre, 0.0)
        out_taps[:, cols] = jnp.concatenate([*rows, jnp.zeros((4, 128), F32)], 0)
        out_grad[...] = gext[...]

    def x_group(g):
        cols = lane_block(g)
        conv_back(xext, xtaps_ref, g_ref[:, cols], cols, dxtaps_ref, ddtx_ref)
        edge_ref[:, cols] = ddtx_ref[:8, :]
        g_ref[:, cols] = ddtx_ref[8:, :]

    over(0, GROUPS, x_group)
    reduce_some(1)
    grad_bc = shares[head_at].astype(F32)
    for o in range(1, 4):
        share(o).wait_recv()
        grad_bc += share_got[o].astype(F32)
    conv_back(bcext, owntaps_ref, grad_bc, slice(0, 128), dbctaps_ref, ddtx_ref)
    edge_ref[:, INNER:] = ddtx_ref[:8, :]
    edge_copy = remote(
        edge_ref, edge_out, edge_sem.at[0], edge_sem.at[1], block_at((me + BLOCKS - 1) % BLOCKS)
    )

    @pl.when(me > 0)
    def _():
        edge_copy.start()

    reduce_some(1)

    def collect(q):
        @pl.when((zl == 1) & (q != at))
        def _():
            from_plane(1, q).wait_recv()
            total_ref[...] += kvgot[1, q].astype(F32)

    over(0, PLANE, collect)

    @pl.when(zl == 1)
    def _():
        relay_ref[...] = total_ref[...].astype(BF16)
        across.start()

    reduce_some(1)

    def collect_own(q):
        from_plane(0, q).wait_recv()
        dkv_ref[...] += kvgot[0, q].astype(F32)

    over(at + 1, PLANE, collect_own)

    @pl.when(zl == 0)
    def _():
        from_plane(1, 0).wait_recv()
        dkv_ref[...] += kvgot[1, 0].astype(F32)

    @pl.when(me < BLOCKS - 1)
    def _():
        edge_copy.wait_recv()

    @pl.when(me == BLOCKS - 1)
    def _():
        edge_out[...] = jnp.zeros_like(edge_out)

    tail = pl.ds(ROWS - 8, 8)
    g_ref[tail, :] += edge_out[:, :INNER]
    ddtx_ref[pl.ds(ROWS, 8), :] += edge_out[:, INNER:]
    dx_ref[...] = g_ref[...].astype(BF16)
    misc_ref[:, :128] = ddtx_ref[8:, :].astype(BF16)
    dkv = dkv_ref[...]
    turned = turn_pairs(dkv * score_scale, cosine, sine, -1.0)
    misc_ref[:, 128:] = jnp.where(c == 0, turned, dkv).astype(BF16)

    reduce_some(rs.steps - done)

    @pl.when(me > 0)
    def _():
        edge_copy.wait_send()

    states.close()
    rs.close()
    left.finish()
    left.close()
    for o in range(1, 4):
        share(o).wait_send()
    to_sibling(me).wait_send()

    def given(k):
        q, _ = plane_peer(k, -1)

        @pl.when(q < at)
        def _():
            to_sibling(zl * PLANE + q).wait_send()
            to_owner(k, 0).wait_send()

        @pl.when(zl == 1)
        def _():
            to_sibling(q).wait_send()
            to_owner(k, 1).wait_send()

    over(0, PLANE - 1, given)

    @pl.when(zl == 1)
    def _():
        to_sibling(at).wait_send()
        across.wait_send()


def head_of_lane_f32(g):
    row = lax.broadcasted_iota(jnp.int32, (128, 128), 0)
    lane = lax.broadcasted_iota(jnp.int32, (128, 128), 1)
    return (lane == 2 * g + (row >= SSM_DIM).astype(jnp.int32)).astype(F32)


def mixer_backward(*args):
    wide = 2 * ROWS
    dma = pltpu.SemaphoreType.DMA
    v = pltpu.VMEM
    piece = (BLOCKS, ROWS, HEAD_DIM)
    return call(
        mixer_backward_kernel, "mixer_backward", args, (23, 25, 26, 21, 22, 24, 30, 0, 1, 2, 5, 27),
        [
            ((ROWS, 2 * HEAD_DIM), BF16),
            ((ROWS, 256), BF16),
            ((ROWS, INNER), BF16),
            ((ROWS, INNER), BF16),
            ((ROWS, 128), BF16),
            ((8, INNER), F32),
            ((8, 128), F32),
            ((8, 128), F32),
            ((64, 12 * WIDE), F32),
            ((OWN, ROWS), BF16),
        ],
        [
            v((ROWS, HEAD_DIM), F32),
            v((HEAD_DIM, wide), F32),
            *[v(piece, BF16)] * 3,
            v((2, PLANE, ROWS, HEAD_DIM), BF16),
            v((ROWS, HEAD_DIM), BF16),
            v((ROWS, HEAD_DIM), F32),
            v((ROWS + 8, INNER), F32),
            v((ROWS + 8, 128), F32),
            v((ROWS + 8, 128), F32),
            v((INNER, STATE), F32),
            *[v((BLOCKS, SCAN_ROWS + 8, STATE), BF16)] * 4,
            v((ROWS, ROWS), F32),
            v((ROWS, ROWS), F32),
            v((128, ROWS), F32),
            v((ROWS, INNER), F32),
            v((ROWS, INNER), F32),
            v((ROWS, BC), F32),
            v((4, ROWS, 128), BF16),
            v((4, ROWS, 128), BF16),
            v((8, GRAD_EDGE), F32),
            v((8, GRAD_EDGE), F32),
            v((INNER, STATE), F32),
            v((ROWS + 8, 128), F32),
            v((ROWS, 128), F32),
            v((ROWS + 8, 128), F32),
            dma((2, PLANE)),
            dma((2, PLANE)),
            dma((BLOCKS,)),
            dma((BLOCKS,)),
            dma((2,)),
            dma((2, BLOCKS)),
            dma((2, BLOCKS)),
            dma((4,)),
            dma((4,)),
            dma((4,)),
            v((CONV, 128), F32),
            *Reduce.scratch(12),
        ],
        2,
    )


SMALL = 8 * 128
SMALL_AT = 5
CHUNKS = 13
GATHER_FROM = CHUNKS


def finish_kernel(
    loads, misc_ref, dx_ref, dz_ref, dq_ref, ddt_ref, gated_ref, att_ref, nt_ref, ntz_ref, mt_ref,
    mtz_ref, ffn_ref, tok_ref, x_w, z_w, q_w, dt_w, dxtaps_ref, dbctaps_ref, dvec_ref,
    gains_ref, bc_all, kv_all, outz_ref,
    w_ref, all_ref, alls_ref, back_sum, ffn_sum,
    back_ref, near_sem, bc_w, kv_w, column_sem, own_small, mine, esum, egot, e_send, e_recv, z_send, z_recv, w_send, w_recv,
    sib_send, sib_recv, s_send, s_recv, t_send, t_recv, part_ref, *rest,
):
    loads.start()
    me, c, zh = block_index(), lax.axis_index("c"), lax.axis_index("zh")
    chip = zh * BLOCKS + me
    sibling = {"c": 1 - c}

    def chip_at(p):
        return {"zh": p // BLOCKS, **block_at(p % BLOCKS)}

    n_rs = len(Reduce.scratch(CHUNKS))
    rs = Reduce(
        [(nt_ref, ntz_ref, 0), (mt_ref, mtz_ref, 9)], CHUNKS, 9, *rest[:7], w_ref, rest[7:n_rs]
    )
    rest = rest[n_rs:]
    n_sum = len(HeadSum.scratch())
    back = HeadSum(back_ref, back_sum, *rest[:3], rest[3:n_sum])
    rest = rest[n_sum:]
    ffn = HeadSum(ffn_ref, ffn_sum, *rest[:3], rest[3:])

    barrier = pltpu.get_barrier_semaphore()
    over(1, CHIPS, lambda o: signal(barrier, chip_at((chip + o) % CHIPS)))
    signal(barrier, sibling)
    pl.semaphore_wait(barrier, CHIPS)

    head = zh * 2 + c
    columns = [
        pltpu.make_async_copy(
            ref.at[:, pl.ds(pl.multiple_of(k * 128, 128), 128)], here, column_sem.at[i]
        )
        for i, (ref, k, here) in enumerate(((bc_all, head, bc_w), (kv_all, c * 2 + zh, kv_w)))
    ]
    for copy in columns:
        copy.start()
    rs.fill([misc_ref, dx_ref, dz_ref, dq_ref])
    rs.r[8, :, :128] = ddt_ref[...]
    rs.r[8, :, 128:] = jnp.zeros_like(ddt_ref)
    over(0, rs.here, lambda k: rs.right(k).start())
    near = pltpu.make_async_copy(outz_ref, rs.rz.at[pl.ds(9, 4)], near_sem)
    near.start()
    loads.need(nt_ref, ntz_ref)

    def partial(rows):
        total = dot(dx_ref[rows, :], x_w[...], 1, 1)
        total += dot(dz_ref[rows, :], z_w[...], 1, 1)
        total += dot(dq_ref[rows, :], q_w[...], 1, 1)
        total += dot(ddt_ref[rows, :], dt_w[...], 1, 1)
        total += dot(misc_ref[rows, :128], bc_w[...], 1, 1)
        back_ref[rows, :] = (total + dot(misc_ref[rows, 128:], kv_w[...], 1, 1)).astype(BF16)

    half = ROWS // 2
    loads.need(x_w, z_w, q_w, dt_w)
    for copy in columns:
        copy.wait()
    rs.step(0)
    partial(pl.ds(pl.multiple_of((1 - c) * half, half), half))
    back.start()
    rs.step(1)
    partial(pl.ds(pl.multiple_of(c * half, half), half))
    loads.need(mt_ref, mtz_ref, ffn_ref, tok_ref, gated_ref, att_ref)
    near.wait()
    rs.fill([gated_ref, att_ref], 9)
    ffn.start()

    at, level = me % PLANE, zh * NZ + lax.axis_index("zl")

    def along_z(o):
        d = (level + o) % 4
        where = {"zh": d // NZ, "zl": d % NZ}
        return remote(mine, all_ref.at[c, at, level], z_send.at[o], z_recv.at[o], where)

    x, y = lax.axis_index("x"), lax.axis_index("y")

    def at_place(i, j):
        return {"x": i, "y": j}, i * NY + j

    def piece(q, h, send, where):
        ref = all_ref.at[c, q, pl.ds(2 * h, 2)]
        return remote(ref, ref, send, w_recv.at[h, q], where)

    def one_way(h, o):
        where = {"x": (x + o) % NX} if h == 0 else {"y": (y + o) % NY}
        return piece(at, h, w_send.at[h, o], where)

    def other_way(h, k, o):
        i, j = ((x + k) % NX, y) if h == 0 else (x, (y + k) % NY)
        where = {"y": (y + o) % NY} if h == 0 else {"x": (x + o) % NX}
        return piece(i * NY + j, h, w_send.at[h, 4 * k + 4 + o], where)

    def arrived(q, h):
        return piece(q, h, w_send.at[0, 0], sibling)

    def to_sibling(q, core):
        return remote(
            all_ref.at[core, q], all_ref.at[core, q], sib_send.at[q], sib_recv.at[q], sibling
        )

    def columns_out():
        for o in range(1, 4):
            along_z(o).wait_recv()
        for o in range(1, 4):
            one_way(0, o).start()
            one_way(1, o).start()
        to_sibling(at, c).start()
        for o in range(1, 4):
            other_way(0, 0, o).start()
            other_way(1, 0, o).start()

    def columns_on():
        for k in range(1, 4):
            for h in range(2):
                i, j = ((x + k) % NX, y) if h == 0 else (x, (y + k) % NY)
                arrived(i * NY + j, h).wait_recv()
                for o in range(1, 4):
                    other_way(h, k, o).start()

    def pass_on(k):
        q, _ = plane_peer(k, -1)
        same_x, same_y = q // NY == x, q % NY == y

        @pl.when(jnp.logical_not(same_y))
        def _():
            arrived(q, 0).wait_recv()

        @pl.when(jnp.logical_not(same_x))
        def _():
            arrived(q, 1).wait_recv()

        to_sibling(q, c).start()

    def share(d):
        return remote(own_small.at[d], egot.at[me], e_send.at[d], e_recv.at[me], block_at(d))

    def shared(s):
        return remote(egot.at[s], egot.at[s], e_send.at[0], e_recv.at[s], block_at(s))

    def small_spread(o):
        d = (chip + o) % CHIPS
        slot = zh * SMALL_AT + me
        return remote(esum, alls_ref.at[c, slot], s_send.at[o], s_recv.at[slot], chip_at(d))

    def small_sibling(slot, core):
        return remote(
            alls_ref.at[core, slot], alls_ref.at[core, slot], t_send.at[slot], t_recv.at[slot],
            sibling,
        )

    def put(row, value):
        own_small[row // 8, row % 8 : row % 8 + 1, :] = value

    def gradient():
        for r in range(0, ROWS, 32):
            rows = pl.ds(r, 32)
            x = tok_ref[rows, :].astype(F32)
            scale = lax.rsqrt(jnp.mean(x * x, 1, keepdims=True) + EPSILON)
            n = x * scale
            grad = back_sum[rows, :].astype(F32)
            gains = jnp.sum(grad * n, 0, keepdims=True)
            for k in range(MODEL // 128):
                piece = gains[:, k * 128 : (k + 1) * 128]
                part_ref[k : k + 1, :] = piece if r == 0 else part_ref[k : k + 1, :] + piece
        own_small[0, :4] = part_ref[pl.ds(head * 4, 4), :]
        for k in range(CONV):
            for g in range(GROUPS):
                put(4 + GROUPS * k + g, dxtaps_ref[k : k + 1, g * 128 : (g + 1) * 128])
            put(28 + k, dbctaps_ref[k : k + 1, :])
            put(32 + k, gains_ref[0:1, lane_block(head * 4 + k)])
        lane = lax.broadcasted_iota(jnp.int32, (1, 128), 1)
        line = jnp.zeros((1, 128), F32)
        for k in range(3):
            moved = dvec_ref[k : k + 1, :] if k == 0 else pltpu.roll(dvec_ref[k : k + 1, :], k * HEADS, 1)
            line = jnp.where((lane >= k * HEADS) & (lane < (k + 1) * HEADS), moved, line)
        put(36, line)
        own_small[4, 5:] = jnp.zeros((3, 128), F32)

        def give(d):
            @pl.when(d != me)
            def _():
                share(d).start()

        over(0, SMALL_AT, give)

    def small_sums():
        @pl.when(me < SMALL_AT)
        def _():
            egot[me] = own_small[me]

            def take(s):
                @pl.when(s != me)
                def _():
                    shared(s).wait_recv()

            over(0, BLOCKS, take)
            total = lax.fori_loop(0, BLOCKS, lambda s, t: t + egot[s], jnp.zeros((8, 128), F32))
            esum[...] = jnp.concatenate([total, jnp.zeros_like(total)], 0).astype(BF16)
            slot = zh * SMALL_AT + me
            alls_ref[c, slot] = esum[...]
            over(1, CHIPS, lambda o: small_spread(o).start())
            small_sibling(slot, c).start()

    def small_pass():
        def one(slot):
            @pl.when(slot != zh * SMALL_AT + me + jnp.where(me < SMALL_AT, 0, CHIPS))
            def _():
                remote(
                    esum, alls_ref.at[c, slot], s_send.at[0], s_recv.at[slot], sibling
                ).wait_recv()
                small_sibling(slot, c).start()

        over(0, 2 * SMALL_AT, one)

    def weights_out():
        mine[...] = w_ref[:, :WIDE].astype(BF16)
        all_ref[c, at, level] = mine[...]
        for o in range(1, 4):
            along_z(o).start()

    batch, first_pass = 3, rs.steps - 5

    def step(i):
        rs.step(i)

        @pl.when(i == LAST)
        def _():
            weights_out()
            back.across()

        @pl.when(i == 8)
        def _():
            columns_out()
            ffn.across()

        @pl.when(i == 11)
        def _():
            back.join()
            columns_on()

        @pl.when(i == 12)
        def _():
            back.finish()
            gradient()

        @pl.when(i == 15)
        def _():
            small_sums()

        @pl.when(i >= first_pass)
        def _():
            k = i - first_pass
            over(k * batch, (k + 1) * batch, pass_on)

    over(2, rs.steps, step)
    ffn.join()
    small_pass()
    ffn.finish()

    over(0, PLANE, lambda q: to_sibling(q, 1 - c).wait_recv())
    over(0, 2 * SMALL_AT, lambda s: small_sibling(s, 1 - c).wait_recv())
    rs.close()
    back.close()
    ffn.close()
    over(0, PLANE, lambda q: to_sibling(q, c).wait_send())
    over(0, 2 * SMALL_AT, lambda s: small_sibling(s, c).wait_send())
    for h in range(2):
        for o in range(1, 4):
            one_way(h, o).wait_send()
            for k in range(4):
                other_way(h, k, o).wait_send()
    for o in range(1, 4):
        along_z(o).wait_send()

    @pl.when(me < SMALL_AT)
    def _():
        over(1, CHIPS, lambda o: small_spread(o).wait_send())

    def given(d):
        @pl.when(d != me)
        def _():
            share(d).wait_send()

    over(0, SMALL_AT, given)


def finish(*args):
    v, dma = pltpu.VMEM, pltpu.SemaphoreType.DMA
    return call(
        finish_kernel, "finish", args, (7, 8, 13, 14, 15, 16, 9, 10, 11, 12, 5, 6),
        [
            ((64, CHUNKS * WIDE), F32),
            ((2, PLANE, 4, 64, WIDE), BF16),
            ((2, 2 * SMALL_AT, 16, 128), BF16),
            ((ROWS, MODEL), BF16),
            ((ROWS, MODEL), BF16),
        ],
        [
            v((ROWS, MODEL), BF16),
            dma,
            v((MODEL, 128), BF16),
            v((MODEL, 128), BF16),
            dma((2,)),
            v((SMALL_AT, 8, 128), F32),
            v((64, WIDE), BF16),
            v((16, 128), BF16),
            v((BLOCKS, 8, 128), F32),
            dma((SMALL_AT,)), dma((BLOCKS,)),
            dma((4,)), dma((4,)),
            dma((2, 20)), dma((2, PLANE)), dma((PLANE,)), dma((PLANE,)),
            dma((CHIPS,)), dma((2 * SMALL_AT,)),
            dma((2 * SMALL_AT,)), dma((2 * SMALL_AT,)),
            v((16, 128), F32),
            *Reduce.scratch(CHUNKS),
            *HeadSum.scratch(),
            *HeadSum.scratch(),
        ],
        3,
        (21, 22, 23),
    )


def place_kernel(
    all_ref, back_ref, ffn_ref, hid_ref, ghid_ref, tok_ref, gain_ref, mixer_ref, ffn_w, small_ref,
    out_ref, dtok_ref, bc_ref, kv_ref, x_w, z_w, q_w, dt_w, out_w, attn_w, gate_w, up_w, down_w,
    xtaps_ref, bctaps_ref, vec_ref, gains_ref,
):
    for c in range(2):
        for p in range(all_ref.shape[1]):
            for zh in range(2):
                rows = slice(p * 64, (p + 1) * 64)
                at, turned = (zh * 2 + c) * 128, (c * 2 + zh) * 128
                bc_ref[rows, at : at + 128] = all_ref[c, p, zh, 0, :, :128].astype(F32)
                kv_ref[rows, turned : turned + 128] = all_ref[c, p, zh, 0, :, 128:].astype(F32)
    for r in range(0, out_ref.shape[0], 32):
        rows = slice(r, r + 32)
        out_ref[rows, :] = (hid_ref[rows, :] + ffn_ref[rows, :].astype(F32)).astype(BF16)
        x = tok_ref[rows, :].astype(F32)
        scale = lax.rsqrt(jnp.mean(x * x, 1, keepdims=True) + EPSILON)
        n = x * scale
        scaled = back_ref[rows, :].astype(F32) * gain_ref[0:1, :]
        along = jnp.mean(n * scaled, 1, keepdims=True)
        dtok_ref[rows, :] = ghid_ref[rows, :] + scale * (scaled - n * along)

    @pl.when(pl.program_id(0) == 0)
    def _():
        at = WIDE
        for ref in (x_w, z_w, q_w, dt_w):
            width = ref.shape[1]
            ref[...] = mixer_ref[:, at : at + width]
            at += max(width, WIDE)
        for ref in (out_w, attn_w):
            ref[...] = mixer_ref[:, at : at + ref.shape[1]]
            at += ref.shape[1]
        at = 0
        for ref in (down_w, gate_w, up_w):
            ref[...] = ffn_w[:, at : at + ref.shape[1]]
            at += ref.shape[1]
        lane = lax.broadcasted_iota(jnp.int32, (1, 128), 1)
        lines = [jnp.zeros((1, 128), F32)] * 3
        for h in range(4):

            def row(k):
                piece = small_ref[h % 2, h // 2 * SMALL_AT + k // 8].astype(F32)
                return piece[k % 8 : k % 8 + 1, :]

            for k in range(CONV):
                for g in range(GROUPS):
                    cols = slice(h * INNER + g * 128, h * INNER + (g + 1) * 128)
                    xtaps_ref[k : k + 1, cols] = row(4 + GROUPS * k + g)
                bctaps_ref[k : k + 1, h * 128 : (h + 1) * 128] = row(28 + k)
                cols = slice((4 * h + k) * 128, (4 * h + k + 1) * 128)
                gains_ref[0:1, cols] = row(k)
                gains_ref[1:2, cols] = row(32 + k)
            for k in range(3):
                shift = (h - k) * HEADS % 128
                moved = pltpu.roll(row(36), shift, 1) if shift else row(36)
                mine = (lane >= h * HEADS) & (lane < (h + 1) * HEADS)
                lines[k] = jnp.where(mine, moved, lines[k])
        for k in range(3):
            vec_ref[k : k + 1, :] = lines[k]
        vec_ref[3:, :] = jnp.zeros((5, 128), F32)
        gains_ref[2:, :] = jnp.zeros((6, MODEL), F32)


def place(gathered, back, ffn, hidden_in, ghid, tokens, gain, mixer_w, ffn_w, small):
    steps = 4
    spans, rows, ff = PLANE * NZ // steps, ROWS // steps, ffn_w.shape[1] // 3
    half = steps // NZ
    s = jax.ShapeDtypeStruct

    def whole(shape):
        return pl.BlockSpec(shape, lambda i: (0,) * len(shape))

    token = pl.BlockSpec((rows, MODEL), lambda i: (i, 0))
    wide = pl.BlockSpec((64 * spans, 512), lambda i: (i, 0))
    kept = [
        (64, INNER), (64, INNER), (64, 256), (64, 128), (64, INNER), (64, 256), (64, ff), (64, ff),
        (64, ff), (CONV, 4 * INNER), (CONV, BC), (8, 128), (8, MODEL),
    ]
    return pl.pallas_call(
        place_kernel,
        name="place",
        out_shape=(
            s((ROWS, MODEL), BF16), s((ROWS, MODEL), F32), s((MODEL, 512), F32),
            s((MODEL, 512), F32), *[s(shape, F32) for shape in kept],
        ),
        grid=(steps,),
        in_specs=[
            pl.BlockSpec((2, spans, 2, 1, 64, WIDE), lambda i: (0, i % half, 0, i // half, 0, 0)),
            token, token, token, token, token, whole((1, MODEL)), whole(mixer_w.shape),
            whole(ffn_w.shape), whole(small.shape),
        ],
        out_specs=(token, token, wide, wide, *[whole(shape) for shape in kept]),
        compiler_params=pltpu.CompilerParams(vmem_limit_bytes=VMEM_LIMIT),
    )(
        gathered.reshape(2, PLANE, 2, NZ, 64, WIDE), back, ffn, hidden_in, ghid, tokens, gain,
        mixer_w, ffn_w, small,
    )


def on_device(
    tokens, segment_ids, cotangent, norm1_gain, x_weight, z_weight, bc_weight, dt_weight,
    x_conv, bc_conv, dt_bias, decay_rate, skip_gain, out_weight, query_weight, kv_weight,
    attn_weight, norm2_gain, gate_weight, up_weight, down_weight,
):
    heads = decay_rate.shape[0]
    inner = x_weight.shape[1]
    positions = block_index() * ROWS + jnp.arange(ROWS)
    half_dim = HEAD_DIM // 2
    frequency = ROPE_BASE ** (-(jnp.arange(half_dim).astype(F32) * 2.0 / HEAD_DIM))
    angles = positions.astype(F32)[:, None] * frequency[None, :]
    cosine, sine = jnp.cos(angles), jnp.sin(angles)
    cosine = jnp.concatenate([cosine, cosine], 1)
    sine = jnp.concatenate([-sine, sine], 1)
    dt_wide = jnp.pad(dt_weight, ((0, 0), (0, 128 - heads)))
    seg = segment_ids.astype(F32)
    seg_row = jnp.broadcast_to(jnp.tile(seg, 2), (8, 2 * ROWS))
    seg_column = jnp.broadcast_to(seg[:, None], (ROWS, 128))
    vectors = jnp.pad(jnp.stack([dt_bias, decay_rate]), ((0, 6), (0, 128 - heads)))
    skip = jnp.broadcast_to(jnp.repeat(skip_gain, SSM_DIM), (8, inner))
    gain_one, gain_two = norm1_gain.reshape(1, MODEL), norm2_gain.reshape(1, MODEL)

    (
        normed_t, cot_t, queries, x_pre, bc_pre, dt_raw, z_val, attended, lse, kv_all, edge_in,
        gated, core, x_act, bc_act, state_in, normed_near, cot_near, attended_low,
    ) = mixer_forward(
        tokens, cotangent, gain_one, query_weight, kv_weight, x_weight, bc_weight, dt_wide,
        z_weight, cosine, sine, seg_column, seg_row, x_conv, bc_conv, vectors, skip,
    )
    (
        hidden_in, two_t, grad_gate, grad_up, hidden, ffn_part, grad_hidden_in, mix_t, gains_two,
        grad_gated, grad_attended, two_near, mixed_near,
    ) = feed_forward(
        gated, attended_low, tokens, cotangent, gain_two, out_weight, attn_weight, gate_weight,
        up_weight, down_weight,
    )
    (
        grad_query, misc, grad_z, grad_x_pre, grad_dt, grad_x_conv, grad_bc_conv, grad_vectors,
        ffn_w, mix_near,
    ) = mixer_backward(
        queries, grad_attended, attended, lse, seg_row, kv_all, grad_gated, z_val, core, x_act,
        bc_act, x_pre, bc_pre, edge_in, dt_raw, state_in, seg_column, x_conv, bc_conv, vectors,
        skip, grad_gate, grad_up, hidden, two_t, cot_t, cot_near, mix_t, cosine, sine, two_near,
    )
    mixer_w, gathered, small_sums, grad_normed, ffn_sum = finish(
        misc, grad_x_pre, grad_z, grad_query, grad_dt, gated, attended_low, normed_t, normed_near,
        mix_t, mix_near, ffn_part, tokens, x_weight, z_weight, query_weight, dt_wide, grad_x_conv,
        grad_bc_conv, grad_vectors, gains_two, bc_weight, kv_weight, mixed_near,
    )
    (
        output, grad_tokens, bc_w, kv_w, x_w, z_w, q_w, dt_w, out_w, attn_w, gate_w, up_w, down_w,
        x_taps, bc_taps, sums, gains,
    ) = place(
        gathered, grad_normed, ffn_sum, hidden_in, grad_hidden_in, tokens, gain_one, mixer_w,
        ffn_w, small_sums,
    )
    all_heads = 4 * heads
    return (
        output, grad_tokens, gains[0], x_w, z_w, bc_w, dt_w[:, :heads], x_taps, bc_taps,
        sums[0, :all_heads], sums[1, :all_heads], sums[2, :all_heads], out_w.T, q_w, kv_w,
        attn_w.T, gains[1], gate_w, up_w, down_w.T,
    )


def solution(mesh):
    split = Mesh(mesh.devices.reshape(NZ, NX, NY, 2, 2), (*SEQ, "zh", "c"))
    head = ("zh", "c")
    rows, columns, both, turned = P(SEQ, None), P(None, head), P(SEQ, head), P(head, SEQ)
    return jax.shard_map(
        on_device,
        mesh=split,
        in_specs=(
            rows, P(SEQ), rows, P(), columns, columns, P(), columns, columns, P(), P(head),
            P(head), P(head), P(head, None), columns, P(), P(head, None), P(), columns, columns,
            P(head, None),
        ),
        out_specs=(
            rows, rows, P(), both, both, P(), both, P(), P(), P(), P(), P(), turned, both, P(),
            turned, P(), both, both, turned,
        ),
        check_vma=False,
    )
```

```python
import functools

import jax
import jax.numpy as jnp
from jax import lax
from jax.experimental import pallas as pl
from jax.experimental.pallas import tpu as pltpu
from jax.sharding import Mesh
from jax.sharding import PartitionSpec as P

SSM_DIM = 64
STATE = 256
CONV = 4
KVHEADS = 2
HEAD_DIM = 128
NZ, NX, NY = 2, 4, 4
BLOCKS = NZ * NX * NY
CHIPS = 2 * BLOCKS
ROWS = 256
MODEL = 2048
SEQ = ("zl", "x", "y")
EPSILON = 1e-05
ROPE_BASE = 100000000000.0
HIGHEST = lax.Precision.HIGHEST
MESH = pl.DeviceIdType.MESH
BF16, F32 = jnp.bfloat16, jnp.float32
MASKED = -1e30
LOG2E = 1.4426950408889634
VMEM_LIMIT = 56 * 2**20


def block_index():
    return (lax.axis_index("zl") * NX + lax.axis_index("x")) * NY + lax.axis_index("y")


def block_at(s):
    return {"zl": s // (NX * NY), "x": (s // NY) % NX, "y": s % NY}


PLANE = NX * NY


def plane_peer(k, sign, stride=13):
    o = 1 + (k * stride) % (PLANE - 1)
    dx, dy = o // NY, o % NY
    x, y = lax.axis_index("x"), lax.axis_index("y")
    if sign < 0:
        dx, dy = NX - dx, NY - dy
    x, y = (x + dx) % NX, (y + dy) % NY
    return x * NY + y, {"x": x, "y": y}


def signal(sem, where):
    pl.semaphore_signal(sem, inc=1, device_id=where, device_id_type=MESH)


def remote(src, dst, send, recv, where):
    return pltpu.make_async_remote_copy(src, dst, send, recv, device_id=where, device_id_type=MESH)


def over(start, stop, body):
    def step(i, carry):
        body(i)
        return carry

    lax.fori_loop(start, stop, step, 0)


def dot(a, b, left=1, right=0):
    return lax.dot_general(
        a, b, (((left,), (right,)), ((), ())), preferred_element_type=F32
    )


def vmem(n):
    return [pl.BlockSpec(memory_space=pltpu.VMEM)] * n


def params(collective_id):
    return pltpu.CompilerParams(
        collective_id=collective_id, has_side_effects=True, vmem_limit_bytes=VMEM_LIMIT
    )


HEADS = 12
INNER = HEADS * SSM_DIM
GROUPS = INNER // 128
BC = 2 * STATE
SCAN_ROWS = INNER // BLOCKS
EDGE_WIDE = INNER + BC + 128
GRAD_EDGE = INNER + 128


def two_parts(v):
    high = v.astype(BF16)
    return high, (v - high.astype(F32)).astype(BF16)


def low_lanes(rows):
    return lax.broadcasted_iota(jnp.int32, (rows, 128), 1) < SSM_DIM


def widen(v, g):
    low = low_lanes(v.shape[0])
    return jnp.where(low, v[:, 2 * g : 2 * g + 1], v[:, 2 * g + 1 : 2 * g + 2])


def per_head(v, g):
    lane = lax.broadcasted_iota(jnp.int32, v.shape, 1)
    first = jnp.sum(jnp.where(lane < SSM_DIM, v, 0.0), 1, keepdims=True)
    second = jnp.sum(jnp.where(lane < SSM_DIM, 0.0, v), 1, keepdims=True)
    return jnp.where(lane == 2 * g, first, jnp.where(lane == 2 * g + 1, second, 0.0))


def triangle():
    row = lax.broadcasted_iota(jnp.int32, (ROWS, ROWS), 0)
    col = lax.broadcasted_iota(jnp.int32, (ROWS, ROWS), 1)
    return (col <= row).astype(F32).astype(BF16)


def running(v, lower, side):
    high, low = two_parts(v)
    middle, lowest = two_parts(v - high.astype(F32))
    return (
        dot(lower, high, side, 0) + dot(lower, middle, side, 0) + dot(lower, lowest, side, 0)
    )


def sigmoid(v):
    return 1.0 / (1.0 + jnp.exp(-v))


def softplus(v):
    return jnp.maximum(v, 0.0) + jnp.log(1.0 + jnp.exp(-jnp.abs(v)))


def lane_block(g):
    return pl.ds(pl.multiple_of(g * 128, 128), 128)


def decays(dt_ref, vec_ref, seg_ref, segx_ref, lower):
    pre = dt_ref[...] + vec_ref[0:1, :]
    step = softplus(pre)
    total = running(-step * vec_ref[1:2, :] * LOG2E, lower, 1)
    last = total[ROWS - 1 : ROWS, :]
    seg = seg_ref[...]
    seg_last, before = seg[ROWS - 1 : ROWS, :], segx_ref[7:8, :]
    carry = jnp.where(seg == seg_last, jnp.exp2(last - total), 0.0)
    entry = jnp.where(seg == before, jnp.exp2(total), 0.0)
    through = jnp.where(seg_last == before, jnp.exp2(last), 0.0)
    return pre, step, total, carry, entry, through


def conv_group(ext_ref, segx_ref, seg_ref, taps_ref, cols):
    total, inputs = None, []
    for k in range(CONV):
        same = segx_ref[pl.ds(5 + k, ROWS), :] == seg_ref[...]
        v = jnp.where(same, ext_ref[pl.ds(5 + k, ROWS), cols], 0.0)
        inputs.append(v)
        term = taps_ref[k : k + 1, cols] * v
        total = term if total is None else total + term
    return total, inputs


def scan_message(msg_ref, state_ref, through):
    high = through.astype(BF16)
    rest = through - high.astype(F32)
    middle = rest.astype(BF16)
    low = rest - middle.astype(F32)
    extra = jnp.concatenate([high.astype(F32), middle.astype(F32), low, jnp.zeros((5, 128), F32)], 0)
    extra = jnp.concatenate([extra, jnp.zeros((8, STATE - 128), F32)], 1)

    def fill(b):
        rows = state_ref[pl.ds(pl.multiple_of(b * SCAN_ROWS, 8), SCAN_ROWS), :]
        msg_ref[b] = jnp.concatenate([rows, extra], 0).astype(BF16)

    over(0, BLOCKS, fill)


class Scan:
    def __init__(self, reverse, me, msg, got, back, out, send, recv):
        self.reverse, self.me = reverse, me
        self.msg, self.got, self.back, self.out = msg, got, back, out
        self.send, self.recv = send, recv

    def there(self, o):
        d = (self.me + o) % BLOCKS
        return remote(
            self.msg.at[d], self.got.at[self.me], self.send.at[0, o], self.recv.at[0, o],
            block_at(d),
        )

    def arrived(self, phase, dst, o):
        s = (self.me + BLOCKS - o) % BLOCKS
        return remote(
            dst.at[s], dst.at[s], self.send.at[phase, o], self.recv.at[phase, o], block_at(s)
        )

    def start(self):
        over(1, BLOCKS, lambda o: self.there(o).start())
        self.got[self.me] = self.msg[self.me]

    def turn(self):
        me = self.me
        over(1, BLOCKS, lambda o: self.arrived(0, self.got, o).wait_recv())
        lane = lax.broadcasted_iota(jnp.int32, (SCAN_ROWS, 128), 1)
        row = lax.broadcasted_iota(jnp.int32, (SCAN_ROWS, 128), 0) + me * SCAN_ROWS
        at_head = (row >= lane * SSM_DIM) & (row < lane * SSM_DIM + SSM_DIM)

        def scan(i, state):
            k = BLOCKS - 1 - i if self.reverse else i
            message = self.got[k].astype(F32)
            self.back[k] = jnp.concatenate([state, jnp.zeros((8, STATE), F32)], 0).astype(BF16)

            @pl.when(k != me)
            def _():
                self.returned(k).start()

            factors = message[SCAN_ROWS : SCAN_ROWS + 1, :128]
            factors += message[SCAN_ROWS + 1 : SCAN_ROWS + 2, :128]
            factors += message[SCAN_ROWS + 2 : SCAN_ROWS + 3, :128]
            through = jnp.sum(jnp.where(at_head, factors, 0.0), 1, keepdims=True)
            return through * state + message[:SCAN_ROWS]

        lax.fori_loop(0, BLOCKS, scan, jnp.zeros((SCAN_ROWS, STATE), F32))
        self.out[me] = self.back[me]

    def returned(self, k):
        o = (k + BLOCKS - self.me) % BLOCKS
        return remote(
            self.back.at[k], self.out.at[self.me], self.send.at[1, o], self.recv.at[1, o],
            block_at(k),
        )

    def finish(self, state_ref):
        over(1, BLOCKS, lambda o: self.arrived(1, self.out, o).wait_recv())

        def fill(b):
            rows = self.out[b].astype(F32)
            state_ref[pl.ds(pl.multiple_of(b * SCAN_ROWS, 8), SCAN_ROWS), :] = rows[:SCAN_ROWS]

        over(0, BLOCKS, fill)

    def close(self):
        def sent(o):
            self.there(o).wait_send()
            self.returned((self.me + o) % BLOCKS).wait_send()

        over(1, BLOCKS, sent)


def key_segments(block):
    turned = jnp.transpose(block.astype(F32))
    return jnp.concatenate([turned[:, 0:1], turned[:, 1:2]], 0)


def causal_mask(s):
    row = lax.broadcasted_iota(jnp.int32, (ROWS, 2 * ROWS), 0)
    col = lax.broadcasted_iota(jnp.int32, (ROWS, 2 * ROWS), 1) % ROWS
    return jnp.where(row <= col, s, MASKED)


def mixing_bias(seg_ref, segrow_ref):
    row = lax.broadcasted_iota(jnp.int32, (ROWS, ROWS), 0)
    col = lax.broadcasted_iota(jnp.int32, (ROWS, ROWS), 1)
    same = segrow_ref[0:1, :ROWS] == seg_ref[:, 0:1]
    return jnp.where((col <= row) & same, 0.0, MASKED)


WIDE = 256
RELAY, MIDDLE, LAST = 2, 4, 6
AHEAD = 4
OWN = MODEL // NZ


class Reduce:
    def __init__(self, lefts, n, here, r_ref, rz, part, rel, gx, half, gy, out_ref, sems):
        self.lefts, self.n, self.here, self.throttled = lefts, n, here, here == n
        self.r, self.rz, self.part, self.rel = r_ref, rz, part, rel
        self.gx, self.half, self.gy, self.out = gx, half, gy, out_ref
        self.rz_sem, self.rel_sem, self.gx_sem, self.gy_sem = (
            (sems[2 * k], sems[2 * k + 1]) for k in range(4)
        )
        self.zl, self.x, self.y = (lax.axis_index(a) for a in SEQ)
        self.other = {"zl": 1 - self.zl}

    @staticmethod
    def scratch(n):
        v, dma = pltpu.VMEM, pltpu.SemaphoreType.DMA
        return [
            v((n, ROWS, WIDE), BF16),
            v((n, ROWS, WIDE), BF16),
            v((n, 4, 4, 64, WIDE), BF16),
            v((n, 2, 2, 64, WIDE), BF16),
            v((n, 2, 4, 64, WIDE), BF16),
            v((n, 4, 64, WIDE), BF16),
            v((n, 3, 64, WIDE), BF16),
            *[dma((n,))] * 8,
        ]

    def fill(self, arrays, c=0):
        for ref in arrays:
            for k in range(ref.shape[1] // WIDE):
                self.r[c] = ref[:, k * WIDE : (k + 1) * WIDE]
                c += 1

    def right(self, c):
        return remote(
            self.r.at[c], self.rz.at[c], self.rz_sem[0].at[c], self.rz_sem[1].at[c], self.other
        )

    def start(self):
        over(0, AHEAD, lambda c: self.right(c).start())

    def place(self, c, phase, o):
        along_x = c % 2 == phase
        x_to = jnp.where(along_x, (self.x + o) % NX, self.x)
        y_to = jnp.where(along_x, self.y, (self.y + o) % NY)
        return {"x": x_to, "y": y_to}, jnp.where(along_x, x_to, y_to)

    def send(self, src, dst, sem, c, where):
        return remote(src, dst, sem[0].at[c], sem[1].at[c], where)

    def send_second(self, c, o):
        where, d = self.place(c, 1, o)
        return self.send(self.half.at[c, d], self.gy.at[c, o - 1], self.gy_sem, c, where)

    def whole(self, got, sem, c):
        return self.send(got.at[c], got.at[c], sem, c, self.other)

    def product(self, c):
        @pl.when((c + AHEAD < self.here) & self.throttled)
        def _():
            self.right(c + AHEAD).start()

        @pl.when(c < self.here)
        def _():
            self.right(c).wait_recv()

        mine, theirs = self.r[c], self.rz[c]
        even = c % 2 == 0
        ends = [first for _, _, first in self.lefts[1:]] + [self.n]
        for (own, near, first), end in zip(self.lefts, ends):
            @pl.when((c >= first) & (c < end))
            def _():
                for i in range(NX):
                    a = own[pl.ds(pl.multiple_of(self.zl * OWN + i * 256, 256), 256), :]
                    b = near[pl.ds(i * 256, 256), :]
                    tile = (dot(a, mine) + dot(b, theirs)).astype(BF16)
                    for j in range(NY):
                        self.part[c, jnp.where(even, i, j), jnp.where(even, j, i)] = (
                            tile[j * 64 : (j + 1) * 64]
                        )
        _, d = self.place(c, 0, 2)
        for k, o in ((0, 1), (1, 3)):
            src = self.part.at[c, d, pl.ds(2 * k, 2)]
            self.send(src, self.rel.at[c, k], self.rel_sem, c, self.place(c, 0, o)[0]).start()

    def relay(self, c):
        self.whole(self.rel, self.rel_sem, c).wait_recv()
        for k, o in ((0, 1), (1, 3)):
            where, d = self.place(c, 0, o)
            for j in (2 * k, 2 * k + 1):
                total = self.part[c, d, j].astype(F32) + self.rel[c, k, j - 2 * k].astype(F32)
                self.part[c, d, j] = total.astype(BF16)
            self.send(self.part.at[c, d], self.gx.at[c, k], self.gx_sem, c, where).start()

    def middle(self, c):
        self.whole(self.gx, self.gx_sem, c).wait_recv()
        mine = jnp.where(c % 2 == 0, self.x, self.y)
        for j in range(4):
            total = self.part[c, mine, j].astype(F32)
            for k in range(2):
                total += self.gx[c, k, j].astype(F32)
            self.half[c, j] = total.astype(BF16)
        for o in range(1, 4):
            self.send_second(c, o).start()

    def last(self, c):
        self.whole(self.gy, self.gy_sem, c).wait_recv()
        mine = jnp.where(c % 2 == 0, self.y, self.x)
        total = self.half[c, mine].astype(F32)
        for o in range(3):
            total += self.gy[c, o].astype(F32)
        self.out[:, pl.ds(pl.multiple_of(c * WIDE, WIDE), WIDE)] = total

    @property
    def steps(self):
        return self.n + LAST

    def step(self, i):
        for late, do in ((0, self.product), (RELAY, self.relay), (MIDDLE, self.middle), (LAST, self.last)):
            @pl.when((i >= late) & (i < self.n + late))
            def _():
                do(i - late)

    def close(self):
        over(0, self.here, lambda c: self.right(c).wait_send())

        def sent(c):
            self.whole(self.rel, self.rel_sem, c).wait_send()
            self.whole(self.gx, self.gx_sem, c).wait_send()
            self.whole(self.gy, self.gy_sem, c).wait_send()

        over(0, self.n, sent)


class Left:
    def __init__(self, l_ref, lz, sems):
        zl, c = lax.axis_index("zl"), lax.axis_index("c")
        half = OWN // 2
        there = pl.ds(pl.multiple_of((1 - zl) * OWN + c * half, half), half)
        near, other = (pl.ds(pl.multiple_of(k * half, half), half) for k in (c, 1 - c))
        sem = [sems.at[k] for k in range(4)]
        self.out = remote(l_ref.at[there], lz.at[near], sem[0], sem[1], {"zl": 1 - zl})
        self.on = remote(lz.at[near], lz.at[near], sem[2], sem[3], {"c": 1 - c})
        self.back = remote(lz.at[other], lz.at[other], sem[2], sem[3], {"c": 1 - c})

    def start(self):
        self.out.start()

    def pass_on(self):
        self.out.wait_recv()
        self.on.start()

    def finish(self):
        self.back.wait_recv()

    def close(self):
        self.out.wait_send()
        self.on.wait_send()


HEAD_CHUNKS = 4


class HeadSum:
    def __init__(self, x, out, near, pair, far, sems):
        self.x, self.out, self.near, self.pair, self.far = x, out, near, pair, far
        self.near_send, self.near_recv, self.far_send, self.far_recv, self.end_send, self.end_recv = sems
        self.c, zh = lax.axis_index("c"), lax.axis_index("zh")
        self.sibling, self.opposite = {"c": 1 - self.c}, {"zh": 1 - zh}
        self.half = x.shape[0] // 2
        self.rows_each = self.half // HEAD_CHUNKS

    @staticmethod
    def scratch():
        v, dma = pltpu.VMEM, pltpu.SemaphoreType.DMA
        return [*[v((ROWS // 2, MODEL), BF16)] * 3, *[dma((HEAD_CHUNKS,))] * 6]

    def rows(self, core, k):
        return pl.ds(pl.multiple_of(k // 2 * self.half + (2 * core + k % 2) * self.rows_each, 16), self.rows_each)

    def local(self, k):
        return pl.ds(k * self.rows_each, self.rows_each)

    def first(self, k):
        return remote(
            self.x.at[self.rows(1 - self.c, k)], self.near.at[self.local(k)],
            self.near_send.at[k], self.near_recv.at[k], self.sibling,
        )

    def second(self, k):
        return remote(
            self.pair.at[self.local(k)], self.far.at[self.local(k)],
            self.far_send.at[k], self.far_recv.at[k], self.opposite,
        )

    def third(self, k, core):
        rows = self.rows(core, k)
        return remote(
            self.out.at[rows], self.out.at[rows], self.end_send.at[k], self.end_recv.at[k],
            self.sibling,
        )

    def start(self, chunks=range(HEAD_CHUNKS)):
        for k in chunks:
            self.first(k).start()

    def across(self, chunks=range(HEAD_CHUNKS)):
        for k in chunks:
            self.first(k).wait_recv()
            own = self.x[self.rows(self.c, k)].astype(F32)
            self.pair[self.local(k)] = (own + self.near[self.local(k)].astype(F32)).astype(BF16)
            self.second(k).start()

    def join(self, chunks=range(HEAD_CHUNKS)):
        for k in chunks:
            self.second(k).wait_recv()
            total = self.pair[self.local(k)].astype(F32) + self.far[self.local(k)].astype(F32)
            self.out[self.rows(self.c, k)] = total.astype(BF16)
            self.third(k, self.c).start()

    def finish(self, chunks=range(HEAD_CHUNKS)):
        for k in chunks:
            self.third(k, 1 - self.c).wait_recv()

    def close(self):
        for k in range(HEAD_CHUNKS):
            self.first(k).wait_send()
            self.second(k).wait_send()
            self.third(k, self.c).wait_send()


class Loads:
    def __init__(self, pairs, sems, results, out_sems):
        self.copies = {
            id(there): pltpu.make_async_copy(here, there, sems.at[i])
            for i, (here, there) in enumerate(pairs)
        }
        self.results = {
            id(here): pltpu.make_async_copy(here, there, out_sems.at[i])
            for i, (here, there) in enumerate(results)
        }
        self.under_way = []

    def start(self):
        for copy in self.copies.values():
            copy.start()

    def need(self, *refs):
        for ref in refs:
            copy = self.copies.pop(id(ref), None)
            if copy is not None:
                copy.wait()

    def put(self, *refs):
        for ref in refs:
            copy = self.results.pop(id(ref))
            copy.start()
            self.under_way.append(copy)

    def flush(self):
        for copy in self.results.values():
            copy.start()
        for copy in (*self.results.values(), *self.under_way):
            copy.wait()


def fetching(kernel, n_in, n_out, late, large):
    def wrapped(*refs):
        ins, outs, rest = list(refs[:n_in]), list(refs[n_in : n_in + n_out]), refs[n_in + n_out :]
        count = len(late) + len(large)
        buffers, (sems, out_sems) = rest[-2 - count : -2], rest[-2:]
        pairs, results = [], []
        for buffer, i in zip(buffers, late):
            pairs.append((ins[i], buffer))
            ins[i] = buffer
        for buffer, i in zip(buffers[len(late) :], large):
            results.append((buffer, outs[i]))
            outs[i] = buffer
        loads = Loads(pairs, sems, results, out_sems)
        kernel(loads, *ins, *outs, *rest[: -2 - count])
        loads.flush()

    return wrapped


def call(kernel, name, args, late, outs, scratch, collective_id, left=()):
    anywhere, here = pl.BlockSpec(memory_space=pl.ANY), pl.BlockSpec(memory_space=pltpu.VMEM)
    shapes = [jax.ShapeDtypeStruct(*o) for o in outs]
    large = [i for i, o in enumerate(shapes) if o.size >= 2**14]
    dma = pltpu.SemaphoreType.DMA
    return pl.pallas_call(
        fetching(kernel, len(args), len(outs), late, large),
        name=name,
        out_shape=tuple(shapes),
        in_specs=[anywhere if i in (*late, *left) else here for i in range(len(args))],
        out_specs=tuple(anywhere if i in large else here for i in range(len(outs))),
        scratch_shapes=[
            *scratch,
            *[pltpu.VMEM(args[i].shape, args[i].dtype) for i in late],
            *[pltpu.VMEM(shapes[i].shape, shapes[i].dtype) for i in large],
            dma((max(len(late), 1),)),
            dma((max(len(large), 1),)),
        ],
        compiler_params=params(collective_id),
    )(*args)


def spread_small(seg, bias, rate, skip, seg_ref, segrow_ref, vec_ref, skip_ref):
    row = seg[...].astype(F32)
    seg_ref[...] = jnp.transpose(jnp.broadcast_to(row, (128, ROWS)))
    segrow_ref[...] = jnp.broadcast_to(jnp.concatenate([row, row], 1), segrow_ref.shape)
    rest = jnp.zeros((1, 128 - HEADS), F32)
    lines = [jnp.concatenate([ref[...], rest], 1) for ref in (bias, rate, skip)]
    vec_ref[...] = jnp.concatenate([*lines, jnp.zeros((5, 128), F32)], 0)
    for g in range(GROUPS):
        skip_ref[:, g * 128 : (g + 1) * 128] = jnp.broadcast_to(widen(lines[2], g), (8, 128))


def small_scratch():
    return [
        pltpu.VMEM((ROWS, 128), F32),
        pltpu.VMEM((8, 2 * ROWS), F32),
        pltpu.VMEM((8, 128), F32),
        pltpu.VMEM((8, INNER), F32),
    ]


def spread_dt(dt_w, wide_ref):
    wide_ref[16:, :] = jnp.zeros((112, MODEL), BF16)
    rows = jnp.concatenate([dt_w[...].astype(F32), jnp.zeros((16 - HEADS, MODEL), F32)], 0)
    wide_ref[:16, :] = rows.astype(BF16)


def turn_pairs(v, cosine, sine, direction):
    return v * cosine + pltpu.roll(v, HEAD_DIM // 2, 1) * (sine * direction)


def transpose_to(out_ref, ref):
    for k in range(ref.shape[1] // 256):
        out_ref[k * 256 : (k + 1) * 256, :] = jnp.transpose(ref[:, k * 256 : (k + 1) * 256])


def feed_forward_kernel(
    loads, gated_ref, att_ref, tok_ref, cot_ref, gain_ref, out_w, attn_w, gate_w, up_w, down_w,
    hid_ref, ft_ref, dgate_ref, dup_ref, hidden_ref, ffn_ref, ghid_ref, mt_ref, gain_out,
    gg_ref, do_ref, ftz_ref, outz_ref,
    x_ref, sum_ref, back_ref, back_sum, normed, mix_ref, outs_ref, left_sem, outz_sem, *sums,
):
    loads.start()
    n_sum = len(HeadSum.scratch())
    first = HeadSum(x_ref, sum_ref, *sums[:3], sums[3:n_sum])
    second = HeadSum(back_ref, back_sum, *sums[n_sum : n_sum + 3], sums[n_sum + 3 :])
    barrier = pltpu.get_barrier_semaphore()
    other_z = {"zl": 1 - lax.axis_index("zl")}
    signal(barrier, first.sibling)
    signal(barrier, first.opposite)
    signal(barrier, other_z)
    pl.semaphore_wait(barrier, 3)
    left = Left(ft_ref, ftz_ref, left_sem)
    outs = remote(outs_ref, outz_ref, outz_sem.at[0], outz_sem.at[1], other_z)
    halves = [(slice(g * 128, (g + 1) * 128), (2 * g, 2 * g + 1)) for g in range(2)]
    loads.need(out_w, attn_w)
    for rows, chunks in halves:
        x_ref[rows, :] = (
            dot(gated_ref[rows, :], out_w[...]) + dot(att_ref[rows, :], attn_w[...])
        ).astype(BF16)
        first.start(chunks)
    first.across()

    wide = 256
    loads.need(cot_ref, down_w)
    for k in range(0, hidden_ref.shape[1], wide):
        ghid_ref[:, k : k + wide] = dot(cot_ref[...], down_w[k : k + wide, :], 1, 1)
    loads.need(tok_ref, gate_w, up_w)

    def norm(half, chunks):
        first.join(chunks)
        first.finish(chunks)
        for r in range(half.start, half.stop, 32):
            rows = slice(r, r + 32)
            x = tok_ref[rows, :].astype(F32) + sum_ref[rows, :].astype(F32)
            hid_ref[rows, :] = x
            scale = lax.rsqrt(jnp.mean(x * x, 1, keepdims=True) + EPSILON)
            normed[rows, :] = (x * scale * gain_ref[0:1, :]).astype(BF16)

    def feed(rows, chunks):
        for k in range(0, hidden_ref.shape[1], wide):
            cols = slice(k, k + wide)
            n = normed[rows, :]
            gate, up = dot(n, gate_w[:, cols]), dot(n, up_w[:, cols])
            grad = ghid_ref[rows, cols]
            sig = sigmoid(gate)
            act = gate * sig
            hidden_ref[rows, cols] = (act * up).astype(BF16)
            dgate_ref[rows, cols] = (grad * up * sig * (1.0 + gate * (1.0 - sig))).astype(BF16)
            dup_ref[rows, cols] = (grad * act).astype(BF16)
        back_ref[rows, :] = (
            dot(dgate_ref[rows, :], gate_w[...], 1, 1) + dot(dup_ref[rows, :], up_w[...], 1, 1)
        ).astype(BF16)
        second.start(chunks)

    def norm_back(half, chunks):
        second.join(chunks)
        second.finish(chunks)
        for r in range(half.start, half.stop, 32):
            rows = slice(r, r + 32)
            x = hid_ref[rows, :]
            scale = lax.rsqrt(jnp.mean(x * x, 1, keepdims=True) + EPSILON)
            n = x * scale
            grad = back_sum[rows, :].astype(F32)
            scaled = grad * gain_ref[0:1, :]
            along = jnp.mean(n * scaled, 1, keepdims=True)
            total = cot_ref[rows, :].astype(F32) + scale * (scaled - n * along)
            ghid_ref[rows, :] = total
            mix_ref[rows, :] = total.astype(BF16)
            gains = jnp.sum(grad * n, 0, keepdims=True)
            gain_out[0:1, :] = gains if r == 0 else gain_out[0:1, :] + gains

    (rows_a, chunks_a), (rows_b, chunks_b) = halves
    norm(rows_a, chunks_a)
    feed(rows_a, chunks_a)
    norm(rows_b, chunks_b)
    second.across(chunks_a)
    transpose_to(ft_ref, normed)
    left.start()
    loads.put(hid_ref, ft_ref)
    feed(rows_b, chunks_b)
    loads.put(hidden_ref, dgate_ref, dup_ref)
    for k in range(3):
        outs_ref[k] = gated_ref[:, k * WIDE : (k + 1) * WIDE]
    outs_ref[3] = att_ref[...]
    second.across(chunks_b)
    outs.start()
    left.pass_on()
    ffn_ref[...] = dot(hidden_ref[...], down_w[...]).astype(BF16)
    loads.put(ffn_ref)
    norm_back(rows_a, chunks_a)
    norm_back(rows_b, chunks_b)
    loads.put(ghid_ref)
    grad_att = dot(mix_ref[...], attn_w[...], 1, 1).astype(BF16)
    for h in range(2):
        do_ref[h * ROWS : (h + 1) * ROWS, :] = grad_att[:, h * HEAD_DIM : (h + 1) * HEAD_DIM]
    gg_ref[...] = dot(mix_ref[...], out_w[...], 1, 1)
    loads.put(gg_ref, do_ref)
    transpose_to(mt_ref, mix_ref)
    loads.put(mt_ref)
    first.close()
    second.close()
    left.finish()
    left.close()
    outs.wait()


def feed_forward(*args):
    v = pltpu.VMEM
    ff = args[7].shape[1]
    return call(
        feed_forward_kernel, "feed_forward", args, (2, 3, 5, 6, 7, 8, 9),
        [
            ((ROWS, MODEL), F32),
            ((MODEL, ROWS), BF16),
            ((ROWS, ff), BF16),
            ((ROWS, ff), BF16),
            ((ROWS, ff), BF16),
            ((ROWS, MODEL), BF16),
            ((ROWS, MODEL), F32),
            ((MODEL, ROWS), BF16),
            ((8, MODEL), F32),
            ((ROWS, INNER), F32),
            ((2 * ROWS, HEAD_DIM), BF16),
            ((OWN, ROWS), BF16),
            ((4, ROWS, WIDE), BF16),
        ],
        [
            *[v((ROWS, MODEL), BF16)] * 6,
            v((4, ROWS, WIDE), BF16),
            pltpu.SemaphoreType.DMA((4,)),
            pltpu.SemaphoreType.DMA((2,)),
            *HeadSum.scratch(),
            *HeadSum.scratch(),
        ],
        4,
    )


EARLY = 6


def mixer_forward_kernel(
    loads, tok_ref, cot_ref, gain_ref, q_w, kv_w, x_w, bc_w, dt_w, z_w, cos_ref, sin_ref, seg,
    xtaps_ref, bctaps_ref, bias, rate, skip,
    nt_ref, ct_ref, q_ref, x_ref, bc_ref, dt_ref, z_ref,
    att_ref, lse_ref, kv_ref, edge_out, gated_ref, core_ref, xact_ref, bcact_ref, state_ref,
    ntz_ref, ctz_ref, attlow_ref,
    m_ref, l_ref, acc_ref, xext, bcext, segx, local, msg, got, back, result, bias_ref, cb_ref,
    cumt_ref, normed, own_ref, edge_ref, kv_cols, seg_ref, segrow_ref, vec_ref, skip_ref, dt_wide,
    send_sem, recv_sem, sib_send, sib_recv, edge_sem, scan_send, scan_recv, left_sem, kv_sem,
):
    me, c, zl = block_index(), lax.axis_index("c"), lax.axis_index("zl")
    at = me % PLANE
    sibling = {"c": 1 - c}
    kv_at = (c * KVHEADS + lax.axis_index("zh")) * HEAD_DIM
    kv_copy = pltpu.make_async_copy(
        kv_w.at[:, pl.ds(pl.multiple_of(kv_at, HEAD_DIM), HEAD_DIM)], kv_cols, kv_sem
    )
    loads.start()
    kv_copy.start()
    barrier = pltpu.get_barrier_semaphore()
    over(1, BLOCKS, lambda o: signal(barrier, block_at((me + o) % BLOCKS)))
    signal(barrier, sibling)

    spread_small(seg, bias, rate, skip, seg_ref, segrow_ref, vec_ref, skip_ref)
    loads.need(tok_ref)
    for r in range(0, ROWS, 32):
        rows = slice(r, r + 32)
        v = tok_ref[rows, :].astype(F32)
        scale = lax.rsqrt(jnp.mean(v * v, 1, keepdims=True) + EPSILON)
        normed[rows, :] = (v * scale * gain_ref[0:1, :]).astype(BF16)
    n = normed[...]
    loads.need(x_w, bc_w)
    x_ref[...] = dot(n, x_w[...]).astype(BF16)
    bc_ref[...] = dot(n, bc_w[...]).astype(BF16)
    edge_ref[:, :INNER] = x_ref[ROWS - 16 :, :]
    edge_ref[:, INNER : INNER + BC] = bc_ref[ROWS - 16 :, :]
    edge_ref[:, INNER + BC :] = seg_ref[ROWS - 16 :, :].astype(BF16)
    pl.semaphore_wait(barrier, BLOCKS)

    def block_copy(src, j, send, where):
        return remote(src, kv_ref.at[c, j], send_sem.at[send], recv_sem.at[j], where)

    def arrival(j):
        return block_copy(own_ref, j, 0, sibling)

    to_sibling = lambda j, src: remote(
        src, kv_ref.at[c, j], sib_send.at[j], sib_recv.at[j], sibling
    )
    from_sibling = lambda j: remote(
        kv_ref.at[1 - c, j], kv_ref.at[1 - c, j], sib_send.at[j], sib_recv.at[j], sibling
    )
    across = block_copy(own_ref, me, PLANE - 1, {"zl": 1 - zl})

    def own_copy(k, wait):
        d, where = plane_peer(k, 1, 8)

        @pl.when(d > at)
        def _():
            copy = block_copy(own_ref, me, k, where)
            copy.wait_send() if wait else copy.start()

    def relay_copy(k, wait):
        copy = block_copy(kv_ref.at[c, at], at, PLANE + k, plane_peer(k, 1, 8)[1])
        copy.wait_send() if wait else copy.start()

    edge_copy = remote(
        edge_ref, edge_out, edge_sem.at[0], edge_sem.at[1], block_at((me + 1) % BLOCKS)
    )
    states = Scan(False, me, msg, got, back, result, scan_send, scan_recv)

    @pl.when(me < BLOCKS - 1)
    def _():
        edge_copy.start()

    cosine, sine = cos_ref[...], sin_ref[...]
    kv_copy.wait()
    raw = dot(n, kv_cols[...])
    turned = turn_pairs(raw, cosine, sine, 1.0)
    own_ref[:ROWS, :] = jnp.where(c == 0, turned, raw).astype(BF16)
    rows = [segrow_ref[0:1, :HEAD_DIM], segrow_ref[0:1, HEAD_DIM : 2 * HEAD_DIM]]
    own_ref[ROWS:, :] = jnp.concatenate([*rows, jnp.zeros((14, HEAD_DIM), F32)], 0).astype(BF16)

    @pl.when(zl == 0)
    def _():
        across.start()

    to_sibling(me, own_ref).start()
    over(0, EARLY, lambda k: own_copy(k, False))
    lefts = [Left(ct_ref, ctz_ref, left_sem.at[0]), Left(nt_ref, ntz_ref, left_sem.at[1])]

    kv_ref[c, me] = own_ref[...]
    spread_dt(dt_w, dt_wide)
    dt_ref[...] = dot(n, dt_wide[...], 1, 1)
    xext[8:, :] = x_ref[...].astype(F32)
    bcext[8:, :] = bc_ref[...].astype(F32)
    segx[8:, :] = seg_ref[...]
    lower = triangle()
    bias_ref[...] = mixing_bias(seg_ref, segrow_ref)

    @pl.when(me > 0)
    def _():
        edge_copy.wait_recv()

    @pl.when(me == 0)
    def _():
        edge_out[...] = jnp.zeros_like(edge_out)

    edge = edge_out[...].astype(F32)[8:]
    xext[:8, :] = edge[:, :INNER]
    bcext[:8, :] = edge[:, INNER : INNER + BC]
    segx[:8, :] = edge[:, INNER + BC :]

    def activate(ext, taps, out):
        def group(g):
            pre, _ = conv_group(ext, segx, seg_ref, taps, lane_block(g))
            out[:, lane_block(g)] = (pre * sigmoid(pre)).astype(BF16)

        over(0, out.shape[1] // 128, group)

    activate(bcext, bctaps_ref, bcact_ref)
    activate(xext, xtaps_ref, xact_ref)

    _, step, total, carry, entry, through = decays(dt_ref, vec_ref, seg_ref, segx, lower)
    cumt_ref[...] = jnp.transpose(total)
    weight = step * carry
    b_low, c_low = bcact_ref[:, :STATE], bcact_ref[:, STATE:]
    for g in range(GROUPS):
        moved = xact_ref[:, g * 128 : (g + 1) * 128].astype(F32) * widen(weight, g)
        local[g * 128 : (g + 1) * 128, :] = dot(moved.astype(BF16), b_low, 0, 0)
    scan_message(msg, local, through)
    states.start()
    over(EARLY, PLANE - 1, lambda k: own_copy(k, False))

    @pl.when(zl == 1)
    def _():
        arrival(at).wait_recv()
        to_sibling(at, kv_ref.at[c, at]).start()
        over(0, PLANE - 1, lambda k: relay_copy(k, False))

    cb_ref[...] = dot(c_low, b_low, 1, 1)
    low_lane = lax.broadcasted_iota(jnp.int32, (ROWS, 128), 1) < SSM_DIM
    for g in range(GROUPS):
        cols = slice(g * 128, (g + 1) * 128)
        u = (xact_ref[:, cols].astype(F32) * widen(step, g)).astype(BF16)
        made = []
        for h in (2 * g, 2 * g + 1):
            gap = total[:, h : h + 1] - cumt_ref[h : h + 1, :] + bias_ref[...]
            made.append(dot((jnp.exp2(gap) * cb_ref[...]).astype(BF16), u))
        core_ref[:, cols] = jnp.where(low_lane, made[0], made[1])

    loads.need(q_w)
    for h in range(2):
        raw = dot(n, q_w[:, h * HEAD_DIM : (h + 1) * HEAD_DIM])
        q_ref[h * ROWS : (h + 1) * ROWS, :] = turn_pairs(raw, cosine, sine, 1.0).astype(BF16)
    scale = LOG2E * HEAD_DIM**-0.5
    queries = q_ref[...]
    qseg = segrow_ref[0:1, :]

    def scores_of(j):
        s = dot(kv_ref[0, j, :ROWS], queries, 1, 1) * scale
        return jnp.where(key_segments(kv_ref[0, j, ROWS:]) == qseg, s, MASKED)

    from_sibling(me).wait_recv()
    s = causal_mask(scores_of(me))
    m = jnp.max(s, 0, keepdims=True)
    p = jnp.exp2(s - m)
    m_ref[...] = m
    l_ref[...] = jnp.sum(p, 0, keepdims=True)
    acc_ref[...] = dot(kv_ref[1, me, :ROWS], p.astype(BF16), 0, 0)

    transpose_to(nt_ref, normed)
    loads.need(cot_ref)
    transpose_to(ct_ref, cot_ref)
    loads.put(nt_ref, ct_ref, q_ref, x_ref, bc_ref, dt_ref, bcact_ref, xact_ref)
    states.turn()
    for left in lefts:
        left.start()
    loads.need(z_w)
    z_ref[...] = dot(n, z_w[...])
    loads.put(z_ref)

    def forward(k):
        q, _ = plane_peer(k, -1, 8)

        def one(j):
            arrival(j).wait_recv()
            to_sibling(j, kv_ref.at[c, j]).start()

        pl.when(q < at)(lambda: one(zl * PLANE + q))
        pl.when(zl == 1)(lambda: one(q))

    def attend(*blocks):
        scores = []
        for j in blocks:
            from_sibling(j).wait_recv()
            scores.append(scores_of(j))
        m_old = m_ref[...]
        m = m_old
        for s in scores:
            m = jnp.maximum(m, jnp.max(s, 0, keepdims=True))
        alpha = jnp.exp2(m_old - m)
        total, acc = l_ref[...] * alpha, acc_ref[...] * alpha
        for j, s in zip(blocks, scores):
            p = jnp.exp2(s - m)
            total += jnp.sum(p, 0, keepdims=True)
            acc += dot(kv_ref[1, j, :ROWS], p.astype(BF16), 0, 0)
        m_ref[...], l_ref[...], acc_ref[...] = m, total, acc

    forward(0)

    @pl.when(zl == 1)
    def _():
        attend(at)

    def step_over(k):
        @pl.when(k + 1 < PLANE - 1)
        def _():
            forward(k + 1)

        q, _ = plane_peer(k, -1, 8)
        pl.when((q < at) & (zl == 1))(lambda: attend(PLANE + q, q))
        pl.when((q < at) & (zl == 0))(lambda: attend(q))
        pl.when((q > at) & (zl == 1))(lambda: attend(q))

    over(0, PLANE - 1, step_over)
    for left in lefts:
        left.pass_on()
    attended = jnp.transpose(acc_ref[...] / l_ref[...])
    att_ref[...] = attended
    for h in range(2):
        attlow_ref[:, h * HEAD_DIM : (h + 1) * HEAD_DIM] = (
            attended[h * ROWS : (h + 1) * ROWS].astype(BF16)
        )
    lse_ref[...] = jnp.broadcast_to(m_ref[...] + jnp.log2(l_ref[...]), lse_ref.shape)

    loads.put(att_ref, kv_ref)
    states.finish(state_ref)
    loads.put(state_ref)
    for g in range(GROUPS):
        cols = slice(g * 128, (g + 1) * 128)
        outer = dot(c_low, state_ref[cols, :].astype(BF16), 1, 1) * widen(entry, g)
        core = core_ref[:, cols] + outer
        core_ref[:, cols] = core
        out = core + skip_ref[0:1, cols] * xact_ref[:, cols].astype(F32)
        z = z_ref[:, cols]
        gated_ref[:, cols] = (out * z * sigmoid(z)).astype(BF16)

    loads.put(gated_ref, core_ref)
    states.close()
    for left in lefts:
        left.finish()
        left.close()
    to_sibling(me, own_ref).wait_send()
    over(0, PLANE - 1, lambda k: own_copy(k, True))

    @pl.when(zl == 0)
    def _():
        across.wait_send()

    @pl.when(zl == 1)
    def _():
        over(0, PLANE - 1, lambda k: relay_copy(k, True))
        over(0, PLANE, lambda j: to_sibling(j, own_ref).wait_send())

    over(0, at, lambda q: to_sibling(zl * PLANE + q, own_ref).wait_send())

    @pl.when(me < BLOCKS - 1)
    def _():
        edge_copy.wait_send()


def mixer_forward(*args):
    wide = 2 * ROWS
    dma = pltpu.SemaphoreType.DMA
    return call(
        mixer_forward_kernel, "mixer_forward", args, (0, 5, 6, 3, 8, 1),
        [
            ((MODEL, ROWS), BF16),
            ((MODEL, ROWS), BF16),
            ((wide, HEAD_DIM), BF16),
            ((ROWS, INNER), BF16),
            ((ROWS, BC), BF16),
            ((ROWS, 128), F32),
            ((ROWS, INNER), F32),
            ((wide, HEAD_DIM), F32),
            ((8, wide), F32),
            ((2, BLOCKS, ROWS + 16, HEAD_DIM), BF16),
            ((16, EDGE_WIDE), BF16),
            ((ROWS, INNER), BF16),
            ((ROWS, INNER), F32),
            ((ROWS, INNER), BF16),
            ((ROWS, BC), BF16),
            ((INNER, STATE), F32),
            ((OWN, ROWS), BF16),
            ((OWN, ROWS), BF16),
            ((ROWS, 2 * HEAD_DIM), BF16),
        ],
        [
            pltpu.VMEM((1, wide), F32),
            pltpu.VMEM((1, wide), F32),
            pltpu.VMEM((HEAD_DIM, wide), F32),
            pltpu.VMEM((ROWS + 8, INNER), F32),
            pltpu.VMEM((ROWS + 8, BC), F32),
            pltpu.VMEM((ROWS + 8, 128), F32),
            pltpu.VMEM((INNER, STATE), F32),
            *[pltpu.VMEM((BLOCKS, SCAN_ROWS + 8, STATE), BF16)] * 4,
            pltpu.VMEM((ROWS, ROWS), F32),
            pltpu.VMEM((ROWS, ROWS), F32),
            pltpu.VMEM((128, ROWS), F32),
            pltpu.VMEM((ROWS, MODEL), BF16),
            pltpu.VMEM((ROWS + 16, HEAD_DIM), BF16),
            pltpu.VMEM((16, EDGE_WIDE), BF16),
            pltpu.VMEM((MODEL, HEAD_DIM), BF16),
            *small_scratch(),
            pltpu.VMEM((128, MODEL), BF16),
            *[dma((BLOCKS,))] * 4,
            dma((2,)),
            dma((2, BLOCKS)),
            dma((2, BLOCKS)),
            dma((2, 4)),
            dma,
        ],
        1,
        (4,),
    )


def mixer_backward_kernel(
    loads, q_ref, do_ref, att_ref, lse_ref, seg, kv_ref, gg_ref, z_ref, core_ref, xact_ref,
    bcact_ref, x_ref, bcown_ref, edge_in, dt_ref, state_ref, bias, xtaps_ref, bctaps_ref,
    rate, skip, dgate_ref, dup_ref, hidden_ref, ft_ref, ct_ref, ctz_ref, mt_ref, cos_ref,
    sin_ref, ftz_ref,
    dqraw_ref, misc_ref, dz_ref, dx_ref, ddt_ref, dxtaps_ref, dbctaps_ref, dvec_ref,
    w_ref, mtz_ref,
    dkv_ref, dqt_ref, mine, theirs, sib, kvgot, relay_ref, total_ref, xext, bcext, segx, local, msg, got, back, result,
    bias_ref, cb_ref, cumt_ref, g_ref, du_ref, dbc_all, shares, share_got, edge_ref,
    edge_out, enter_ref, gext, dcum_ref, ddtx_ref,
    send_sem, recv_sem, sib_send, sib_recv, edge_sem, scan_send, scan_recv, share_send, share_recv,
    left_sem, owntaps_ref, seg_ref, segrow_ref, vec_ref, skip_ref, *reduce,
):
    me, c, zh, zl = block_index(), *(lax.axis_index(a) for a in ("c", "zh", "zl"))
    head_at = zh * 2 + c
    sibling = {"c": 1 - c}
    at_head = lambda d: {"zh": d // 2, "c": d % 2}
    loads.start()
    barrier = pltpu.get_barrier_semaphore()
    over(1, BLOCKS, lambda o: signal(barrier, block_at((me + o) % BLOCKS)))
    for o in range(1, 4):
        signal(barrier, at_head((head_at + o) % 4))
    pl.semaphore_wait(barrier, BLOCKS + 2)

    at = me % PLANE
    to_sibling = lambda j: remote(
        theirs.at[j], sib.at[j], sib_send.at[j], sib_recv.at[j], sibling
    )

    def to_owner(k, kind):
        q, where = plane_peer(k, -1)
        j = q if kind else zl * PLANE + q
        return remote(
            mine.at[j], kvgot.at[kind, at], send_sem.at[kind, k], recv_sem.at[kind, at], where
        )

    def from_plane(kind, q):
        return remote(
            kvgot.at[kind, q], kvgot.at[kind, q], send_sem.at[kind, 0], recv_sem.at[kind, q],
            sibling,
        )

    across = remote(
        relay_ref, kvgot.at[1, 0], send_sem.at[0, PLANE - 1], recv_sem.at[1, 0], {"zl": 1 - zl}
    )
    states = Scan(True, me, msg, got, back, result, scan_send, scan_recv)
    rs = Reduce(
        [(ct_ref, ctz_ref, 0), (ft_ref, ftz_ref, 4)], 12, 12, *reduce[:7], w_ref, reduce[7:]
    )
    left = Left(mt_ref, mtz_ref, left_sem)
    loads.need(hidden_ref)
    rs.fill([hidden_ref])
    rs.start()
    loads.need(dgate_ref, dup_ref)
    rs.fill([dgate_ref, dup_ref], 4)
    done = 0

    def reduce_some(n):
        nonlocal done
        over(done, done + n, rs.step)
        done += n


    spread_small(seg, bias, rate, skip, seg_ref, segrow_ref, vec_ref, skip_ref)
    lower = triangle()
    edge = edge_in[...].astype(F32)[8:]
    xext[:8, :] = edge[:, :INNER]
    segx[:8, :] = edge[:, INNER + BC :]
    xext[8:, :] = x_ref[...].astype(F32)
    segx[8:, :] = seg_ref[...]
    bc_cols = lane_block(head_at)
    edge_cols = lane_block(head_at + INNER // 128)
    bcext[:8, :] = edge_in[:, edge_cols].astype(F32)[8:]
    bcext[8:, :] = bcown_ref[:, bc_cols].astype(F32)
    owntaps_ref[...] = bctaps_ref[:, bc_cols]
    bias_ref[...] = mixing_bias(seg_ref, segrow_ref)
    pre_dt, step, total, carry, entry, through = decays(dt_ref, vec_ref, seg_ref, segx, lower)
    cumt_ref[...] = jnp.transpose(total)
    b_low, c_low = bcact_ref[:, :STATE], bcact_ref[:, STATE:]
    for g in range(GROUPS):
        cols = slice(g * 128, (g + 1) * 128)
        z = z_ref[:, cols]
        grad = gg_ref[:, cols] * z * sigmoid(z)
        g_ref[:, cols] = grad
        entered = (grad * widen(entry, g)).astype(BF16)
        du_ref[:, cols] = entered.astype(F32)
        local[cols, :] = dot(entered, c_low, 0, 0)
    scan_message(msg, local, through)
    states.start()
    loads.need(ct_ref, ctz_ref, ft_ref, ftz_ref)
    reduce_some(1)

    dcum = jnp.zeros((ROWS, 128), F32)
    dskip = jnp.zeros((8, 128), F32)
    dc = jnp.zeros((ROWS, STATE), F32)
    for g in range(GROUPS):
        cols = slice(g * 128, (g + 1) * 128)
        z, core, x = z_ref[:, cols], core_ref[:, cols], xact_ref[:, cols].astype(F32)
        sig = sigmoid(z)
        out = core + skip_ref[0:1, cols] * x
        dz_ref[:, cols] = (gg_ref[:, cols] * out * sig * (1.0 + z * (1.0 - sig))).astype(BF16)
        grad = g_ref[:, cols]
        dcum += per_head(grad * core, g)
        dskip += per_head(jnp.broadcast_to(jnp.sum(grad * x, 0, keepdims=True), (8, 128)), g)
        dc += dot(du_ref[:, cols].astype(BF16), state_ref[cols, :].astype(BF16))
    dbc_all[:, STATE:] = dc
    loads.put(dz_ref)
    reduce_some(1)

    cb_ref[...] = dot(c_low, b_low, 1, 1)
    low_lane = lax.broadcasted_iota(jnp.int32, (ROWS, 128), 1) < SSM_DIM
    dcb = jnp.zeros((ROWS, ROWS), F32)
    for g in range(GROUPS):
        cols = slice(g * 128, (g + 1) * 128)
        u = xact_ref[:, cols].astype(F32) * widen(step, g)
        u_low, grad = u.astype(BF16), g_ref[:, cols]
        grad_low = grad.astype(BF16)
        made = []
        for i in range(2):
            h = 2 * g + i
            decay = jnp.exp2(total[:, h : h + 1] - cumt_ref[h : h + 1, :] + bias_ref[...])
            mixing = (decay * cb_ref[...]).astype(BF16)
            made.append(dot(mixing, grad_low, 0, 0))
            half = jnp.where(low_lane if i == 0 else ~low_lane, grad, 0.0).astype(BF16)
            dcb += decay * dot(half, u_low, 1, 1)
        du = jnp.where(low_lane, made[0], made[1])
        du_ref[:, cols] = du
        dcum -= per_head(u * du, g)
    dcum_ref[...] = dcum
    reduce_some(1)
    dcb_low = dcb.astype(BF16)
    dbc_all[:, :STATE] = dot(dcb_low, c_low, 0, 0)
    dbc_all[:, STATE:] += dot(dcb_low, b_low)

    loads.need(q_ref, do_ref, att_ref, kv_ref)
    scale = LOG2E * HEAD_DIM**-0.5
    queries, grads = q_ref[...], do_ref[...]
    lse, qseg = lse_ref[0:1, :], segrow_ref[0:1, :]
    high, low = two_parts(grads.astype(F32) * att_ref[...])
    ones = jnp.ones((8, HEAD_DIM), BF16)
    delta = (dot(ones, high, 1, 1) + dot(ones, low, 1, 1))[0:1, :]

    def block(*blocks, own=False):
        change, results = None, []
        for t in blocks:
            keys = kv_ref[0, t, :ROWS]
            s = dot(keys, queries, 1, 1) * scale
            s = jnp.where(key_segments(kv_ref[0, t, ROWS:]) == qseg, s, MASKED)
            if own:
                s = causal_mask(s)
            p = jnp.exp2(s - lse)
            ds = (p * (dot(kv_ref[1, t, :ROWS], grads, 1, 1) - delta)).astype(BF16)
            dk = dot(ds, queries)
            dv = dot(p.astype(BF16), grads)
            part = dot(keys, ds, 0, 0)
            change = part if change is None else change + part
            results.append((jnp.where(c == 0, dk, dv), jnp.where(c == 0, dv, dk)))
        dqt_ref[...] = change if own else dqt_ref[...] + change
        for t, (kept, given) in zip(blocks, results):
            mine[t] = kept.astype(BF16)
            theirs[t] = given.astype(BF16)
            to_sibling(t).start()

    def pair(t):
        to_sibling(t).wait_recv()
        return mine[t].astype(F32) + sib[t].astype(F32)

    block(me, own=True)
    reduce_some(1)
    states.turn()
    loads.need(mt_ref)
    left.start()
    before = done

    @pl.when(zl == 1)
    def _():
        block(at)

    def give(k):
        q, _ = plane_peer(k, -1)

        @pl.when(q < at)
        def _():
            j = zl * PLANE + q
            mine[j] = pair(j).astype(BF16)
            to_owner(k, 0).start()

        @pl.when(zl == 1)
        def _():
            mine[q] = pair(q).astype(BF16)
            to_owner(k, 1).start()

    def step_over(k):
        q, _ = plane_peer(k, -1)
        pl.when((q < at) & (zl == 1))(lambda: block(PLANE + q, q))
        pl.when((q < at) & (zl == 0))(lambda: block(q))
        pl.when((q > at) & (zl == 1))(lambda: block(q))

        @pl.when(k >= 1)
        def _():
            give(k - 1)

        @pl.when(k % 2 == 1)
        def _():
            rs.step(before + k // 2)

    over(0, PLANE - 1, step_over)
    give(PLANE - 2)
    done += (PLANE - 1) // 2
    reduce_some(1)
    left.pass_on()
    dkv_ref[...] = pair(me)

    @pl.when(zl == 1)
    def _():
        total_ref[...] = pair(at)

    score_scale = HEAD_DIM**-0.5
    dq = jnp.transpose(dqt_ref[...]) * score_scale
    cosine, sine = cos_ref[...], sin_ref[...]
    for h in range(2):
        raw = turn_pairs(dq[h * ROWS : (h + 1) * ROWS], cosine, sine, -1.0)
        dqraw_ref[:, h * HEAD_DIM : (h + 1) * HEAD_DIM] = raw.astype(BF16)

    states.finish(enter_ref)
    dcum = dcum_ref[...]
    dstep = jnp.zeros((ROWS, 128), F32)
    dlast = jnp.zeros((8, 128), F32)
    db = jnp.zeros((ROWS, STATE), F32)
    for g in range(GROUPS):
        cols = slice(g * 128, (g + 1) * 128)
        entering = enter_ref[cols, :]
        entering_low = entering.astype(BF16)
        x = xact_ref[:, cols].astype(F32)
        steps, carries = widen(step, g), widen(carry, g)
        v = x * steps * carries
        dv = dot(b_low, entering_low, 1, 1)
        db += dot(v.astype(BF16), entering_low)
        dcarry = per_head(v * dv, g)
        dcum -= dcarry
        dlast += jnp.broadcast_to(jnp.sum(dcarry, 0, keepdims=True), (8, 128))
        du = du_ref[:, cols] + carries * dv
        dstep += per_head(x * du, g)
        pieces = jnp.sum(entering * state_ref[cols, :], 1, keepdims=True)
        both = jnp.sum(jnp.broadcast_to(pieces, (128, 128)) * head_of_lane_f32(g), 0, keepdims=True)
        dlast += through * both
        g_ref[:, cols] = steps * du + skip_ref[0:1, cols] * g_ref[:, cols]
    dbc_all[:, :STATE] += db
    last_row = lax.broadcasted_iota(jnp.int32, (ROWS, 128), 0) == ROWS - 1
    dcum += jnp.where(last_row, dlast[0:1, :], 0.0)
    da = running(dcum, lower, 0)
    drate = -jnp.sum(step * da, 0, keepdims=True)
    ddt = (dstep - vec_ref[1:2, :] * da) * sigmoid(pre_dt)
    ddt_ref[...] = ddt.astype(BF16)
    dbias = jnp.sum(ddt, 0, keepdims=True)
    dvec_ref[...] = jnp.concatenate([dbias, drate, dskip[0:1, :], jnp.zeros((5, 128), F32)], 0)

    reduce_some(1)

    for d in range(4):
        shares[d] = dbc_all[:, d * 128 : (d + 1) * 128].astype(BF16)
    share = lambda o: remote(
        shares.at[(head_at + o) % 4], share_got.at[o], share_send.at[o], share_recv.at[o],
        at_head((head_at + o) % 4),
    )
    for o in range(1, 4):
        share(o).start()

    def conv_back(ext, taps, grad, cols, out_taps, out_grad):
        pre, inputs = conv_group(ext, segx, seg_ref, taps, cols)
        sig = sigmoid(pre)
        dpre = grad * sig * (1.0 + pre * (1.0 - sig))
        gext[...] = jnp.zeros_like(gext)
        rows = []
        for k in range(CONV):
            rows.append(jnp.sum(dpre * inputs[k], 0, keepdims=True))
            same = segx[pl.ds(5 + k, ROWS), :] == seg_ref[...]
            gext[pl.ds(5 + k, ROWS), :] += jnp.where(same, taps[k : k + 1, cols] * dpre, 0.0)
        out_taps[:, cols] = jnp.concatenate([*rows, jnp.zeros((4, 128), F32)], 0)
        out_grad[...] = gext[...]

    def x_group(g):
        cols = lane_block(g)
        conv_back(xext, xtaps_ref, g_ref[:, cols], cols, dxtaps_ref, ddtx_ref)
        edge_ref[:, cols] = ddtx_ref[:8, :]
        g_ref[:, cols] = ddtx_ref[8:, :]

    over(0, GROUPS, x_group)
    reduce_some(1)
    grad_bc = shares[head_at].astype(F32)
    for o in range(1, 4):
        share(o).wait_recv()
        grad_bc += share_got[o].astype(F32)
    conv_back(bcext, owntaps_ref, grad_bc, slice(0, 128), dbctaps_ref, ddtx_ref)
    edge_ref[:, INNER:] = ddtx_ref[:8, :]
    edge_copy = remote(
        edge_ref, edge_out, edge_sem.at[0], edge_sem.at[1], block_at((me + BLOCKS - 1) % BLOCKS)
    )

    @pl.when(me > 0)
    def _():
        edge_copy.start()

    reduce_some(1)

    def collect(q):
        @pl.when((zl == 1) & (q != at))
        def _():
            from_plane(1, q).wait_recv()
            total_ref[...] += kvgot[1, q].astype(F32)

    over(0, PLANE, collect)

    @pl.when(zl == 1)
    def _():
        relay_ref[...] = total_ref[...].astype(BF16)
        across.start()

    reduce_some(1)

    def collect_own(q):
        from_plane(0, q).wait_recv()
        dkv_ref[...] += kvgot[0, q].astype(F32)

    over(at + 1, PLANE, collect_own)

    @pl.when(zl == 0)
    def _():
        from_plane(1, 0).wait_recv()
        dkv_ref[...] += kvgot[1, 0].astype(F32)

    @pl.when(me < BLOCKS - 1)
    def _():
        edge_copy.wait_recv()

    @pl.when(me == BLOCKS - 1)
    def _():
        edge_out[...] = jnp.zeros_like(edge_out)

    tail = pl.ds(ROWS - 8, 8)
    g_ref[tail, :] += edge_out[:, :INNER]
    ddtx_ref[pl.ds(ROWS, 8), :] += edge_out[:, INNER:]
    dx_ref[...] = g_ref[...].astype(BF16)
    misc_ref[:, :128] = ddtx_ref[8:, :].astype(BF16)
    dkv = dkv_ref[...]
    turned = turn_pairs(dkv * score_scale, cosine, sine, -1.0)
    misc_ref[:, 128:] = jnp.where(c == 0, turned, dkv).astype(BF16)

    reduce_some(rs.steps - done)

    @pl.when(me > 0)
    def _():
        edge_copy.wait_send()

    states.close()
    rs.close()
    left.finish()
    left.close()
    for o in range(1, 4):
        share(o).wait_send()
    to_sibling(me).wait_send()

    def given(k):
        q, _ = plane_peer(k, -1)

        @pl.when(q < at)
        def _():
            to_sibling(zl * PLANE + q).wait_send()
            to_owner(k, 0).wait_send()

        @pl.when(zl == 1)
        def _():
            to_sibling(q).wait_send()
            to_owner(k, 1).wait_send()

    over(0, PLANE - 1, given)

    @pl.when(zl == 1)
    def _():
        to_sibling(at).wait_send()
        across.wait_send()


def head_of_lane_f32(g):
    row = lax.broadcasted_iota(jnp.int32, (128, 128), 0)
    lane = lax.broadcasted_iota(jnp.int32, (128, 128), 1)
    return (lane == 2 * g + (row >= SSM_DIM).astype(jnp.int32)).astype(F32)


def mixer_backward(*args):
    wide = 2 * ROWS
    dma = pltpu.SemaphoreType.DMA
    v = pltpu.VMEM
    piece = (BLOCKS, ROWS, HEAD_DIM)
    return call(
        mixer_backward_kernel, "mixer_backward", args, (23, 25, 26, 21, 22, 24, 30, 0, 1, 2, 5, 27),
        [
            ((ROWS, 2 * HEAD_DIM), BF16),
            ((ROWS, 256), BF16),
            ((ROWS, INNER), BF16),
            ((ROWS, INNER), BF16),
            ((ROWS, 128), BF16),
            ((8, INNER), F32),
            ((8, 128), F32),
            ((8, 128), F32),
            ((64, 12 * WIDE), F32),
            ((OWN, ROWS), BF16),
        ],
        [
            v((ROWS, HEAD_DIM), F32),
            v((HEAD_DIM, wide), F32),
            *[v(piece, BF16)] * 3,
            v((2, PLANE, ROWS, HEAD_DIM), BF16),
            v((ROWS, HEAD_DIM), BF16),
            v((ROWS, HEAD_DIM), F32),
            v((ROWS + 8, INNER), F32),
            v((ROWS + 8, 128), F32),
            v((ROWS + 8, 128), F32),
            v((INNER, STATE), F32),
            *[v((BLOCKS, SCAN_ROWS + 8, STATE), BF16)] * 4,
            v((ROWS, ROWS), F32),
            v((ROWS, ROWS), F32),
            v((128, ROWS), F32),
            v((ROWS, INNER), F32),
            v((ROWS, INNER), F32),
            v((ROWS, BC), F32),
            v((4, ROWS, 128), BF16),
            v((4, ROWS, 128), BF16),
            v((8, GRAD_EDGE), F32),
            v((8, GRAD_EDGE), F32),
            v((INNER, STATE), F32),
            v((ROWS + 8, 128), F32),
            v((ROWS, 128), F32),
            v((ROWS + 8, 128), F32),
            dma((2, PLANE)),
            dma((2, PLANE)),
            dma((BLOCKS,)),
            dma((BLOCKS,)),
            dma((2,)),
            dma((2, BLOCKS)),
            dma((2, BLOCKS)),
            dma((4,)),
            dma((4,)),
            dma((4,)),
            v((CONV, 128), F32),
            *small_scratch(),
            *Reduce.scratch(12),
        ],
        2,
    )


SMALL = 8 * 128
SMALL_AT = 5
CHUNKS = 13
GATHER_FROM = CHUNKS


def finish_kernel(
    loads, misc_ref, dx_ref, dz_ref, dq_ref, ddt_ref, gated_ref, att_ref, nt_ref, ntz_ref, mt_ref,
    mtz_ref, ffn_ref, tok_ref, x_w, z_w, q_w, dt_w, dxtaps_ref, dbctaps_ref, dvec_ref,
    gains_ref, bc_all, kv_all, outz_ref,
    w_ref, all_ref, alls_ref, back_sum, ffn_sum,
    back_ref, near_sem, bc_w, kv_w, column_sem, dt_wide, own_small, mine, esum, egot, e_send, e_recv, z_send, z_recv, w_send, w_recv,
    sib_send, sib_recv, s_send, s_recv, t_send, t_recv, part_ref, *rest,
):
    loads.start()
    me, c, zh = block_index(), lax.axis_index("c"), lax.axis_index("zh")
    chip = zh * BLOCKS + me
    sibling = {"c": 1 - c}

    def chip_at(p):
        return {"zh": p // BLOCKS, **block_at(p % BLOCKS)}

    n_rs = len(Reduce.scratch(CHUNKS))
    rs = Reduce(
        [(nt_ref, ntz_ref, 0), (mt_ref, mtz_ref, 9)], CHUNKS, 9, *rest[:7], w_ref, rest[7:n_rs]
    )
    rest = rest[n_rs:]
    n_sum = len(HeadSum.scratch())
    back = HeadSum(back_ref, back_sum, *rest[:3], rest[3:n_sum])
    rest = rest[n_sum:]
    ffn = HeadSum(ffn_ref, ffn_sum, *rest[:3], rest[3:])

    barrier = pltpu.get_barrier_semaphore()
    over(1, CHIPS, lambda o: signal(barrier, chip_at((chip + o) % CHIPS)))
    signal(barrier, sibling)
    pl.semaphore_wait(barrier, CHIPS)

    head = zh * 2 + c
    columns = [
        pltpu.make_async_copy(
            ref.at[:, pl.ds(pl.multiple_of(k * 128, 128), 128)], here, column_sem.at[i]
        )
        for i, (ref, k, here) in enumerate(((bc_all, head, bc_w), (kv_all, c * 2 + zh, kv_w)))
    ]
    for copy in columns:
        copy.start()
    rs.fill([misc_ref, dx_ref, dz_ref, dq_ref])
    rs.r[8, :, :128] = ddt_ref[...]
    rs.r[8, :, 128:] = jnp.zeros_like(ddt_ref)
    over(0, rs.here, lambda k: rs.right(k).start())
    near = pltpu.make_async_copy(outz_ref, rs.rz.at[pl.ds(9, 4)], near_sem)
    near.start()
    loads.need(nt_ref, ntz_ref)

    def partial(rows):
        total = dot(dx_ref[rows, :], x_w[...], 1, 1)
        total += dot(dz_ref[rows, :], z_w[...], 1, 1)
        total += dot(dq_ref[rows, :], q_w[...], 1, 1)
        total += dot(ddt_ref[rows, :], dt_wide[...])
        total += dot(misc_ref[rows, :128], bc_w[...], 1, 1)
        back_ref[rows, :] = (total + dot(misc_ref[rows, 128:], kv_w[...], 1, 1)).astype(BF16)

    spread_dt(dt_w, dt_wide)
    loads.need(x_w, z_w, q_w)
    for copy in columns:
        copy.wait()
    rs.step(0)
    partial(slice(0, ROWS // 2))
    back.start((0, 1))
    rs.step(1)
    partial(slice(ROWS // 2, ROWS))
    back.start((2, 3))
    loads.need(mt_ref, mtz_ref, ffn_ref, tok_ref, gated_ref, att_ref)
    near.wait()
    rs.fill([gated_ref, att_ref], 9)
    ffn.start()

    at, level = me % PLANE, zh * NZ + lax.axis_index("zl")

    def along_z(o):
        d = (level + o) % 4
        where = {"zh": d // NZ, "zl": d % NZ}
        return remote(mine, all_ref.at[c, at, level], z_send.at[o], z_recv.at[o], where)

    x, y = lax.axis_index("x"), lax.axis_index("y")

    def at_place(i, j):
        return {"x": i, "y": j}, i * NY + j

    def piece(q, h, send, where):
        ref = all_ref.at[c, q, pl.ds(2 * h, 2)]
        return remote(ref, ref, send, w_recv.at[h, q], where)

    def one_way(h, o):
        where = {"x": (x + o) % NX} if h == 0 else {"y": (y + o) % NY}
        return piece(at, h, w_send.at[h, o], where)

    def other_way(h, k, o):
        i, j = ((x + k) % NX, y) if h == 0 else (x, (y + k) % NY)
        where = {"y": (y + o) % NY} if h == 0 else {"x": (x + o) % NX}
        return piece(i * NY + j, h, w_send.at[h, 4 * k + 4 + o], where)

    def arrived(q, h):
        return piece(q, h, w_send.at[0, 0], sibling)

    def to_sibling(q, core):
        return remote(
            all_ref.at[core, q], all_ref.at[core, q], sib_send.at[q], sib_recv.at[q], sibling
        )

    def columns_out():
        for o in range(1, 4):
            along_z(o).wait_recv()
        for o in range(1, 4):
            one_way(0, o).start()
            one_way(1, o).start()
        to_sibling(at, c).start()
        for o in range(1, 4):
            other_way(0, 0, o).start()
            other_way(1, 0, o).start()

    def columns_on():
        for k in range(1, 4):
            for h in range(2):
                i, j = ((x + k) % NX, y) if h == 0 else (x, (y + k) % NY)
                arrived(i * NY + j, h).wait_recv()
                for o in range(1, 4):
                    other_way(h, k, o).start()

    def pass_on(k):
        q, _ = plane_peer(k, -1)
        same_x, same_y = q // NY == x, q % NY == y

        @pl.when(jnp.logical_not(same_y))
        def _():
            arrived(q, 0).wait_recv()

        @pl.when(jnp.logical_not(same_x))
        def _():
            arrived(q, 1).wait_recv()

        to_sibling(q, c).start()

    def share(d):
        return remote(own_small.at[d], egot.at[me], e_send.at[d], e_recv.at[me], block_at(d))

    def shared(s):
        return remote(egot.at[s], egot.at[s], e_send.at[0], e_recv.at[s], block_at(s))

    def small_spread(o):
        d = (chip + o) % CHIPS
        slot = zh * SMALL_AT + me
        return remote(esum, alls_ref.at[c, slot], s_send.at[o], s_recv.at[slot], chip_at(d))

    def small_sibling(slot, core):
        return remote(
            alls_ref.at[core, slot], alls_ref.at[core, slot], t_send.at[slot], t_recv.at[slot],
            sibling,
        )

    def put(row, value):
        own_small[row // 8, row % 8 : row % 8 + 1, :] = value

    def gradient():
        for r in range(0, ROWS, 32):
            rows = pl.ds(r, 32)
            x = tok_ref[rows, :].astype(F32)
            scale = lax.rsqrt(jnp.mean(x * x, 1, keepdims=True) + EPSILON)
            n = x * scale
            grad = back_sum[rows, :].astype(F32)
            gains = jnp.sum(grad * n, 0, keepdims=True)
            for k in range(MODEL // 128):
                piece = gains[:, k * 128 : (k + 1) * 128]
                part_ref[k : k + 1, :] = piece if r == 0 else part_ref[k : k + 1, :] + piece
        own_small[0, :4] = part_ref[pl.ds(head * 4, 4), :]
        for k in range(CONV):
            for g in range(GROUPS):
                put(4 + GROUPS * k + g, dxtaps_ref[k : k + 1, g * 128 : (g + 1) * 128])
            put(28 + k, dbctaps_ref[k : k + 1, :])
            put(32 + k, gains_ref[0:1, lane_block(head * 4 + k)])
        lane = lax.broadcasted_iota(jnp.int32, (1, 128), 1)
        line = jnp.zeros((1, 128), F32)
        for k in range(3):
            moved = dvec_ref[k : k + 1, :] if k == 0 else pltpu.roll(dvec_ref[k : k + 1, :], k * HEADS, 1)
            line = jnp.where((lane >= k * HEADS) & (lane < (k + 1) * HEADS), moved, line)
        put(36, line)
        own_small[4, 5:] = jnp.zeros((3, 128), F32)

        def give(d):
            @pl.when(d != me)
            def _():
                share(d).start()

        over(0, SMALL_AT, give)

    def small_sums():
        @pl.when(me < SMALL_AT)
        def _():
            egot[me] = own_small[me]

            def take(s):
                @pl.when(s != me)
                def _():
                    shared(s).wait_recv()

            over(0, BLOCKS, take)
            total = lax.fori_loop(0, BLOCKS, lambda s, t: t + egot[s], jnp.zeros((8, 128), F32))
            esum[...] = jnp.concatenate([total, jnp.zeros_like(total)], 0).astype(BF16)
            slot = zh * SMALL_AT + me
            alls_ref[c, slot] = esum[...]
            over(1, CHIPS, lambda o: small_spread(o).start())
            small_sibling(slot, c).start()

    def small_pass():
        def one(slot):
            @pl.when(slot != zh * SMALL_AT + me + jnp.where(me < SMALL_AT, 0, CHIPS))
            def _():
                remote(
                    esum, alls_ref.at[c, slot], s_send.at[0], s_recv.at[slot], sibling
                ).wait_recv()
                small_sibling(slot, c).start()

        over(0, 2 * SMALL_AT, one)

    def weights_out():
        mine[...] = w_ref[:, :WIDE].astype(BF16)
        all_ref[c, at, level] = mine[...]
        for o in range(1, 4):
            along_z(o).start()

    batch, first_pass = 3, rs.steps - 5

    def step(i):
        rs.step(i)

        @pl.when(i == LAST)
        def _():
            weights_out()
            back.across()

        @pl.when(i == 8)
        def _():
            columns_out()
            ffn.across()

        @pl.when(i == 11)
        def _():
            back.join()
            columns_on()

        @pl.when(i == 12)
        def _():
            back.finish()
            gradient()

        @pl.when(i == 15)
        def _():
            small_sums()

        @pl.when(i >= first_pass)
        def _():
            k = i - first_pass
            over(k * batch, (k + 1) * batch, pass_on)

    over(2, rs.steps, step)
    loads.put(w_ref, back_sum)
    ffn.join()
    small_pass()
    ffn.finish()
    loads.put(ffn_sum)

    over(0, PLANE, lambda q: to_sibling(q, 1 - c).wait_recv())
    over(0, 2 * SMALL_AT, lambda s: small_sibling(s, 1 - c).wait_recv())
    rs.close()
    back.close()
    ffn.close()
    over(0, PLANE, lambda q: to_sibling(q, c).wait_send())
    over(0, 2 * SMALL_AT, lambda s: small_sibling(s, c).wait_send())
    for h in range(2):
        for o in range(1, 4):
            one_way(h, o).wait_send()
            for k in range(4):
                other_way(h, k, o).wait_send()
    for o in range(1, 4):
        along_z(o).wait_send()

    @pl.when(me < SMALL_AT)
    def _():
        over(1, CHIPS, lambda o: small_spread(o).wait_send())

    def given(d):
        @pl.when(d != me)
        def _():
            share(d).wait_send()

    over(0, SMALL_AT, given)


def finish(*args):
    v, dma = pltpu.VMEM, pltpu.SemaphoreType.DMA
    return call(
        finish_kernel, "finish", args, (7, 8, 13, 14, 15, 9, 10, 11, 12, 5, 6),
        [
            ((64, CHUNKS * WIDE), F32),
            ((2, PLANE, 4, 64, WIDE), BF16),
            ((2, 2 * SMALL_AT, 16, 128), BF16),
            ((ROWS, MODEL), BF16),
            ((ROWS, MODEL), BF16),
        ],
        [
            v((ROWS, MODEL), BF16),
            dma,
            v((MODEL, 128), BF16),
            v((MODEL, 128), BF16),
            dma((2,)),
            v((128, MODEL), BF16),
            v((SMALL_AT, 8, 128), F32),
            v((64, WIDE), BF16),
            v((16, 128), BF16),
            v((BLOCKS, 8, 128), F32),
            dma((SMALL_AT,)), dma((BLOCKS,)),
            dma((4,)), dma((4,)),
            dma((2, 20)), dma((2, PLANE)), dma((PLANE,)), dma((PLANE,)),
            dma((CHIPS,)), dma((2 * SMALL_AT,)),
            dma((2 * SMALL_AT,)), dma((2 * SMALL_AT,)),
            v((16, 128), F32),
            *Reduce.scratch(CHUNKS),
            *HeadSum.scratch(),
            *HeadSum.scratch(),
        ],
        3,
        (21, 22, 23),
    )


def place_kernel(
    all_ref, back_ref, ffn_ref, hid_ref, ghid_ref, tok_ref, gain_ref, mixer_ref, ffn_w, small_ref,
    out_ref, dtok_ref, bc_ref, kv_ref, x_w, z_w, q_w, dt_w, out_w, attn_w, gate_w, up_w, down_w,
    xtaps_ref, bctaps_ref, bias_ref, rate_ref, skip_ref, one_ref, two_ref,
):
    for c in range(2):
        for p in range(all_ref.shape[1]):
            for zh in range(2):
                rows = slice(p * 64, (p + 1) * 64)
                at, turned = (zh * 2 + c) * 128, (c * 2 + zh) * 128
                bc_ref[rows, at : at + 128] = all_ref[c, p, zh, 0, :, :128].astype(F32)
                kv_ref[rows, turned : turned + 128] = all_ref[c, p, zh, 0, :, 128:].astype(F32)
    for r in range(0, out_ref.shape[0], 32):
        rows = slice(r, r + 32)
        out_ref[rows, :] = (hid_ref[rows, :] + ffn_ref[rows, :].astype(F32)).astype(BF16)
        x = tok_ref[rows, :].astype(F32)
        scale = lax.rsqrt(jnp.mean(x * x, 1, keepdims=True) + EPSILON)
        n = x * scale
        scaled = back_ref[rows, :].astype(F32) * gain_ref[0:1, :]
        along = jnp.mean(n * scaled, 1, keepdims=True)
        dtok_ref[rows, :] = ghid_ref[rows, :] + scale * (scaled - n * along)

    @pl.when(pl.program_id(0) == 0)
    def _():
        at = WIDE
        for ref in (x_w, z_w, q_w):
            ref[...] = mixer_ref[:, at : at + ref.shape[1]]
            at += ref.shape[1]
        dt_w[...] = jnp.transpose(mixer_ref[:, at : at + 128])[:HEADS, :]
        at += WIDE
        for ref in (out_w, attn_w):
            ref[...] = mixer_ref[:, at : at + ref.shape[1]]
            at += ref.shape[1]
        at = 0
        for ref in (down_w, gate_w, up_w):
            ref[...] = ffn_w[:, at : at + ref.shape[1]]
            at += ref.shape[1]
        lane = lax.broadcasted_iota(jnp.int32, (1, 128), 1)
        lines = [jnp.zeros((1, 128), F32)] * 3
        for h in range(4):

            def row(k):
                piece = small_ref[h % 2, h // 2 * SMALL_AT + k // 8].astype(F32)
                return piece[k % 8 : k % 8 + 1, :]

            for k in range(CONV):
                for g in range(GROUPS):
                    cols = slice(h * INNER + g * 128, h * INNER + (g + 1) * 128)
                    xtaps_ref[k : k + 1, cols] = row(4 + GROUPS * k + g)
                bctaps_ref[k : k + 1, h * 128 : (h + 1) * 128] = row(28 + k)
                cols = pl.ds((4 * h + k) * 128, 128)
                one_ref[cols] = row(k).reshape(128)
                two_ref[cols] = row(32 + k).reshape(128)
            for k in range(3):
                shift = (h - k) * HEADS % 128
                moved = pltpu.roll(row(36), shift, 1) if shift else row(36)
                mine = (lane >= h * HEADS) & (lane < (h + 1) * HEADS)
                lines[k] = jnp.where(mine, moved, lines[k])
        for ref, line in zip((bias_ref, rate_ref, skip_ref), lines):
            ref[...] = line.reshape(128)[: 4 * HEADS]


def place(gathered, back, ffn, hidden_in, ghid, tokens, gain, mixer_w, ffn_w, small):
    steps = 4
    spans, rows, ff = PLANE * NZ // steps, ROWS // steps, ffn_w.shape[1] // 3
    half = steps // NZ
    s = jax.ShapeDtypeStruct

    def whole(shape):
        return pl.BlockSpec(shape, lambda i: (0,) * len(shape))

    token = pl.BlockSpec((rows, MODEL), lambda i: (i, 0))
    wide = pl.BlockSpec((64 * spans, 512), lambda i: (i, 0))
    kept = [
        (64, INNER), (64, INNER), (64, 256), (HEADS, 64), (64, INNER), (64, 256), (64, ff), (64, ff),
        (64, ff), (CONV, 4 * INNER), (CONV, BC), (4 * HEADS,), (4 * HEADS,), (4 * HEADS,), (MODEL,), (MODEL,),
    ]
    return pl.pallas_call(
        place_kernel,
        name="place",
        out_shape=(
            s((ROWS, MODEL), BF16), s((ROWS, MODEL), F32), s((MODEL, 512), F32),
            s((MODEL, 512), F32), *[s(shape, F32) for shape in kept],
        ),
        grid=(steps,),
        in_specs=[
            pl.BlockSpec((2, spans, 2, 1, 64, WIDE), lambda i: (0, i % half, 0, i // half, 0, 0)),
            token, token, token, token, token, whole((1, MODEL)), whole(mixer_w.shape),
            whole(ffn_w.shape), whole(small.shape),
        ],
        out_specs=(token, token, wide, wide, *[whole(shape) for shape in kept]),
        compiler_params=pltpu.CompilerParams(vmem_limit_bytes=VMEM_LIMIT),
    )(
        gathered.reshape(2, PLANE, 2, NZ, 64, WIDE), back, ffn, hidden_in, ghid, tokens, gain,
        mixer_w, ffn_w, small,
    )


def on_device(
    tokens, segment_ids, cotangent, norm1_gain, x_weight, z_weight, bc_weight, dt_weight,
    x_conv, bc_conv, dt_bias, decay_rate, skip_gain, out_weight, query_weight, kv_weight,
    attn_weight, norm2_gain, gate_weight, up_weight, down_weight,
):
    heads = decay_rate.shape[0]
    positions = block_index() * ROWS + jnp.arange(ROWS)
    half_dim = HEAD_DIM // 2
    frequency = ROPE_BASE ** (-(jnp.arange(half_dim).astype(F32) * 2.0 / HEAD_DIM))
    angles = positions.astype(F32)[:, None] * frequency[None, :]
    cosine, sine = jnp.cos(angles), jnp.sin(angles)
    cosine = jnp.concatenate([cosine, cosine], 1)
    sine = jnp.concatenate([-sine, sine], 1)
    dt_t, seg = dt_weight.T, segment_ids.reshape(1, ROWS)
    bias, rate, skip = (v.reshape(1, heads) for v in (dt_bias, decay_rate, skip_gain))
    gain_one, gain_two = norm1_gain.reshape(1, MODEL), norm2_gain.reshape(1, MODEL)

    (
        normed_t, cot_t, queries, x_pre, bc_pre, dt_raw, z_val, attended, lse, kv_all, edge_in,
        gated, core, x_act, bc_act, state_in, normed_near, cot_near, attended_low,
    ) = mixer_forward(
        tokens, cotangent, gain_one, query_weight, kv_weight, x_weight, bc_weight, dt_t, z_weight,
        cosine, sine, seg, x_conv, bc_conv, bias, rate, skip,
    )
    (
        hidden_in, two_t, grad_gate, grad_up, hidden, ffn_part, grad_hidden_in, mix_t, gains_two,
        grad_gated, grad_attended, two_near, mixed_near,
    ) = feed_forward(
        gated, attended_low, tokens, cotangent, gain_two, out_weight, attn_weight, gate_weight,
        up_weight, down_weight,
    )
    (
        grad_query, misc, grad_z, grad_x_pre, grad_dt, grad_x_conv, grad_bc_conv, grad_vectors,
        ffn_w, mix_near,
    ) = mixer_backward(
        queries, grad_attended, attended, lse, seg, kv_all, grad_gated, z_val, core, x_act,
        bc_act, x_pre, bc_pre, edge_in, dt_raw, state_in, bias, x_conv, bc_conv, rate,
        skip, grad_gate, grad_up, hidden, two_t, cot_t, cot_near, mix_t, cosine, sine, two_near,
    )
    mixer_w, gathered, small_sums, grad_normed, ffn_sum = finish(
        misc, grad_x_pre, grad_z, grad_query, grad_dt, gated, attended_low, normed_t, normed_near,
        mix_t, mix_near, ffn_part, tokens, x_weight, z_weight, query_weight, dt_t, grad_x_conv,
        grad_bc_conv, grad_vectors, gains_two, bc_weight, kv_weight, mixed_near,
    )
    (
        output, grad_tokens, bc_w, kv_w, x_w, z_w, q_w, dt_w, out_w, attn_w, gate_w, up_w, down_w,
        x_taps, bc_taps, bias_sum, rate_sum, skip_sum, gain_one_sum, gain_two_sum,
    ) = place(
        gathered, grad_normed, ffn_sum, hidden_in, grad_hidden_in, tokens, gain_one, mixer_w,
        ffn_w, small_sums,
    )
    return (
        output, grad_tokens, gain_one_sum, x_w, z_w, bc_w, dt_w.T, x_taps, bc_taps, bias_sum,
        rate_sum, skip_sum, out_w.T, q_w, kv_w, attn_w.T, gain_two_sum, gate_w, up_w, down_w.T,
    )


def solution(mesh):
    split = Mesh(mesh.devices.reshape(NZ, NX, NY, 2, 2), (*SEQ, "zh", "c"))
    head = ("zh", "c")
    rows, columns, both, turned = P(SEQ, None), P(None, head), P(SEQ, head), P(head, SEQ)
    return jax.shard_map(
        on_device,
        mesh=split,
        in_specs=(
            rows, P(SEQ), rows, P(), columns, columns, P(), columns, columns, P(), P(head),
            P(head), P(head), P(head, None), columns, P(), P(head, None), P(), columns, columns,
            P(head, None),
        ),
        out_specs=(
            rows, rows, P(), both, both, P(), both, P(), P(), P(), P(), P(), turned, both, P(),
            turned, P(), both, both, turned,
        ),
        check_vma=False,
    )
```

```python
import functools

import jax
import jax.numpy as jnp
from jax import lax
from jax.experimental import pallas as pl
from jax.experimental.pallas import tpu as pltpu
from jax.sharding import Mesh
from jax.sharding import PartitionSpec as P

SSM_DIM = 64
STATE = 256
CONV = 4
KVHEADS = 2
HEAD_DIM = 128
NZ, NX, NY = 2, 4, 4
BLOCKS = NZ * NX * NY
CHIPS = 2 * BLOCKS
ROWS = 256
MODEL = 2048
SEQ = ("zl", "x", "y")
EPSILON = 1e-05
ROPE_BASE = 100000000000.0
HIGHEST = lax.Precision.HIGHEST
MESH = pl.DeviceIdType.MESH
BF16, F32 = jnp.bfloat16, jnp.float32
MASKED = -1e30
LOG2E = 1.4426950408889634
VMEM_LIMIT = 56 * 2**20


def block_index():
    return (lax.axis_index("zl") * NX + lax.axis_index("x")) * NY + lax.axis_index("y")


def block_at(s):
    return {"zl": s // (NX * NY), "x": (s // NY) % NX, "y": s % NY}


PLANE = NX * NY


def plane_peer(k, sign, stride=13):
    o = 1 + (k * stride) % (PLANE - 1)
    dx, dy = o // NY, o % NY
    x, y = lax.axis_index("x"), lax.axis_index("y")
    if sign < 0:
        dx, dy = NX - dx, NY - dy
    x, y = (x + dx) % NX, (y + dy) % NY
    return x * NY + y, {"x": x, "y": y}


def signal(sem, where):
    pl.semaphore_signal(sem, inc=1, device_id=where, device_id_type=MESH)


def remote(src, dst, send, recv, where):
    return pltpu.make_async_remote_copy(src, dst, send, recv, device_id=where, device_id_type=MESH)


def over(start, stop, body):
    def step(i, carry):
        body(i)
        return carry

    lax.fori_loop(start, stop, step, 0)


def dot(a, b, left=1, right=0):
    return lax.dot_general(
        a, b, (((left,), (right,)), ((), ())), preferred_element_type=F32
    )


def vmem(n):
    return [pl.BlockSpec(memory_space=pltpu.VMEM)] * n


def params(collective_id):
    return pltpu.CompilerParams(
        collective_id=collective_id, has_side_effects=True, vmem_limit_bytes=VMEM_LIMIT
    )


HEADS = 12
INNER = HEADS * SSM_DIM
GROUPS = INNER // 128
BC = 2 * STATE
SCAN_ROWS = INNER // BLOCKS
EDGE_WIDE = INNER + BC + 128
GRAD_EDGE = INNER + 128


def two_parts(v):
    high = v.astype(BF16)
    return high, (v - high.astype(F32)).astype(BF16)


def low_lanes(rows):
    return lax.broadcasted_iota(jnp.int32, (rows, 128), 1) < SSM_DIM


def widen(v, g):
    low = low_lanes(v.shape[0])
    return jnp.where(low, v[:, 2 * g : 2 * g + 1], v[:, 2 * g + 1 : 2 * g + 2])


def per_head(v, g):
    lane = lax.broadcasted_iota(jnp.int32, v.shape, 1)
    first = jnp.sum(jnp.where(lane < SSM_DIM, v, 0.0), 1, keepdims=True)
    second = jnp.sum(jnp.where(lane < SSM_DIM, 0.0, v), 1, keepdims=True)
    return jnp.where(lane == 2 * g, first, jnp.where(lane == 2 * g + 1, second, 0.0))


def triangle():
    row = lax.broadcasted_iota(jnp.int32, (ROWS, ROWS), 0)
    col = lax.broadcasted_iota(jnp.int32, (ROWS, ROWS), 1)
    return (col <= row).astype(F32).astype(BF16)


def running(v, lower, side):
    high, low = two_parts(v)
    middle, lowest = two_parts(v - high.astype(F32))
    return (
        dot(lower, high, side, 0) + dot(lower, middle, side, 0) + dot(lower, lowest, side, 0)
    )


def sigmoid(v):
    return 1.0 / (1.0 + jnp.exp(-v))


def softplus(v):
    return jnp.maximum(v, 0.0) + jnp.log(1.0 + jnp.exp(-jnp.abs(v)))


def lane_block(g):
    return pl.ds(pl.multiple_of(g * 128, 128), 128)


def decays(dt_ref, vec_ref, seg_ref, segx_ref, lower):
    pre = dt_ref[...] + vec_ref[0:1, :]
    step = softplus(pre)
    total = running(-step * vec_ref[1:2, :] * LOG2E, lower, 1)
    last = total[ROWS - 1 : ROWS, :]
    seg = seg_ref[...]
    seg_last, before = seg[ROWS - 1 : ROWS, :], segx_ref[7:8, :]
    carry = jnp.where(seg == seg_last, jnp.exp2(last - total), 0.0)
    entry = jnp.where(seg == before, jnp.exp2(total), 0.0)
    through = jnp.where(seg_last == before, jnp.exp2(last), 0.0)
    return pre, step, total, carry, entry, through


def conv_group(ext_ref, segx_ref, seg_ref, taps_ref, cols):
    total, inputs = None, []
    for k in range(CONV):
        same = segx_ref[pl.ds(5 + k, ROWS), :] == seg_ref[...]
        v = jnp.where(same, ext_ref[pl.ds(5 + k, ROWS), cols], 0.0)
        inputs.append(v)
        term = taps_ref[k : k + 1, cols] * v
        total = term if total is None else total + term
    return total, inputs


def by_fours(body):
    def four(i):
        for k in range(4):
            body(i * 4 + k)

    over(0, BLOCKS // 4, four)


def scan_message(msg_ref, state_ref, through):
    high = through.astype(BF16)
    rest = through - high.astype(F32)
    middle = rest.astype(BF16)
    low = rest - middle.astype(F32)
    extra = jnp.concatenate([high.astype(F32), middle.astype(F32), low, jnp.zeros((5, 128), F32)], 0)
    extra = jnp.concatenate([extra, jnp.zeros((8, STATE - 128), F32)], 1)

    def fill(b):
        rows = state_ref[pl.ds(pl.multiple_of(b * SCAN_ROWS, 8), SCAN_ROWS), :]
        msg_ref[b] = jnp.concatenate([rows, extra], 0).astype(BF16)

    by_fours(fill)


class Scan:
    def __init__(self, reverse, me, msg, got, back, out, send, recv):
        self.reverse, self.me = reverse, me
        self.msg, self.got, self.back, self.out = msg, got, back, out
        self.send, self.recv = send, recv

    def there(self, o):
        d = (self.me + o) % BLOCKS
        return remote(
            self.msg.at[d], self.got.at[self.me], self.send.at[0, o], self.recv.at[0, o],
            block_at(d),
        )

    def arrived(self, phase, dst, o):
        s = (self.me + BLOCKS - o) % BLOCKS
        return remote(
            dst.at[s], dst.at[s], self.send.at[phase, o], self.recv.at[phase, o], block_at(s)
        )

    def start(self):
        over(1, BLOCKS, lambda o: self.there(o).start())
        self.got[self.me] = self.msg[self.me]

    def turn(self):
        me = self.me
        over(1, BLOCKS, lambda o: self.arrived(0, self.got, o).wait_recv())
        lane = lax.broadcasted_iota(jnp.int32, (SCAN_ROWS, 128), 1)
        row = lax.broadcasted_iota(jnp.int32, (SCAN_ROWS, 128), 0) + me * SCAN_ROWS
        at_head = (row >= lane * SSM_DIM) & (row < lane * SSM_DIM + SSM_DIM)

        def scan(i, state):
            blocks, messages, factors = [], [], []
            for n in range(4):
                k = BLOCKS - 1 - (4 * i + n) if self.reverse else 4 * i + n
                message = self.got[k].astype(F32)
                row = message[SCAN_ROWS : SCAN_ROWS + 1, :128]
                row += message[SCAN_ROWS + 1 : SCAN_ROWS + 2, :128]
                row += message[SCAN_ROWS + 2 : SCAN_ROWS + 3, :128]
                blocks.append(k)
                messages.append(message)
                factors.append(jnp.sum(jnp.where(at_head, row, 0.0), 1, keepdims=True))
            for k, message, through in zip(blocks, messages, factors):
                self.back[k] = jnp.concatenate([state, jnp.zeros((8, STATE), F32)], 0).astype(BF16)
                state = through * state + message[:SCAN_ROWS]
            for k in blocks:
                pl.when(k != me)(lambda: self.returned(k).start())
            return state

        lax.fori_loop(0, BLOCKS // 4, scan, jnp.zeros((SCAN_ROWS, STATE), F32))
        self.out[me] = self.back[me]

    def returned(self, k):
        o = (k + BLOCKS - self.me) % BLOCKS
        return remote(
            self.back.at[k], self.out.at[self.me], self.send.at[1, o], self.recv.at[1, o],
            block_at(k),
        )

    def finish(self, state_ref):
        over(1, BLOCKS, lambda o: self.arrived(1, self.out, o).wait_recv())

        def fill(b):
            rows = self.out[b].astype(F32)
            state_ref[pl.ds(pl.multiple_of(b * SCAN_ROWS, 8), SCAN_ROWS), :] = rows[:SCAN_ROWS]

        by_fours(fill)

    def close(self):
        def sent(o):
            self.there(o).wait_send()
            self.returned((self.me + o) % BLOCKS).wait_send()

        over(1, BLOCKS, sent)


def key_segments(block):
    turned = jnp.transpose(block.astype(F32))
    return jnp.concatenate([turned[:, 0:1], turned[:, 1:2]], 0)


def causal_mask(s):
    row = lax.broadcasted_iota(jnp.int32, (ROWS, 2 * ROWS), 0)
    col = lax.broadcasted_iota(jnp.int32, (ROWS, 2 * ROWS), 1) % ROWS
    return jnp.where(row <= col, s, MASKED)


def mixing_bias(seg_ref, segrow_ref):
    row = lax.broadcasted_iota(jnp.int32, (ROWS, ROWS), 0)
    col = lax.broadcasted_iota(jnp.int32, (ROWS, ROWS), 1)
    same = segrow_ref[0:1, :ROWS] == seg_ref[:, 0:1]
    return jnp.where((col <= row) & same, 0.0, MASKED)


WIDE = 256
RELAY, MIDDLE, LAST = 2, 4, 6
AHEAD = 4
OWN = MODEL // NZ


class Reduce:
    def __init__(self, lefts, n, here, r_ref, rz, part, rel, gx, half, gy, out_ref, sems):
        self.lefts, self.n, self.here, self.throttled = lefts, n, here, True
        self.r, self.rz, self.part, self.rel = r_ref, rz, part, rel
        self.gx, self.half, self.gy, self.out = gx, half, gy, out_ref
        self.rz_sem, self.rel_sem, self.gx_sem, self.gy_sem = (
            (sems[2 * k], sems[2 * k + 1]) for k in range(4)
        )
        self.zl, self.x, self.y = (lax.axis_index(a) for a in SEQ)
        self.other = {"zl": 1 - self.zl}

    @staticmethod
    def scratch(n):
        v, dma = pltpu.VMEM, pltpu.SemaphoreType.DMA
        return [
            v((n, ROWS, WIDE), BF16),
            v((n, ROWS, WIDE), BF16),
            v((n, 4, 4, 64, WIDE), BF16),
            v((n, 2, 2, 64, WIDE), BF16),
            v((n, 2, 4, 64, WIDE), BF16),
            v((n, 4, 64, WIDE), BF16),
            v((n, 3, 64, WIDE), BF16),
            *[dma((n,))] * 8,
        ]

    def fill(self, arrays, c=0):
        for ref in arrays:
            for k in range(ref.shape[1] // WIDE):
                self.r[c] = ref[:, k * WIDE : (k + 1) * WIDE]
                c += 1

    def right(self, c):
        return remote(
            self.r.at[c], self.rz.at[c], self.rz_sem[0].at[c], self.rz_sem[1].at[c], self.other
        )

    def start(self):
        over(0, AHEAD, lambda c: self.right(c).start())

    def place(self, c, phase, o):
        along_x = c % 2 == phase
        x_to = jnp.where(along_x, (self.x + o) % NX, self.x)
        y_to = jnp.where(along_x, self.y, (self.y + o) % NY)
        return {"x": x_to, "y": y_to}, jnp.where(along_x, x_to, y_to)

    def send(self, src, dst, sem, c, where):
        return remote(src, dst, sem[0].at[c], sem[1].at[c], where)

    def send_second(self, c, o):
        where, d = self.place(c, 1, o)
        return self.send(self.half.at[c, d], self.gy.at[c, o - 1], self.gy_sem, c, where)

    def whole(self, got, sem, c):
        return self.send(got.at[c], got.at[c], sem, c, self.other)

    def product(self, c):
        @pl.when((c + AHEAD < self.here) & self.throttled)
        def _():
            self.right(c + AHEAD).start()

        @pl.when(c < self.here)
        def _():
            self.right(c).wait_recv()

        mine, theirs = self.r[c], self.rz[c]
        even = c % 2 == 0
        ends = [first for _, _, first in self.lefts[1:]] + [self.n]
        for (own, near, first), end in zip(self.lefts, ends):
            @pl.when((c >= first) & (c < end))
            def _():
                for i in range(NX):
                    a = own[pl.ds(pl.multiple_of(self.zl * OWN + i * 256, 256), 256), :]
                    b = near[pl.ds(i * 256, 256), :]
                    tile = (dot(a, mine) + dot(b, theirs)).astype(BF16)
                    for j in range(NY):
                        self.part[c, jnp.where(even, i, j), jnp.where(even, j, i)] = (
                            tile[j * 64 : (j + 1) * 64]
                        )
        _, d = self.place(c, 0, 2)
        for k, o in ((0, 1), (1, 3)):
            src = self.part.at[c, d, pl.ds(2 * k, 2)]
            self.send(src, self.rel.at[c, k], self.rel_sem, c, self.place(c, 0, o)[0]).start()

    def relay(self, c):
        self.whole(self.rel, self.rel_sem, c).wait_recv()
        for k, o in ((0, 1), (1, 3)):
            where, d = self.place(c, 0, o)
            for j in (2 * k, 2 * k + 1):
                total = self.part[c, d, j].astype(F32) + self.rel[c, k, j - 2 * k].astype(F32)
                self.part[c, d, j] = total.astype(BF16)
            self.send(self.part.at[c, d], self.gx.at[c, k], self.gx_sem, c, where).start()

    def middle(self, c):
        self.whole(self.gx, self.gx_sem, c).wait_recv()
        mine = jnp.where(c % 2 == 0, self.x, self.y)
        for j in range(4):
            total = self.part[c, mine, j].astype(F32)
            for k in range(2):
                total += self.gx[c, k, j].astype(F32)
            self.half[c, j] = total.astype(BF16)
        for o in range(1, 4):
            self.send_second(c, o).start()

    def last(self, c):
        self.whole(self.gy, self.gy_sem, c).wait_recv()
        mine = jnp.where(c % 2 == 0, self.y, self.x)
        total = self.half[c, mine].astype(F32)
        for o in range(3):
            total += self.gy[c, o].astype(F32)
        self.out[:, pl.ds(pl.multiple_of(c * WIDE, WIDE), WIDE)] = total

    @property
    def steps(self):
        return self.n + LAST

    def step(self, i):
        for late, do in ((0, self.product), (RELAY, self.relay), (MIDDLE, self.middle), (LAST, self.last)):
            @pl.when((i >= late) & (i < self.n + late))
            def _():
                do(i - late)

    def close(self):
        over(0, self.here, lambda c: self.right(c).wait_send())

        def sent(c):
            self.whole(self.rel, self.rel_sem, c).wait_send()
            self.whole(self.gx, self.gx_sem, c).wait_send()
            self.whole(self.gy, self.gy_sem, c).wait_send()

        over(0, self.n, sent)


class Left:
    def __init__(self, l_ref, lz, sems):
        zl, c = lax.axis_index("zl"), lax.axis_index("c")
        half = OWN // 2
        there = pl.ds(pl.multiple_of((1 - zl) * OWN + c * half, half), half)
        near, other = (pl.ds(pl.multiple_of(k * half, half), half) for k in (c, 1 - c))
        sem = [sems.at[k] for k in range(4)]
        self.out = remote(l_ref.at[there], lz.at[near], sem[0], sem[1], {"zl": 1 - zl})
        self.on = remote(lz.at[near], lz.at[near], sem[2], sem[3], {"c": 1 - c})
        self.back = remote(lz.at[other], lz.at[other], sem[2], sem[3], {"c": 1 - c})

    def start(self):
        self.out.start()

    def pass_on(self):
        self.out.wait_recv()
        self.on.start()

    def finish(self):
        self.back.wait_recv()

    def close(self):
        self.out.wait_send()
        self.on.wait_send()


HEAD_CHUNKS = 4


class HeadSum:
    def __init__(self, x, out, near, pair, far, sems):
        self.x, self.out, self.near, self.pair, self.far = x, out, near, pair, far
        self.near_send, self.near_recv, self.far_send, self.far_recv, self.end_send, self.end_recv = sems
        self.c, zh = lax.axis_index("c"), lax.axis_index("zh")
        self.sibling, self.opposite = {"c": 1 - self.c}, {"zh": 1 - zh}
        self.half = x.shape[0] // 2
        self.rows_each = self.half // HEAD_CHUNKS

    @staticmethod
    def scratch():
        v, dma = pltpu.VMEM, pltpu.SemaphoreType.DMA
        return [*[v((ROWS // 2, MODEL), BF16)] * 3, *[dma((HEAD_CHUNKS,))] * 6]

    def rows(self, core, k):
        return pl.ds(pl.multiple_of(k // 2 * self.half + (2 * core + k % 2) * self.rows_each, 16), self.rows_each)

    def local(self, k):
        return pl.ds(k * self.rows_each, self.rows_each)

    def first(self, k):
        return remote(
            self.x.at[self.rows(1 - self.c, k)], self.near.at[self.local(k)],
            self.near_send.at[k], self.near_recv.at[k], self.sibling,
        )

    def second(self, k):
        return remote(
            self.pair.at[self.local(k)], self.far.at[self.local(k)],
            self.far_send.at[k], self.far_recv.at[k], self.opposite,
        )

    def third(self, k, core):
        rows = self.rows(core, k)
        return remote(
            self.out.at[rows], self.out.at[rows], self.end_send.at[k], self.end_recv.at[k],
            self.sibling,
        )

    def start(self, chunks=range(HEAD_CHUNKS)):
        for k in chunks:
            self.first(k).start()

    def across(self, chunks=range(HEAD_CHUNKS)):
        for k in chunks:
            self.first(k).wait_recv()
            own = self.x[self.rows(self.c, k)].astype(F32)
            self.pair[self.local(k)] = (own + self.near[self.local(k)].astype(F32)).astype(BF16)
            self.second(k).start()

    def join(self, chunks=range(HEAD_CHUNKS)):
        for k in chunks:
            self.second(k).wait_recv()
            total = self.pair[self.local(k)].astype(F32) + self.far[self.local(k)].astype(F32)
            self.out[self.rows(self.c, k)] = total.astype(BF16)
            self.third(k, self.c).start()

    def finish(self, chunks=range(HEAD_CHUNKS)):
        for k in chunks:
            self.third(k, 1 - self.c).wait_recv()

    def close(self):
        for k in range(HEAD_CHUNKS):
            self.first(k).wait_send()
            self.second(k).wait_send()
            self.third(k, self.c).wait_send()


class Loads:
    def __init__(self, pairs, sems, results, out_sems):
        self.copies = {
            id(there): pltpu.make_async_copy(here, there, sems.at[i])
            for i, (here, there) in enumerate(pairs)
        }
        self.results = {
            id(here): pltpu.make_async_copy(here, there, out_sems.at[i])
            for i, (here, there) in enumerate(results)
        }
        self.under_way = []

    def start(self):
        for copy in self.copies.values():
            copy.start()

    def need(self, *refs):
        for ref in refs:
            copy = self.copies.pop(id(ref), None)
            if copy is not None:
                copy.wait()

    def put(self, *refs):
        for ref in refs:
            copy = self.results.pop(id(ref))
            copy.start()
            self.under_way.append(copy)

    def flush(self):
        for copy in self.results.values():
            copy.start()
        for copy in (*self.results.values(), *self.under_way):
            copy.wait()


def fetching(kernel, n_in, n_out, late, large):
    def wrapped(*refs):
        ins, outs, rest = list(refs[:n_in]), list(refs[n_in : n_in + n_out]), refs[n_in + n_out :]
        count = len(late) + len(large)
        buffers, (sems, out_sems) = rest[-2 - count : -2], rest[-2:]
        pairs, results = [], []
        for buffer, i in zip(buffers, late):
            pairs.append((ins[i], buffer))
            ins[i] = buffer
        for buffer, i in zip(buffers[len(late) :], large):
            results.append((buffer, outs[i]))
            outs[i] = buffer
        loads = Loads(pairs, sems, results, out_sems)
        kernel(loads, *ins, *outs, *rest[: -2 - count])
        loads.flush()

    return wrapped


def call(kernel, name, args, late, outs, scratch, collective_id, left=()):
    anywhere, here = pl.BlockSpec(memory_space=pl.ANY), pl.BlockSpec(memory_space=pltpu.VMEM)
    shapes = [jax.ShapeDtypeStruct(*o) for o in outs]
    large = [i for i, o in enumerate(shapes) if o.size >= 2**14]
    dma = pltpu.SemaphoreType.DMA
    return pl.pallas_call(
        fetching(kernel, len(args), len(outs), late, large),
        name=name,
        out_shape=tuple(shapes),
        in_specs=[anywhere if i in (*late, *left) else here for i in range(len(args))],
        out_specs=tuple(anywhere if i in large else here for i in range(len(outs))),
        scratch_shapes=[
            *scratch,
            *[pltpu.VMEM(args[i].shape, args[i].dtype) for i in late],
            *[pltpu.VMEM(shapes[i].shape, shapes[i].dtype) for i in large],
            dma((max(len(late), 1),)),
            dma((max(len(large), 1),)),
        ],
        compiler_params=params(collective_id),
    )(*args)


def spread_small(seg, bias, rate, skip, seg_ref, segrow_ref, vec_ref, skip_ref):
    row = seg[...].astype(F32)
    seg_ref[...] = jnp.transpose(jnp.broadcast_to(row, (128, ROWS)))
    segrow_ref[...] = jnp.broadcast_to(jnp.concatenate([row, row], 1), segrow_ref.shape)
    rest = jnp.zeros((1, 128 - HEADS), F32)
    lines = [jnp.concatenate([ref[...], rest], 1) for ref in (bias, rate, skip)]
    vec_ref[...] = jnp.concatenate([*lines, jnp.zeros((5, 128), F32)], 0)
    for g in range(GROUPS):
        skip_ref[:, g * 128 : (g + 1) * 128] = jnp.broadcast_to(widen(lines[2], g), (8, 128))


def small_scratch():
    return [
        pltpu.VMEM((ROWS, 128), F32),
        pltpu.VMEM((8, 2 * ROWS), F32),
        pltpu.VMEM((8, 128), F32),
        pltpu.VMEM((8, INNER), F32),
    ]


def spread_dt(dt_w, wide_ref):
    wide_ref[16:, :] = jnp.zeros((112, MODEL), BF16)
    rows = jnp.concatenate([dt_w[...].astype(F32), jnp.zeros((16 - HEADS, MODEL), F32)], 0)
    wide_ref[:16, :] = rows.astype(BF16)


def turn_pairs(v, cosine, sine, direction):
    return v * cosine + pltpu.roll(v, HEAD_DIM // 2, 1) * (sine * direction)


def transpose_to(out_ref, ref):
    for k in range(ref.shape[1] // 256):
        out_ref[k * 256 : (k + 1) * 256, :] = jnp.transpose(ref[:, k * 256 : (k + 1) * 256])


def feed_forward_kernel(
    loads, gated_ref, att_ref, tok_ref, cot_ref, gain_ref, out_w, attn_w, gate_w, up_w, down_w,
    hid_ref, ft_ref, dgate_ref, dup_ref, hidden_ref, ffn_ref, ghid_ref, mt_ref, gain_out,
    gg_ref, do_ref, ftz_ref,
    x_ref, sum_ref, back_ref, back_sum, normed, mix_ref, left_sem, *sums,
):
    loads.start()
    n_sum = len(HeadSum.scratch())
    first = HeadSum(x_ref, sum_ref, *sums[:3], sums[3:n_sum])
    second = HeadSum(back_ref, back_sum, *sums[n_sum : n_sum + 3], sums[n_sum + 3 :])
    barrier = pltpu.get_barrier_semaphore()
    other_z = {"zl": 1 - lax.axis_index("zl")}
    signal(barrier, first.sibling)
    signal(barrier, first.opposite)
    signal(barrier, other_z)
    pl.semaphore_wait(barrier, 3)
    left = Left(ft_ref, ftz_ref, left_sem)
    halves = [(slice(g * 128, (g + 1) * 128), (2 * g, 2 * g + 1)) for g in range(2)]
    loads.need(out_w, attn_w)
    for rows, chunks in halves:
        x_ref[rows, :] = (
            dot(gated_ref[rows, :], out_w[...]) + dot(att_ref[rows, :], attn_w[...])
        ).astype(BF16)
        first.start(chunks)
    first.across()

    wide = 256
    loads.need(cot_ref, down_w)
    for k in range(0, hidden_ref.shape[1], wide):
        ghid_ref[:, k : k + wide] = dot(cot_ref[...], down_w[k : k + wide, :], 1, 1)
    loads.need(tok_ref, gate_w, up_w)

    def norm(half, chunks):
        first.join(chunks)
        first.finish(chunks)
        for r in range(half.start, half.stop, 32):
            rows = slice(r, r + 32)
            x = tok_ref[rows, :].astype(F32) + sum_ref[rows, :].astype(F32)
            hid_ref[rows, :] = x
            scale = lax.rsqrt(jnp.mean(x * x, 1, keepdims=True) + EPSILON)
            normed[rows, :] = (x * scale * gain_ref[0:1, :]).astype(BF16)

    def feed(rows, chunks):
        for k in range(0, hidden_ref.shape[1], wide):
            cols = slice(k, k + wide)
            n = normed[rows, :]
            gate, up = dot(n, gate_w[:, cols]), dot(n, up_w[:, cols])
            grad = ghid_ref[rows, cols]
            sig = sigmoid(gate)
            act = gate * sig
            hidden_ref[rows, cols] = (act * up).astype(BF16)
            dgate_ref[rows, cols] = (grad * up * sig * (1.0 + gate * (1.0 - sig))).astype(BF16)
            dup_ref[rows, cols] = (grad * act).astype(BF16)
        back_ref[rows, :] = (
            dot(dgate_ref[rows, :], gate_w[...], 1, 1) + dot(dup_ref[rows, :], up_w[...], 1, 1)
        ).astype(BF16)
        second.start(chunks)

    def norm_back(half, chunks):
        second.join(chunks)
        second.finish(chunks)
        for r in range(half.start, half.stop, 32):
            rows = slice(r, r + 32)
            x = hid_ref[rows, :]
            scale = lax.rsqrt(jnp.mean(x * x, 1, keepdims=True) + EPSILON)
            n = x * scale
            grad = back_sum[rows, :].astype(F32)
            scaled = grad * gain_ref[0:1, :]
            along = jnp.mean(n * scaled, 1, keepdims=True)
            total = cot_ref[rows, :].astype(F32) + scale * (scaled - n * along)
            ghid_ref[rows, :] = total
            mix_ref[rows, :] = total.astype(BF16)
            gains = jnp.sum(grad * n, 0, keepdims=True)
            gain_out[0:1, :] = gains if r == 0 else gain_out[0:1, :] + gains

    (rows_a, chunks_a), (rows_b, chunks_b) = halves
    norm(rows_a, chunks_a)
    feed(rows_a, chunks_a)
    norm(rows_b, chunks_b)
    second.across(chunks_a)
    transpose_to(ft_ref, normed)
    left.start()
    loads.put(hid_ref, ft_ref)
    feed(rows_b, chunks_b)
    loads.put(hidden_ref, dgate_ref, dup_ref)
    second.across(chunks_b)
    left.pass_on()
    ffn_ref[...] = dot(hidden_ref[...], down_w[...]).astype(BF16)
    loads.put(ffn_ref)
    norm_back(rows_a, chunks_a)
    norm_back(rows_b, chunks_b)
    loads.put(ghid_ref)
    grad_att = dot(mix_ref[...], attn_w[...], 1, 1).astype(BF16)
    for h in range(2):
        do_ref[h * ROWS : (h + 1) * ROWS, :] = grad_att[:, h * HEAD_DIM : (h + 1) * HEAD_DIM]
    gg_ref[...] = dot(mix_ref[...], out_w[...], 1, 1)
    loads.put(gg_ref, do_ref)
    transpose_to(mt_ref, mix_ref)
    loads.put(mt_ref)
    first.close()
    second.close()
    left.finish()
    left.close()


def feed_forward(*args):
    v = pltpu.VMEM
    ff = args[7].shape[1]
    return call(
        feed_forward_kernel, "feed_forward", args, (2, 3, 5, 6, 7, 8, 9),
        [
            ((ROWS, MODEL), F32),
            ((MODEL, ROWS), BF16),
            ((ROWS, ff), BF16),
            ((ROWS, ff), BF16),
            ((ROWS, ff), BF16),
            ((ROWS, MODEL), BF16),
            ((ROWS, MODEL), F32),
            ((MODEL, ROWS), BF16),
            ((8, MODEL), F32),
            ((ROWS, INNER), F32),
            ((2 * ROWS, HEAD_DIM), BF16),
            ((OWN, ROWS), BF16),
        ],
        [
            *[v((ROWS, MODEL), BF16)] * 6,
            pltpu.SemaphoreType.DMA((4,)),
            *HeadSum.scratch(),
            *HeadSum.scratch(),
        ],
        4,
    )


EARLY = 6


def mixer_forward_kernel(
    loads, tok_ref, cot_ref, gain_ref, q_w, kv_w, x_w, bc_w, dt_w, z_w, cos_ref, sin_ref, seg,
    xtaps_ref, bctaps_ref, bias, rate, skip,
    nt_ref, ct_ref, q_ref, x_ref, bc_ref, dt_ref, z_ref,
    att_ref, lse_ref, kv_ref, edge_out, gated_ref, core_ref, xact_ref, bcact_ref, state_ref,
    ntz_ref, ctz_ref, attlow_ref,
    m_ref, l_ref, acc_ref, xext, bcext, segx, local, msg, got, back, result, bias_ref, cb_ref,
    cumt_ref, normed, own_ref, edge_ref, kv_cols, seg_ref, segrow_ref, vec_ref, skip_ref, dt_wide,
    send_sem, recv_sem, sib_send, sib_recv, edge_sem, scan_send, scan_recv, left_sem, kv_sem,
):
    me, c, zl = block_index(), lax.axis_index("c"), lax.axis_index("zl")
    at = me % PLANE
    sibling = {"c": 1 - c}
    kv_at = (c * KVHEADS + lax.axis_index("zh")) * HEAD_DIM
    kv_copy = pltpu.make_async_copy(
        kv_w.at[:, pl.ds(pl.multiple_of(kv_at, HEAD_DIM), HEAD_DIM)], kv_cols, kv_sem
    )
    loads.start()
    kv_copy.start()
    barrier = pltpu.get_barrier_semaphore()
    over(1, BLOCKS, lambda o: signal(barrier, block_at((me + o) % BLOCKS)))
    signal(barrier, sibling)

    spread_small(seg, bias, rate, skip, seg_ref, segrow_ref, vec_ref, skip_ref)
    loads.need(tok_ref)
    for r in range(0, ROWS, 32):
        rows = slice(r, r + 32)
        v = tok_ref[rows, :].astype(F32)
        scale = lax.rsqrt(jnp.mean(v * v, 1, keepdims=True) + EPSILON)
        normed[rows, :] = (v * scale * gain_ref[0:1, :]).astype(BF16)
    n = normed[...]
    loads.need(x_w, bc_w)
    x_ref[...] = dot(n, x_w[...]).astype(BF16)
    bc_ref[...] = dot(n, bc_w[...]).astype(BF16)
    edge_ref[:, :INNER] = x_ref[ROWS - 16 :, :]
    edge_ref[:, INNER : INNER + BC] = bc_ref[ROWS - 16 :, :]
    edge_ref[:, INNER + BC :] = seg_ref[ROWS - 16 :, :].astype(BF16)
    pl.semaphore_wait(barrier, BLOCKS)

    def block_copy(src, j, send, where):
        return remote(src, kv_ref.at[c, j], send_sem.at[send], recv_sem.at[j], where)

    def arrival(j):
        return block_copy(own_ref, j, 0, sibling)

    to_sibling = lambda j, src: remote(
        src, kv_ref.at[c, j], sib_send.at[j], sib_recv.at[j], sibling
    )
    from_sibling = lambda j: remote(
        kv_ref.at[1 - c, j], kv_ref.at[1 - c, j], sib_send.at[j], sib_recv.at[j], sibling
    )
    across = block_copy(own_ref, me, PLANE - 1, {"zl": 1 - zl})

    def own_copy(k, wait):
        d, where = plane_peer(k, 1, 8)

        @pl.when(d > at)
        def _():
            copy = block_copy(own_ref, me, k, where)
            copy.wait_send() if wait else copy.start()

    def relay_copy(k, wait):
        copy = block_copy(kv_ref.at[c, at], at, PLANE + k, plane_peer(k, 1, 8)[1])
        copy.wait_send() if wait else copy.start()

    edge_copy = remote(
        edge_ref, edge_out, edge_sem.at[0], edge_sem.at[1], block_at((me + 1) % BLOCKS)
    )
    states = Scan(False, me, msg, got, back, result, scan_send, scan_recv)

    @pl.when(me < BLOCKS - 1)
    def _():
        edge_copy.start()

    cosine, sine = cos_ref[...], sin_ref[...]
    kv_copy.wait()
    raw = dot(n, kv_cols[...])
    turned = turn_pairs(raw, cosine, sine, 1.0)
    own_ref[:ROWS, :] = jnp.where(c == 0, turned, raw).astype(BF16)
    rows = [segrow_ref[0:1, :HEAD_DIM], segrow_ref[0:1, HEAD_DIM : 2 * HEAD_DIM]]
    own_ref[ROWS:, :] = jnp.concatenate([*rows, jnp.zeros((14, HEAD_DIM), F32)], 0).astype(BF16)

    @pl.when(zl == 0)
    def _():
        across.start()

    to_sibling(me, own_ref).start()
    over(0, EARLY, lambda k: own_copy(k, False))
    lefts = [Left(ct_ref, ctz_ref, left_sem.at[0]), Left(nt_ref, ntz_ref, left_sem.at[1])]

    kv_ref[c, me] = own_ref[...]
    spread_dt(dt_w, dt_wide)
    dt_ref[...] = dot(n, dt_wide[...], 1, 1)
    xext[8:, :] = x_ref[...].astype(F32)
    bcext[8:, :] = bc_ref[...].astype(F32)
    segx[8:, :] = seg_ref[...]
    lower = triangle()
    bias_ref[...] = mixing_bias(seg_ref, segrow_ref)

    @pl.when(me > 0)
    def _():
        edge_copy.wait_recv()

    @pl.when(me == 0)
    def _():
        edge_out[...] = jnp.zeros_like(edge_out)

    edge = edge_out[...].astype(F32)[8:]
    xext[:8, :] = edge[:, :INNER]
    bcext[:8, :] = edge[:, INNER : INNER + BC]
    segx[:8, :] = edge[:, INNER + BC :]

    def activate(ext, taps, out):
        def group(g):
            pre, _ = conv_group(ext, segx, seg_ref, taps, lane_block(g))
            out[:, lane_block(g)] = (pre * sigmoid(pre)).astype(BF16)

        over(0, out.shape[1] // 128, group)

    activate(bcext, bctaps_ref, bcact_ref)
    activate(xext, xtaps_ref, xact_ref)

    _, step, total, carry, entry, through = decays(dt_ref, vec_ref, seg_ref, segx, lower)
    cumt_ref[...] = jnp.transpose(total)
    weight = step * carry
    b_low, c_low = bcact_ref[:, :STATE], bcact_ref[:, STATE:]
    for g in range(GROUPS):
        moved = xact_ref[:, g * 128 : (g + 1) * 128].astype(F32) * widen(weight, g)
        local[g * 128 : (g + 1) * 128, :] = dot(moved.astype(BF16), b_low, 0, 0)
    transpose_to(nt_ref, normed)
    loads.need(cot_ref)
    transpose_to(ct_ref, cot_ref)
    for left in lefts:
        left.start()
    scan_message(msg, local, through)
    states.start()
    over(EARLY, PLANE - 1, lambda k: own_copy(k, False))

    @pl.when(zl == 1)
    def _():
        arrival(at).wait_recv()
        to_sibling(at, kv_ref.at[c, at]).start()
        over(0, PLANE - 1, lambda k: relay_copy(k, False))

    cb_ref[...] = dot(c_low, b_low, 1, 1)
    low_lane = lax.broadcasted_iota(jnp.int32, (ROWS, 128), 1) < SSM_DIM
    for g in range(GROUPS):
        cols = slice(g * 128, (g + 1) * 128)
        u = (xact_ref[:, cols].astype(F32) * widen(step, g)).astype(BF16)
        made = []
        for h in (2 * g, 2 * g + 1):
            gap = total[:, h : h + 1] - cumt_ref[h : h + 1, :] + bias_ref[...]
            made.append(dot((jnp.exp2(gap) * cb_ref[...]).astype(BF16), u))
        core_ref[:, cols] = jnp.where(low_lane, made[0], made[1])

    loads.need(q_w)
    for h in range(2):
        raw = dot(n, q_w[:, h * HEAD_DIM : (h + 1) * HEAD_DIM])
        q_ref[h * ROWS : (h + 1) * ROWS, :] = turn_pairs(raw, cosine, sine, 1.0).astype(BF16)
    scale = LOG2E * HEAD_DIM**-0.5
    queries = q_ref[...]
    qseg = segrow_ref[0:1, :]

    def scores_of(j):
        s = dot(kv_ref[0, j, :ROWS], queries, 1, 1) * scale
        return jnp.where(key_segments(kv_ref[0, j, ROWS:]) == qseg, s, MASKED)

    from_sibling(me).wait_recv()
    s = causal_mask(scores_of(me))
    m = jnp.max(s, 0, keepdims=True)
    p = jnp.exp2(s - m)
    m_ref[...] = m
    l_ref[...] = jnp.sum(p, 0, keepdims=True)
    acc_ref[...] = dot(kv_ref[1, me, :ROWS], p.astype(BF16), 0, 0)

    loads.put(nt_ref, ct_ref, q_ref, x_ref, bc_ref, dt_ref, bcact_ref, xact_ref)
    states.turn()
    loads.need(z_w)
    z_ref[...] = dot(n, z_w[...])
    loads.put(z_ref)

    def forward(k):
        q, _ = plane_peer(k, -1, 8)

        def one(j):
            arrival(j).wait_recv()
            to_sibling(j, kv_ref.at[c, j]).start()

        pl.when(q < at)(lambda: one(zl * PLANE + q))
        pl.when(zl == 1)(lambda: one(q))

    def attend(*blocks):
        scores = []
        for j in blocks:
            from_sibling(j).wait_recv()
            scores.append(scores_of(j))
        m_old = m_ref[...]
        m = m_old
        for s in scores:
            m = jnp.maximum(m, jnp.max(s, 0, keepdims=True))
        alpha = jnp.exp2(m_old - m)
        total, acc = l_ref[...] * alpha, acc_ref[...] * alpha
        for j, s in zip(blocks, scores):
            p = jnp.exp2(s - m)
            total += jnp.sum(p, 0, keepdims=True)
            acc += dot(kv_ref[1, j, :ROWS], p.astype(BF16), 0, 0)
        m_ref[...], l_ref[...], acc_ref[...] = m, total, acc

    forward(0)

    @pl.when(zl == 1)
    def _():
        attend(at)

    def step_over(k):
        @pl.when(k + 1 < PLANE - 1)
        def _():
            forward(k + 1)

        q, _ = plane_peer(k, -1, 8)
        pl.when((q < at) & (zl == 1))(lambda: attend(PLANE + q, q))
        pl.when((q < at) & (zl == 0))(lambda: attend(q))
        pl.when((q > at) & (zl == 1))(lambda: attend(q))

    over(0, PLANE - 1, step_over)
    for left in lefts:
        left.pass_on()
    attended = jnp.transpose(acc_ref[...] / l_ref[...])
    att_ref[...] = attended
    for h in range(2):
        attlow_ref[:, h * HEAD_DIM : (h + 1) * HEAD_DIM] = (
            attended[h * ROWS : (h + 1) * ROWS].astype(BF16)
        )
    lse_ref[...] = jnp.broadcast_to(m_ref[...] + jnp.log2(l_ref[...]), lse_ref.shape)

    loads.put(att_ref, kv_ref)
    states.finish(state_ref)
    loads.put(state_ref)
    for g in range(GROUPS):
        cols = slice(g * 128, (g + 1) * 128)
        outer = dot(c_low, state_ref[cols, :].astype(BF16), 1, 1) * widen(entry, g)
        core = core_ref[:, cols] + outer
        core_ref[:, cols] = core
        out = core + skip_ref[0:1, cols] * xact_ref[:, cols].astype(F32)
        z = z_ref[:, cols]
        gated_ref[:, cols] = (out * z * sigmoid(z)).astype(BF16)

    loads.put(gated_ref, core_ref)
    states.close()
    for left in lefts:
        left.finish()
        left.close()
    to_sibling(me, own_ref).wait_send()
    over(0, PLANE - 1, lambda k: own_copy(k, True))

    @pl.when(zl == 0)
    def _():
        across.wait_send()

    @pl.when(zl == 1)
    def _():
        over(0, PLANE - 1, lambda k: relay_copy(k, True))
        over(0, PLANE, lambda j: to_sibling(j, own_ref).wait_send())

    over(0, at, lambda q: to_sibling(zl * PLANE + q, own_ref).wait_send())

    @pl.when(me < BLOCKS - 1)
    def _():
        edge_copy.wait_send()


def mixer_forward(*args):
    wide = 2 * ROWS
    dma = pltpu.SemaphoreType.DMA
    return call(
        mixer_forward_kernel, "mixer_forward", args, (0, 5, 6, 3, 8, 1),
        [
            ((MODEL, ROWS), BF16),
            ((MODEL, ROWS), BF16),
            ((wide, HEAD_DIM), BF16),
            ((ROWS, INNER), BF16),
            ((ROWS, BC), BF16),
            ((ROWS, 128), F32),
            ((ROWS, INNER), F32),
            ((wide, HEAD_DIM), F32),
            ((8, wide), F32),
            ((2, BLOCKS, ROWS + 16, HEAD_DIM), BF16),
            ((16, EDGE_WIDE), BF16),
            ((ROWS, INNER), BF16),
            ((ROWS, INNER), F32),
            ((ROWS, INNER), BF16),
            ((ROWS, BC), BF16),
            ((INNER, STATE), F32),
            ((OWN, ROWS), BF16),
            ((OWN, ROWS), BF16),
            ((ROWS, 2 * HEAD_DIM), BF16),
        ],
        [
            pltpu.VMEM((1, wide), F32),
            pltpu.VMEM((1, wide), F32),
            pltpu.VMEM((HEAD_DIM, wide), F32),
            pltpu.VMEM((ROWS + 8, INNER), F32),
            pltpu.VMEM((ROWS + 8, BC), F32),
            pltpu.VMEM((ROWS + 8, 128), F32),
            pltpu.VMEM((INNER, STATE), F32),
            *[pltpu.VMEM((BLOCKS, SCAN_ROWS + 8, STATE), BF16)] * 4,
            pltpu.VMEM((ROWS, ROWS), F32),
            pltpu.VMEM((ROWS, ROWS), F32),
            pltpu.VMEM((128, ROWS), F32),
            pltpu.VMEM((ROWS, MODEL), BF16),
            pltpu.VMEM((ROWS + 16, HEAD_DIM), BF16),
            pltpu.VMEM((16, EDGE_WIDE), BF16),
            pltpu.VMEM((MODEL, HEAD_DIM), BF16),
            *small_scratch(),
            pltpu.VMEM((128, MODEL), BF16),
            *[dma((BLOCKS,))] * 4,
            dma((2,)),
            dma((2, BLOCKS)),
            dma((2, BLOCKS)),
            dma((2, 4)),
            dma,
        ],
        1,
        (4,),
    )


def mixer_backward_kernel(
    loads, q_ref, do_ref, att_ref, lse_ref, seg, kv_ref, gg_ref, z_ref, core_ref, xact_ref,
    bcact_ref, x_ref, bcown_ref, edge_in, dt_ref, state_ref, bias, xtaps_ref, bctaps_ref,
    rate, skip, dgate_ref, dup_ref, hidden_ref, ft_ref, ct_ref, ctz_ref, mt_ref, cos_ref,
    sin_ref, ftz_ref,
    dqraw_ref, misc_ref, dz_ref, dx_ref, ddt_ref, dxtaps_ref, dbctaps_ref, dvec_ref,
    w_ref, mtz_ref,
    dkv_ref, dqt_ref, mine, theirs, sib, kvgot, relay_ref, total_ref, xext, bcext, segx, local, msg, got, back, result,
    bias_ref, cb_ref, cumt_ref, g_ref, du_ref, dbc_all, shares, share_got, edge_ref,
    edge_out, enter_ref, gext, dcum_ref, ddtx_ref,
    send_sem, recv_sem, sib_send, sib_recv, edge_sem, scan_send, scan_recv, share_send, share_recv,
    left_sem, owntaps_ref, seg_ref, segrow_ref, vec_ref, skip_ref, *reduce,
):
    me, c, zh, zl = block_index(), *(lax.axis_index(a) for a in ("c", "zh", "zl"))
    head_at = zh * 2 + c
    sibling = {"c": 1 - c}
    at_head = lambda d: {"zh": d // 2, "c": d % 2}
    loads.start()
    barrier = pltpu.get_barrier_semaphore()
    over(1, BLOCKS, lambda o: signal(barrier, block_at((me + o) % BLOCKS)))
    for o in range(1, 4):
        signal(barrier, at_head((head_at + o) % 4))
    pl.semaphore_wait(barrier, BLOCKS + 2)

    at = me % PLANE
    to_sibling = lambda j: remote(
        theirs.at[j], sib.at[j], sib_send.at[j], sib_recv.at[j], sibling
    )

    def to_owner(k, kind):
        q, where = plane_peer(k, -1)
        j = q if kind else zl * PLANE + q
        return remote(
            mine.at[j], kvgot.at[kind, at], send_sem.at[kind, k], recv_sem.at[kind, at], where
        )

    def from_plane(kind, q):
        return remote(
            kvgot.at[kind, q], kvgot.at[kind, q], send_sem.at[kind, 0], recv_sem.at[kind, q],
            sibling,
        )

    across = remote(
        relay_ref, kvgot.at[1, 0], send_sem.at[0, PLANE - 1], recv_sem.at[1, 0], {"zl": 1 - zl}
    )
    states = Scan(True, me, msg, got, back, result, scan_send, scan_recv)
    rs = Reduce(
        [(ct_ref, ctz_ref, 0), (ft_ref, ftz_ref, 4)], 12, 12, *reduce[:7], w_ref, reduce[7:]
    )
    left = Left(mt_ref, mtz_ref, left_sem)
    loads.need(hidden_ref)
    rs.fill([hidden_ref])
    rs.start()
    loads.need(dgate_ref, dup_ref)
    rs.fill([dgate_ref, dup_ref], 4)
    done = 0

    def reduce_some(n):
        nonlocal done
        over(done, done + n, rs.step)
        done += n


    spread_small(seg, bias, rate, skip, seg_ref, segrow_ref, vec_ref, skip_ref)
    lower = triangle()
    edge = edge_in[...].astype(F32)[8:]
    xext[:8, :] = edge[:, :INNER]
    segx[:8, :] = edge[:, INNER + BC :]
    xext[8:, :] = x_ref[...].astype(F32)
    segx[8:, :] = seg_ref[...]
    bc_cols = lane_block(head_at)
    edge_cols = lane_block(head_at + INNER // 128)
    bcext[:8, :] = edge_in[:, edge_cols].astype(F32)[8:]
    bcext[8:, :] = bcown_ref[:, bc_cols].astype(F32)
    owntaps_ref[...] = bctaps_ref[:, bc_cols]
    bias_ref[...] = mixing_bias(seg_ref, segrow_ref)
    pre_dt, step, total, carry, entry, through = decays(dt_ref, vec_ref, seg_ref, segx, lower)
    cumt_ref[...] = jnp.transpose(total)
    b_low, c_low = bcact_ref[:, :STATE], bcact_ref[:, STATE:]
    for g in range(GROUPS):
        cols = slice(g * 128, (g + 1) * 128)
        z = z_ref[:, cols]
        grad = gg_ref[:, cols] * z * sigmoid(z)
        g_ref[:, cols] = grad
        entered = (grad * widen(entry, g)).astype(BF16)
        du_ref[:, cols] = entered.astype(F32)
        local[cols, :] = dot(entered, c_low, 0, 0)
    scan_message(msg, local, through)
    states.start()
    loads.need(ct_ref, ctz_ref, ft_ref, ftz_ref)
    reduce_some(1)

    dcum = jnp.zeros((ROWS, 128), F32)
    dskip = jnp.zeros((8, 128), F32)
    dc = jnp.zeros((ROWS, STATE), F32)
    for g in range(GROUPS):
        cols = slice(g * 128, (g + 1) * 128)
        z, core, x = z_ref[:, cols], core_ref[:, cols], xact_ref[:, cols].astype(F32)
        sig = sigmoid(z)
        out = core + skip_ref[0:1, cols] * x
        dz_ref[:, cols] = (gg_ref[:, cols] * out * sig * (1.0 + z * (1.0 - sig))).astype(BF16)
        grad = g_ref[:, cols]
        dcum += per_head(grad * core, g)
        dskip += per_head(jnp.broadcast_to(jnp.sum(grad * x, 0, keepdims=True), (8, 128)), g)
        dc += dot(du_ref[:, cols].astype(BF16), state_ref[cols, :].astype(BF16))
    dbc_all[:, STATE:] = dc
    loads.put(dz_ref)
    reduce_some(1)

    cb_ref[...] = dot(c_low, b_low, 1, 1)
    low_lane = lax.broadcasted_iota(jnp.int32, (ROWS, 128), 1) < SSM_DIM
    dcb = jnp.zeros((ROWS, ROWS), F32)
    for g in range(GROUPS):
        cols = slice(g * 128, (g + 1) * 128)
        u = xact_ref[:, cols].astype(F32) * widen(step, g)
        u_low, grad = u.astype(BF16), g_ref[:, cols]
        grad_low = grad.astype(BF16)
        made = []
        for i in range(2):
            h = 2 * g + i
            decay = jnp.exp2(total[:, h : h + 1] - cumt_ref[h : h + 1, :] + bias_ref[...])
            mixing = (decay * cb_ref[...]).astype(BF16)
            made.append(dot(mixing, grad_low, 0, 0))
            half = jnp.where(low_lane if i == 0 else ~low_lane, grad, 0.0).astype(BF16)
            dcb += decay * dot(half, u_low, 1, 1)
        du = jnp.where(low_lane, made[0], made[1])
        du_ref[:, cols] = du
        dcum -= per_head(u * du, g)
    dcum_ref[...] = dcum
    reduce_some(1)
    dcb_low = dcb.astype(BF16)
    dbc_all[:, :STATE] = dot(dcb_low, c_low, 0, 0)
    dbc_all[:, STATE:] += dot(dcb_low, b_low)

    loads.need(q_ref, do_ref, att_ref, kv_ref)
    scale = LOG2E * HEAD_DIM**-0.5
    queries, grads = q_ref[...], do_ref[...]
    lse, qseg = lse_ref[0:1, :], segrow_ref[0:1, :]
    high, low = two_parts(grads.astype(F32) * att_ref[...])
    ones = jnp.ones((8, HEAD_DIM), BF16)
    delta = (dot(ones, high, 1, 1) + dot(ones, low, 1, 1))[0:1, :]

    def block(*blocks, own=False):
        change, results = None, []
        for t in blocks:
            keys = kv_ref[0, t, :ROWS]
            s = dot(keys, queries, 1, 1) * scale
            s = jnp.where(key_segments(kv_ref[0, t, ROWS:]) == qseg, s, MASKED)
            if own:
                s = causal_mask(s)
            p = jnp.exp2(s - lse)
            ds = (p * (dot(kv_ref[1, t, :ROWS], grads, 1, 1) - delta)).astype(BF16)
            dk = dot(ds, queries)
            dv = dot(p.astype(BF16), grads)
            part = dot(keys, ds, 0, 0)
            change = part if change is None else change + part
            results.append((jnp.where(c == 0, dk, dv), jnp.where(c == 0, dv, dk)))
        dqt_ref[...] = change if own else dqt_ref[...] + change
        for t, (kept, given) in zip(blocks, results):
            mine[t] = kept.astype(BF16)
            theirs[t] = given.astype(BF16)
            to_sibling(t).start()

    def pair(t):
        to_sibling(t).wait_recv()
        return mine[t].astype(F32) + sib[t].astype(F32)

    block(me, own=True)
    reduce_some(1)
    states.turn()
    loads.need(mt_ref)
    left.start()
    before = done

    @pl.when(zl == 1)
    def _():
        block(at)

    def give(k):
        q, _ = plane_peer(k, -1)

        @pl.when(q < at)
        def _():
            j = zl * PLANE + q
            mine[j] = pair(j).astype(BF16)
            to_owner(k, 0).start()

        @pl.when(zl == 1)
        def _():
            mine[q] = pair(q).astype(BF16)
            to_owner(k, 1).start()

    def step_over(k):
        q, _ = plane_peer(k, -1)
        pl.when((q < at) & (zl == 1))(lambda: block(PLANE + q, q))
        pl.when((q < at) & (zl == 0))(lambda: block(q))
        pl.when((q > at) & (zl == 1))(lambda: block(q))

        @pl.when(k >= 1)
        def _():
            give(k - 1)

        @pl.when(k % 2 == 1)
        def _():
            rs.step(before + k // 2)

    over(0, PLANE - 1, step_over)
    give(PLANE - 2)
    done += (PLANE - 1) // 2
    reduce_some(1)
    left.pass_on()
    dkv_ref[...] = pair(me)

    @pl.when(zl == 1)
    def _():
        total_ref[...] = pair(at)

    score_scale = HEAD_DIM**-0.5
    dq = jnp.transpose(dqt_ref[...]) * score_scale
    cosine, sine = cos_ref[...], sin_ref[...]
    for h in range(2):
        raw = turn_pairs(dq[h * ROWS : (h + 1) * ROWS], cosine, sine, -1.0)
        dqraw_ref[:, h * HEAD_DIM : (h + 1) * HEAD_DIM] = raw.astype(BF16)

    states.finish(enter_ref)
    dcum = dcum_ref[...]
    dstep = jnp.zeros((ROWS, 128), F32)
    dlast = jnp.zeros((8, 128), F32)
    db = jnp.zeros((ROWS, STATE), F32)
    for g in range(GROUPS):
        cols = slice(g * 128, (g + 1) * 128)
        entering = enter_ref[cols, :]
        entering_low = entering.astype(BF16)
        x = xact_ref[:, cols].astype(F32)
        steps, carries = widen(step, g), widen(carry, g)
        v = x * steps * carries
        dv = dot(b_low, entering_low, 1, 1)
        db += dot(v.astype(BF16), entering_low)
        dcarry = per_head(v * dv, g)
        dcum -= dcarry
        dlast += jnp.broadcast_to(jnp.sum(dcarry, 0, keepdims=True), (8, 128))
        du = du_ref[:, cols] + carries * dv
        dstep += per_head(x * du, g)
        pieces = jnp.sum(entering * state_ref[cols, :], 1, keepdims=True)
        both = jnp.sum(jnp.broadcast_to(pieces, (128, 128)) * head_of_lane_f32(g), 0, keepdims=True)
        dlast += through * both
        g_ref[:, cols] = steps * du + skip_ref[0:1, cols] * g_ref[:, cols]
    dbc_all[:, :STATE] += db
    last_row = lax.broadcasted_iota(jnp.int32, (ROWS, 128), 0) == ROWS - 1
    dcum += jnp.where(last_row, dlast[0:1, :], 0.0)
    da = running(dcum, lower, 0)
    drate = -jnp.sum(step * da, 0, keepdims=True)
    ddt = (dstep - vec_ref[1:2, :] * da) * sigmoid(pre_dt)
    ddt_ref[...] = ddt.astype(BF16)
    dbias = jnp.sum(ddt, 0, keepdims=True)
    dvec_ref[...] = jnp.concatenate([dbias, drate, dskip[0:1, :], jnp.zeros((5, 128), F32)], 0)

    reduce_some(1)

    for d in range(4):
        shares[d] = dbc_all[:, d * 128 : (d + 1) * 128].astype(BF16)
    share = lambda o: remote(
        shares.at[(head_at + o) % 4], share_got.at[o], share_send.at[o], share_recv.at[o],
        at_head((head_at + o) % 4),
    )
    for o in range(1, 4):
        share(o).start()

    def conv_back(ext, taps, grad, cols, out_taps, out_grad):
        pre, inputs = conv_group(ext, segx, seg_ref, taps, cols)
        sig = sigmoid(pre)
        dpre = grad * sig * (1.0 + pre * (1.0 - sig))
        gext[...] = jnp.zeros_like(gext)
        rows = []
        for k in range(CONV):
            rows.append(jnp.sum(dpre * inputs[k], 0, keepdims=True))
            same = segx[pl.ds(5 + k, ROWS), :] == seg_ref[...]
            gext[pl.ds(5 + k, ROWS), :] += jnp.where(same, taps[k : k + 1, cols] * dpre, 0.0)
        out_taps[:, cols] = jnp.concatenate([*rows, jnp.zeros((4, 128), F32)], 0)
        out_grad[...] = gext[...]

    def x_group(g):
        cols = lane_block(g)
        conv_back(xext, xtaps_ref, g_ref[:, cols], cols, dxtaps_ref, ddtx_ref)
        edge_ref[:, cols] = ddtx_ref[:8, :]
        g_ref[:, cols] = ddtx_ref[8:, :]

    over(0, GROUPS, x_group)
    reduce_some(1)
    grad_bc = shares[head_at].astype(F32)
    for o in range(1, 4):
        share(o).wait_recv()
        grad_bc += share_got[o].astype(F32)
    conv_back(bcext, owntaps_ref, grad_bc, slice(0, 128), dbctaps_ref, ddtx_ref)
    edge_ref[:, INNER:] = ddtx_ref[:8, :]
    edge_copy = remote(
        edge_ref, edge_out, edge_sem.at[0], edge_sem.at[1], block_at((me + BLOCKS - 1) % BLOCKS)
    )

    @pl.when(me > 0)
    def _():
        edge_copy.start()

    reduce_some(1)

    def collect(q):
        @pl.when((zl == 1) & (q != at))
        def _():
            from_plane(1, q).wait_recv()
            total_ref[...] += kvgot[1, q].astype(F32)

    over(0, PLANE, collect)

    @pl.when(zl == 1)
    def _():
        relay_ref[...] = total_ref[...].astype(BF16)
        across.start()

    reduce_some(1)

    def collect_own(q):
        from_plane(0, q).wait_recv()
        dkv_ref[...] += kvgot[0, q].astype(F32)

    over(at + 1, PLANE, collect_own)

    @pl.when(zl == 0)
    def _():
        from_plane(1, 0).wait_recv()
        dkv_ref[...] += kvgot[1, 0].astype(F32)

    @pl.when(me < BLOCKS - 1)
    def _():
        edge_copy.wait_recv()

    @pl.when(me == BLOCKS - 1)
    def _():
        edge_out[...] = jnp.zeros_like(edge_out)

    tail = pl.ds(ROWS - 8, 8)
    g_ref[tail, :] += edge_out[:, :INNER]
    ddtx_ref[pl.ds(ROWS, 8), :] += edge_out[:, INNER:]
    dx_ref[...] = g_ref[...].astype(BF16)
    misc_ref[:, :128] = ddtx_ref[8:, :].astype(BF16)
    dkv = dkv_ref[...]
    turned = turn_pairs(dkv * score_scale, cosine, sine, -1.0)
    misc_ref[:, 128:] = jnp.where(c == 0, turned, dkv).astype(BF16)

    reduce_some(rs.steps - done)

    @pl.when(me > 0)
    def _():
        edge_copy.wait_send()

    states.close()
    rs.close()
    left.finish()
    left.close()
    for o in range(1, 4):
        share(o).wait_send()
    to_sibling(me).wait_send()

    def given(k):
        q, _ = plane_peer(k, -1)

        @pl.when(q < at)
        def _():
            to_sibling(zl * PLANE + q).wait_send()
            to_owner(k, 0).wait_send()

        @pl.when(zl == 1)
        def _():
            to_sibling(q).wait_send()
            to_owner(k, 1).wait_send()

    over(0, PLANE - 1, given)

    @pl.when(zl == 1)
    def _():
        to_sibling(at).wait_send()
        across.wait_send()


def head_of_lane_f32(g):
    row = lax.broadcasted_iota(jnp.int32, (128, 128), 0)
    lane = lax.broadcasted_iota(jnp.int32, (128, 128), 1)
    return (lane == 2 * g + (row >= SSM_DIM).astype(jnp.int32)).astype(F32)


def mixer_backward(*args):
    wide = 2 * ROWS
    dma = pltpu.SemaphoreType.DMA
    v = pltpu.VMEM
    piece = (BLOCKS, ROWS, HEAD_DIM)
    return call(
        mixer_backward_kernel, "mixer_backward", args, (23, 25, 26, 21, 22, 24, 30, 0, 1, 2, 5, 27),
        [
            ((ROWS, 2 * HEAD_DIM), BF16),
            ((ROWS, 256), BF16),
            ((ROWS, INNER), BF16),
            ((ROWS, INNER), BF16),
            ((ROWS, 128), BF16),
            ((8, INNER), F32),
            ((8, 128), F32),
            ((8, 128), F32),
            ((64, 12 * WIDE), F32),
            ((OWN, ROWS), BF16),
        ],
        [
            v((ROWS, HEAD_DIM), F32),
            v((HEAD_DIM, wide), F32),
            *[v(piece, BF16)] * 3,
            v((2, PLANE, ROWS, HEAD_DIM), BF16),
            v((ROWS, HEAD_DIM), BF16),
            v((ROWS, HEAD_DIM), F32),
            v((ROWS + 8, INNER), F32),
            v((ROWS + 8, 128), F32),
            v((ROWS + 8, 128), F32),
            v((INNER, STATE), F32),
            *[v((BLOCKS, SCAN_ROWS + 8, STATE), BF16)] * 4,
            v((ROWS, ROWS), F32),
            v((ROWS, ROWS), F32),
            v((128, ROWS), F32),
            v((ROWS, INNER), F32),
            v((ROWS, INNER), F32),
            v((ROWS, BC), F32),
            v((4, ROWS, 128), BF16),
            v((4, ROWS, 128), BF16),
            v((8, GRAD_EDGE), F32),
            v((8, GRAD_EDGE), F32),
            v((INNER, STATE), F32),
            v((ROWS + 8, 128), F32),
            v((ROWS, 128), F32),
            v((ROWS + 8, 128), F32),
            dma((2, PLANE)),
            dma((2, PLANE)),
            dma((BLOCKS,)),
            dma((BLOCKS,)),
            dma((2,)),
            dma((2, BLOCKS)),
            dma((2, BLOCKS)),
            dma((4,)),
            dma((4,)),
            dma((4,)),
            v((CONV, 128), F32),
            *small_scratch(),
            *Reduce.scratch(12),
        ],
        2,
    )


SMALL = 8 * 128
SMALL_AT = 5
CHUNKS = 13
GATHER_FROM = CHUNKS


def finish_kernel(
    loads, misc_ref, dx_ref, dz_ref, dq_ref, ddt_ref, gated_ref, att_ref, nt_ref, ntz_ref, mt_ref,
    mtz_ref, ffn_ref, tok_ref, x_w, z_w, q_w, dt_w, dxtaps_ref, dbctaps_ref, dvec_ref,
    gains_ref, bc_all, kv_all,
    w_ref, all_ref, alls_ref, back_sum, ffn_sum,
    back_ref, bc_w, kv_w, column_sem, dt_wide, own_small, mine, esum, egot, e_send, e_recv, z_send, z_recv, w_send, w_recv,
    sib_send, sib_recv, s_send, s_recv, t_send, t_recv, part_ref, *rest,
):
    loads.start()
    me, c, zh = block_index(), lax.axis_index("c"), lax.axis_index("zh")
    chip = zh * BLOCKS + me
    sibling = {"c": 1 - c}

    def chip_at(p):
        return {"zh": p // BLOCKS, **block_at(p % BLOCKS)}

    n_rs = len(Reduce.scratch(CHUNKS))
    rs = Reduce(
        [(nt_ref, ntz_ref, 0), (mt_ref, mtz_ref, 9)], CHUNKS, CHUNKS, *rest[:7], w_ref, rest[7:n_rs]
    )
    rest = rest[n_rs:]
    n_sum = len(HeadSum.scratch())
    back = HeadSum(back_ref, back_sum, *rest[:3], rest[3:n_sum])
    rest = rest[n_sum:]
    ffn = HeadSum(ffn_ref, ffn_sum, *rest[:3], rest[3:])

    barrier = pltpu.get_barrier_semaphore()
    over(1, CHIPS, lambda o: signal(barrier, chip_at((chip + o) % CHIPS)))
    signal(barrier, sibling)
    pl.semaphore_wait(barrier, CHIPS)

    head = zh * 2 + c
    columns = [
        pltpu.make_async_copy(
            ref.at[:, pl.ds(pl.multiple_of(k * 128, 128), 128)], here, column_sem.at[i]
        )
        for i, (ref, k, here) in enumerate(((bc_all, head, bc_w), (kv_all, c * 2 + zh, kv_w)))
    ]
    for copy in columns:
        copy.start()
    rs.fill([misc_ref, dx_ref, dz_ref, dq_ref])
    rs.r[8, :, :128] = ddt_ref[...]
    rs.r[8, :, 128:] = jnp.zeros_like(ddt_ref)
    rs.throttled = False
    over(0, 9, lambda k: rs.right(k).start())
    loads.need(nt_ref, ntz_ref)

    def partial(rows):
        total = dot(dx_ref[rows, :], x_w[...], 1, 1)
        total += dot(dz_ref[rows, :], z_w[...], 1, 1)
        total += dot(dq_ref[rows, :], q_w[...], 1, 1)
        total += dot(ddt_ref[rows, :], dt_wide[...])
        total += dot(misc_ref[rows, :128], bc_w[...], 1, 1)
        back_ref[rows, :] = (total + dot(misc_ref[rows, 128:], kv_w[...], 1, 1)).astype(BF16)

    spread_dt(dt_w, dt_wide)
    loads.need(x_w, z_w, q_w)
    for copy in columns:
        copy.wait()
    rs.step(0)
    partial(slice(0, ROWS // 2))
    back.start((0, 1))
    rs.step(1)
    partial(slice(ROWS // 2, ROWS))
    back.start((2, 3))
    loads.need(mt_ref, mtz_ref, ffn_ref, tok_ref, gated_ref, att_ref)
    rs.fill([gated_ref, att_ref], 9)
    over(9, CHUNKS, lambda k: rs.right(k).start())
    ffn.start()

    at, level = me % PLANE, zh * NZ + lax.axis_index("zl")

    def along_z(o):
        d = (level + o) % 4
        where = {"zh": d // NZ, "zl": d % NZ}
        return remote(mine, all_ref.at[c, at, level], z_send.at[o], z_recv.at[o], where)

    x, y = lax.axis_index("x"), lax.axis_index("y")

    def at_place(i, j):
        return {"x": i, "y": j}, i * NY + j

    def piece(q, h, send, where):
        ref = all_ref.at[c, q, pl.ds(2 * h, 2)]
        return remote(ref, ref, send, w_recv.at[h, q], where)

    def one_way(h, o):
        where = {"x": (x + o) % NX} if h == 0 else {"y": (y + o) % NY}
        return piece(at, h, w_send.at[h, o], where)

    def other_way(h, k, o):
        i, j = ((x + k) % NX, y) if h == 0 else (x, (y + k) % NY)
        where = {"y": (y + o) % NY} if h == 0 else {"x": (x + o) % NX}
        return piece(i * NY + j, h, w_send.at[h, 4 * k + 4 + o], where)

    def arrived(q, h):
        return piece(q, h, w_send.at[0, 0], sibling)

    def to_sibling(q, core):
        return remote(
            all_ref.at[core, q], all_ref.at[core, q], sib_send.at[q], sib_recv.at[q], sibling
        )

    def columns_out():
        for o in range(1, 4):
            along_z(o).wait_recv()
        for o in range(1, 4):
            one_way(0, o).start()
            one_way(1, o).start()
        to_sibling(at, c).start()
        for o in range(1, 4):
            other_way(0, 0, o).start()
            other_way(1, 0, o).start()

    def columns_on():
        for k in range(1, 4):
            for h in range(2):
                i, j = ((x + k) % NX, y) if h == 0 else (x, (y + k) % NY)
                arrived(i * NY + j, h).wait_recv()
                for o in range(1, 4):
                    other_way(h, k, o).start()

    def pass_on(k):
        q, _ = plane_peer(k, -1)
        same_x, same_y = q // NY == x, q % NY == y

        @pl.when(jnp.logical_not(same_y))
        def _():
            arrived(q, 0).wait_recv()

        @pl.when(jnp.logical_not(same_x))
        def _():
            arrived(q, 1).wait_recv()

        to_sibling(q, c).start()

    def share(d):
        return remote(own_small.at[d], egot.at[me], e_send.at[d], e_recv.at[me], block_at(d))

    def shared(s):
        return remote(egot.at[s], egot.at[s], e_send.at[0], e_recv.at[s], block_at(s))

    def small_spread(o):
        d = (chip + o) % CHIPS
        slot = zh * SMALL_AT + me
        return remote(esum, alls_ref.at[c, slot], s_send.at[o], s_recv.at[slot], chip_at(d))

    def small_sibling(slot, core):
        return remote(
            alls_ref.at[core, slot], alls_ref.at[core, slot], t_send.at[slot], t_recv.at[slot],
            sibling,
        )

    def put(row, value):
        own_small[row // 8, row % 8 : row % 8 + 1, :] = value

    def gradient():
        for r in range(0, ROWS, 32):
            rows = pl.ds(r, 32)
            x = tok_ref[rows, :].astype(F32)
            scale = lax.rsqrt(jnp.mean(x * x, 1, keepdims=True) + EPSILON)
            n = x * scale
            grad = back_sum[rows, :].astype(F32)
            gains = jnp.sum(grad * n, 0, keepdims=True)
            for k in range(MODEL // 128):
                piece = gains[:, k * 128 : (k + 1) * 128]
                part_ref[k : k + 1, :] = piece if r == 0 else part_ref[k : k + 1, :] + piece
        own_small[0, :4] = part_ref[pl.ds(head * 4, 4), :]
        for k in range(CONV):
            for g in range(GROUPS):
                put(4 + GROUPS * k + g, dxtaps_ref[k : k + 1, g * 128 : (g + 1) * 128])
            put(28 + k, dbctaps_ref[k : k + 1, :])
            put(32 + k, gains_ref[0:1, lane_block(head * 4 + k)])
        lane = lax.broadcasted_iota(jnp.int32, (1, 128), 1)
        line = jnp.zeros((1, 128), F32)
        for k in range(3):
            moved = dvec_ref[k : k + 1, :] if k == 0 else pltpu.roll(dvec_ref[k : k + 1, :], k * HEADS, 1)
            line = jnp.where((lane >= k * HEADS) & (lane < (k + 1) * HEADS), moved, line)
        put(36, line)
        own_small[4, 5:] = jnp.zeros((3, 128), F32)

        def give(d):
            @pl.when(d != me)
            def _():
                share(d).start()

        over(0, SMALL_AT, give)

    def small_sums():
        @pl.when(me < SMALL_AT)
        def _():
            egot[me] = own_small[me]

            def take(s):
                @pl.when(s != me)
                def _():
                    shared(s).wait_recv()

            over(0, BLOCKS, take)
            total = lax.fori_loop(0, BLOCKS, lambda s, t: t + egot[s], jnp.zeros((8, 128), F32))
            esum[...] = jnp.concatenate([total, jnp.zeros_like(total)], 0).astype(BF16)
            slot = zh * SMALL_AT + me
            alls_ref[c, slot] = esum[...]
            over(1, CHIPS, lambda o: small_spread(o).start())
            small_sibling(slot, c).start()

    def small_pass():
        def one(slot):
            @pl.when(slot != zh * SMALL_AT + me + jnp.where(me < SMALL_AT, 0, CHIPS))
            def _():
                remote(
                    esum, alls_ref.at[c, slot], s_send.at[0], s_recv.at[slot], sibling
                ).wait_recv()
                small_sibling(slot, c).start()

        over(0, 2 * SMALL_AT, one)

    def weights_out():
        mine[...] = w_ref[:, :WIDE].astype(BF16)
        all_ref[c, at, level] = mine[...]
        for o in range(1, 4):
            along_z(o).start()

    def step(i):
        rs.step(i)

        @pl.when(i == LAST)
        def _():
            weights_out()
            back.across()

        @pl.when(i == 8)
        def _():
            ffn.across()

        @pl.when(i == 10)
        def _():
            columns_out()

        @pl.when(i == 12)
        def _():
            back.join()

        @pl.when(i == 14)
        def _():
            columns_on()

        @pl.when(i == 13)
        def _():
            back.finish()
            gradient()

        @pl.when(i == 16)
        def _():
            small_sums()

    over(2, rs.steps, step)
    loads.put(w_ref, back_sum)
    over(0, PLANE - 1, pass_on)
    ffn.join()
    small_pass()
    ffn.finish()
    loads.put(ffn_sum)

    over(0, PLANE, lambda q: to_sibling(q, 1 - c).wait_recv())
    over(0, 2 * SMALL_AT, lambda s: small_sibling(s, 1 - c).wait_recv())
    rs.close()
    back.close()
    ffn.close()
    over(0, PLANE, lambda q: to_sibling(q, c).wait_send())
    over(0, 2 * SMALL_AT, lambda s: small_sibling(s, c).wait_send())
    for h in range(2):
        for o in range(1, 4):
            one_way(h, o).wait_send()
            for k in range(4):
                other_way(h, k, o).wait_send()
    for o in range(1, 4):
        along_z(o).wait_send()

    @pl.when(me < SMALL_AT)
    def _():
        over(1, CHIPS, lambda o: small_spread(o).wait_send())

    def given(d):
        @pl.when(d != me)
        def _():
            share(d).wait_send()

    over(0, SMALL_AT, given)


def finish(*args):
    v, dma = pltpu.VMEM, pltpu.SemaphoreType.DMA
    return call(
        finish_kernel, "finish", args, (7, 8, 13, 14, 15, 9, 10, 11, 12, 5, 6),
        [
            ((64, CHUNKS * WIDE), F32),
            ((2, PLANE, 4, 64, WIDE), BF16),
            ((2, 2 * SMALL_AT, 16, 128), BF16),
            ((ROWS, MODEL), BF16),
            ((ROWS, MODEL), BF16),
        ],
        [
            v((ROWS, MODEL), BF16),
            v((MODEL, 128), BF16),
            v((MODEL, 128), BF16),
            dma((2,)),
            v((128, MODEL), BF16),
            v((SMALL_AT, 8, 128), F32),
            v((64, WIDE), BF16),
            v((16, 128), BF16),
            v((BLOCKS, 8, 128), F32),
            dma((SMALL_AT,)), dma((BLOCKS,)),
            dma((4,)), dma((4,)),
            dma((2, 20)), dma((2, PLANE)), dma((PLANE,)), dma((PLANE,)),
            dma((CHIPS,)), dma((2 * SMALL_AT,)),
            dma((2 * SMALL_AT,)), dma((2 * SMALL_AT,)),
            v((16, 128), F32),
            *Reduce.scratch(CHUNKS),
            *HeadSum.scratch(),
            *HeadSum.scratch(),
        ],
        3,
        (21, 22),
    )


def place_kernel(
    all_ref, back_ref, ffn_ref, hid_ref, ghid_ref, tok_ref, gain_ref, mixer_ref, ffn_w, small_ref,
    out_ref, dtok_ref, bc_ref, kv_ref, x_w, z_w, q_w, dt_w, out_w, attn_w, gate_w, up_w, down_w,
    xtaps_ref, bctaps_ref, bias_ref, rate_ref, skip_ref, one_ref, two_ref,
):
    for c in range(2):
        for p in range(all_ref.shape[1]):
            for zh in range(2):
                rows = slice(p * 64, (p + 1) * 64)
                at, turned = (zh * 2 + c) * 128, (c * 2 + zh) * 128
                bc_ref[rows, at : at + 128] = all_ref[c, p, zh, 0, :, :128].astype(F32)
                kv_ref[rows, turned : turned + 128] = all_ref[c, p, zh, 0, :, 128:].astype(F32)
    for r in range(0, out_ref.shape[0], 32):
        rows = slice(r, r + 32)
        out_ref[rows, :] = (hid_ref[rows, :] + ffn_ref[rows, :].astype(F32)).astype(BF16)
        x = tok_ref[rows, :].astype(F32)
        scale = lax.rsqrt(jnp.mean(x * x, 1, keepdims=True) + EPSILON)
        n = x * scale
        scaled = back_ref[rows, :].astype(F32) * gain_ref[0:1, :]
        along = jnp.mean(n * scaled, 1, keepdims=True)
        dtok_ref[rows, :] = ghid_ref[rows, :] + scale * (scaled - n * along)

    @pl.when(pl.program_id(0) == 0)
    def _():
        at = WIDE
        for ref in (x_w, z_w, q_w):
            ref[...] = mixer_ref[:, at : at + ref.shape[1]]
            at += ref.shape[1]
        dt_w[...] = jnp.transpose(mixer_ref[:, at : at + 128])[:HEADS, :]
        at += WIDE
        for ref in (out_w, attn_w):
            ref[...] = mixer_ref[:, at : at + ref.shape[1]]
            at += ref.shape[1]
        at = 0
        for ref in (down_w, gate_w, up_w):
            ref[...] = ffn_w[:, at : at + ref.shape[1]]
            at += ref.shape[1]
        lane = lax.broadcasted_iota(jnp.int32, (1, 128), 1)
        lines = [jnp.zeros((1, 128), F32)] * 3
        for h in range(4):

            def row(k):
                piece = small_ref[h % 2, h // 2 * SMALL_AT + k // 8].astype(F32)
                return piece[k % 8 : k % 8 + 1, :]

            for k in range(CONV):
                for g in range(GROUPS):
                    cols = slice(h * INNER + g * 128, h * INNER + (g + 1) * 128)
                    xtaps_ref[k : k + 1, cols] = row(4 + GROUPS * k + g)
                bctaps_ref[k : k + 1, h * 128 : (h + 1) * 128] = row(28 + k)
                cols = pl.ds((4 * h + k) * 128, 128)
                one_ref[cols] = row(k).reshape(128)
                two_ref[cols] = row(32 + k).reshape(128)
            for k in range(3):
                shift = (h - k) * HEADS % 128
                moved = pltpu.roll(row(36), shift, 1) if shift else row(36)
                mine = (lane >= h * HEADS) & (lane < (h + 1) * HEADS)
                lines[k] = jnp.where(mine, moved, lines[k])
        for ref, line in zip((bias_ref, rate_ref, skip_ref), lines):
            ref[...] = line.reshape(128)[: 4 * HEADS]


def place(gathered, back, ffn, hidden_in, ghid, tokens, gain, mixer_w, ffn_w, small):
    steps = 4
    spans, rows, ff = PLANE * NZ // steps, ROWS // steps, ffn_w.shape[1] // 3
    half = steps // NZ
    s = jax.ShapeDtypeStruct

    def whole(shape):
        return pl.BlockSpec(shape, lambda i: (0,) * len(shape))

    token = pl.BlockSpec((rows, MODEL), lambda i: (i, 0))
    wide = pl.BlockSpec((64 * spans, 512), lambda i: (i, 0))
    kept = [
        (64, INNER), (64, INNER), (64, 256), (HEADS, 64), (64, INNER), (64, 256), (64, ff), (64, ff),
        (64, ff), (CONV, 4 * INNER), (CONV, BC), (4 * HEADS,), (4 * HEADS,), (4 * HEADS,), (MODEL,), (MODEL,),
    ]
    return pl.pallas_call(
        place_kernel,
        name="place",
        out_shape=(
            s((ROWS, MODEL), BF16), s((ROWS, MODEL), F32), s((MODEL, 512), F32),
            s((MODEL, 512), F32), *[s(shape, F32) for shape in kept],
        ),
        grid=(steps,),
        in_specs=[
            pl.BlockSpec((2, spans, 2, 1, 64, WIDE), lambda i: (0, i % half, 0, i // half, 0, 0)),
            token, token, token, token, token, whole((1, MODEL)), whole(mixer_w.shape),
            whole(ffn_w.shape), whole(small.shape),
        ],
        out_specs=(token, token, wide, wide, *[whole(shape) for shape in kept]),
        compiler_params=pltpu.CompilerParams(vmem_limit_bytes=VMEM_LIMIT),
    )(
        gathered.reshape(2, PLANE, 2, NZ, 64, WIDE), back, ffn, hidden_in, ghid, tokens, gain,
        mixer_w, ffn_w, small,
    )


def on_device(
    tokens, segment_ids, cotangent, norm1_gain, x_weight, z_weight, bc_weight, dt_weight,
    x_conv, bc_conv, dt_bias, decay_rate, skip_gain, out_weight, query_weight, kv_weight,
    attn_weight, norm2_gain, gate_weight, up_weight, down_weight,
):
    heads = decay_rate.shape[0]
    positions = block_index() * ROWS + jnp.arange(ROWS)
    half_dim = HEAD_DIM // 2
    frequency = ROPE_BASE ** (-(jnp.arange(half_dim).astype(F32) * 2.0 / HEAD_DIM))
    angles = positions.astype(F32)[:, None] * frequency[None, :]
    cosine, sine = jnp.cos(angles), jnp.sin(angles)
    cosine = jnp.concatenate([cosine, cosine], 1)
    sine = jnp.concatenate([-sine, sine], 1)
    dt_t, seg = dt_weight.T, segment_ids.reshape(1, ROWS)
    bias, rate, skip = (v.reshape(1, heads) for v in (dt_bias, decay_rate, skip_gain))
    gain_one, gain_two = norm1_gain.reshape(1, MODEL), norm2_gain.reshape(1, MODEL)

    (
        normed_t, cot_t, queries, x_pre, bc_pre, dt_raw, z_val, attended, lse, kv_all, edge_in,
        gated, core, x_act, bc_act, state_in, normed_near, cot_near, attended_low,
    ) = mixer_forward(
        tokens, cotangent, gain_one, query_weight, kv_weight, x_weight, bc_weight, dt_t, z_weight,
        cosine, sine, seg, x_conv, bc_conv, bias, rate, skip,
    )
    (
        hidden_in, two_t, grad_gate, grad_up, hidden, ffn_part, grad_hidden_in, mix_t, gains_two,
        grad_gated, grad_attended, two_near,
    ) = feed_forward(
        gated, attended_low, tokens, cotangent, gain_two, out_weight, attn_weight, gate_weight,
        up_weight, down_weight,
    )
    (
        grad_query, misc, grad_z, grad_x_pre, grad_dt, grad_x_conv, grad_bc_conv, grad_vectors,
        ffn_w, mix_near,
    ) = mixer_backward(
        queries, grad_attended, attended, lse, seg, kv_all, grad_gated, z_val, core, x_act,
        bc_act, x_pre, bc_pre, edge_in, dt_raw, state_in, bias, x_conv, bc_conv, rate,
        skip, grad_gate, grad_up, hidden, two_t, cot_t, cot_near, mix_t, cosine, sine, two_near,
    )
    mixer_w, gathered, small_sums, grad_normed, ffn_sum = finish(
        misc, grad_x_pre, grad_z, grad_query, grad_dt, gated, attended_low, normed_t, normed_near,
        mix_t, mix_near, ffn_part, tokens, x_weight, z_weight, query_weight, dt_t, grad_x_conv,
        grad_bc_conv, grad_vectors, gains_two, bc_weight, kv_weight,
    )
    (
        output, grad_tokens, bc_w, kv_w, x_w, z_w, q_w, dt_w, out_w, attn_w, gate_w, up_w, down_w,
        x_taps, bc_taps, bias_sum, rate_sum, skip_sum, gain_one_sum, gain_two_sum,
    ) = place(
        gathered, grad_normed, ffn_sum, hidden_in, grad_hidden_in, tokens, gain_one, mixer_w,
        ffn_w, small_sums,
    )
    return (
        output, grad_tokens, gain_one_sum, x_w, z_w, bc_w, dt_w.T, x_taps, bc_taps, bias_sum,
        rate_sum, skip_sum, out_w.T, q_w, kv_w, attn_w.T, gain_two_sum, gate_w, up_w, down_w.T,
    )


def solution(mesh):
    split = Mesh(mesh.devices.reshape(NZ, NX, NY, 2, 2), (*SEQ, "zh", "c"))
    head = ("zh", "c")
    rows, columns, both, turned = P(SEQ, None), P(None, head), P(SEQ, head), P(head, SEQ)
    return jax.shard_map(
        on_device,
        mesh=split,
        in_specs=(
            rows, P(SEQ), rows, P(), columns, columns, P(), columns, columns, P(), P(head),
            P(head), P(head), P(head, None), columns, P(), P(head, None), P(), columns, columns,
            P(head, None),
        ),
        out_specs=(
            rows, rows, P(), both, both, P(), both, P(), P(), P(), P(), P(), turned, both, P(),
            turned, P(), both, both, turned,
        ),
        check_vma=False,
    )
```

```python
import functools

import jax
import jax.numpy as jnp
from jax import lax
from jax.experimental import pallas as pl
from jax.experimental.pallas import tpu as pltpu
from jax.sharding import Mesh
from jax.sharding import PartitionSpec as P

SSM_DIM = 64
STATE = 256
CONV = 4
KVHEADS = 2
HEAD_DIM = 128
NZ, NX, NY = 2, 4, 4
BLOCKS = NZ * NX * NY
CHIPS = 2 * BLOCKS
ROWS = 256
MODEL = 2048
SEQ = ("zl", "x", "y")
EPSILON = 1e-05
ROPE_BASE = 100000000000.0
HIGHEST = lax.Precision.HIGHEST
MESH = pl.DeviceIdType.MESH
BF16, F32 = jnp.bfloat16, jnp.float32
MASKED = -1e30
LOG2E = 1.4426950408889634
VMEM_LIMIT = 56 * 2**20


def block_index():
    return (lax.axis_index("zl") * NX + lax.axis_index("x")) * NY + lax.axis_index("y")


def block_at(s):
    return {"zl": s // (NX * NY), "x": (s // NY) % NX, "y": s % NY}


PLANE = NX * NY


def plane_peer(k, sign, stride=13):
    o = 1 + (k * stride) % (PLANE - 1)
    dx, dy = o // NY, o % NY
    x, y = lax.axis_index("x"), lax.axis_index("y")
    if sign < 0:
        dx, dy = NX - dx, NY - dy
    x, y = (x + dx) % NX, (y + dy) % NY
    return x * NY + y, {"x": x, "y": y}


def signal(sem, where):
    pl.semaphore_signal(sem, inc=1, device_id=where, device_id_type=MESH)


def remote(src, dst, send, recv, where):
    return pltpu.make_async_remote_copy(src, dst, send, recv, device_id=where, device_id_type=MESH)


def over(start, stop, body):
    def step(i, carry):
        body(i)
        return carry

    lax.fori_loop(start, stop, step, 0)


def dot(a, b, left=1, right=0):
    return lax.dot_general(
        a, b, (((left,), (right,)), ((), ())), preferred_element_type=F32
    )


def vmem(n):
    return [pl.BlockSpec(memory_space=pltpu.VMEM)] * n


def params(collective_id):
    return pltpu.CompilerParams(
        collective_id=collective_id, has_side_effects=True, vmem_limit_bytes=VMEM_LIMIT
    )


HEADS = 12
INNER = HEADS * SSM_DIM
GROUPS = INNER // 128
BC = 2 * STATE
SCAN_ROWS = INNER // BLOCKS
EDGE_WIDE = INNER + BC + 128
GRAD_EDGE = INNER + 128


def two_parts(v):
    high = v.astype(BF16)
    return high, (v - high.astype(F32)).astype(BF16)


def low_lanes(rows):
    return lax.broadcasted_iota(jnp.int32, (rows, 128), 1) < SSM_DIM


def widen(v, g):
    low = low_lanes(v.shape[0])
    return jnp.where(low, v[:, 2 * g : 2 * g + 1], v[:, 2 * g + 1 : 2 * g + 2])


def per_head(v, g):
    lane = lax.broadcasted_iota(jnp.int32, v.shape, 1)
    first = jnp.sum(jnp.where(lane < SSM_DIM, v, 0.0), 1, keepdims=True)
    second = jnp.sum(jnp.where(lane < SSM_DIM, 0.0, v), 1, keepdims=True)
    return jnp.where(lane == 2 * g, first, jnp.where(lane == 2 * g + 1, second, 0.0))


def triangle():
    row = lax.broadcasted_iota(jnp.int32, (ROWS, ROWS), 0)
    col = lax.broadcasted_iota(jnp.int32, (ROWS, ROWS), 1)
    return (col <= row).astype(F32).astype(BF16)


def running(v, lower, side):
    high, low = two_parts(v)
    middle, lowest = two_parts(v - high.astype(F32))
    return (
        dot(lower, high, side, 0) + dot(lower, middle, side, 0) + dot(lower, lowest, side, 0)
    )


def sigmoid(v):
    return 1.0 / (1.0 + jnp.exp(-v))


def softplus(v):
    return jnp.maximum(v, 0.0) + jnp.log(1.0 + jnp.exp(-jnp.abs(v)))


def lane_block(g):
    return pl.ds(pl.multiple_of(g * 128, 128), 128)


def decays(dt_ref, vec_ref, seg_ref, segx_ref, lower):
    pre = dt_ref[...] + vec_ref[0:1, :]
    step = softplus(pre)
    total = running(-step * vec_ref[1:2, :] * LOG2E, lower, 1)
    last = total[ROWS - 1 : ROWS, :]
    seg = seg_ref[...]
    seg_last, before = seg[ROWS - 1 : ROWS, :], segx_ref[7:8, :]
    carry = jnp.where(seg == seg_last, jnp.exp2(last - total), 0.0)
    entry = jnp.where(seg == before, jnp.exp2(total), 0.0)
    through = jnp.where(seg_last == before, jnp.exp2(last), 0.0)
    return pre, step, total, carry, entry, through


def conv_group(ext_ref, segx_ref, seg_ref, taps_ref, cols):
    total, inputs = None, []
    for k in range(CONV):
        same = segx_ref[pl.ds(5 + k, ROWS), :] == seg_ref[...]
        v = jnp.where(same, ext_ref[pl.ds(5 + k, ROWS), cols], 0.0)
        inputs.append(v)
        term = taps_ref[k : k + 1, cols] * v
        total = term if total is None else total + term
    return total, inputs


def by_fours(body):
    def four(i):
        for k in range(4):
            body(i * 4 + k)

    over(0, BLOCKS // 4, four)


def scan_message(msg_ref, state_ref, through):
    high = through.astype(BF16)
    rest = through - high.astype(F32)
    middle = rest.astype(BF16)
    low = rest - middle.astype(F32)
    extra = jnp.concatenate([high.astype(F32), middle.astype(F32), low, jnp.zeros((5, 128), F32)], 0)
    extra = jnp.concatenate([extra, jnp.zeros((8, STATE - 128), F32)], 1)

    def fill(b):
        rows = state_ref[pl.ds(pl.multiple_of(b * SCAN_ROWS, 8), SCAN_ROWS), :]
        msg_ref[b] = jnp.concatenate([rows, extra], 0).astype(BF16)

    by_fours(fill)


class Scan:
    def __init__(self, reverse, me, msg, got, back, out, send, recv):
        self.reverse, self.me = reverse, me
        self.msg, self.got, self.back, self.out = msg, got, back, out
        self.send, self.recv = send, recv

    def there(self, o):
        d = (self.me + o) % BLOCKS
        return remote(
            self.msg.at[d], self.got.at[self.me], self.send.at[0, o], self.recv.at[0, o],
            block_at(d),
        )

    def arrived(self, phase, dst, o):
        s = (self.me + BLOCKS - o) % BLOCKS
        return remote(
            dst.at[s], dst.at[s], self.send.at[phase, o], self.recv.at[phase, o], block_at(s)
        )

    def start(self):
        over(1, BLOCKS, lambda o: self.there(o).start())
        self.got[self.me] = self.msg[self.me]

    def turn(self):
        me = self.me
        over(1, BLOCKS, lambda o: self.arrived(0, self.got, o).wait_recv())
        lane = lax.broadcasted_iota(jnp.int32, (SCAN_ROWS, 128), 1)
        row = lax.broadcasted_iota(jnp.int32, (SCAN_ROWS, 128), 0) + me * SCAN_ROWS
        at_head = (row >= lane * SSM_DIM) & (row < lane * SSM_DIM + SSM_DIM)

        def scan(i, state):
            blocks, messages, factors = [], [], []
            for n in range(4):
                k = BLOCKS - 1 - (4 * i + n) if self.reverse else 4 * i + n
                message = self.got[k].astype(F32)
                row = message[SCAN_ROWS : SCAN_ROWS + 1, :128]
                row += message[SCAN_ROWS + 1 : SCAN_ROWS + 2, :128]
                row += message[SCAN_ROWS + 2 : SCAN_ROWS + 3, :128]
                blocks.append(k)
                messages.append(message)
                factors.append(jnp.sum(jnp.where(at_head, row, 0.0), 1, keepdims=True))
            for k, message, through in zip(blocks, messages, factors):
                self.back[k] = jnp.concatenate([state, jnp.zeros((8, STATE), F32)], 0).astype(BF16)
                state = through * state + message[:SCAN_ROWS]
            for k in blocks:
                pl.when(k != me)(lambda: self.returned(k).start())
            return state

        lax.fori_loop(0, BLOCKS // 4, scan, jnp.zeros((SCAN_ROWS, STATE), F32))
        self.out[me] = self.back[me]

    def returned(self, k):
        o = (k + BLOCKS - self.me) % BLOCKS
        return remote(
            self.back.at[k], self.out.at[self.me], self.send.at[1, o], self.recv.at[1, o],
            block_at(k),
        )

    def finish(self, state_ref):
        over(1, BLOCKS, lambda o: self.arrived(1, self.out, o).wait_recv())

        def fill(b):
            rows = self.out[b].astype(F32)
            state_ref[pl.ds(pl.multiple_of(b * SCAN_ROWS, 8), SCAN_ROWS), :] = rows[:SCAN_ROWS]

        by_fours(fill)

    def close(self):
        def sent(o):
            self.there(o).wait_send()
            self.returned((self.me + o) % BLOCKS).wait_send()

        over(1, BLOCKS, sent)


def key_segments(block):
    turned = jnp.transpose(block.astype(F32))
    return jnp.concatenate([turned[:, 0:1], turned[:, 1:2]], 0)


def causal_mask(s):
    row = lax.broadcasted_iota(jnp.int32, (ROWS, 2 * ROWS), 0)
    col = lax.broadcasted_iota(jnp.int32, (ROWS, 2 * ROWS), 1) % ROWS
    return jnp.where(row <= col, s, MASKED)


def mixing_bias(seg_ref, segrow_ref):
    row = lax.broadcasted_iota(jnp.int32, (ROWS, ROWS), 0)
    col = lax.broadcasted_iota(jnp.int32, (ROWS, ROWS), 1)
    same = segrow_ref[0:1, :ROWS] == seg_ref[:, 0:1]
    return jnp.where((col <= row) & same, 0.0, MASKED)


WIDE = 256
RELAY, MIDDLE, LAST = 2, 4, 6
AHEAD = 4
OWN = MODEL // NZ


class Reduce:
    def __init__(self, lefts, n, here, r_ref, rz, part, rel, gx, half, gy, out_ref, sems):
        self.lefts, self.n, self.here, self.throttled = lefts, n, here, here == n
        self.r, self.rz, self.part, self.rel = r_ref, rz, part, rel
        self.gx, self.half, self.gy, self.out = gx, half, gy, out_ref
        self.rz_sem, self.rel_sem, self.gx_sem, self.gy_sem = (
            (sems[2 * k], sems[2 * k + 1]) for k in range(4)
        )
        self.zl, self.x, self.y = (lax.axis_index(a) for a in SEQ)
        self.other = {"zl": 1 - self.zl}

    @staticmethod
    def scratch(n):
        v, dma = pltpu.VMEM, pltpu.SemaphoreType.DMA
        return [
            v((n, ROWS, WIDE), BF16),
            v((n, ROWS, WIDE), BF16),
            v((n, 4, 4, 64, WIDE), BF16),
            v((n, 2, 2, 64, WIDE), BF16),
            v((n, 2, 4, 64, WIDE), BF16),
            v((n, 4, 64, WIDE), BF16),
            v((n, 3, 64, WIDE), BF16),
            *[dma((n,))] * 8,
        ]

    def fill(self, arrays, c=0):
        for ref in arrays:
            for k in range(ref.shape[1] // WIDE):
                self.r[c] = ref[:, k * WIDE : (k + 1) * WIDE]
                c += 1

    def right(self, c):
        return remote(
            self.r.at[c], self.rz.at[c], self.rz_sem[0].at[c], self.rz_sem[1].at[c], self.other
        )

    def start(self):
        over(0, AHEAD, lambda c: self.right(c).start())

    def place(self, c, phase, o):
        along_x = c % 2 == phase
        x_to = jnp.where(along_x, (self.x + o) % NX, self.x)
        y_to = jnp.where(along_x, self.y, (self.y + o) % NY)
        return {"x": x_to, "y": y_to}, jnp.where(along_x, x_to, y_to)

    def send(self, src, dst, sem, c, where):
        return remote(src, dst, sem[0].at[c], sem[1].at[c], where)

    def send_second(self, c, o):
        where, d = self.place(c, 1, o)
        return self.send(self.half.at[c, d], self.gy.at[c, o - 1], self.gy_sem, c, where)

    def whole(self, got, sem, c):
        return self.send(got.at[c], got.at[c], sem, c, self.other)

    def product(self, c):
        @pl.when((c + AHEAD < self.here) & self.throttled)
        def _():
            self.right(c + AHEAD).start()

        @pl.when(c < self.here)
        def _():
            self.right(c).wait_recv()

        mine, theirs = self.r[c], self.rz[c]
        even = c % 2 == 0
        ends = [first for _, _, first in self.lefts[1:]] + [self.n]
        for (own, near, first), end in zip(self.lefts, ends):
            @pl.when((c >= first) & (c < end))
            def _():
                for i in range(NX):
                    a = own[pl.ds(pl.multiple_of(self.zl * OWN + i * 256, 256), 256), :]
                    b = near[pl.ds(i * 256, 256), :]
                    tile = (dot(a, mine) + dot(b, theirs)).astype(BF16)
                    for j in range(NY):
                        self.part[c, jnp.where(even, i, j), jnp.where(even, j, i)] = (
                            tile[j * 64 : (j + 1) * 64]
                        )
        _, d = self.place(c, 0, 2)
        for k, o in ((0, 1), (1, 3)):
            src = self.part.at[c, d, pl.ds(2 * k, 2)]
            self.send(src, self.rel.at[c, k], self.rel_sem, c, self.place(c, 0, o)[0]).start()

    def relay(self, c):
        self.whole(self.rel, self.rel_sem, c).wait_recv()
        for k, o in ((0, 1), (1, 3)):
            where, d = self.place(c, 0, o)
            for j in (2 * k, 2 * k + 1):
                total = self.part[c, d, j].astype(F32) + self.rel[c, k, j - 2 * k].astype(F32)
                self.part[c, d, j] = total.astype(BF16)
            self.send(self.part.at[c, d], self.gx.at[c, k], self.gx_sem, c, where).start()

    def middle(self, c):
        self.whole(self.gx, self.gx_sem, c).wait_recv()
        mine = jnp.where(c % 2 == 0, self.x, self.y)
        for j in range(4):
            total = self.part[c, mine, j].astype(F32)
            for k in range(2):
                total += self.gx[c, k, j].astype(F32)
            self.half[c, j] = total.astype(BF16)
        for o in range(1, 4):
            self.send_second(c, o).start()

    def last(self, c):
        self.whole(self.gy, self.gy_sem, c).wait_recv()
        mine = jnp.where(c % 2 == 0, self.y, self.x)
        total = self.half[c, mine].astype(F32)
        for o in range(3):
            total += self.gy[c, o].astype(F32)
        self.out[:, pl.ds(pl.multiple_of(c * WIDE, WIDE), WIDE)] = total

    @property
    def steps(self):
        return self.n + LAST

    def step(self, i):
        for late, do in ((0, self.product), (RELAY, self.relay), (MIDDLE, self.middle), (LAST, self.last)):
            @pl.when((i >= late) & (i < self.n + late))
            def _():
                do(i - late)

    def close(self):
        over(0, self.here, lambda c: self.right(c).wait_send())

        def sent(c):
            self.whole(self.rel, self.rel_sem, c).wait_send()
            self.whole(self.gx, self.gx_sem, c).wait_send()
            self.whole(self.gy, self.gy_sem, c).wait_send()

        over(0, self.n, sent)


class Left:
    def __init__(self, l_ref, lz, sems):
        zl, c = lax.axis_index("zl"), lax.axis_index("c")
        half = OWN // 2
        there = pl.ds(pl.multiple_of((1 - zl) * OWN + c * half, half), half)
        near, other = (pl.ds(pl.multiple_of(k * half, half), half) for k in (c, 1 - c))
        sem = [sems.at[k] for k in range(4)]
        self.out = remote(l_ref.at[there], lz.at[near], sem[0], sem[1], {"zl": 1 - zl})
        self.on = remote(lz.at[near], lz.at[near], sem[2], sem[3], {"c": 1 - c})
        self.back = remote(lz.at[other], lz.at[other], sem[2], sem[3], {"c": 1 - c})

    def start(self):
        self.out.start()

    def pass_on(self):
        self.out.wait_recv()
        self.on.start()

    def finish(self):
        self.back.wait_recv()

    def close(self):
        self.out.wait_send()
        self.on.wait_send()


HEAD_CHUNKS = 4


class HeadSum:
    def __init__(self, x, out, near, pair, far, sems):
        self.x, self.out, self.near, self.pair, self.far = x, out, near, pair, far
        self.near_send, self.near_recv, self.far_send, self.far_recv, self.end_send, self.end_recv = sems
        self.c, zh = lax.axis_index("c"), lax.axis_index("zh")
        self.sibling, self.opposite = {"c": 1 - self.c}, {"zh": 1 - zh}
        self.half = x.shape[0] // 2
        self.rows_each = self.half // HEAD_CHUNKS

    @staticmethod
    def scratch():
        v, dma = pltpu.VMEM, pltpu.SemaphoreType.DMA
        return [*[v((ROWS // 2, MODEL), BF16)] * 3, *[dma((HEAD_CHUNKS,))] * 6]

    def rows(self, core, k):
        return pl.ds(pl.multiple_of(k // 2 * self.half + (2 * core + k % 2) * self.rows_each, 16), self.rows_each)

    def local(self, k):
        return pl.ds(k * self.rows_each, self.rows_each)

    def first(self, k):
        return remote(
            self.x.at[self.rows(1 - self.c, k)], self.near.at[self.local(k)],
            self.near_send.at[k], self.near_recv.at[k], self.sibling,
        )

    def second(self, k):
        return remote(
            self.pair.at[self.local(k)], self.far.at[self.local(k)],
            self.far_send.at[k], self.far_recv.at[k], self.opposite,
        )

    def third(self, k, core):
        rows = self.rows(core, k)
        return remote(
            self.out.at[rows], self.out.at[rows], self.end_send.at[k], self.end_recv.at[k],
            self.sibling,
        )

    def start(self, chunks=range(HEAD_CHUNKS)):
        for k in chunks:
            self.first(k).start()

    def across(self, chunks=range(HEAD_CHUNKS)):
        for k in chunks:
            self.first(k).wait_recv()
            own = self.x[self.rows(self.c, k)].astype(F32)
            self.pair[self.local(k)] = (own + self.near[self.local(k)].astype(F32)).astype(BF16)
            self.second(k).start()

    def join(self, chunks=range(HEAD_CHUNKS)):
        for k in chunks:
            self.second(k).wait_recv()
            total = self.pair[self.local(k)].astype(F32) + self.far[self.local(k)].astype(F32)
            self.out[self.rows(self.c, k)] = total.astype(BF16)
            self.third(k, self.c).start()

    def finish(self, chunks=range(HEAD_CHUNKS)):
        for k in chunks:
            self.third(k, 1 - self.c).wait_recv()

    def close(self):
        for k in range(HEAD_CHUNKS):
            self.first(k).wait_send()
            self.second(k).wait_send()
            self.third(k, self.c).wait_send()


class Loads:
    def __init__(self, pairs, sems, results, out_sems):
        self.copies = {
            id(there): pltpu.make_async_copy(here, there, sems.at[i])
            for i, (here, there) in enumerate(pairs)
        }
        self.results = {
            id(here): pltpu.make_async_copy(here, there, out_sems.at[i])
            for i, (here, there) in enumerate(results)
        }
        self.under_way = []

    def start(self):
        for copy in self.copies.values():
            copy.start()

    def need(self, *refs):
        for ref in refs:
            copy = self.copies.pop(id(ref), None)
            if copy is not None:
                copy.wait()

    def put(self, *refs):
        for ref in refs:
            copy = self.results.pop(id(ref))
            copy.start()
            self.under_way.append(copy)

    def flush(self):
        for copy in self.results.values():
            copy.start()
        for copy in (*self.results.values(), *self.under_way):
            copy.wait()


def fetching(kernel, n_in, n_out, late, large):
    def wrapped(*refs):
        ins, outs, rest = list(refs[:n_in]), list(refs[n_in : n_in + n_out]), refs[n_in + n_out :]
        count = len(late) + len(large)
        buffers, (sems, out_sems) = rest[-2 - count : -2], rest[-2:]
        pairs, results = [], []
        for buffer, i in zip(buffers, late):
            pairs.append((ins[i], buffer))
            ins[i] = buffer
        for buffer, i in zip(buffers[len(late) :], large):
            results.append((buffer, outs[i]))
            outs[i] = buffer
        loads = Loads(pairs, sems, results, out_sems)
        kernel(loads, *ins, *outs, *rest[: -2 - count])
        loads.flush()

    return wrapped


def call(kernel, name, args, late, outs, scratch, collective_id, left=()):
    anywhere, here = pl.BlockSpec(memory_space=pl.ANY), pl.BlockSpec(memory_space=pltpu.VMEM)
    shapes = [jax.ShapeDtypeStruct(*o) for o in outs]
    large = [i for i, o in enumerate(shapes) if o.size >= 2**14]
    dma = pltpu.SemaphoreType.DMA
    return pl.pallas_call(
        fetching(kernel, len(args), len(outs), late, large),
        name=name,
        out_shape=tuple(shapes),
        in_specs=[anywhere if i in (*late, *left) else here for i in range(len(args))],
        out_specs=tuple(anywhere if i in large else here for i in range(len(outs))),
        scratch_shapes=[
            *scratch,
            *[pltpu.VMEM(args[i].shape, args[i].dtype) for i in late],
            *[pltpu.VMEM(shapes[i].shape, shapes[i].dtype) for i in large],
            dma((max(len(late), 1),)),
            dma((max(len(large), 1),)),
        ],
        compiler_params=params(collective_id),
    )(*args)


def spread_small(seg, bias, rate, skip, seg_ref, segrow_ref, vec_ref, skip_ref):
    row = seg[...].astype(F32)
    seg_ref[...] = jnp.transpose(jnp.broadcast_to(row, (128, ROWS)))
    segrow_ref[...] = jnp.broadcast_to(jnp.concatenate([row, row], 1), segrow_ref.shape)
    rest = jnp.zeros((1, 128 - HEADS), F32)
    lines = [jnp.concatenate([ref[...], rest], 1) for ref in (bias, rate, skip)]
    vec_ref[...] = jnp.concatenate([*lines, jnp.zeros((5, 128), F32)], 0)
    for g in range(GROUPS):
        skip_ref[:, g * 128 : (g + 1) * 128] = jnp.broadcast_to(widen(lines[2], g), (8, 128))


def small_scratch():
    return [
        pltpu.VMEM((ROWS, 128), F32),
        pltpu.VMEM((8, 2 * ROWS), F32),
        pltpu.VMEM((8, 128), F32),
        pltpu.VMEM((8, INNER), F32),
    ]


def spread_dt(dt_w, wide_ref):
    wide_ref[16:, :] = jnp.zeros((112, MODEL), BF16)
    rows = jnp.concatenate([dt_w[...].astype(F32), jnp.zeros((16 - HEADS, MODEL), F32)], 0)
    wide_ref[:16, :] = rows.astype(BF16)


def turn_pairs(v, cosine, sine, direction):
    return v * cosine + pltpu.roll(v, HEAD_DIM // 2, 1) * (sine * direction)


def transpose_to(out_ref, ref):
    for k in range(ref.shape[1] // 256):
        out_ref[k * 256 : (k + 1) * 256, :] = jnp.transpose(ref[:, k * 256 : (k + 1) * 256])


def feed_forward_kernel(
    loads, gated_ref, att_ref, tok_ref, cot_ref, gain_ref, out_w, attn_w, gate_w, up_w, down_w,
    hid_ref, ft_ref, dgate_ref, dup_ref, hidden_ref, ffn_ref, ghid_ref, mt_ref, gain_out,
    gg_ref, do_ref, ftz_ref,
    x_ref, sum_ref, back_ref, back_sum, normed, mix_ref, left_sem, *sums,
):
    loads.start()
    n_sum = len(HeadSum.scratch())
    first = HeadSum(x_ref, sum_ref, *sums[:3], sums[3:n_sum])
    second = HeadSum(back_ref, back_sum, *sums[n_sum : n_sum + 3], sums[n_sum + 3 :])
    barrier = pltpu.get_barrier_semaphore()
    other_z = {"zl": 1 - lax.axis_index("zl")}
    signal(barrier, first.sibling)
    signal(barrier, first.opposite)
    signal(barrier, other_z)
    pl.semaphore_wait(barrier, 3)
    left = Left(ft_ref, ftz_ref, left_sem)
    halves = [(slice(g * 128, (g + 1) * 128), (2 * g, 2 * g + 1)) for g in range(2)]
    loads.need(out_w, attn_w)
    for rows, chunks in halves:
        x_ref[rows, :] = (
            dot(gated_ref[rows, :], out_w[...]) + dot(att_ref[rows, :], attn_w[...])
        ).astype(BF16)
        first.start(chunks)
    first.across()

    wide = 256
    loads.need(cot_ref, down_w)
    for k in range(0, hidden_ref.shape[1], wide):
        ghid_ref[:, k : k + wide] = dot(cot_ref[...], down_w[k : k + wide, :], 1, 1)
    loads.need(tok_ref, gate_w, up_w)

    def norm(half, chunks):
        first.join(chunks)
        first.finish(chunks)
        for r in range(half.start, half.stop, 32):
            rows = slice(r, r + 32)
            x = tok_ref[rows, :].astype(F32) + sum_ref[rows, :].astype(F32)
            hid_ref[rows, :] = x
            scale = lax.rsqrt(jnp.mean(x * x, 1, keepdims=True) + EPSILON)
            normed[rows, :] = (x * scale * gain_ref[0:1, :]).astype(BF16)

    def feed(rows, chunks):
        for k in range(0, hidden_ref.shape[1], wide):
            cols = slice(k, k + wide)
            n = normed[rows, :]
            gate, up = dot(n, gate_w[:, cols]), dot(n, up_w[:, cols])
            grad = ghid_ref[rows, cols]
            sig = sigmoid(gate)
            act = gate * sig
            hidden_ref[rows, cols] = (act * up).astype(BF16)
            dgate_ref[rows, cols] = (grad * up * sig * (1.0 + gate * (1.0 - sig))).astype(BF16)
            dup_ref[rows, cols] = (grad * act).astype(BF16)
        back_ref[rows, :] = (
            dot(dgate_ref[rows, :], gate_w[...], 1, 1) + dot(dup_ref[rows, :], up_w[...], 1, 1)
        ).astype(BF16)
        second.start(chunks)

    def norm_back(half, chunks):
        second.join(chunks)
        second.finish(chunks)
        for r in range(half.start, half.stop, 32):
            rows = slice(r, r + 32)
            x = hid_ref[rows, :]
            scale = lax.rsqrt(jnp.mean(x * x, 1, keepdims=True) + EPSILON)
            n = x * scale
            grad = back_sum[rows, :].astype(F32)
            scaled = grad * gain_ref[0:1, :]
            along = jnp.mean(n * scaled, 1, keepdims=True)
            total = cot_ref[rows, :].astype(F32) + scale * (scaled - n * along)
            ghid_ref[rows, :] = total
            mix_ref[rows, :] = total.astype(BF16)
            gains = jnp.sum(grad * n, 0, keepdims=True)
            gain_out[0:1, :] = gains if r == 0 else gain_out[0:1, :] + gains

    (rows_a, chunks_a), (rows_b, chunks_b) = halves
    norm(rows_a, chunks_a)
    feed(rows_a, chunks_a)
    norm(rows_b, chunks_b)
    second.across(chunks_a)
    loads.put(hid_ref)
    feed(rows_b, chunks_b)
    loads.put(hidden_ref, dgate_ref, dup_ref)
    second.across(chunks_b)
    transpose_to(ft_ref, normed)
    left.start()
    loads.put(ft_ref)
    ffn_ref[...] = dot(hidden_ref[...], down_w[...]).astype(BF16)
    loads.put(ffn_ref)
    norm_back(rows_a, chunks_a)
    norm_back(rows_b, chunks_b)
    loads.put(ghid_ref)
    grad_att = dot(mix_ref[...], attn_w[...], 1, 1).astype(BF16)
    for h in range(2):
        do_ref[h * ROWS : (h + 1) * ROWS, :] = grad_att[:, h * HEAD_DIM : (h + 1) * HEAD_DIM]
    gg_ref[...] = dot(mix_ref[...], out_w[...], 1, 1)
    loads.put(gg_ref, do_ref)
    left.pass_on()
    transpose_to(mt_ref, mix_ref)
    loads.put(mt_ref)
    first.close()
    second.close()
    left.finish()
    left.close()


def feed_forward(*args):
    v = pltpu.VMEM
    ff = args[7].shape[1]
    return call(
        feed_forward_kernel, "feed_forward", args, (2, 3, 5, 6, 7, 8, 9),
        [
            ((ROWS, MODEL), F32),
            ((MODEL, ROWS), BF16),
            ((ROWS, ff), BF16),
            ((ROWS, ff), BF16),
            ((ROWS, ff), BF16),
            ((ROWS, MODEL), BF16),
            ((ROWS, MODEL), F32),
            ((MODEL, ROWS), BF16),
            ((8, MODEL), F32),
            ((ROWS, INNER), F32),
            ((2 * ROWS, HEAD_DIM), BF16),
            ((OWN, ROWS), BF16),
        ],
        [
            *[v((ROWS, MODEL), BF16)] * 6,
            pltpu.SemaphoreType.DMA((4,)),
            *HeadSum.scratch(),
            *HeadSum.scratch(),
        ],
        4,
    )


EARLY = 6


def mixer_forward_kernel(
    loads, tok_ref, cot_ref, gain_ref, q_w, kv_w, x_w, bc_w, dt_w, z_w, cos_ref, sin_ref, seg,
    xtaps_ref, bctaps_ref, bias, rate, skip,
    nt_ref, ct_ref, q_ref, x_ref, bc_ref, dt_ref, z_ref,
    att_ref, lse_ref, kv_ref, edge_out, gated_ref, core_ref, xact_ref, bcact_ref, state_ref,
    ntz_ref, ctz_ref, attlow_ref,
    m_ref, l_ref, acc_ref, xext, bcext, segx, local, msg, got, back, result, bias_ref, cb_ref,
    cumt_ref, normed, own_ref, edge_ref, kv_cols, seg_ref, segrow_ref, vec_ref, skip_ref, dt_wide,
    send_sem, recv_sem, sib_send, sib_recv, edge_sem, scan_send, scan_recv, left_sem, kv_sem,
):
    me, c, zl = block_index(), lax.axis_index("c"), lax.axis_index("zl")
    at = me % PLANE
    sibling = {"c": 1 - c}
    kv_at = (c * KVHEADS + lax.axis_index("zh")) * HEAD_DIM
    kv_copy = pltpu.make_async_copy(
        kv_w.at[:, pl.ds(pl.multiple_of(kv_at, HEAD_DIM), HEAD_DIM)], kv_cols, kv_sem
    )
    loads.start()
    kv_copy.start()
    barrier = pltpu.get_barrier_semaphore()
    over(1, BLOCKS, lambda o: signal(barrier, block_at((me + o) % BLOCKS)))
    signal(barrier, sibling)

    spread_small(seg, bias, rate, skip, seg_ref, segrow_ref, vec_ref, skip_ref)
    loads.need(tok_ref)
    for r in range(0, ROWS, 32):
        rows = slice(r, r + 32)
        v = tok_ref[rows, :].astype(F32)
        scale = lax.rsqrt(jnp.mean(v * v, 1, keepdims=True) + EPSILON)
        normed[rows, :] = (v * scale * gain_ref[0:1, :]).astype(BF16)
    n = normed[...]
    loads.need(x_w, bc_w)
    x_ref[...] = dot(n, x_w[...]).astype(BF16)
    bc_ref[...] = dot(n, bc_w[...]).astype(BF16)
    edge_ref[:, :INNER] = x_ref[ROWS - 16 :, :]
    edge_ref[:, INNER : INNER + BC] = bc_ref[ROWS - 16 :, :]
    edge_ref[:, INNER + BC :] = seg_ref[ROWS - 16 :, :].astype(BF16)
    pl.semaphore_wait(barrier, BLOCKS)

    def block_copy(src, j, send, where):
        return remote(src, kv_ref.at[c, j], send_sem.at[send], recv_sem.at[j], where)

    def arrival(j):
        return block_copy(own_ref, j, 0, sibling)

    to_sibling = lambda j, src: remote(
        src, kv_ref.at[c, j], sib_send.at[j], sib_recv.at[j], sibling
    )
    from_sibling = lambda j: remote(
        kv_ref.at[1 - c, j], kv_ref.at[1 - c, j], sib_send.at[j], sib_recv.at[j], sibling
    )
    across = block_copy(own_ref, me, PLANE - 1, {"zl": 1 - zl})

    def own_copy(k, wait):
        d, where = plane_peer(k, 1, 8)

        @pl.when(d > at)
        def _():
            copy = block_copy(own_ref, me, k, where)
            copy.wait_send() if wait else copy.start()

    def relay_copy(k, wait):
        copy = block_copy(kv_ref.at[c, at], at, PLANE + k, plane_peer(k, 1, 8)[1])
        copy.wait_send() if wait else copy.start()

    edge_copy = remote(
        edge_ref, edge_out, edge_sem.at[0], edge_sem.at[1], block_at((me + 1) % BLOCKS)
    )
    states = Scan(False, me, msg, got, back, result, scan_send, scan_recv)

    @pl.when(me < BLOCKS - 1)
    def _():
        edge_copy.start()

    cosine, sine = cos_ref[...], sin_ref[...]
    kv_copy.wait()
    raw = dot(n, kv_cols[...])
    turned = turn_pairs(raw, cosine, sine, 1.0)
    own_ref[:ROWS, :] = jnp.where(c == 0, turned, raw).astype(BF16)
    rows = [segrow_ref[0:1, :HEAD_DIM], segrow_ref[0:1, HEAD_DIM : 2 * HEAD_DIM]]
    own_ref[ROWS:, :] = jnp.concatenate([*rows, jnp.zeros((14, HEAD_DIM), F32)], 0).astype(BF16)

    @pl.when(zl == 0)
    def _():
        across.start()

    to_sibling(me, own_ref).start()
    over(0, EARLY, lambda k: own_copy(k, False))
    lefts = [Left(ct_ref, ctz_ref, left_sem.at[0]), Left(nt_ref, ntz_ref, left_sem.at[1])]

    kv_ref[c, me] = own_ref[...]
    spread_dt(dt_w, dt_wide)
    dt_ref[...] = dot(n, dt_wide[...], 1, 1)
    xext[8:, :] = x_ref[...].astype(F32)
    bcext[8:, :] = bc_ref[...].astype(F32)
    segx[8:, :] = seg_ref[...]
    lower = triangle()
    bias_ref[...] = mixing_bias(seg_ref, segrow_ref)

    @pl.when(me > 0)
    def _():
        edge_copy.wait_recv()

    @pl.when(me == 0)
    def _():
        edge_out[...] = jnp.zeros_like(edge_out)

    edge = edge_out[...].astype(F32)[8:]
    xext[:8, :] = edge[:, :INNER]
    bcext[:8, :] = edge[:, INNER : INNER + BC]
    segx[:8, :] = edge[:, INNER + BC :]

    def activate(ext, taps, out):
        def group(g):
            pre, _ = conv_group(ext, segx, seg_ref, taps, lane_block(g))
            out[:, lane_block(g)] = (pre * sigmoid(pre)).astype(BF16)

        over(0, out.shape[1] // 128, group)

    activate(bcext, bctaps_ref, bcact_ref)
    activate(xext, xtaps_ref, xact_ref)

    _, step, total, carry, entry, through = decays(dt_ref, vec_ref, seg_ref, segx, lower)
    cumt_ref[...] = jnp.transpose(total)
    weight = step * carry
    b_low, c_low = bcact_ref[:, :STATE], bcact_ref[:, STATE:]
    for g in range(GROUPS):
        moved = xact_ref[:, g * 128 : (g + 1) * 128].astype(F32) * widen(weight, g)
        local[g * 128 : (g + 1) * 128, :] = dot(moved.astype(BF16), b_low, 0, 0)
    transpose_to(nt_ref, normed)
    loads.need(cot_ref)
    transpose_to(ct_ref, cot_ref)
    for left in lefts:
        left.start()
    scan_message(msg, local, through)
    states.start()
    over(EARLY, PLANE - 1, lambda k: own_copy(k, False))

    @pl.when(zl == 1)
    def _():
        arrival(at).wait_recv()
        to_sibling(at, kv_ref.at[c, at]).start()
        over(0, PLANE - 1, lambda k: relay_copy(k, False))

    cb_ref[...] = dot(c_low, b_low, 1, 1)
    low_lane = lax.broadcasted_iota(jnp.int32, (ROWS, 128), 1) < SSM_DIM
    for g in range(GROUPS):
        cols = slice(g * 128, (g + 1) * 128)
        u = (xact_ref[:, cols].astype(F32) * widen(step, g)).astype(BF16)
        made = []
        for h in (2 * g, 2 * g + 1):
            gap = total[:, h : h + 1] - cumt_ref[h : h + 1, :] + bias_ref[...]
            made.append(dot((jnp.exp2(gap) * cb_ref[...]).astype(BF16), u))
        core_ref[:, cols] = jnp.where(low_lane, made[0], made[1])

    loads.need(q_w)
    for h in range(2):
        raw = dot(n, q_w[:, h * HEAD_DIM : (h + 1) * HEAD_DIM])
        q_ref[h * ROWS : (h + 1) * ROWS, :] = turn_pairs(raw, cosine, sine, 1.0).astype(BF16)
    scale = LOG2E * HEAD_DIM**-0.5
    queries = q_ref[...]
    qseg = segrow_ref[0:1, :]

    def scores_of(j):
        s = dot(kv_ref[0, j, :ROWS], queries, 1, 1) * scale
        return jnp.where(key_segments(kv_ref[0, j, ROWS:]) == qseg, s, MASKED)

    from_sibling(me).wait_recv()
    s = causal_mask(scores_of(me))
    m = jnp.max(s, 0, keepdims=True)
    p = jnp.exp2(s - m)
    m_ref[...] = m
    l_ref[...] = jnp.sum(p, 0, keepdims=True)
    acc_ref[...] = dot(kv_ref[1, me, :ROWS], p.astype(BF16), 0, 0)

    loads.put(nt_ref, ct_ref, q_ref, x_ref, bc_ref, dt_ref, bcact_ref, xact_ref)
    states.turn()
    loads.need(z_w)
    z_ref[...] = dot(n, z_w[...])
    loads.put(z_ref)

    def forward(k):
        q, _ = plane_peer(k, -1, 8)

        def one(j):
            arrival(j).wait_recv()
            to_sibling(j, kv_ref.at[c, j]).start()

        pl.when(q < at)(lambda: one(zl * PLANE + q))
        pl.when(zl == 1)(lambda: one(q))

    def attend(*blocks):
        scores = []
        for j in blocks:
            from_sibling(j).wait_recv()
            scores.append(scores_of(j))
        m_old = m_ref[...]
        m = m_old
        for s in scores:
            m = jnp.maximum(m, jnp.max(s, 0, keepdims=True))
        alpha = jnp.exp2(m_old - m)
        total, acc = l_ref[...] * alpha, acc_ref[...] * alpha
        for j, s in zip(blocks, scores):
            p = jnp.exp2(s - m)
            total += jnp.sum(p, 0, keepdims=True)
            acc += dot(kv_ref[1, j, :ROWS], p.astype(BF16), 0, 0)
        m_ref[...], l_ref[...], acc_ref[...] = m, total, acc

    forward(0)

    @pl.when(zl == 1)
    def _():
        attend(at)

    def step_over(k):
        @pl.when(k + 1 < PLANE - 1)
        def _():
            forward(k + 1)

        q, _ = plane_peer(k, -1, 8)
        pl.when((q < at) & (zl == 1))(lambda: attend(PLANE + q, q))
        pl.when((q < at) & (zl == 0))(lambda: attend(q))
        pl.when((q > at) & (zl == 1))(lambda: attend(q))

    over(0, PLANE - 1, step_over)
    for left in lefts:
        left.pass_on()
    attended = jnp.transpose(acc_ref[...] / l_ref[...])
    att_ref[...] = attended
    for h in range(2):
        attlow_ref[:, h * HEAD_DIM : (h + 1) * HEAD_DIM] = (
            attended[h * ROWS : (h + 1) * ROWS].astype(BF16)
        )
    lse_ref[...] = jnp.broadcast_to(m_ref[...] + jnp.log2(l_ref[...]), lse_ref.shape)

    loads.put(att_ref, kv_ref)
    states.finish(state_ref)
    loads.put(state_ref)
    for g in range(GROUPS):
        cols = slice(g * 128, (g + 1) * 128)
        outer = dot(c_low, state_ref[cols, :].astype(BF16), 1, 1) * widen(entry, g)
        core = core_ref[:, cols] + outer
        core_ref[:, cols] = core
        out = core + skip_ref[0:1, cols] * xact_ref[:, cols].astype(F32)
        z = z_ref[:, cols]
        gated_ref[:, cols] = (out * z * sigmoid(z)).astype(BF16)

    loads.put(gated_ref, core_ref)
    states.close()
    for left in lefts:
        left.finish()
        left.close()
    to_sibling(me, own_ref).wait_send()
    over(0, PLANE - 1, lambda k: own_copy(k, True))

    @pl.when(zl == 0)
    def _():
        across.wait_send()

    @pl.when(zl == 1)
    def _():
        over(0, PLANE - 1, lambda k: relay_copy(k, True))
        over(0, PLANE, lambda j: to_sibling(j, own_ref).wait_send())

    over(0, at, lambda q: to_sibling(zl * PLANE + q, own_ref).wait_send())

    @pl.when(me < BLOCKS - 1)
    def _():
        edge_copy.wait_send()


def mixer_forward(*args):
    wide = 2 * ROWS
    dma = pltpu.SemaphoreType.DMA
    return call(
        mixer_forward_kernel, "mixer_forward", args, (0, 5, 6, 3, 8, 1),
        [
            ((MODEL, ROWS), BF16),
            ((MODEL, ROWS), BF16),
            ((wide, HEAD_DIM), BF16),
            ((ROWS, INNER), BF16),
            ((ROWS, BC), BF16),
            ((ROWS, 128), F32),
            ((ROWS, INNER), F32),
            ((wide, HEAD_DIM), F32),
            ((8, wide), F32),
            ((2, BLOCKS, ROWS + 16, HEAD_DIM), BF16),
            ((16, EDGE_WIDE), BF16),
            ((ROWS, INNER), BF16),
            ((ROWS, INNER), F32),
            ((ROWS, INNER), BF16),
            ((ROWS, BC), BF16),
            ((INNER, STATE), F32),
            ((OWN, ROWS), BF16),
            ((OWN, ROWS), BF16),
            ((ROWS, 2 * HEAD_DIM), BF16),
        ],
        [
            pltpu.VMEM((1, wide), F32),
            pltpu.VMEM((1, wide), F32),
            pltpu.VMEM((HEAD_DIM, wide), F32),
            pltpu.VMEM((ROWS + 8, INNER), F32),
            pltpu.VMEM((ROWS + 8, BC), F32),
            pltpu.VMEM((ROWS + 8, 128), F32),
            pltpu.VMEM((INNER, STATE), F32),
            *[pltpu.VMEM((BLOCKS, SCAN_ROWS + 8, STATE), BF16)] * 4,
            pltpu.VMEM((ROWS, ROWS), F32),
            pltpu.VMEM((ROWS, ROWS), F32),
            pltpu.VMEM((128, ROWS), F32),
            pltpu.VMEM((ROWS, MODEL), BF16),
            pltpu.VMEM((ROWS + 16, HEAD_DIM), BF16),
            pltpu.VMEM((16, EDGE_WIDE), BF16),
            pltpu.VMEM((MODEL, HEAD_DIM), BF16),
            *small_scratch(),
            pltpu.VMEM((128, MODEL), BF16),
            *[dma((BLOCKS,))] * 4,
            dma((2,)),
            dma((2, BLOCKS)),
            dma((2, BLOCKS)),
            dma((2, 4)),
            dma,
        ],
        1,
        (4,),
    )


def mixer_backward_kernel(
    loads, q_ref, do_ref, att_ref, lse_ref, seg, kv_ref, gg_ref, z_ref, core_ref, xact_ref,
    bcact_ref, x_ref, bcown_ref, edge_in, dt_ref, state_ref, bias, xtaps_ref, bctaps_ref,
    rate, skip, dgate_ref, dup_ref, hidden_ref, ft_ref, ct_ref, ctz_ref, mt_ref, cos_ref,
    sin_ref, ftz_ref, gated_ref, attlow_ref,
    dqraw_ref, misc_ref, dz_ref, dx_ref, ddt_ref, dxtaps_ref, dbctaps_ref, dvec_ref,
    w_ref, mtz_ref, outz_ref,
    dkv_ref, dqt_ref, mine, theirs, sib, kvgot, relay_ref, total_ref, xext, bcext, segx, local, msg, got, back, result,
    bias_ref, cb_ref, cumt_ref, g_ref, du_ref, dbc_all, shares, share_got, edge_ref,
    edge_out, enter_ref, gext, dcum_ref, ddtx_ref,
    send_sem, recv_sem, sib_send, sib_recv, edge_sem, scan_send, scan_recv, share_send, share_recv,
    left_sem, outs_ref, outz_sem, outs_sem, owntaps_ref, seg_ref, segrow_ref, vec_ref, skip_ref, *reduce,
):
    me, c, zh, zl = block_index(), *(lax.axis_index(a) for a in ("c", "zh", "zl"))
    head_at = zh * 2 + c
    sibling = {"c": 1 - c}
    at_head = lambda d: {"zh": d // 2, "c": d % 2}
    loads.start()
    barrier = pltpu.get_barrier_semaphore()
    over(1, BLOCKS, lambda o: signal(barrier, block_at((me + o) % BLOCKS)))
    for o in range(1, 4):
        signal(barrier, at_head((head_at + o) % 4))
    pl.semaphore_wait(barrier, BLOCKS + 2)

    at = me % PLANE
    to_sibling = lambda j: remote(
        theirs.at[j], sib.at[j], sib_send.at[j], sib_recv.at[j], sibling
    )

    def to_owner(k, kind):
        q, where = plane_peer(k, -1)
        j = q if kind else zl * PLANE + q
        return remote(
            mine.at[j], kvgot.at[kind, at], send_sem.at[kind, k], recv_sem.at[kind, at], where
        )

    def from_plane(kind, q):
        return remote(
            kvgot.at[kind, q], kvgot.at[kind, q], send_sem.at[kind, 0], recv_sem.at[kind, q],
            sibling,
        )

    across = remote(
        relay_ref, kvgot.at[1, 0], send_sem.at[0, PLANE - 1], recv_sem.at[1, 0], {"zl": 1 - zl}
    )
    states = Scan(True, me, msg, got, back, result, scan_send, scan_recv)
    rs = Reduce(
        [(ct_ref, ctz_ref, 0), (ft_ref, ftz_ref, 4)], 12, 12, *reduce[:7], w_ref, reduce[7:]
    )
    left = Left(mt_ref, mtz_ref, left_sem)
    loads.need(hidden_ref)
    rs.fill([hidden_ref])
    rs.start()
    loads.need(dgate_ref, dup_ref)
    rs.fill([dgate_ref, dup_ref], 4)
    done = 0

    def reduce_some(n):
        nonlocal done
        over(done, done + n, rs.step)
        done += n


    spread_small(seg, bias, rate, skip, seg_ref, segrow_ref, vec_ref, skip_ref)
    lower = triangle()
    edge = edge_in[...].astype(F32)[8:]
    xext[:8, :] = edge[:, :INNER]
    segx[:8, :] = edge[:, INNER + BC :]
    xext[8:, :] = x_ref[...].astype(F32)
    segx[8:, :] = seg_ref[...]
    bc_cols = lane_block(head_at)
    edge_cols = lane_block(head_at + INNER // 128)
    bcext[:8, :] = edge_in[:, edge_cols].astype(F32)[8:]
    bcext[8:, :] = bcown_ref[:, bc_cols].astype(F32)
    owntaps_ref[...] = bctaps_ref[:, bc_cols]
    bias_ref[...] = mixing_bias(seg_ref, segrow_ref)
    pre_dt, step, total, carry, entry, through = decays(dt_ref, vec_ref, seg_ref, segx, lower)
    cumt_ref[...] = jnp.transpose(total)
    b_low, c_low = bcact_ref[:, :STATE], bcact_ref[:, STATE:]
    for g in range(GROUPS):
        cols = slice(g * 128, (g + 1) * 128)
        z = z_ref[:, cols]
        grad = gg_ref[:, cols] * z * sigmoid(z)
        g_ref[:, cols] = grad
        entered = (grad * widen(entry, g)).astype(BF16)
        du_ref[:, cols] = entered.astype(F32)
        local[cols, :] = dot(entered, c_low, 0, 0)
    scan_message(msg, local, through)
    states.start()
    loads.need(ct_ref, ctz_ref, ft_ref, ftz_ref)
    reduce_some(1)

    dcum = jnp.zeros((ROWS, 128), F32)
    dskip = jnp.zeros((8, 128), F32)
    dc = jnp.zeros((ROWS, STATE), F32)
    for g in range(GROUPS):
        cols = slice(g * 128, (g + 1) * 128)
        z, core, x = z_ref[:, cols], core_ref[:, cols], xact_ref[:, cols].astype(F32)
        sig = sigmoid(z)
        out = core + skip_ref[0:1, cols] * x
        dz_ref[:, cols] = (gg_ref[:, cols] * out * sig * (1.0 + z * (1.0 - sig))).astype(BF16)
        grad = g_ref[:, cols]
        dcum += per_head(grad * core, g)
        dskip += per_head(jnp.broadcast_to(jnp.sum(grad * x, 0, keepdims=True), (8, 128)), g)
        dc += dot(du_ref[:, cols].astype(BF16), state_ref[cols, :].astype(BF16))
    dbc_all[:, STATE:] = dc
    loads.put(dz_ref)
    reduce_some(1)

    cb_ref[...] = dot(c_low, b_low, 1, 1)
    low_lane = lax.broadcasted_iota(jnp.int32, (ROWS, 128), 1) < SSM_DIM
    dcb = jnp.zeros((ROWS, ROWS), F32)
    for g in range(GROUPS):
        cols = slice(g * 128, (g + 1) * 128)
        u = xact_ref[:, cols].astype(F32) * widen(step, g)
        u_low, grad = u.astype(BF16), g_ref[:, cols]
        grad_low = grad.astype(BF16)
        made = []
        for i in range(2):
            h = 2 * g + i
            decay = jnp.exp2(total[:, h : h + 1] - cumt_ref[h : h + 1, :] + bias_ref[...])
            mixing = (decay * cb_ref[...]).astype(BF16)
            made.append(dot(mixing, grad_low, 0, 0))
            half = jnp.where(low_lane if i == 0 else ~low_lane, grad, 0.0).astype(BF16)
            dcb += decay * dot(half, u_low, 1, 1)
        du = jnp.where(low_lane, made[0], made[1])
        du_ref[:, cols] = du
        dcum -= per_head(u * du, g)
    dcum_ref[...] = dcum
    reduce_some(1)
    dcb_low = dcb.astype(BF16)
    dbc_all[:, :STATE] = dot(dcb_low, c_low, 0, 0)
    dbc_all[:, STATE:] += dot(dcb_low, b_low)

    loads.need(q_ref, do_ref, att_ref, kv_ref)
    scale = LOG2E * HEAD_DIM**-0.5
    queries, grads = q_ref[...], do_ref[...]
    lse, qseg = lse_ref[0:1, :], segrow_ref[0:1, :]
    high, low = two_parts(grads.astype(F32) * att_ref[...])
    ones = jnp.ones((8, HEAD_DIM), BF16)
    delta = (dot(ones, high, 1, 1) + dot(ones, low, 1, 1))[0:1, :]

    def block(*blocks, own=False):
        change, results = None, []
        for t in blocks:
            keys = kv_ref[0, t, :ROWS]
            s = dot(keys, queries, 1, 1) * scale
            s = jnp.where(key_segments(kv_ref[0, t, ROWS:]) == qseg, s, MASKED)
            if own:
                s = causal_mask(s)
            p = jnp.exp2(s - lse)
            ds = (p * (dot(kv_ref[1, t, :ROWS], grads, 1, 1) - delta)).astype(BF16)
            dk = dot(ds, queries)
            dv = dot(p.astype(BF16), grads)
            part = dot(keys, ds, 0, 0)
            change = part if change is None else change + part
            results.append((jnp.where(c == 0, dk, dv), jnp.where(c == 0, dv, dk)))
        dqt_ref[...] = change if own else dqt_ref[...] + change
        for t, (kept, given) in zip(blocks, results):
            mine[t] = kept.astype(BF16)
            theirs[t] = given.astype(BF16)
            to_sibling(t).start()

    def pair(t):
        to_sibling(t).wait_recv()
        return mine[t].astype(F32) + sib[t].astype(F32)

    block(me, own=True)
    reduce_some(1)
    states.turn()
    loads.need(mt_ref)
    left.start()
    pieces = [gated_ref.at[:, k * WIDE : (k + 1) * WIDE] for k in range(3)] + [attlow_ref]
    fetched = [
        pltpu.make_async_copy(piece, outs_ref.at[k], outs_sem.at[k])
        for k, piece in enumerate(pieces)
    ]
    for copy in fetched:
        copy.start()
    for copy in fetched:
        copy.wait()

    def outs(p):
        return remote(
            outs_ref.at[p], outz_ref.at[p], outz_sem.at[0, p], outz_sem.at[1, p], {"zl": 1 - zl}
        )

    before = done

    @pl.when(zl == 1)
    def _():
        block(at)

    def give(k):
        q, _ = plane_peer(k, -1)

        @pl.when(q < at)
        def _():
            j = zl * PLANE + q
            mine[j] = pair(j).astype(BF16)
            to_owner(k, 0).start()

        @pl.when(zl == 1)
        def _():
            mine[q] = pair(q).astype(BF16)
            to_owner(k, 1).start()

    def step_over(k):
        q, _ = plane_peer(k, -1)
        pl.when((q < at) & (zl == 1))(lambda: block(PLANE + q, q))
        pl.when((q < at) & (zl == 0))(lambda: block(q))
        pl.when((q > at) & (zl == 1))(lambda: block(q))

        @pl.when(k >= 1)
        def _():
            give(k - 1)

        @pl.when((k % 3 == 0) & (k >= 3))
        def _():
            outs(k // 3 - 1).start()

        @pl.when(k % 2 == 1)
        def _():
            rs.step(before + k // 2)

    over(0, PLANE - 1, step_over)
    give(PLANE - 2)
    done += (PLANE - 1) // 2
    reduce_some(1)
    left.pass_on()
    dkv_ref[...] = pair(me)

    @pl.when(zl == 1)
    def _():
        total_ref[...] = pair(at)

    score_scale = HEAD_DIM**-0.5
    dq = jnp.transpose(dqt_ref[...]) * score_scale
    cosine, sine = cos_ref[...], sin_ref[...]
    for h in range(2):
        raw = turn_pairs(dq[h * ROWS : (h + 1) * ROWS], cosine, sine, -1.0)
        dqraw_ref[:, h * HEAD_DIM : (h + 1) * HEAD_DIM] = raw.astype(BF16)

    states.finish(enter_ref)
    dcum = dcum_ref[...]
    dstep = jnp.zeros((ROWS, 128), F32)
    dlast = jnp.zeros((8, 128), F32)
    db = jnp.zeros((ROWS, STATE), F32)
    for g in range(GROUPS):
        cols = slice(g * 128, (g + 1) * 128)
        entering = enter_ref[cols, :]
        entering_low = entering.astype(BF16)
        x = xact_ref[:, cols].astype(F32)
        steps, carries = widen(step, g), widen(carry, g)
        v = x * steps * carries
        dv = dot(b_low, entering_low, 1, 1)
        db += dot(v.astype(BF16), entering_low)
        dcarry = per_head(v * dv, g)
        dcum -= dcarry
        dlast += jnp.broadcast_to(jnp.sum(dcarry, 0, keepdims=True), (8, 128))
        du = du_ref[:, cols] + carries * dv
        dstep += per_head(x * du, g)
        pieces = jnp.sum(entering * state_ref[cols, :], 1, keepdims=True)
        both = jnp.sum(jnp.broadcast_to(pieces, (128, 128)) * head_of_lane_f32(g), 0, keepdims=True)
        dlast += through * both
        g_ref[:, cols] = steps * du + skip_ref[0:1, cols] * g_ref[:, cols]
    dbc_all[:, :STATE] += db
    last_row = lax.broadcasted_iota(jnp.int32, (ROWS, 128), 0) == ROWS - 1
    dcum += jnp.where(last_row, dlast[0:1, :], 0.0)
    da = running(dcum, lower, 0)
    drate = -jnp.sum(step * da, 0, keepdims=True)
    ddt = (dstep - vec_ref[1:2, :] * da) * sigmoid(pre_dt)
    ddt_ref[...] = ddt.astype(BF16)
    dbias = jnp.sum(ddt, 0, keepdims=True)
    dvec_ref[...] = jnp.concatenate([dbias, drate, dskip[0:1, :], jnp.zeros((5, 128), F32)], 0)

    reduce_some(1)

    for d in range(4):
        shares[d] = dbc_all[:, d * 128 : (d + 1) * 128].astype(BF16)
    share = lambda o: remote(
        shares.at[(head_at + o) % 4], share_got.at[o], share_send.at[o], share_recv.at[o],
        at_head((head_at + o) % 4),
    )
    for o in range(1, 4):
        share(o).start()

    def conv_back(ext, taps, grad, cols, out_taps, out_grad):
        pre, inputs = conv_group(ext, segx, seg_ref, taps, cols)
        sig = sigmoid(pre)
        dpre = grad * sig * (1.0 + pre * (1.0 - sig))
        gext[...] = jnp.zeros_like(gext)
        rows = []
        for k in range(CONV):
            rows.append(jnp.sum(dpre * inputs[k], 0, keepdims=True))
            same = segx[pl.ds(5 + k, ROWS), :] == seg_ref[...]
            gext[pl.ds(5 + k, ROWS), :] += jnp.where(same, taps[k : k + 1, cols] * dpre, 0.0)
        out_taps[:, cols] = jnp.concatenate([*rows, jnp.zeros((4, 128), F32)], 0)
        out_grad[...] = gext[...]

    def x_group(g):
        cols = lane_block(g)
        conv_back(xext, xtaps_ref, g_ref[:, cols], cols, dxtaps_ref, ddtx_ref)
        edge_ref[:, cols] = ddtx_ref[:8, :]
        g_ref[:, cols] = ddtx_ref[8:, :]

    over(0, GROUPS, x_group)
    reduce_some(1)
    grad_bc = shares[head_at].astype(F32)
    for o in range(1, 4):
        share(o).wait_recv()
        grad_bc += share_got[o].astype(F32)
    conv_back(bcext, owntaps_ref, grad_bc, slice(0, 128), dbctaps_ref, ddtx_ref)
    edge_ref[:, INNER:] = ddtx_ref[:8, :]
    edge_copy = remote(
        edge_ref, edge_out, edge_sem.at[0], edge_sem.at[1], block_at((me + BLOCKS - 1) % BLOCKS)
    )

    @pl.when(me > 0)
    def _():
        edge_copy.start()

    reduce_some(1)

    def collect(q):
        @pl.when((zl == 1) & (q != at))
        def _():
            from_plane(1, q).wait_recv()
            total_ref[...] += kvgot[1, q].astype(F32)

    over(0, PLANE, collect)

    @pl.when(zl == 1)
    def _():
        relay_ref[...] = total_ref[...].astype(BF16)
        across.start()

    reduce_some(1)

    def collect_own(q):
        from_plane(0, q).wait_recv()
        dkv_ref[...] += kvgot[0, q].astype(F32)

    over(at + 1, PLANE, collect_own)

    @pl.when(zl == 0)
    def _():
        from_plane(1, 0).wait_recv()
        dkv_ref[...] += kvgot[1, 0].astype(F32)

    @pl.when(me < BLOCKS - 1)
    def _():
        edge_copy.wait_recv()

    @pl.when(me == BLOCKS - 1)
    def _():
        edge_out[...] = jnp.zeros_like(edge_out)

    tail = pl.ds(ROWS - 8, 8)
    g_ref[tail, :] += edge_out[:, :INNER]
    ddtx_ref[pl.ds(ROWS, 8), :] += edge_out[:, INNER:]
    dx_ref[...] = g_ref[...].astype(BF16)
    misc_ref[:, :128] = ddtx_ref[8:, :].astype(BF16)
    dkv = dkv_ref[...]
    turned = turn_pairs(dkv * score_scale, cosine, sine, -1.0)
    misc_ref[:, 128:] = jnp.where(c == 0, turned, dkv).astype(BF16)

    reduce_some(rs.steps - done)

    @pl.when(me > 0)
    def _():
        edge_copy.wait_send()

    states.close()
    rs.close()
    left.finish()
    left.close()
    over(0, 4, lambda p: outs(p).wait())
    for o in range(1, 4):
        share(o).wait_send()
    to_sibling(me).wait_send()

    def given(k):
        q, _ = plane_peer(k, -1)

        @pl.when(q < at)
        def _():
            to_sibling(zl * PLANE + q).wait_send()
            to_owner(k, 0).wait_send()

        @pl.when(zl == 1)
        def _():
            to_sibling(q).wait_send()
            to_owner(k, 1).wait_send()

    over(0, PLANE - 1, given)

    @pl.when(zl == 1)
    def _():
        to_sibling(at).wait_send()
        across.wait_send()


def head_of_lane_f32(g):
    row = lax.broadcasted_iota(jnp.int32, (128, 128), 0)
    lane = lax.broadcasted_iota(jnp.int32, (128, 128), 1)
    return (lane == 2 * g + (row >= SSM_DIM).astype(jnp.int32)).astype(F32)


def mixer_backward(*args):
    wide = 2 * ROWS
    dma = pltpu.SemaphoreType.DMA
    v = pltpu.VMEM
    piece = (BLOCKS, ROWS, HEAD_DIM)
    return call(
        mixer_backward_kernel, "mixer_backward", args, (23, 25, 26, 21, 22, 24, 30, 0, 1, 2, 5, 27),
        [
            ((ROWS, 2 * HEAD_DIM), BF16),
            ((ROWS, 256), BF16),
            ((ROWS, INNER), BF16),
            ((ROWS, INNER), BF16),
            ((ROWS, 128), BF16),
            ((8, INNER), F32),
            ((8, 128), F32),
            ((8, 128), F32),
            ((64, 12 * WIDE), F32),
            ((OWN, ROWS), BF16),
            ((4, ROWS, WIDE), BF16),
        ],
        [
            v((ROWS, HEAD_DIM), F32),
            v((HEAD_DIM, wide), F32),
            *[v(piece, BF16)] * 3,
            v((2, PLANE, ROWS, HEAD_DIM), BF16),
            v((ROWS, HEAD_DIM), BF16),
            v((ROWS, HEAD_DIM), F32),
            v((ROWS + 8, INNER), F32),
            v((ROWS + 8, 128), F32),
            v((ROWS + 8, 128), F32),
            v((INNER, STATE), F32),
            *[v((BLOCKS, SCAN_ROWS + 8, STATE), BF16)] * 4,
            v((ROWS, ROWS), F32),
            v((ROWS, ROWS), F32),
            v((128, ROWS), F32),
            v((ROWS, INNER), F32),
            v((ROWS, INNER), F32),
            v((ROWS, BC), F32),
            v((4, ROWS, 128), BF16),
            v((4, ROWS, 128), BF16),
            v((8, GRAD_EDGE), F32),
            v((8, GRAD_EDGE), F32),
            v((INNER, STATE), F32),
            v((ROWS + 8, 128), F32),
            v((ROWS, 128), F32),
            v((ROWS + 8, 128), F32),
            dma((2, PLANE)),
            dma((2, PLANE)),
            dma((BLOCKS,)),
            dma((BLOCKS,)),
            dma((2,)),
            dma((2, BLOCKS)),
            dma((2, BLOCKS)),
            dma((4,)),
            dma((4,)),
            dma((4,)),
            v((4, ROWS, WIDE), BF16),
            dma((2, 4)),
            dma((4,)),
            v((CONV, 128), F32),
            *small_scratch(),
            *Reduce.scratch(12),
        ],
        2,
        (31, 32),
    )


SMALL = 8 * 128
SMALL_AT = 5
CHUNKS = 13
GATHER_FROM = CHUNKS


def finish_kernel(
    loads, misc_ref, dx_ref, dz_ref, dq_ref, ddt_ref, gated_ref, att_ref, nt_ref, ntz_ref, mt_ref,
    mtz_ref, ffn_ref, tok_ref, x_w, z_w, q_w, dt_w, dxtaps_ref, dbctaps_ref, dvec_ref,
    gains_ref, bc_all, kv_all, outz_ref,
    w_ref, all_ref, alls_ref, back_sum, ffn_sum,
    back_ref, near_sem, bc_w, kv_w, column_sem, dt_wide, own_small, mine, esum, egot, e_send, e_recv, z_send, z_recv, w_send, w_recv,
    sib_send, sib_recv, s_send, s_recv, t_send, t_recv, part_ref, *rest,
):
    loads.start()
    me, c, zh = block_index(), lax.axis_index("c"), lax.axis_index("zh")
    chip = zh * BLOCKS + me
    sibling = {"c": 1 - c}

    def chip_at(p):
        return {"zh": p // BLOCKS, **block_at(p % BLOCKS)}

    n_rs = len(Reduce.scratch(CHUNKS))
    rs = Reduce(
        [(nt_ref, ntz_ref, 0), (mt_ref, mtz_ref, 9)], CHUNKS, 9, *rest[:7], w_ref, rest[7:n_rs]
    )
    rest = rest[n_rs:]
    n_sum = len(HeadSum.scratch())
    back = HeadSum(back_ref, back_sum, *rest[:3], rest[3:n_sum])
    rest = rest[n_sum:]
    ffn = HeadSum(ffn_ref, ffn_sum, *rest[:3], rest[3:])

    barrier = pltpu.get_barrier_semaphore()
    over(1, CHIPS, lambda o: signal(barrier, chip_at((chip + o) % CHIPS)))
    signal(barrier, sibling)
    pl.semaphore_wait(barrier, CHIPS)

    head = zh * 2 + c
    columns = [
        pltpu.make_async_copy(
            ref.at[:, pl.ds(pl.multiple_of(k * 128, 128), 128)], here, column_sem.at[i]
        )
        for i, (ref, k, here) in enumerate(((bc_all, head, bc_w), (kv_all, c * 2 + zh, kv_w)))
    ]
    for copy in columns:
        copy.start()
    rs.fill([misc_ref, dx_ref, dz_ref, dq_ref])
    rs.r[8, :, :128] = ddt_ref[...]
    rs.r[8, :, 128:] = jnp.zeros_like(ddt_ref)
    over(0, rs.here, lambda k: rs.right(k).start())
    near = pltpu.make_async_copy(outz_ref, rs.rz.at[pl.ds(9, 4)], near_sem)
    near.start()
    loads.need(nt_ref, ntz_ref)

    def partial(rows):
        total = dot(dx_ref[rows, :], x_w[...], 1, 1)
        total += dot(dz_ref[rows, :], z_w[...], 1, 1)
        total += dot(dq_ref[rows, :], q_w[...], 1, 1)
        total += dot(ddt_ref[rows, :], dt_wide[...])
        total += dot(misc_ref[rows, :128], bc_w[...], 1, 1)
        back_ref[rows, :] = (total + dot(misc_ref[rows, 128:], kv_w[...], 1, 1)).astype(BF16)

    spread_dt(dt_w, dt_wide)
    loads.need(x_w, z_w, q_w)
    for copy in columns:
        copy.wait()
    rs.step(0)
    partial(slice(0, ROWS // 2))
    back.start((0, 1))
    rs.step(1)
    partial(slice(ROWS // 2, ROWS))
    back.start((2, 3))
    loads.need(mt_ref, mtz_ref, ffn_ref, tok_ref, gated_ref, att_ref)
    near.wait()
    rs.fill([gated_ref, att_ref], 9)
    ffn.start()

    at, level = me % PLANE, zh * NZ + lax.axis_index("zl")

    def along_z(o):
        d = (level + o) % 4
        where = {"zh": d // NZ, "zl": d % NZ}
        return remote(mine, all_ref.at[c, at, level], z_send.at[o], z_recv.at[o], where)

    x, y = lax.axis_index("x"), lax.axis_index("y")

    def at_place(i, j):
        return {"x": i, "y": j}, i * NY + j

    def piece(q, h, send, where):
        ref = all_ref.at[c, q, pl.ds(2 * h, 2)]
        return remote(ref, ref, send, w_recv.at[h, q], where)

    def one_way(h, o):
        where = {"x": (x + o) % NX} if h == 0 else {"y": (y + o) % NY}
        return piece(at, h, w_send.at[h, o], where)

    def other_way(h, k, o):
        i, j = ((x + k) % NX, y) if h == 0 else (x, (y + k) % NY)
        where = {"y": (y + o) % NY} if h == 0 else {"x": (x + o) % NX}
        return piece(i * NY + j, h, w_send.at[h, 4 * k + 4 + o], where)

    def arrived(q, h):
        return piece(q, h, w_send.at[0, 0], sibling)

    def to_sibling(q, core):
        return remote(
            all_ref.at[core, q], all_ref.at[core, q], sib_send.at[q], sib_recv.at[q], sibling
        )

    def columns_out():
        for o in range(1, 4):
            along_z(o).wait_recv()
        for o in range(1, 4):
            one_way(0, o).start()
            one_way(1, o).start()
        to_sibling(at, c).start()
        for o in range(1, 4):
            other_way(0, 0, o).start()
            other_way(1, 0, o).start()

    def columns_on():
        for k in range(1, 4):
            for h in range(2):
                i, j = ((x + k) % NX, y) if h == 0 else (x, (y + k) % NY)
                arrived(i * NY + j, h).wait_recv()
                for o in range(1, 4):
                    other_way(h, k, o).start()

    def pass_on(k):
        q, _ = plane_peer(k, -1)
        same_x, same_y = q // NY == x, q % NY == y

        @pl.when(jnp.logical_not(same_y))
        def _():
            arrived(q, 0).wait_recv()

        @pl.when(jnp.logical_not(same_x))
        def _():
            arrived(q, 1).wait_recv()

        to_sibling(q, c).start()

    def share(d):
        return remote(own_small.at[d], egot.at[me], e_send.at[d], e_recv.at[me], block_at(d))

    def shared(s):
        return remote(egot.at[s], egot.at[s], e_send.at[0], e_recv.at[s], block_at(s))

    def small_spread(o):
        d = (chip + o) % CHIPS
        slot = zh * SMALL_AT + me
        return remote(esum, alls_ref.at[c, slot], s_send.at[o], s_recv.at[slot], chip_at(d))

    def small_sibling(slot, core):
        return remote(
            alls_ref.at[core, slot], alls_ref.at[core, slot], t_send.at[slot], t_recv.at[slot],
            sibling,
        )

    def put(row, value):
        own_small[row // 8, row % 8 : row % 8 + 1, :] = value

    def gradient():
        for r in range(0, ROWS, 32):
            rows = pl.ds(r, 32)
            x = tok_ref[rows, :].astype(F32)
            scale = lax.rsqrt(jnp.mean(x * x, 1, keepdims=True) + EPSILON)
            n = x * scale
            grad = back_sum[rows, :].astype(F32)
            gains = jnp.sum(grad * n, 0, keepdims=True)
            for k in range(MODEL // 128):
                piece = gains[:, k * 128 : (k + 1) * 128]
                part_ref[k : k + 1, :] = piece if r == 0 else part_ref[k : k + 1, :] + piece
        own_small[0, :4] = part_ref[pl.ds(head * 4, 4), :]
        for k in range(CONV):
            for g in range(GROUPS):
                put(4 + GROUPS * k + g, dxtaps_ref[k : k + 1, g * 128 : (g + 1) * 128])
            put(28 + k, dbctaps_ref[k : k + 1, :])
            put(32 + k, gains_ref[0:1, lane_block(head * 4 + k)])
        lane = lax.broadcasted_iota(jnp.int32, (1, 128), 1)
        line = jnp.zeros((1, 128), F32)
        for k in range(3):
            moved = dvec_ref[k : k + 1, :] if k == 0 else pltpu.roll(dvec_ref[k : k + 1, :], k * HEADS, 1)
            line = jnp.where((lane >= k * HEADS) & (lane < (k + 1) * HEADS), moved, line)
        put(36, line)
        own_small[4, 5:] = jnp.zeros((3, 128), F32)

        def give(d):
            @pl.when(d != me)
            def _():
                share(d).start()

        over(0, SMALL_AT, give)

    def small_sums():
        @pl.when(me < SMALL_AT)
        def _():
            egot[me] = own_small[me]

            def take(s):
                @pl.when(s != me)
                def _():
                    shared(s).wait_recv()

            over(0, BLOCKS, take)
            total = lax.fori_loop(0, BLOCKS, lambda s, t: t + egot[s], jnp.zeros((8, 128), F32))
            esum[...] = jnp.concatenate([total, jnp.zeros_like(total)], 0).astype(BF16)
            slot = zh * SMALL_AT + me
            alls_ref[c, slot] = esum[...]
            over(1, CHIPS, lambda o: small_spread(o).start())
            small_sibling(slot, c).start()

    def small_pass():
        def one(slot):
            @pl.when(slot != zh * SMALL_AT + me + jnp.where(me < SMALL_AT, 0, CHIPS))
            def _():
                remote(
                    esum, alls_ref.at[c, slot], s_send.at[0], s_recv.at[slot], sibling
                ).wait_recv()
                small_sibling(slot, c).start()

        over(0, 2 * SMALL_AT, one)

    def weights_out():
        mine[...] = w_ref[:, :WIDE].astype(BF16)
        all_ref[c, at, level] = mine[...]
        for o in range(1, 4):
            along_z(o).start()

    def step(i):
        rs.step(i)

        @pl.when(i == LAST)
        def _():
            weights_out()
            back.across()

        @pl.when(i == 8)
        def _():
            ffn.across()

        @pl.when(i == 10)
        def _():
            columns_out()

        @pl.when(i == 11)
        def _():
            back.join()

        @pl.when(i == 14)
        def _():
            columns_on()

        @pl.when(i == 12)
        def _():
            back.finish()
            gradient()

        @pl.when(i == 15)
        def _():
            small_sums()

    over(2, rs.steps, step)
    loads.put(w_ref, back_sum)
    over(0, PLANE - 1, pass_on)
    ffn.join()
    small_pass()
    ffn.finish()
    loads.put(ffn_sum)

    over(0, PLANE, lambda q: to_sibling(q, 1 - c).wait_recv())
    over(0, 2 * SMALL_AT, lambda s: small_sibling(s, 1 - c).wait_recv())
    rs.close()
    back.close()
    ffn.close()
    over(0, PLANE, lambda q: to_sibling(q, c).wait_send())
    over(0, 2 * SMALL_AT, lambda s: small_sibling(s, c).wait_send())
    for h in range(2):
        for o in range(1, 4):
            one_way(h, o).wait_send()
            for k in range(4):
                other_way(h, k, o).wait_send()
    for o in range(1, 4):
        along_z(o).wait_send()

    @pl.when(me < SMALL_AT)
    def _():
        over(1, CHIPS, lambda o: small_spread(o).wait_send())

    def given(d):
        @pl.when(d != me)
        def _():
            share(d).wait_send()

    over(0, SMALL_AT, given)


def finish(*args):
    v, dma = pltpu.VMEM, pltpu.SemaphoreType.DMA
    return call(
        finish_kernel, "finish", args, (7, 8, 13, 14, 15, 9, 10, 11, 12, 5, 6),
        [
            ((64, CHUNKS * WIDE), F32),
            ((2, PLANE, 4, 64, WIDE), BF16),
            ((2, 2 * SMALL_AT, 16, 128), BF16),
            ((ROWS, MODEL), BF16),
            ((ROWS, MODEL), BF16),
        ],
        [
            v((ROWS, MODEL), BF16),
            dma,
            v((MODEL, 128), BF16),
            v((MODEL, 128), BF16),
            dma((2,)),
            v((128, MODEL), BF16),
            v((SMALL_AT, 8, 128), F32),
            v((64, WIDE), BF16),
            v((16, 128), BF16),
            v((BLOCKS, 8, 128), F32),
            dma((SMALL_AT,)), dma((BLOCKS,)),
            dma((4,)), dma((4,)),
            dma((2, 20)), dma((2, PLANE)), dma((PLANE,)), dma((PLANE,)),
            dma((CHIPS,)), dma((2 * SMALL_AT,)),
            dma((2 * SMALL_AT,)), dma((2 * SMALL_AT,)),
            v((16, 128), F32),
            *Reduce.scratch(CHUNKS),
            *HeadSum.scratch(),
            *HeadSum.scratch(),
        ],
        3,
        (21, 22, 23),
    )


def place_kernel(
    all_ref, back_ref, ffn_ref, hid_ref, ghid_ref, tok_ref, gain_ref, mixer_ref, ffn_w, small_ref,
    out_ref, dtok_ref, bc_ref, kv_ref, x_w, z_w, q_w, dt_w, out_w, attn_w, gate_w, up_w, down_w,
    xtaps_ref, bctaps_ref, bias_ref, rate_ref, skip_ref, one_ref, two_ref,
):
    for c in range(2):
        for p in range(all_ref.shape[1]):
            for zh in range(2):
                rows = slice(p * 64, (p + 1) * 64)
                at, turned = (zh * 2 + c) * 128, (c * 2 + zh) * 128
                bc_ref[rows, at : at + 128] = all_ref[c, p, zh, 0, :, :128].astype(F32)
                kv_ref[rows, turned : turned + 128] = all_ref[c, p, zh, 0, :, 128:].astype(F32)
    for r in range(0, out_ref.shape[0], 32):
        rows = slice(r, r + 32)
        out_ref[rows, :] = (hid_ref[rows, :] + ffn_ref[rows, :].astype(F32)).astype(BF16)
        x = tok_ref[rows, :].astype(F32)
        scale = lax.rsqrt(jnp.mean(x * x, 1, keepdims=True) + EPSILON)
        n = x * scale
        scaled = back_ref[rows, :].astype(F32) * gain_ref[0:1, :]
        along = jnp.mean(n * scaled, 1, keepdims=True)
        dtok_ref[rows, :] = ghid_ref[rows, :] + scale * (scaled - n * along)

    @pl.when(pl.program_id(0) == 0)
    def _():
        at = WIDE
        for ref in (x_w, z_w, q_w):
            ref[...] = mixer_ref[:, at : at + ref.shape[1]]
            at += ref.shape[1]
        dt_w[...] = jnp.transpose(mixer_ref[:, at : at + 128])[:HEADS, :]
        at += WIDE
        for ref in (out_w, attn_w):
            ref[...] = mixer_ref[:, at : at + ref.shape[1]]
            at += ref.shape[1]
        at = 0
        for ref in (down_w, gate_w, up_w):
            ref[...] = ffn_w[:, at : at + ref.shape[1]]
            at += ref.shape[1]
        lane = lax.broadcasted_iota(jnp.int32, (1, 128), 1)
        lines = [jnp.zeros((1, 128), F32)] * 3
        for h in range(4):

            def row(k):
                piece = small_ref[h % 2, h // 2 * SMALL_AT + k // 8].astype(F32)
                return piece[k % 8 : k % 8 + 1, :]

            for k in range(CONV):
                for g in range(GROUPS):
                    cols = slice(h * INNER + g * 128, h * INNER + (g + 1) * 128)
                    xtaps_ref[k : k + 1, cols] = row(4 + GROUPS * k + g)
                bctaps_ref[k : k + 1, h * 128 : (h + 1) * 128] = row(28 + k)
                cols = pl.ds((4 * h + k) * 128, 128)
                one_ref[cols] = row(k).reshape(128)
                two_ref[cols] = row(32 + k).reshape(128)
            for k in range(3):
                shift = (h - k) * HEADS % 128
                moved = pltpu.roll(row(36), shift, 1) if shift else row(36)
                mine = (lane >= h * HEADS) & (lane < (h + 1) * HEADS)
                lines[k] = jnp.where(mine, moved, lines[k])
        for ref, line in zip((bias_ref, rate_ref, skip_ref), lines):
            ref[...] = line.reshape(128)[: 4 * HEADS]


def place(gathered, back, ffn, hidden_in, ghid, tokens, gain, mixer_w, ffn_w, small):
    steps = 2
    spans, rows, ff = PLANE * NZ // steps, ROWS // steps, ffn_w.shape[1] // 3
    half = steps // NZ
    s = jax.ShapeDtypeStruct

    def whole(shape):
        return pl.BlockSpec(shape, lambda i: (0,) * len(shape))

    token = pl.BlockSpec((rows, MODEL), lambda i: (i, 0))
    wide = pl.BlockSpec((64 * spans, 512), lambda i: (i, 0))
    kept = [
        (64, INNER), (64, INNER), (64, 256), (HEADS, 64), (64, INNER), (64, 256), (64, ff), (64, ff),
        (64, ff), (CONV, 4 * INNER), (CONV, BC), (4 * HEADS,), (4 * HEADS,), (4 * HEADS,), (MODEL,), (MODEL,),
    ]
    return pl.pallas_call(
        place_kernel,
        name="place",
        out_shape=(
            s((ROWS, MODEL), BF16), s((ROWS, MODEL), F32), s((MODEL, 512), F32),
            s((MODEL, 512), F32), *[s(shape, F32) for shape in kept],
        ),
        grid=(steps,),
        in_specs=[
            pl.BlockSpec((2, spans, 2, 1, 64, WIDE), lambda i: (0, i % half, 0, i // half, 0, 0)),
            token, token, token, token, token, whole((1, MODEL)), whole(mixer_w.shape),
            whole(ffn_w.shape), whole(small.shape),
        ],
        out_specs=(token, token, wide, wide, *[whole(shape) for shape in kept]),
        compiler_params=pltpu.CompilerParams(vmem_limit_bytes=VMEM_LIMIT),
    )(
        gathered.reshape(2, PLANE, 2, NZ, 64, WIDE), back, ffn, hidden_in, ghid, tokens, gain,
        mixer_w, ffn_w, small,
    )


def on_device(
    tokens, segment_ids, cotangent, norm1_gain, x_weight, z_weight, bc_weight, dt_weight,
    x_conv, bc_conv, dt_bias, decay_rate, skip_gain, out_weight, query_weight, kv_weight,
    attn_weight, norm2_gain, gate_weight, up_weight, down_weight,
):
    heads = decay_rate.shape[0]
    positions = block_index() * ROWS + jnp.arange(ROWS)
    half_dim = HEAD_DIM // 2
    frequency = ROPE_BASE ** (-(jnp.arange(half_dim).astype(F32) * 2.0 / HEAD_DIM))
    angles = positions.astype(F32)[:, None] * frequency[None, :]
    cosine, sine = jnp.cos(angles), jnp.sin(angles)
    cosine = jnp.concatenate([cosine, cosine], 1)
    sine = jnp.concatenate([-sine, sine], 1)
    dt_t, seg = dt_weight.T, segment_ids.reshape(1, ROWS)
    bias, rate, skip = (v.reshape(1, heads) for v in (dt_bias, decay_rate, skip_gain))
    gain_one, gain_two = norm1_gain.reshape(1, MODEL), norm2_gain.reshape(1, MODEL)

    (
        normed_t, cot_t, queries, x_pre, bc_pre, dt_raw, z_val, attended, lse, kv_all, edge_in,
        gated, core, x_act, bc_act, state_in, normed_near, cot_near, attended_low,
    ) = mixer_forward(
        tokens, cotangent, gain_one, query_weight, kv_weight, x_weight, bc_weight, dt_t, z_weight,
        cosine, sine, seg, x_conv, bc_conv, bias, rate, skip,
    )
    (
        hidden_in, two_t, grad_gate, grad_up, hidden, ffn_part, grad_hidden_in, mix_t, gains_two,
        grad_gated, grad_attended, two_near,
    ) = feed_forward(
        gated, attended_low, tokens, cotangent, gain_two, out_weight, attn_weight, gate_weight,
        up_weight, down_weight,
    )
    (
        grad_query, misc, grad_z, grad_x_pre, grad_dt, grad_x_conv, grad_bc_conv, grad_vectors,
        ffn_w, mix_near, mixed_near,
    ) = mixer_backward(
        queries, grad_attended, attended, lse, seg, kv_all, grad_gated, z_val, core, x_act,
        bc_act, x_pre, bc_pre, edge_in, dt_raw, state_in, bias, x_conv, bc_conv, rate,
        skip, grad_gate, grad_up, hidden, two_t, cot_t, cot_near, mix_t, cosine, sine, two_near,
        gated, attended_low,
    )
    mixer_w, gathered, small_sums, grad_normed, ffn_sum = finish(
        misc, grad_x_pre, grad_z, grad_query, grad_dt, gated, attended_low, normed_t, normed_near,
        mix_t, mix_near, ffn_part, tokens, x_weight, z_weight, query_weight, dt_t, grad_x_conv,
        grad_bc_conv, grad_vectors, gains_two, bc_weight, kv_weight, mixed_near,
    )
    (
        output, grad_tokens, bc_w, kv_w, x_w, z_w, q_w, dt_w, out_w, attn_w, gate_w, up_w, down_w,
        x_taps, bc_taps, bias_sum, rate_sum, skip_sum, gain_one_sum, gain_two_sum,
    ) = place(
        gathered, grad_normed, ffn_sum, hidden_in, grad_hidden_in, tokens, gain_one, mixer_w,
        ffn_w, small_sums,
    )
    return (
        output, grad_tokens, gain_one_sum, x_w, z_w, bc_w, dt_w.T, x_taps, bc_taps, bias_sum,
        rate_sum, skip_sum, out_w.T, q_w, kv_w, attn_w.T, gain_two_sum, gate_w, up_w, down_w.T,
    )


def solution(mesh):
    split = Mesh(mesh.devices.reshape(NZ, NX, NY, 2, 2), (*SEQ, "zh", "c"))
    head = ("zh", "c")
    rows, columns, both, turned = P(SEQ, None), P(None, head), P(SEQ, head), P(head, SEQ)
    return jax.shard_map(
        on_device,
        mesh=split,
        in_specs=(
            rows, P(SEQ), rows, P(), columns, columns, P(), columns, columns, P(), P(head),
            P(head), P(head), P(head, None), columns, P(), P(head, None), P(), columns, columns,
            P(head, None),
        ),
        out_specs=(
            rows, rows, P(), both, both, P(), both, P(), P(), P(), P(), P(), turned, both, P(),
            turned, P(), both, both, turned,
        ),
        check_vma=False,
    )
```

```python
import functools

import jax
import jax.numpy as jnp
from jax import lax
from jax.experimental import pallas as pl
from jax.experimental.pallas import tpu as pltpu
from jax.sharding import Mesh
from jax.sharding import PartitionSpec as P

SSM_DIM = 64
STATE = 256
CONV = 4
KVHEADS = 2
HEAD_DIM = 128
NZ, NX, NY = 2, 4, 4
BLOCKS = NZ * NX * NY
CHIPS = 2 * BLOCKS
ROWS = 256
MODEL = 2048
SEQ = ("zl", "x", "y")
EPSILON = 1e-05
ROPE_BASE = 100000000000.0
HIGHEST = lax.Precision.HIGHEST
MESH = pl.DeviceIdType.MESH
BF16, F32 = jnp.bfloat16, jnp.float32
MASKED = -1e30
LOG2E = 1.4426950408889634
VMEM_LIMIT = 56 * 2**20


def block_index():
    return (lax.axis_index("zl") * NX + lax.axis_index("x")) * NY + lax.axis_index("y")


def block_at(s):
    return {"zl": s // (NX * NY), "x": (s // NY) % NX, "y": s % NY}


PLANE = NX * NY


def plane_peer(k, sign, stride=13):
    o = 1 + (k * stride) % (PLANE - 1)
    dx, dy = o // NY, o % NY
    x, y = lax.axis_index("x"), lax.axis_index("y")
    if sign < 0:
        dx, dy = NX - dx, NY - dy
    x, y = (x + dx) % NX, (y + dy) % NY
    return x * NY + y, {"x": x, "y": y}


def signal(sem, where):
    pl.semaphore_signal(sem, inc=1, device_id=where, device_id_type=MESH)


def remote(src, dst, send, recv, where):
    return pltpu.make_async_remote_copy(src, dst, send, recv, device_id=where, device_id_type=MESH)


def over(start, stop, body):
    def step(i, carry):
        body(i)
        return carry

    lax.fori_loop(start, stop, step, 0)


def dot(a, b, left=1, right=0):
    return lax.dot_general(
        a, b, (((left,), (right,)), ((), ())), preferred_element_type=F32
    )


def vmem(n):
    return [pl.BlockSpec(memory_space=pltpu.VMEM)] * n


def params(collective_id):
    return pltpu.CompilerParams(
        collective_id=collective_id, has_side_effects=True, vmem_limit_bytes=VMEM_LIMIT
    )


HEADS = 12
INNER = HEADS * SSM_DIM
GROUPS = INNER // 128
BC = 2 * STATE
SCAN_ROWS = INNER // BLOCKS
EDGE_WIDE = INNER + BC + 128
GRAD_EDGE = INNER + 128


def two_parts(v):
    high = v.astype(BF16)
    return high, (v - high.astype(F32)).astype(BF16)


def low_lanes(rows):
    return lax.broadcasted_iota(jnp.int32, (rows, 128), 1) < SSM_DIM


def widen(v, g):
    low = low_lanes(v.shape[0])
    return jnp.where(low, v[:, 2 * g : 2 * g + 1], v[:, 2 * g + 1 : 2 * g + 2])


def per_head(v, g):
    lane = lax.broadcasted_iota(jnp.int32, v.shape, 1)
    first = jnp.sum(jnp.where(lane < SSM_DIM, v, 0.0), 1, keepdims=True)
    second = jnp.sum(jnp.where(lane < SSM_DIM, 0.0, v), 1, keepdims=True)
    return jnp.where(lane == 2 * g, first, jnp.where(lane == 2 * g + 1, second, 0.0))


def triangle():
    row = lax.broadcasted_iota(jnp.int32, (ROWS, ROWS), 0)
    col = lax.broadcasted_iota(jnp.int32, (ROWS, ROWS), 1)
    return (col <= row).astype(F32).astype(BF16)


def running(v, lower, side):
    high, low = two_parts(v)
    middle, lowest = two_parts(v - high.astype(F32))
    return (
        dot(lower, high, side, 0) + dot(lower, middle, side, 0) + dot(lower, lowest, side, 0)
    )


def sigmoid(v):
    return 1.0 / (1.0 + jnp.exp(-v))


def softplus(v):
    return jnp.maximum(v, 0.0) + jnp.log(1.0 + jnp.exp(-jnp.abs(v)))


def lane_block(g):
    return pl.ds(pl.multiple_of(g * 128, 128), 128)


def decays(dt_ref, vec_ref, seg_ref, segx_ref, lower):
    pre = dt_ref[...] + vec_ref[0:1, :]
    step = softplus(pre)
    total = running(-step * vec_ref[1:2, :] * LOG2E, lower, 1)
    last = total[ROWS - 1 : ROWS, :]
    seg = seg_ref[...]
    seg_last, before = seg[ROWS - 1 : ROWS, :], segx_ref[7:8, :]
    carry = jnp.where(seg == seg_last, jnp.exp2(last - total), 0.0)
    entry = jnp.where(seg == before, jnp.exp2(total), 0.0)
    through = jnp.where(seg_last == before, jnp.exp2(last), 0.0)
    return pre, step, total, carry, entry, through


def conv_group(ext_ref, segx_ref, seg_ref, taps_ref, cols):
    total, inputs = None, []
    for k in range(CONV):
        same = segx_ref[pl.ds(5 + k, ROWS), :] == seg_ref[...]
        v = jnp.where(same, ext_ref[pl.ds(5 + k, ROWS), cols], 0.0)
        inputs.append(v)
        term = taps_ref[k : k + 1, cols] * v
        total = term if total is None else total + term
    return total, inputs


def by_fours(body):
    def four(i):
        for k in range(4):
            body(i * 4 + k)

    over(0, BLOCKS // 4, four)


def scan_message(msg_ref, state_ref, through):
    high = through.astype(BF16)
    rest = through - high.astype(F32)
    middle = rest.astype(BF16)
    low = rest - middle.astype(F32)
    extra = jnp.concatenate([high.astype(F32), middle.astype(F32), low, jnp.zeros((5, 128), F32)], 0)
    extra = jnp.concatenate([extra, jnp.zeros((8, STATE - 128), F32)], 1)

    def fill(b):
        rows = state_ref[pl.ds(pl.multiple_of(b * SCAN_ROWS, 8), SCAN_ROWS), :]
        msg_ref[b] = jnp.concatenate([rows, extra], 0).astype(BF16)

    by_fours(fill)


class Scan:
    def __init__(self, reverse, me, msg, got, back, out, send, recv):
        self.reverse, self.me = reverse, me
        self.msg, self.got, self.back, self.out = msg, got, back, out
        self.send, self.recv = send, recv

    def there(self, o):
        d = (self.me + o) % BLOCKS
        return remote(
            self.msg.at[d], self.got.at[self.me], self.send.at[0, o], self.recv.at[0, o],
            block_at(d),
        )

    def arrived(self, phase, dst, o):
        s = (self.me + BLOCKS - o) % BLOCKS
        return remote(
            dst.at[s], dst.at[s], self.send.at[phase, o], self.recv.at[phase, o], block_at(s)
        )

    def start(self):
        over(1, BLOCKS, lambda o: self.there(o).start())
        self.got[self.me] = self.msg[self.me]

    def turn(self):
        me = self.me
        over(1, BLOCKS, lambda o: self.arrived(0, self.got, o).wait_recv())
        lane = lax.broadcasted_iota(jnp.int32, (SCAN_ROWS, 128), 1)
        row = lax.broadcasted_iota(jnp.int32, (SCAN_ROWS, 128), 0) + me * SCAN_ROWS
        at_head = (row >= lane * SSM_DIM) & (row < lane * SSM_DIM + SSM_DIM)

        def scan(i, state):
            blocks, messages, factors = [], [], []
            for n in range(4):
                k = BLOCKS - 1 - (4 * i + n) if self.reverse else 4 * i + n
                message = self.got[k].astype(F32)
                row = message[SCAN_ROWS : SCAN_ROWS + 1, :128]
                row += message[SCAN_ROWS + 1 : SCAN_ROWS + 2, :128]
                row += message[SCAN_ROWS + 2 : SCAN_ROWS + 3, :128]
                blocks.append(k)
                messages.append(message)
                factors.append(jnp.sum(jnp.where(at_head, row, 0.0), 1, keepdims=True))
            for k, message, through in zip(blocks, messages, factors):
                low = jnp.concatenate([state[16:, :128], state[16:, 128:]], 0)
                self.back[k] = jnp.concatenate([state[:16], low], 1).astype(BF16)
                state = through * state + message[:SCAN_ROWS]
            for k in blocks:
                pl.when(k != me)(lambda: self.returned(k).start())
            return state

        lax.fori_loop(0, BLOCKS // 4, scan, jnp.zeros((SCAN_ROWS, STATE), F32))
        self.out[me] = self.back[me]

    def returned(self, k):
        o = (k + BLOCKS - self.me) % BLOCKS
        return remote(
            self.back.at[k], self.out.at[self.me], self.send.at[1, o], self.recv.at[1, o],
            block_at(k),
        )

    def finish(self, state_ref):
        over(1, BLOCKS, lambda o: self.arrived(1, self.out, o).wait_recv())

        def fill(b):
            rows = self.out[b].astype(F32)
            low = jnp.concatenate([rows[:8, STATE:], rows[8:, STATE:]], 1)
            at = pl.multiple_of(b * SCAN_ROWS, 8)
            state_ref[pl.ds(at, SCAN_ROWS), :] = jnp.concatenate([rows[:, :STATE], low], 0)

        by_fours(fill)

    def close(self):
        def sent(o):
            self.there(o).wait_send()
            self.returned((self.me + o) % BLOCKS).wait_send()

        over(1, BLOCKS, sent)


def key_segments(block):
    turned = jnp.transpose(block.astype(F32))
    return jnp.concatenate([turned[:, 0:1], turned[:, 1:2]], 0)


def causal_mask(s):
    row = lax.broadcasted_iota(jnp.int32, (ROWS, 2 * ROWS), 0)
    col = lax.broadcasted_iota(jnp.int32, (ROWS, 2 * ROWS), 1) % ROWS
    return jnp.where(row <= col, s, MASKED)


def mixing_bias(seg_ref, segrow_ref):
    row = lax.broadcasted_iota(jnp.int32, (ROWS, ROWS), 0)
    col = lax.broadcasted_iota(jnp.int32, (ROWS, ROWS), 1)
    same = segrow_ref[0:1, :ROWS] == seg_ref[:, 0:1]
    return jnp.where((col <= row) & same, 0.0, MASKED)


WIDE = 256
RELAY, MIDDLE, LAST = 2, 4, 6
AHEAD = 4
OWN = MODEL // NZ


class Reduce:
    def __init__(self, lefts, n, here, r_ref, rz, part, rel, gx, half, gy, out_ref, sems):
        self.lefts, self.n, self.here, self.throttled = lefts, n, here, here == n
        self.r, self.rz, self.part, self.rel = r_ref, rz, part, rel
        self.gx, self.half, self.gy, self.out = gx, half, gy, out_ref
        self.rz_sem, self.rel_sem, self.gx_sem, self.gy_sem = (
            (sems[2 * k], sems[2 * k + 1]) for k in range(4)
        )
        self.zl, self.x, self.y = (lax.axis_index(a) for a in SEQ)
        self.other = {"zl": 1 - self.zl}

    @staticmethod
    def scratch(n):
        v, dma = pltpu.VMEM, pltpu.SemaphoreType.DMA
        return [
            v((n, ROWS, WIDE), BF16),
            v((n, ROWS, WIDE), BF16),
            v((n, 4, 4, 64, WIDE), BF16),
            v((n, 2, 2, 64, WIDE), BF16),
            v((n, 2, 4, 64, WIDE), BF16),
            v((n, 4, 64, WIDE), BF16),
            v((n, 3, 64, WIDE), BF16),
            *[dma((n,))] * 8,
        ]

    def fill(self, arrays, c=0):
        for ref in arrays:
            for k in range(ref.shape[1] // WIDE):
                self.r[c] = ref[:, k * WIDE : (k + 1) * WIDE]
                c += 1

    def right(self, c):
        return remote(
            self.r.at[c], self.rz.at[c], self.rz_sem[0].at[c], self.rz_sem[1].at[c], self.other
        )

    def start(self):
        over(0, AHEAD, lambda c: self.right(c).start())

    def place(self, c, phase, o):
        along_x = c % 2 == phase
        x_to = jnp.where(along_x, (self.x + o) % NX, self.x)
        y_to = jnp.where(along_x, self.y, (self.y + o) % NY)
        return {"x": x_to, "y": y_to}, jnp.where(along_x, x_to, y_to)

    def send(self, src, dst, sem, c, where):
        return remote(src, dst, sem[0].at[c], sem[1].at[c], where)

    def send_second(self, c, o):
        where, d = self.place(c, 1, o)
        return self.send(self.half.at[c, d], self.gy.at[c, o - 1], self.gy_sem, c, where)

    def whole(self, got, sem, c):
        return self.send(got.at[c], got.at[c], sem, c, self.other)

    def product(self, c):
        @pl.when((c + AHEAD < self.here) & self.throttled)
        def _():
            self.right(c + AHEAD).start()

        @pl.when(c < self.here)
        def _():
            self.right(c).wait_recv()

        mine, theirs = self.r[c], self.rz[c]
        even = c % 2 == 0
        ends = [first for _, _, first in self.lefts[1:]] + [self.n]
        for (own, near, first), end in zip(self.lefts, ends):
            @pl.when((c >= first) & (c < end))
            def _():
                for i in range(NX):
                    a = own[pl.ds(pl.multiple_of(self.zl * OWN + i * 256, 256), 256), :]
                    b = near[pl.ds(i * 256, 256), :]
                    tile = (dot(a, mine) + dot(b, theirs)).astype(BF16)
                    for j in range(NY):
                        self.part[c, jnp.where(even, i, j), jnp.where(even, j, i)] = (
                            tile[j * 64 : (j + 1) * 64]
                        )
        _, d = self.place(c, 0, 2)
        for k, o in ((0, 1), (1, 3)):
            src = self.part.at[c, d, pl.ds(2 * k, 2)]
            self.send(src, self.rel.at[c, k], self.rel_sem, c, self.place(c, 0, o)[0]).start()

    def relay(self, c):
        self.whole(self.rel, self.rel_sem, c).wait_recv()
        for k, o in ((0, 1), (1, 3)):
            where, d = self.place(c, 0, o)
            for j in (2 * k, 2 * k + 1):
                total = self.part[c, d, j].astype(F32) + self.rel[c, k, j - 2 * k].astype(F32)
                self.part[c, d, j] = total.astype(BF16)
            self.send(self.part.at[c, d], self.gx.at[c, k], self.gx_sem, c, where).start()

    def middle(self, c):
        self.whole(self.gx, self.gx_sem, c).wait_recv()
        mine = jnp.where(c % 2 == 0, self.x, self.y)
        for j in range(4):
            total = self.part[c, mine, j].astype(F32)
            for k in range(2):
                total += self.gx[c, k, j].astype(F32)
            self.half[c, j] = total.astype(BF16)
        for o in range(1, 4):
            self.send_second(c, o).start()

    def last(self, c):
        self.whole(self.gy, self.gy_sem, c).wait_recv()
        mine = jnp.where(c % 2 == 0, self.y, self.x)
        total = self.half[c, mine].astype(F32)
        for o in range(3):
            total += self.gy[c, o].astype(F32)
        self.out[:, pl.ds(pl.multiple_of(c * WIDE, WIDE), WIDE)] = total

    @property
    def steps(self):
        return self.n + LAST

    def step(self, i):
        for late, do in ((0, self.product), (RELAY, self.relay), (MIDDLE, self.middle), (LAST, self.last)):
            @pl.when((i >= late) & (i < self.n + late))
            def _():
                do(i - late)

    def close(self):
        over(0, self.here, lambda c: self.right(c).wait_send())

        def sent(c):
            self.whole(self.rel, self.rel_sem, c).wait_send()
            self.whole(self.gx, self.gx_sem, c).wait_send()
            self.whole(self.gy, self.gy_sem, c).wait_send()

        over(0, self.n, sent)


class Left:
    def __init__(self, l_ref, lz, sems):
        zl, c = lax.axis_index("zl"), lax.axis_index("c")
        half = OWN // 2
        there = pl.ds(pl.multiple_of((1 - zl) * OWN + c * half, half), half)
        near, other = (pl.ds(pl.multiple_of(k * half, half), half) for k in (c, 1 - c))
        sem = [sems.at[k] for k in range(4)]
        self.out = remote(l_ref.at[there], lz.at[near], sem[0], sem[1], {"zl": 1 - zl})
        self.on = remote(lz.at[near], lz.at[near], sem[2], sem[3], {"c": 1 - c})
        self.back = remote(lz.at[other], lz.at[other], sem[2], sem[3], {"c": 1 - c})

    def start(self):
        self.out.start()

    def pass_on(self):
        self.out.wait_recv()
        self.on.start()

    def finish(self):
        self.back.wait_recv()

    def close(self):
        self.out.wait_send()
        self.on.wait_send()


HEAD_CHUNKS = 4


class HeadSum:
    def __init__(self, x, out, near, pair, far, sems):
        self.x, self.out, self.near, self.pair, self.far = x, out, near, pair, far
        self.near_send, self.near_recv, self.far_send, self.far_recv, self.end_send, self.end_recv = sems
        self.c, zh = lax.axis_index("c"), lax.axis_index("zh")
        self.sibling, self.opposite = {"c": 1 - self.c}, {"zh": 1 - zh}
        self.half = x.shape[0] // 2
        self.rows_each = self.half // HEAD_CHUNKS

    @staticmethod
    def scratch():
        v, dma = pltpu.VMEM, pltpu.SemaphoreType.DMA
        return [*[v((ROWS // 2, MODEL), BF16)] * 3, *[dma((HEAD_CHUNKS,))] * 6]

    def rows(self, core, k):
        return pl.ds(pl.multiple_of(k // 2 * self.half + (2 * core + k % 2) * self.rows_each, 16), self.rows_each)

    def local(self, k):
        return pl.ds(k * self.rows_each, self.rows_each)

    def first(self, k):
        return remote(
            self.x.at[self.rows(1 - self.c, k)], self.near.at[self.local(k)],
            self.near_send.at[k], self.near_recv.at[k], self.sibling,
        )

    def second(self, k):
        return remote(
            self.pair.at[self.local(k)], self.far.at[self.local(k)],
            self.far_send.at[k], self.far_recv.at[k], self.opposite,
        )

    def third(self, k, core):
        rows = self.rows(core, k)
        return remote(
            self.out.at[rows], self.out.at[rows], self.end_send.at[k], self.end_recv.at[k],
            self.sibling,
        )

    def start(self, chunks=range(HEAD_CHUNKS)):
        for k in chunks:
            self.first(k).start()

    def across(self, chunks=range(HEAD_CHUNKS)):
        for k in chunks:
            self.first(k).wait_recv()
            own = self.x[self.rows(self.c, k)].astype(F32)
            self.pair[self.local(k)] = (own + self.near[self.local(k)].astype(F32)).astype(BF16)
            self.second(k).start()

    def join(self, chunks=range(HEAD_CHUNKS)):
        for k in chunks:
            self.second(k).wait_recv()
            total = self.pair[self.local(k)].astype(F32) + self.far[self.local(k)].astype(F32)
            self.out[self.rows(self.c, k)] = total.astype(BF16)
            self.third(k, self.c).start()

    def finish(self, chunks=range(HEAD_CHUNKS)):
        for k in chunks:
            self.third(k, 1 - self.c).wait_recv()

    def close(self):
        for k in range(HEAD_CHUNKS):
            self.first(k).wait_send()
            self.second(k).wait_send()
            self.third(k, self.c).wait_send()


class Loads:
    def __init__(self, pairs, sems, results, out_sems):
        self.copies = {
            id(there): pltpu.make_async_copy(here, there, sems.at[i])
            for i, (here, there) in enumerate(pairs)
        }
        self.results = {
            id(here): pltpu.make_async_copy(here, there, out_sems.at[i])
            for i, (here, there) in enumerate(results)
        }
        self.under_way = []

    def start(self):
        for copy in self.copies.values():
            copy.start()

    def need(self, *refs):
        for ref in refs:
            copy = self.copies.pop(id(ref), None)
            if copy is not None:
                copy.wait()

    def put(self, *refs):
        for ref in refs:
            copy = self.results.pop(id(ref))
            copy.start()
            self.under_way.append(copy)

    def flush(self):
        for copy in self.results.values():
            copy.start()
        for copy in (*self.results.values(), *self.under_way):
            copy.wait()


def fetching(kernel, n_in, n_out, late, large):
    def wrapped(*refs):
        ins, outs, rest = list(refs[:n_in]), list(refs[n_in : n_in + n_out]), refs[n_in + n_out :]
        count = len(late) + len(large)
        buffers, (sems, out_sems) = rest[-2 - count : -2], rest[-2:]
        pairs, results = [], []
        for buffer, i in zip(buffers, late):
            pairs.append((ins[i], buffer))
            ins[i] = buffer
        for buffer, i in zip(buffers[len(late) :], large):
            results.append((buffer, outs[i]))
            outs[i] = buffer
        loads = Loads(pairs, sems, results, out_sems)
        kernel(loads, *ins, *outs, *rest[: -2 - count])
        loads.flush()

    return wrapped


def call(kernel, name, args, late, outs, scratch, collective_id, left=()):
    anywhere, here = pl.BlockSpec(memory_space=pl.ANY), pl.BlockSpec(memory_space=pltpu.VMEM)
    shapes = [jax.ShapeDtypeStruct(*o) for o in outs]
    large = [i for i, o in enumerate(shapes) if o.size >= 2**14]
    dma = pltpu.SemaphoreType.DMA
    return pl.pallas_call(
        fetching(kernel, len(args), len(outs), late, large),
        name=name,
        out_shape=tuple(shapes),
        in_specs=[anywhere if i in (*late, *left) else here for i in range(len(args))],
        out_specs=tuple(anywhere if i in large else here for i in range(len(outs))),
        scratch_shapes=[
            *scratch,
            *[pltpu.VMEM(args[i].shape, args[i].dtype) for i in late],
            *[pltpu.VMEM(shapes[i].shape, shapes[i].dtype) for i in large],
            dma((max(len(late), 1),)),
            dma((max(len(large), 1),)),
        ],
        compiler_params=params(collective_id),
    )(*args)


def spread_small(seg, bias, rate, skip, seg_ref, segrow_ref, vec_ref, skip_ref):
    row = seg[...].astype(F32)
    seg_ref[...] = jnp.transpose(jnp.broadcast_to(row, (128, ROWS)))
    segrow_ref[...] = jnp.broadcast_to(jnp.concatenate([row, row], 1), segrow_ref.shape)
    rest = jnp.zeros((1, 128 - HEADS), F32)
    lines = [jnp.concatenate([ref[...], rest], 1) for ref in (bias, rate, skip)]
    vec_ref[...] = jnp.concatenate([*lines, jnp.zeros((5, 128), F32)], 0)
    for g in range(GROUPS):
        skip_ref[:, g * 128 : (g + 1) * 128] = jnp.broadcast_to(widen(lines[2], g), (8, 128))


def small_scratch():
    return [
        pltpu.VMEM((ROWS, 128), F32),
        pltpu.VMEM((8, 2 * ROWS), F32),
        pltpu.VMEM((8, 128), F32),
        pltpu.VMEM((8, INNER), F32),
    ]


def spread_dt(dt_w, wide_ref):
    wide_ref[16:, :] = jnp.zeros((112, MODEL), BF16)
    rows = jnp.concatenate([dt_w[...].astype(F32), jnp.zeros((16 - HEADS, MODEL), F32)], 0)
    wide_ref[:16, :] = rows.astype(BF16)


def turn_pairs(v, cosine, sine, direction):
    return v * cosine + pltpu.roll(v, HEAD_DIM // 2, 1) * (sine * direction)


def transpose_to(out_ref, ref):
    for k in range(ref.shape[1] // 256):
        out_ref[k * 256 : (k + 1) * 256, :] = jnp.transpose(ref[:, k * 256 : (k + 1) * 256])


def feed_forward_kernel(
    loads, gated_ref, att_ref, tok_ref, cot_ref, gain_ref, out_w, attn_w, gate_w, up_w, down_w,
    hid_ref, ft_ref, dgate_ref, dup_ref, hidden_ref, ffn_ref, ghid_ref, mt_ref, gain_out,
    gg_ref, do_ref, ftz_ref,
    x_ref, sum_ref, back_ref, back_sum, normed, mix_ref, left_sem, *sums,
):
    loads.start()
    n_sum = len(HeadSum.scratch())
    first = HeadSum(x_ref, sum_ref, *sums[:3], sums[3:n_sum])
    second = HeadSum(back_ref, back_sum, *sums[n_sum : n_sum + 3], sums[n_sum + 3 :])
    barrier = pltpu.get_barrier_semaphore()
    other_z = {"zl": 1 - lax.axis_index("zl")}
    signal(barrier, first.sibling)
    signal(barrier, first.opposite)
    signal(barrier, other_z)
    pl.semaphore_wait(barrier, 3)
    left = Left(ft_ref, ftz_ref, left_sem)
    halves = [(slice(g * 128, (g + 1) * 128), (2 * g, 2 * g + 1)) for g in range(2)]
    loads.need(out_w, attn_w)
    for rows, chunks in halves:
        x_ref[rows, :] = (
            dot(gated_ref[rows, :], out_w[...]) + dot(att_ref[rows, :], attn_w[...])
        ).astype(BF16)
        first.start(chunks)
    first.across()

    wide = 256
    loads.need(cot_ref, down_w)
    for k in range(0, hidden_ref.shape[1], wide):
        ghid_ref[:, k : k + wide] = dot(cot_ref[...], down_w[k : k + wide, :], 1, 1)
    loads.need(tok_ref, gate_w, up_w)

    def norm(half, chunks):
        first.join(chunks)
        first.finish(chunks)
        for r in range(half.start, half.stop, 32):
            rows = slice(r, r + 32)
            x = tok_ref[rows, :].astype(F32) + sum_ref[rows, :].astype(F32)
            hid_ref[rows, :] = x
            scale = lax.rsqrt(jnp.mean(x * x, 1, keepdims=True) + EPSILON)
            normed[rows, :] = (x * scale * gain_ref[0:1, :]).astype(BF16)

    def feed(rows, chunks):
        for k in range(0, hidden_ref.shape[1], wide):
            cols = slice(k, k + wide)
            n = normed[rows, :]
            gate, up = dot(n, gate_w[:, cols]), dot(n, up_w[:, cols])
            grad = ghid_ref[rows, cols]
            sig = sigmoid(gate)
            act = gate * sig
            hidden_ref[rows, cols] = (act * up).astype(BF16)
            dgate_ref[rows, cols] = (grad * up * sig * (1.0 + gate * (1.0 - sig))).astype(BF16)
            dup_ref[rows, cols] = (grad * act).astype(BF16)
        back_ref[rows, :] = (
            dot(dgate_ref[rows, :], gate_w[...], 1, 1) + dot(dup_ref[rows, :], up_w[...], 1, 1)
        ).astype(BF16)
        second.start(chunks)

    def norm_back(half, chunks):
        second.join(chunks)
        second.finish(chunks)
        for r in range(half.start, half.stop, 32):
            rows = slice(r, r + 32)
            x = hid_ref[rows, :]
            scale = lax.rsqrt(jnp.mean(x * x, 1, keepdims=True) + EPSILON)
            n = x * scale
            grad = back_sum[rows, :].astype(F32)
            scaled = grad * gain_ref[0:1, :]
            along = jnp.mean(n * scaled, 1, keepdims=True)
            total = cot_ref[rows, :].astype(F32) + scale * (scaled - n * along)
            ghid_ref[rows, :] = total
            mix_ref[rows, :] = total.astype(BF16)
            gains = jnp.sum(grad * n, 0, keepdims=True)
            gain_out[0:1, :] = gains if r == 0 else gain_out[0:1, :] + gains

    (rows_a, chunks_a), (rows_b, chunks_b) = halves
    norm(rows_a, chunks_a)
    feed(rows_a, chunks_a)
    norm(rows_b, chunks_b)
    second.across(chunks_a)
    transpose_to(ft_ref, normed)
    left.start()
    loads.put(hid_ref, ft_ref)
    feed(rows_b, chunks_b)
    loads.put(hidden_ref, dgate_ref, dup_ref)
    second.across(chunks_b)
    left.pass_on()
    ffn_ref[...] = dot(hidden_ref[...], down_w[...]).astype(BF16)
    loads.put(ffn_ref)
    norm_back(rows_a, chunks_a)
    norm_back(rows_b, chunks_b)
    loads.put(ghid_ref)
    grad_att = dot(mix_ref[...], attn_w[...], 1, 1).astype(BF16)
    for h in range(2):
        do_ref[h * ROWS : (h + 1) * ROWS, :] = grad_att[:, h * HEAD_DIM : (h + 1) * HEAD_DIM]
    gg_ref[...] = dot(mix_ref[...], out_w[...], 1, 1)
    loads.put(gg_ref, do_ref)
    transpose_to(mt_ref, mix_ref)
    loads.put(mt_ref)
    first.close()
    second.close()
    left.finish()
    left.close()


def feed_forward(*args):
    v = pltpu.VMEM
    ff = args[7].shape[1]
    return call(
        feed_forward_kernel, "feed_forward", args, (2, 3, 5, 6, 7, 8, 9),
        [
            ((ROWS, MODEL), F32),
            ((MODEL, ROWS), BF16),
            ((ROWS, ff), BF16),
            ((ROWS, ff), BF16),
            ((ROWS, ff), BF16),
            ((ROWS, MODEL), BF16),
            ((ROWS, MODEL), F32),
            ((MODEL, ROWS), BF16),
            ((8, MODEL), F32),
            ((ROWS, INNER), F32),
            ((2 * ROWS, HEAD_DIM), BF16),
            ((OWN, ROWS), BF16),
        ],
        [
            *[v((ROWS, MODEL), BF16)] * 6,
            pltpu.SemaphoreType.DMA((4,)),
            *HeadSum.scratch(),
            *HeadSum.scratch(),
        ],
        4,
    )


EARLY = 6


def mixer_forward_kernel(
    loads, tok_ref, cot_ref, gain_ref, q_w, kv_w, x_w, bc_w, dt_w, z_w, cos_ref, sin_ref, seg,
    xtaps_ref, bctaps_ref, bias, rate, skip,
    nt_ref, ct_ref, q_ref, x_ref, bc_ref, dt_ref, z_ref,
    att_ref, lse_ref, kv_ref, edge_out, gated_ref, core_ref, xact_ref, bcact_ref, state_ref,
    ntz_ref, ctz_ref, attlow_ref,
    m_ref, l_ref, acc_ref, xext, bcext, segx, local, msg, got, back, result, bias_ref, cb_ref,
    cumt_ref, normed, own_ref, edge_ref, kv_cols, seg_ref, segrow_ref, vec_ref, skip_ref, dt_wide,
    send_sem, recv_sem, sib_send, sib_recv, edge_sem, scan_send, scan_recv, left_sem, kv_sem,
):
    me, c, zl = block_index(), lax.axis_index("c"), lax.axis_index("zl")
    at = me % PLANE
    sibling = {"c": 1 - c}
    kv_at = (c * KVHEADS + lax.axis_index("zh")) * HEAD_DIM
    kv_copy = pltpu.make_async_copy(
        kv_w.at[:, pl.ds(pl.multiple_of(kv_at, HEAD_DIM), HEAD_DIM)], kv_cols, kv_sem
    )
    loads.start()
    kv_copy.start()
    barrier = pltpu.get_barrier_semaphore()
    over(1, BLOCKS, lambda o: signal(barrier, block_at((me + o) % BLOCKS)))
    signal(barrier, sibling)

    spread_small(seg, bias, rate, skip, seg_ref, segrow_ref, vec_ref, skip_ref)
    loads.need(tok_ref)
    for r in range(0, ROWS, 32):
        rows = slice(r, r + 32)
        v = tok_ref[rows, :].astype(F32)
        scale = lax.rsqrt(jnp.mean(v * v, 1, keepdims=True) + EPSILON)
        normed[rows, :] = (v * scale * gain_ref[0:1, :]).astype(BF16)
    n = normed[...]
    loads.need(x_w, bc_w)
    x_ref[...] = dot(n, x_w[...]).astype(BF16)
    bc_ref[...] = dot(n, bc_w[...]).astype(BF16)
    edge_ref[:, :INNER] = x_ref[ROWS - 16 :, :]
    edge_ref[:, INNER : INNER + BC] = bc_ref[ROWS - 16 :, :]
    edge_ref[:, INNER + BC :] = seg_ref[ROWS - 16 :, :].astype(BF16)
    pl.semaphore_wait(barrier, BLOCKS)

    def block_copy(src, j, send, where):
        return remote(src, kv_ref.at[c, j], send_sem.at[send], recv_sem.at[j], where)

    def arrival(j):
        return block_copy(own_ref, j, 0, sibling)

    to_sibling = lambda j, src: remote(
        src, kv_ref.at[c, j], sib_send.at[j], sib_recv.at[j], sibling
    )
    from_sibling = lambda j: remote(
        kv_ref.at[1 - c, j], kv_ref.at[1 - c, j], sib_send.at[j], sib_recv.at[j], sibling
    )
    across = block_copy(own_ref, me, PLANE - 1, {"zl": 1 - zl})

    def own_copy(k, wait):
        d, where = plane_peer(k, 1, 8)

        @pl.when(d > at)
        def _():
            copy = block_copy(own_ref, me, k, where)
            copy.wait_send() if wait else copy.start()

    def relay_copy(k, wait):
        copy = block_copy(kv_ref.at[c, at], at, PLANE + k, plane_peer(k, 1, 8)[1])
        copy.wait_send() if wait else copy.start()

    edge_copy = remote(
        edge_ref, edge_out, edge_sem.at[0], edge_sem.at[1], block_at((me + 1) % BLOCKS)
    )
    states = Scan(False, me, msg, got, back, result, scan_send, scan_recv)

    @pl.when(me < BLOCKS - 1)
    def _():
        edge_copy.start()

    cosine, sine = cos_ref[...], sin_ref[...]
    kv_copy.wait()
    raw = dot(n, kv_cols[...])
    turned = turn_pairs(raw, cosine, sine, 1.0)
    own_ref[:ROWS, :] = jnp.where(c == 0, turned, raw).astype(BF16)
    rows = [segrow_ref[0:1, :HEAD_DIM], segrow_ref[0:1, HEAD_DIM : 2 * HEAD_DIM]]
    own_ref[ROWS:, :] = jnp.concatenate([*rows, jnp.zeros((14, HEAD_DIM), F32)], 0).astype(BF16)

    @pl.when(zl == 0)
    def _():
        across.start()

    to_sibling(me, own_ref).start()
    over(0, EARLY, lambda k: own_copy(k, False))
    lefts = [Left(ct_ref, ctz_ref, left_sem.at[0]), Left(nt_ref, ntz_ref, left_sem.at[1])]

    kv_ref[c, me] = own_ref[...]
    spread_dt(dt_w, dt_wide)
    dt_ref[...] = dot(n, dt_wide[...], 1, 1)
    xext[8:, :] = x_ref[...].astype(F32)
    bcext[8:, :] = bc_ref[...].astype(F32)
    segx[8:, :] = seg_ref[...]
    lower = triangle()
    bias_ref[...] = mixing_bias(seg_ref, segrow_ref)

    @pl.when(me > 0)
    def _():
        edge_copy.wait_recv()

    @pl.when(me == 0)
    def _():
        edge_out[...] = jnp.zeros_like(edge_out)

    edge = edge_out[...].astype(F32)[8:]
    xext[:8, :] = edge[:, :INNER]
    bcext[:8, :] = edge[:, INNER : INNER + BC]
    segx[:8, :] = edge[:, INNER + BC :]

    def activate(ext, taps, out):
        def group(g):
            pre, _ = conv_group(ext, segx, seg_ref, taps, lane_block(g))
            out[:, lane_block(g)] = (pre * sigmoid(pre)).astype(BF16)

        over(0, out.shape[1] // 128, group)

    activate(bcext, bctaps_ref, bcact_ref)
    activate(xext, xtaps_ref, xact_ref)

    _, step, total, carry, entry, through = decays(dt_ref, vec_ref, seg_ref, segx, lower)
    cumt_ref[...] = jnp.transpose(total)
    weight = step * carry
    b_low, c_low = bcact_ref[:, :STATE], bcact_ref[:, STATE:]
    for g in range(GROUPS):
        moved = xact_ref[:, g * 128 : (g + 1) * 128].astype(F32) * widen(weight, g)
        local[g * 128 : (g + 1) * 128, :] = dot(moved.astype(BF16), b_low, 0, 0)
    transpose_to(nt_ref, normed)
    loads.need(cot_ref)
    transpose_to(ct_ref, cot_ref)
    for left in lefts:
        left.start()
    scan_message(msg, local, through)
    states.start()
    over(EARLY, PLANE - 1, lambda k: own_copy(k, False))

    @pl.when(zl == 1)
    def _():
        arrival(at).wait_recv()
        to_sibling(at, kv_ref.at[c, at]).start()
        over(0, PLANE - 1, lambda k: relay_copy(k, False))

    cb_ref[...] = dot(c_low, b_low, 1, 1)
    low_lane = lax.broadcasted_iota(jnp.int32, (ROWS, 128), 1) < SSM_DIM
    for g in range(GROUPS):
        cols = slice(g * 128, (g + 1) * 128)
        u = (xact_ref[:, cols].astype(F32) * widen(step, g)).astype(BF16)
        made = []
        for h in (2 * g, 2 * g + 1):
            gap = total[:, h : h + 1] - cumt_ref[h : h + 1, :] + bias_ref[...]
            made.append(dot((jnp.exp2(gap) * cb_ref[...]).astype(BF16), u))
        core_ref[:, cols] = jnp.where(low_lane, made[0], made[1])

    loads.need(q_w)
    for h in range(2):
        raw = dot(n, q_w[:, h * HEAD_DIM : (h + 1) * HEAD_DIM])
        q_ref[h * ROWS : (h + 1) * ROWS, :] = turn_pairs(raw, cosine, sine, 1.0).astype(BF16)
    scale = LOG2E * HEAD_DIM**-0.5
    queries = q_ref[...]
    qseg = segrow_ref[0:1, :]

    def scores_of(j):
        s = dot(kv_ref[0, j, :ROWS], queries, 1, 1) * scale
        return jnp.where(key_segments(kv_ref[0, j, ROWS:]) == qseg, s, MASKED)

    from_sibling(me).wait_recv()
    s = causal_mask(scores_of(me))
    m = jnp.max(s, 0, keepdims=True)
    p = jnp.exp2(s - m)
    m_ref[...] = m
    l_ref[...] = jnp.sum(p, 0, keepdims=True)
    acc_ref[...] = dot(kv_ref[1, me, :ROWS], p.astype(BF16), 0, 0)

    loads.put(nt_ref, ct_ref, q_ref, x_ref, bc_ref, dt_ref, bcact_ref, xact_ref)
    states.turn()
    loads.need(z_w)
    z_ref[...] = dot(n, z_w[...])
    loads.put(z_ref)

    def forward(k):
        q, _ = plane_peer(k, -1, 8)

        def one(j):
            arrival(j).wait_recv()
            to_sibling(j, kv_ref.at[c, j]).start()

        pl.when(q < at)(lambda: one(zl * PLANE + q))
        pl.when(zl == 1)(lambda: one(q))

    def attend(*blocks):
        scores = []
        for j in blocks:
            from_sibling(j).wait_recv()
            scores.append(scores_of(j))
        m_old = m_ref[...]
        m = m_old
        for s in scores:
            m = jnp.maximum(m, jnp.max(s, 0, keepdims=True))
        alpha = jnp.exp2(m_old - m)
        total, acc = l_ref[...] * alpha, acc_ref[...] * alpha
        for j, s in zip(blocks, scores):
            p = jnp.exp2(s - m)
            total += jnp.sum(p, 0, keepdims=True)
            acc += dot(kv_ref[1, j, :ROWS], p.astype(BF16), 0, 0)
        m_ref[...], l_ref[...], acc_ref[...] = m, total, acc

    forward(0)

    @pl.when(zl == 1)
    def _():
        attend(at)

    def step_over(k):
        @pl.when(k + 1 < PLANE - 1)
        def _():
            forward(k + 1)

        q, _ = plane_peer(k, -1, 8)
        pl.when((q < at) & (zl == 1))(lambda: attend(PLANE + q, q))
        pl.when((q < at) & (zl == 0))(lambda: attend(q))
        pl.when((q > at) & (zl == 1))(lambda: attend(q))

    over(0, PLANE - 1, step_over)
    for left in lefts:
        left.pass_on()
    attended = jnp.transpose(acc_ref[...] / l_ref[...])
    att_ref[...] = attended
    for h in range(2):
        attlow_ref[:, h * HEAD_DIM : (h + 1) * HEAD_DIM] = (
            attended[h * ROWS : (h + 1) * ROWS].astype(BF16)
        )
    lse_ref[...] = jnp.broadcast_to(m_ref[...] + jnp.log2(l_ref[...]), lse_ref.shape)

    loads.put(att_ref, kv_ref)
    states.finish(state_ref)
    loads.put(state_ref)
    for g in range(GROUPS):
        cols = slice(g * 128, (g + 1) * 128)
        outer = dot(c_low, state_ref[cols, :].astype(BF16), 1, 1) * widen(entry, g)
        core = core_ref[:, cols] + outer
        core_ref[:, cols] = core
        out = core + skip_ref[0:1, cols] * xact_ref[:, cols].astype(F32)
        z = z_ref[:, cols]
        gated_ref[:, cols] = (out * z * sigmoid(z)).astype(BF16)

    loads.put(gated_ref, core_ref)
    states.close()
    for left in lefts:
        left.finish()
        left.close()
    to_sibling(me, own_ref).wait_send()
    over(0, PLANE - 1, lambda k: own_copy(k, True))

    @pl.when(zl == 0)
    def _():
        across.wait_send()

    @pl.when(zl == 1)
    def _():
        over(0, PLANE - 1, lambda k: relay_copy(k, True))
        over(0, PLANE, lambda j: to_sibling(j, own_ref).wait_send())

    over(0, at, lambda q: to_sibling(zl * PLANE + q, own_ref).wait_send())

    @pl.when(me < BLOCKS - 1)
    def _():
        edge_copy.wait_send()


def mixer_forward(*args):
    wide = 2 * ROWS
    dma = pltpu.SemaphoreType.DMA
    return call(
        mixer_forward_kernel, "mixer_forward", args, (0, 5, 6, 3, 8, 1),
        [
            ((MODEL, ROWS), BF16),
            ((MODEL, ROWS), BF16),
            ((wide, HEAD_DIM), BF16),
            ((ROWS, INNER), BF16),
            ((ROWS, BC), BF16),
            ((ROWS, 128), F32),
            ((ROWS, INNER), F32),
            ((wide, HEAD_DIM), F32),
            ((8, wide), F32),
            ((2, BLOCKS, ROWS + 16, HEAD_DIM), BF16),
            ((16, EDGE_WIDE), BF16),
            ((ROWS, INNER), BF16),
            ((ROWS, INNER), F32),
            ((ROWS, INNER), BF16),
            ((ROWS, BC), BF16),
            ((INNER, STATE), F32),
            ((OWN, ROWS), BF16),
            ((OWN, ROWS), BF16),
            ((ROWS, 2 * HEAD_DIM), BF16),
        ],
        [
            pltpu.VMEM((1, wide), F32),
            pltpu.VMEM((1, wide), F32),
            pltpu.VMEM((HEAD_DIM, wide), F32),
            pltpu.VMEM((ROWS + 8, INNER), F32),
            pltpu.VMEM((ROWS + 8, BC), F32),
            pltpu.VMEM((ROWS + 8, 128), F32),
            pltpu.VMEM((INNER, STATE), F32),
            *[pltpu.VMEM((BLOCKS, SCAN_ROWS + 8, STATE), BF16)] * 2,
            *[pltpu.VMEM((BLOCKS, 16, STATE + 128), BF16)] * 2,
            pltpu.VMEM((ROWS, ROWS), F32),
            pltpu.VMEM((ROWS, ROWS), F32),
            pltpu.VMEM((128, ROWS), F32),
            pltpu.VMEM((ROWS, MODEL), BF16),
            pltpu.VMEM((ROWS + 16, HEAD_DIM), BF16),
            pltpu.VMEM((16, EDGE_WIDE), BF16),
            pltpu.VMEM((MODEL, HEAD_DIM), BF16),
            *small_scratch(),
            pltpu.VMEM((128, MODEL), BF16),
            *[dma((BLOCKS,))] * 4,
            dma((2,)),
            dma((2, BLOCKS)),
            dma((2, BLOCKS)),
            dma((2, 4)),
            dma,
        ],
        1,
        (4,),
    )


def mixer_backward_kernel(
    loads, q_ref, do_ref, att_ref, lse_ref, seg, kv_ref, gg_ref, z_ref, core_ref, xact_ref,
    bcact_ref, x_ref, bcown_ref, edge_in, dt_ref, state_ref, bias, xtaps_ref, bctaps_ref,
    rate, skip, dgate_ref, dup_ref, hidden_ref, ft_ref, ct_ref, ctz_ref, mt_ref, cos_ref,
    sin_ref, ftz_ref, gated_ref, attlow_ref,
    dqraw_ref, misc_ref, dz_ref, dx_ref, ddt_ref, dxtaps_ref, dbctaps_ref, dvec_ref,
    w_ref, mtz_ref, outz_ref,
    dkv_ref, dqt_ref, mine, theirs, sib, kvgot, relay_ref, total_ref, xext, bcext, segx, local, msg, got, back, result,
    bias_ref, cb_ref, cumt_ref, g_ref, du_ref, dbc_all, shares, share_got, edge_ref,
    edge_out, enter_ref, gext, dcum_ref, ddtx_ref,
    send_sem, recv_sem, sib_send, sib_recv, edge_sem, scan_send, scan_recv, share_send, share_recv,
    left_sem, outs_ref, outz_sem, outs_sem, owntaps_ref, seg_ref, segrow_ref, vec_ref, skip_ref, *reduce,
):
    me, c, zh, zl = block_index(), *(lax.axis_index(a) for a in ("c", "zh", "zl"))
    head_at = zh * 2 + c
    sibling = {"c": 1 - c}
    at_head = lambda d: {"zh": d // 2, "c": d % 2}
    loads.start()
    barrier = pltpu.get_barrier_semaphore()
    over(1, BLOCKS, lambda o: signal(barrier, block_at((me + o) % BLOCKS)))
    for o in range(1, 4):
        signal(barrier, at_head((head_at + o) % 4))
    pl.semaphore_wait(barrier, BLOCKS + 2)

    at = me % PLANE
    to_sibling = lambda j: remote(
        theirs.at[j], sib.at[j], sib_send.at[j], sib_recv.at[j], sibling
    )

    def to_owner(k, kind):
        q, where = plane_peer(k, -1)
        j = q if kind else zl * PLANE + q
        return remote(
            mine.at[j], kvgot.at[kind, at], send_sem.at[kind, k], recv_sem.at[kind, at], where
        )

    def from_plane(kind, q):
        return remote(
            kvgot.at[kind, q], kvgot.at[kind, q], send_sem.at[kind, 0], recv_sem.at[kind, q],
            sibling,
        )

    across = remote(
        relay_ref, kvgot.at[1, 0], send_sem.at[0, PLANE - 1], recv_sem.at[1, 0], {"zl": 1 - zl}
    )
    states = Scan(True, me, msg, got, back, result, scan_send, scan_recv)
    rs = Reduce(
        [(ct_ref, ctz_ref, 0), (ft_ref, ftz_ref, 4)], 12, 12, *reduce[:7], w_ref, reduce[7:]
    )
    left = Left(mt_ref, mtz_ref, left_sem)
    loads.need(hidden_ref)
    rs.fill([hidden_ref])
    rs.start()
    loads.need(dgate_ref, dup_ref)
    rs.fill([dgate_ref, dup_ref], 4)
    done = 0

    def reduce_some(n):
        nonlocal done
        over(done, done + n, rs.step)
        done += n


    spread_small(seg, bias, rate, skip, seg_ref, segrow_ref, vec_ref, skip_ref)
    lower = triangle()
    edge = edge_in[...].astype(F32)[8:]
    xext[:8, :] = edge[:, :INNER]
    segx[:8, :] = edge[:, INNER + BC :]
    xext[8:, :] = x_ref[...].astype(F32)
    segx[8:, :] = seg_ref[...]
    bc_cols = lane_block(head_at)
    edge_cols = lane_block(head_at + INNER // 128)
    bcext[:8, :] = edge_in[:, edge_cols].astype(F32)[8:]
    bcext[8:, :] = bcown_ref[:, bc_cols].astype(F32)
    owntaps_ref[...] = bctaps_ref[:, bc_cols]
    bias_ref[...] = mixing_bias(seg_ref, segrow_ref)
    pre_dt, step, total, carry, entry, through = decays(dt_ref, vec_ref, seg_ref, segx, lower)
    cumt_ref[...] = jnp.transpose(total)
    b_low, c_low = bcact_ref[:, :STATE], bcact_ref[:, STATE:]
    for g in range(GROUPS):
        cols = slice(g * 128, (g + 1) * 128)
        z = z_ref[:, cols]
        grad = gg_ref[:, cols] * z * sigmoid(z)
        g_ref[:, cols] = grad
        entered = (grad * widen(entry, g)).astype(BF16)
        du_ref[:, cols] = entered.astype(F32)
        local[cols, :] = dot(entered, c_low, 0, 0)
    scan_message(msg, local, through)
    states.start()
    loads.need(ct_ref, ctz_ref, ft_ref, ftz_ref)
    reduce_some(1)

    dcum = jnp.zeros((ROWS, 128), F32)
    dskip = jnp.zeros((8, 128), F32)
    dc = jnp.zeros((ROWS, STATE), F32)
    for g in range(GROUPS):
        cols = slice(g * 128, (g + 1) * 128)
        z, core, x = z_ref[:, cols], core_ref[:, cols], xact_ref[:, cols].astype(F32)
        sig = sigmoid(z)
        out = core + skip_ref[0:1, cols] * x
        dz_ref[:, cols] = (gg_ref[:, cols] * out * sig * (1.0 + z * (1.0 - sig))).astype(BF16)
        grad = g_ref[:, cols]
        dcum += per_head(grad * core, g)
        dskip += per_head(jnp.broadcast_to(jnp.sum(grad * x, 0, keepdims=True), (8, 128)), g)
        dc += dot(du_ref[:, cols].astype(BF16), state_ref[cols, :].astype(BF16))
    dbc_all[:, STATE:] = dc
    loads.put(dz_ref)
    reduce_some(1)

    cb_ref[...] = dot(c_low, b_low, 1, 1)
    low_lane = lax.broadcasted_iota(jnp.int32, (ROWS, 128), 1) < SSM_DIM
    dcb = jnp.zeros((ROWS, ROWS), F32)
    for g in range(GROUPS):
        cols = slice(g * 128, (g + 1) * 128)
        u = xact_ref[:, cols].astype(F32) * widen(step, g)
        u_low, grad = u.astype(BF16), g_ref[:, cols]
        grad_low = grad.astype(BF16)
        made = []
        for i in range(2):
            h = 2 * g + i
            decay = jnp.exp2(total[:, h : h + 1] - cumt_ref[h : h + 1, :] + bias_ref[...])
            mixing = (decay * cb_ref[...]).astype(BF16)
            made.append(dot(mixing, grad_low, 0, 0))
            half = jnp.where(low_lane if i == 0 else ~low_lane, grad, 0.0).astype(BF16)
            dcb += decay * dot(half, u_low, 1, 1)
        du = jnp.where(low_lane, made[0], made[1])
        du_ref[:, cols] = du
        dcum -= per_head(u * du, g)
    dcum_ref[...] = dcum
    reduce_some(1)
    dcb_low = dcb.astype(BF16)
    dbc_all[:, :STATE] = dot(dcb_low, c_low, 0, 0)
    dbc_all[:, STATE:] += dot(dcb_low, b_low)

    loads.need(q_ref, do_ref, att_ref, kv_ref)
    scale = LOG2E * HEAD_DIM**-0.5
    queries, grads = q_ref[...], do_ref[...]
    lse, qseg = lse_ref[0:1, :], segrow_ref[0:1, :]
    high, low = two_parts(grads.astype(F32) * att_ref[...])
    ones = jnp.ones((8, HEAD_DIM), BF16)
    delta = (dot(ones, high, 1, 1) + dot(ones, low, 1, 1))[0:1, :]

    def block(*blocks, own=False):
        change, results = None, []
        for t in blocks:
            keys = kv_ref[0, t, :ROWS]
            s = dot(keys, queries, 1, 1) * scale
            s = jnp.where(key_segments(kv_ref[0, t, ROWS:]) == qseg, s, MASKED)
            if own:
                s = causal_mask(s)
            p = jnp.exp2(s - lse)
            ds = (p * (dot(kv_ref[1, t, :ROWS], grads, 1, 1) - delta)).astype(BF16)
            dk = dot(ds, queries)
            dv = dot(p.astype(BF16), grads)
            part = dot(keys, ds, 0, 0)
            change = part if change is None else change + part
            results.append((jnp.where(c == 0, dk, dv), jnp.where(c == 0, dv, dk)))
        dqt_ref[...] = change if own else dqt_ref[...] + change
        for t, (kept, given) in zip(blocks, results):
            mine[t] = kept.astype(BF16)
            theirs[t] = given.astype(BF16)
            to_sibling(t).start()

    def pair(t):
        to_sibling(t).wait_recv()
        return mine[t].astype(F32) + sib[t].astype(F32)

    block(me, own=True)
    reduce_some(1)
    states.turn()
    loads.need(mt_ref)
    left.start()
    pieces = [gated_ref.at[:, k * WIDE : (k + 1) * WIDE] for k in range(3)] + [attlow_ref]
    fetched = [
        pltpu.make_async_copy(piece, outs_ref.at[k], outs_sem.at[k])
        for k, piece in enumerate(pieces)
    ]
    for copy in fetched:
        copy.start()
    for copy in fetched:
        copy.wait()

    def outs(p):
        return remote(
            outs_ref.at[p], outz_ref.at[p], outz_sem.at[0, p], outz_sem.at[1, p], {"zl": 1 - zl}
        )

    before = done

    @pl.when(zl == 1)
    def _():
        block(at)

    def give(k):
        q, _ = plane_peer(k, -1)

        @pl.when(q < at)
        def _():
            j = zl * PLANE + q
            mine[j] = pair(j).astype(BF16)
            to_owner(k, 0).start()

        @pl.when(zl == 1)
        def _():
            mine[q] = pair(q).astype(BF16)
            to_owner(k, 1).start()

    def step_over(k):
        q, _ = plane_peer(k, -1)
        pl.when((q < at) & (zl == 1))(lambda: block(PLANE + q, q))
        pl.when((q < at) & (zl == 0))(lambda: block(q))
        pl.when((q > at) & (zl == 1))(lambda: block(q))

        @pl.when(k >= 1)
        def _():
            give(k - 1)

        @pl.when((k % 3 == 0) & (k >= 3))
        def _():
            outs(k // 3 - 1).start()

        @pl.when(k % 2 == 1)
        def _():
            rs.step(before + k // 2)

    over(0, PLANE - 1, step_over)
    give(PLANE - 2)
    done += (PLANE - 1) // 2
    reduce_some(1)
    left.pass_on()
    dkv_ref[...] = pair(me)

    @pl.when(zl == 1)
    def _():
        total_ref[...] = pair(at)

    score_scale = HEAD_DIM**-0.5
    dq = jnp.transpose(dqt_ref[...]) * score_scale
    cosine, sine = cos_ref[...], sin_ref[...]
    for h in range(2):
        raw = turn_pairs(dq[h * ROWS : (h + 1) * ROWS], cosine, sine, -1.0)
        dqraw_ref[:, h * HEAD_DIM : (h + 1) * HEAD_DIM] = raw.astype(BF16)

    states.finish(enter_ref)
    dcum = dcum_ref[...]
    dstep = jnp.zeros((ROWS, 128), F32)
    dlast = jnp.zeros((8, 128), F32)
    db = jnp.zeros((ROWS, STATE), F32)
    for g in range(GROUPS):
        cols = slice(g * 128, (g + 1) * 128)
        entering = enter_ref[cols, :]
        entering_low = entering.astype(BF16)
        x = xact_ref[:, cols].astype(F32)
        steps, carries = widen(step, g), widen(carry, g)
        v = x * steps * carries
        dv = dot(b_low, entering_low, 1, 1)
        db += dot(v.astype(BF16), entering_low)
        dcarry = per_head(v * dv, g)
        dcum -= dcarry
        dlast += jnp.broadcast_to(jnp.sum(dcarry, 0, keepdims=True), (8, 128))
        du = du_ref[:, cols] + carries * dv
        dstep += per_head(x * du, g)
        pieces = jnp.sum(entering * state_ref[cols, :], 1, keepdims=True)
        both = jnp.sum(jnp.broadcast_to(pieces, (128, 128)) * head_of_lane_f32(g), 0, keepdims=True)
        dlast += through * both
        g_ref[:, cols] = steps * du + skip_ref[0:1, cols] * g_ref[:, cols]
    dbc_all[:, :STATE] += db
    last_row = lax.broadcasted_iota(jnp.int32, (ROWS, 128), 0) == ROWS - 1
    dcum += jnp.where(last_row, dlast[0:1, :], 0.0)
    da = running(dcum, lower, 0)
    drate = -jnp.sum(step * da, 0, keepdims=True)
    ddt = (dstep - vec_ref[1:2, :] * da) * sigmoid(pre_dt)
    ddt_ref[...] = ddt.astype(BF16)
    dbias = jnp.sum(ddt, 0, keepdims=True)
    dvec_ref[...] = jnp.concatenate([dbias, drate, dskip[0:1, :], jnp.zeros((5, 128), F32)], 0)

    reduce_some(1)

    for d in range(4):
        shares[d] = dbc_all[:, d * 128 : (d + 1) * 128].astype(BF16)
    share = lambda o: remote(
        shares.at[(head_at + o) % 4], share_got.at[o], share_send.at[o], share_recv.at[o],
        at_head((head_at + o) % 4),
    )
    for o in range(1, 4):
        share(o).start()

    def conv_back(ext, taps, grad, cols, out_taps, out_grad):
        pre, inputs = conv_group(ext, segx, seg_ref, taps, cols)
        sig = sigmoid(pre)
        dpre = grad * sig * (1.0 + pre * (1.0 - sig))
        gext[...] = jnp.zeros_like(gext)
        rows = []
        for k in range(CONV):
            rows.append(jnp.sum(dpre * inputs[k], 0, keepdims=True))
            same = segx[pl.ds(5 + k, ROWS), :] == seg_ref[...]
            gext[pl.ds(5 + k, ROWS), :] += jnp.where(same, taps[k : k + 1, cols] * dpre, 0.0)
        out_taps[:, cols] = jnp.concatenate([*rows, jnp.zeros((4, 128), F32)], 0)
        out_grad[...] = gext[...]

    def x_group(g):
        cols = lane_block(g)
        conv_back(xext, xtaps_ref, g_ref[:, cols], cols, dxtaps_ref, ddtx_ref)
        edge_ref[:, cols] = ddtx_ref[:8, :]
        g_ref[:, cols] = ddtx_ref[8:, :]

    over(0, GROUPS, x_group)
    reduce_some(1)
    grad_bc = shares[head_at].astype(F32)
    for o in range(1, 4):
        share(o).wait_recv()
        grad_bc += share_got[o].astype(F32)
    conv_back(bcext, owntaps_ref, grad_bc, slice(0, 128), dbctaps_ref, ddtx_ref)
    edge_ref[:, INNER:] = ddtx_ref[:8, :]
    edge_copy = remote(
        edge_ref, edge_out, edge_sem.at[0], edge_sem.at[1], block_at((me + BLOCKS - 1) % BLOCKS)
    )

    @pl.when(me > 0)
    def _():
        edge_copy.start()

    reduce_some(1)

    def collect(q):
        @pl.when((zl == 1) & (q != at))
        def _():
            from_plane(1, q).wait_recv()
            total_ref[...] += kvgot[1, q].astype(F32)

    over(0, PLANE, collect)

    @pl.when(zl == 1)
    def _():
        relay_ref[...] = total_ref[...].astype(BF16)
        across.start()

    reduce_some(1)

    def collect_own(q):
        from_plane(0, q).wait_recv()
        dkv_ref[...] += kvgot[0, q].astype(F32)

    over(at + 1, PLANE, collect_own)

    @pl.when(zl == 0)
    def _():
        from_plane(1, 0).wait_recv()
        dkv_ref[...] += kvgot[1, 0].astype(F32)

    @pl.when(me < BLOCKS - 1)
    def _():
        edge_copy.wait_recv()

    @pl.when(me == BLOCKS - 1)
    def _():
        edge_out[...] = jnp.zeros_like(edge_out)

    tail = pl.ds(ROWS - 8, 8)
    g_ref[tail, :] += edge_out[:, :INNER]
    ddtx_ref[pl.ds(ROWS, 8), :] += edge_out[:, INNER:]
    dx_ref[...] = g_ref[...].astype(BF16)
    misc_ref[:, :128] = ddtx_ref[8:, :].astype(BF16)
    dkv = dkv_ref[...]
    turned = turn_pairs(dkv * score_scale, cosine, sine, -1.0)
    misc_ref[:, 128:] = jnp.where(c == 0, turned, dkv).astype(BF16)

    reduce_some(rs.steps - done)

    @pl.when(me > 0)
    def _():
        edge_copy.wait_send()

    states.close()
    rs.close()
    left.finish()
    left.close()
    over(0, 4, lambda p: outs(p).wait())
    for o in range(1, 4):
        share(o).wait_send()
    to_sibling(me).wait_send()

    def given(k):
        q, _ = plane_peer(k, -1)

        @pl.when(q < at)
        def _():
            to_sibling(zl * PLANE + q).wait_send()
            to_owner(k, 0).wait_send()

        @pl.when(zl == 1)
        def _():
            to_sibling(q).wait_send()
            to_owner(k, 1).wait_send()

    over(0, PLANE - 1, given)

    @pl.when(zl == 1)
    def _():
        to_sibling(at).wait_send()
        across.wait_send()


def head_of_lane_f32(g):
    row = lax.broadcasted_iota(jnp.int32, (128, 128), 0)
    lane = lax.broadcasted_iota(jnp.int32, (128, 128), 1)
    return (lane == 2 * g + (row >= SSM_DIM).astype(jnp.int32)).astype(F32)


def mixer_backward(*args):
    wide = 2 * ROWS
    dma = pltpu.SemaphoreType.DMA
    v = pltpu.VMEM
    piece = (BLOCKS, ROWS, HEAD_DIM)
    return call(
        mixer_backward_kernel, "mixer_backward", args, (23, 25, 26, 21, 22, 24, 30, 0, 1, 2, 5, 27),
        [
            ((ROWS, 2 * HEAD_DIM), BF16),
            ((ROWS, 256), BF16),
            ((ROWS, INNER), BF16),
            ((ROWS, INNER), BF16),
            ((ROWS, 128), BF16),
            ((8, INNER), F32),
            ((8, 128), F32),
            ((8, 128), F32),
            ((64, 12 * WIDE), F32),
            ((OWN, ROWS), BF16),
            ((4, ROWS, WIDE), BF16),
        ],
        [
            v((ROWS, HEAD_DIM), F32),
            v((HEAD_DIM, wide), F32),
            *[v(piece, BF16)] * 3,
            v((2, PLANE, ROWS, HEAD_DIM), BF16),
            v((ROWS, HEAD_DIM), BF16),
            v((ROWS, HEAD_DIM), F32),
            v((ROWS + 8, INNER), F32),
            v((ROWS + 8, 128), F32),
            v((ROWS + 8, 128), F32),
            v((INNER, STATE), F32),
            *[v((BLOCKS, SCAN_ROWS + 8, STATE), BF16)] * 2,
            *[v((BLOCKS, 16, STATE + 128), BF16)] * 2,
            v((ROWS, ROWS), F32),
            v((ROWS, ROWS), F32),
            v((128, ROWS), F32),
            v((ROWS, INNER), F32),
            v((ROWS, INNER), F32),
            v((ROWS, BC), F32),
            v((4, ROWS, 128), BF16),
            v((4, ROWS, 128), BF16),
            v((8, GRAD_EDGE), F32),
            v((8, GRAD_EDGE), F32),
            v((INNER, STATE), F32),
            v((ROWS + 8, 128), F32),
            v((ROWS, 128), F32),
            v((ROWS + 8, 128), F32),
            dma((2, PLANE)),
            dma((2, PLANE)),
            dma((BLOCKS,)),
            dma((BLOCKS,)),
            dma((2,)),
            dma((2, BLOCKS)),
            dma((2, BLOCKS)),
            dma((4,)),
            dma((4,)),
            dma((4,)),
            v((4, ROWS, WIDE), BF16),
            dma((2, 4)),
            dma((4,)),
            v((CONV, 128), F32),
            *small_scratch(),
            *Reduce.scratch(12),
        ],
        2,
        (31, 32),
    )


SMALL = 8 * 128
SMALL_AT = 5
CHUNKS = 13
GATHER_FROM = CHUNKS


def finish_kernel(
    loads, misc_ref, dx_ref, dz_ref, dq_ref, ddt_ref, gated_ref, att_ref, nt_ref, ntz_ref, mt_ref,
    mtz_ref, ffn_ref, tok_ref, x_w, z_w, q_w, dt_w, dxtaps_ref, dbctaps_ref, dvec_ref,
    gains_ref, bc_all, kv_all, outz_ref,
    w_ref, all_ref, alls_ref, back_sum, ffn_sum,
    back_ref, near_sem, bc_w, kv_w, column_sem, dt_wide, own_small, mine, esum, egot, e_send, e_recv, z_send, z_recv, w_send, w_recv,
    sib_send, sib_recv, s_send, s_recv, t_send, t_recv, part_ref, *rest,
):
    loads.start()
    me, c, zh = block_index(), lax.axis_index("c"), lax.axis_index("zh")
    chip = zh * BLOCKS + me
    sibling = {"c": 1 - c}

    def chip_at(p):
        return {"zh": p // BLOCKS, **block_at(p % BLOCKS)}

    n_rs = len(Reduce.scratch(CHUNKS))
    rs = Reduce(
        [(nt_ref, ntz_ref, 0), (mt_ref, mtz_ref, 9)], CHUNKS, 9, *rest[:7], w_ref, rest[7:n_rs]
    )
    rest = rest[n_rs:]
    n_sum = len(HeadSum.scratch())
    back = HeadSum(back_ref, back_sum, *rest[:3], rest[3:n_sum])
    rest = rest[n_sum:]
    ffn = HeadSum(ffn_ref, ffn_sum, *rest[:3], rest[3:])

    barrier = pltpu.get_barrier_semaphore()
    over(1, CHIPS, lambda o: signal(barrier, chip_at((chip + o) % CHIPS)))
    signal(barrier, sibling)
    pl.semaphore_wait(barrier, CHIPS)

    head = zh * 2 + c
    columns = [
        pltpu.make_async_copy(
            ref.at[:, pl.ds(pl.multiple_of(k * 128, 128), 128)], here, column_sem.at[i]
        )
        for i, (ref, k, here) in enumerate(((bc_all, head, bc_w), (kv_all, c * 2 + zh, kv_w)))
    ]
    for copy in columns:
        copy.start()
    rs.fill([misc_ref, dx_ref, dz_ref, dq_ref])
    rs.r[8, :, :128] = ddt_ref[...]
    rs.r[8, :, 128:] = jnp.zeros_like(ddt_ref)
    over(0, rs.here, lambda k: rs.right(k).start())
    near = pltpu.make_async_copy(outz_ref, rs.rz.at[pl.ds(9, 4)], near_sem)
    near.start()
    loads.need(nt_ref, ntz_ref)

    def partial(rows):
        total = dot(dx_ref[rows, :], x_w[...], 1, 1)
        total += dot(dz_ref[rows, :], z_w[...], 1, 1)
        total += dot(dq_ref[rows, :], q_w[...], 1, 1)
        total += dot(ddt_ref[rows, :], dt_wide[...])
        total += dot(misc_ref[rows, :128], bc_w[...], 1, 1)
        back_ref[rows, :] = (total + dot(misc_ref[rows, 128:], kv_w[...], 1, 1)).astype(BF16)

    spread_dt(dt_w, dt_wide)
    loads.need(x_w, z_w, q_w)
    for copy in columns:
        copy.wait()
    rs.step(0)
    partial(slice(0, ROWS // 2))
    back.start((0, 1))
    rs.step(1)
    partial(slice(ROWS // 2, ROWS))
    back.start((2, 3))
    loads.need(mt_ref, mtz_ref, ffn_ref, tok_ref, gated_ref, att_ref)
    near.wait()
    rs.fill([gated_ref, att_ref], 9)
    ffn.start()

    at, level = me % PLANE, zh * NZ + lax.axis_index("zl")

    def along_z(o):
        d = (level + o) % 4
        where = {"zh": d // NZ, "zl": d % NZ}
        return remote(mine, all_ref.at[c, at, level], z_send.at[o], z_recv.at[o], where)

    x, y = lax.axis_index("x"), lax.axis_index("y")

    def at_place(i, j):
        return {"x": i, "y": j}, i * NY + j

    def piece(q, h, send, where):
        ref = all_ref.at[c, q, pl.ds(2 * h, 2)]
        return remote(ref, ref, send, w_recv.at[h, q], where)

    def one_way(h, o):
        where = {"x": (x + o) % NX} if h == 0 else {"y": (y + o) % NY}
        return piece(at, h, w_send.at[h, o], where)

    def other_way(h, k, o):
        i, j = ((x + k) % NX, y) if h == 0 else (x, (y + k) % NY)
        where = {"y": (y + o) % NY} if h == 0 else {"x": (x + o) % NX}
        return piece(i * NY + j, h, w_send.at[h, 4 * k + 4 + o], where)

    def arrived(q, h):
        return piece(q, h, w_send.at[0, 0], sibling)

    def to_sibling(q, core):
        return remote(
            all_ref.at[core, q], all_ref.at[core, q], sib_send.at[q], sib_recv.at[q], sibling
        )

    def columns_out():
        for o in range(1, 4):
            along_z(o).wait_recv()
        for o in range(1, 4):
            one_way(0, o).start()
            one_way(1, o).start()
        to_sibling(at, c).start()
        for o in range(1, 4):
            other_way(0, 0, o).start()
            other_way(1, 0, o).start()

    def columns_on():
        for k in range(1, 4):
            for h in range(2):
                i, j = ((x + k) % NX, y) if h == 0 else (x, (y + k) % NY)
                arrived(i * NY + j, h).wait_recv()
                for o in range(1, 4):
                    other_way(h, k, o).start()

    def pass_on(k):
        q, _ = plane_peer(k, -1)
        same_x, same_y = q // NY == x, q % NY == y

        @pl.when(jnp.logical_not(same_y))
        def _():
            arrived(q, 0).wait_recv()

        @pl.when(jnp.logical_not(same_x))
        def _():
            arrived(q, 1).wait_recv()

        to_sibling(q, c).start()

    def share(d):
        return remote(own_small.at[d], egot.at[me], e_send.at[d], e_recv.at[me], block_at(d))

    def shared(s):
        return remote(egot.at[s], egot.at[s], e_send.at[0], e_recv.at[s], block_at(s))

    def small_spread(o):
        d = (chip + o) % CHIPS
        slot = zh * SMALL_AT + me
        return remote(esum, alls_ref.at[c, slot], s_send.at[o], s_recv.at[slot], chip_at(d))

    def small_sibling(slot, core):
        return remote(
            alls_ref.at[core, slot], alls_ref.at[core, slot], t_send.at[slot], t_recv.at[slot],
            sibling,
        )

    def put(row, value):
        own_small[row // 8, row % 8 : row % 8 + 1, :] = value

    def gradient():
        for r in range(0, ROWS, 32):
            rows = pl.ds(r, 32)
            x = tok_ref[rows, :].astype(F32)
            scale = lax.rsqrt(jnp.mean(x * x, 1, keepdims=True) + EPSILON)
            n = x * scale
            grad = back_sum[rows, :].astype(F32)
            gains = jnp.sum(grad * n, 0, keepdims=True)
            for k in range(MODEL // 128):
                piece = gains[:, k * 128 : (k + 1) * 128]
                part_ref[k : k + 1, :] = piece if r == 0 else part_ref[k : k + 1, :] + piece
        own_small[0, :4] = part_ref[pl.ds(head * 4, 4), :]
        for k in range(CONV):
            for g in range(GROUPS):
                put(4 + GROUPS * k + g, dxtaps_ref[k : k + 1, g * 128 : (g + 1) * 128])
            put(28 + k, dbctaps_ref[k : k + 1, :])
            put(32 + k, gains_ref[0:1, lane_block(head * 4 + k)])
        lane = lax.broadcasted_iota(jnp.int32, (1, 128), 1)
        line = jnp.zeros((1, 128), F32)
        for k in range(3):
            moved = dvec_ref[k : k + 1, :] if k == 0 else pltpu.roll(dvec_ref[k : k + 1, :], k * HEADS, 1)
            line = jnp.where((lane >= k * HEADS) & (lane < (k + 1) * HEADS), moved, line)
        put(36, line)
        own_small[4, 5:] = jnp.zeros((3, 128), F32)

        def give(d):
            @pl.when(d != me)
            def _():
                share(d).start()

        over(0, SMALL_AT, give)

    def small_sums():
        @pl.when(me < SMALL_AT)
        def _():
            egot[me] = own_small[me]

            def take(s):
                @pl.when(s != me)
                def _():
                    shared(s).wait_recv()

            over(0, BLOCKS, take)
            total = lax.fori_loop(0, BLOCKS, lambda s, t: t + egot[s], jnp.zeros((8, 128), F32))
            esum[...] = jnp.concatenate([total, jnp.zeros_like(total)], 0).astype(BF16)
            slot = zh * SMALL_AT + me
            alls_ref[c, slot] = esum[...]
            over(1, CHIPS, lambda o: small_spread(o).start())
            small_sibling(slot, c).start()

    def small_pass():
        def one(slot):
            @pl.when(slot != zh * SMALL_AT + me + jnp.where(me < SMALL_AT, 0, CHIPS))
            def _():
                remote(
                    esum, alls_ref.at[c, slot], s_send.at[0], s_recv.at[slot], sibling
                ).wait_recv()
                small_sibling(slot, c).start()

        over(0, 2 * SMALL_AT, one)

    def weights_out():
        mine[...] = w_ref[:, :WIDE].astype(BF16)
        all_ref[c, at, level] = mine[...]
        for o in range(1, 4):
            along_z(o).start()

    def step(i):
        rs.step(i)

        @pl.when(i == LAST)
        def _():
            weights_out()
            back.across()

        @pl.when(i == 8)
        def _():
            ffn.across()

        @pl.when(i == 10)
        def _():
            columns_out()

        @pl.when(i == 11)
        def _():
            back.join()

        @pl.when(i == 14)
        def _():
            columns_on()

        @pl.when(i == 12)
        def _():
            back.finish()
            gradient()

        @pl.when(i == 15)
        def _():
            small_sums()

    over(2, rs.steps, step)
    loads.put(w_ref, back_sum)
    over(0, PLANE - 1, pass_on)
    ffn.join()
    small_pass()
    ffn.finish()
    loads.put(ffn_sum)

    over(0, PLANE, lambda q: to_sibling(q, 1 - c).wait_recv())
    over(0, 2 * SMALL_AT, lambda s: small_sibling(s, 1 - c).wait_recv())
    rs.close()
    back.close()
    ffn.close()
    over(0, PLANE, lambda q: to_sibling(q, c).wait_send())
    over(0, 2 * SMALL_AT, lambda s: small_sibling(s, c).wait_send())
    for h in range(2):
        for o in range(1, 4):
            one_way(h, o).wait_send()
            for k in range(4):
                other_way(h, k, o).wait_send()
    for o in range(1, 4):
        along_z(o).wait_send()

    @pl.when(me < SMALL_AT)
    def _():
        over(1, CHIPS, lambda o: small_spread(o).wait_send())

    def given(d):
        @pl.when(d != me)
        def _():
            share(d).wait_send()

    over(0, SMALL_AT, given)


def finish(*args):
    v, dma = pltpu.VMEM, pltpu.SemaphoreType.DMA
    return call(
        finish_kernel, "finish", args, (7, 8, 13, 14, 15, 9, 10, 11, 12, 5, 6),
        [
            ((64, CHUNKS * WIDE), F32),
            ((2, PLANE, 4, 64, WIDE), BF16),
            ((2, 2 * SMALL_AT, 16, 128), BF16),
            ((ROWS, MODEL), BF16),
            ((ROWS, MODEL), BF16),
        ],
        [
            v((ROWS, MODEL), BF16),
            dma,
            v((MODEL, 128), BF16),
            v((MODEL, 128), BF16),
            dma((2,)),
            v((128, MODEL), BF16),
            v((SMALL_AT, 8, 128), F32),
            v((64, WIDE), BF16),
            v((16, 128), BF16),
            v((BLOCKS, 8, 128), F32),
            dma((SMALL_AT,)), dma((BLOCKS,)),
            dma((4,)), dma((4,)),
            dma((2, 20)), dma((2, PLANE)), dma((PLANE,)), dma((PLANE,)),
            dma((CHIPS,)), dma((2 * SMALL_AT,)),
            dma((2 * SMALL_AT,)), dma((2 * SMALL_AT,)),
            v((16, 128), F32),
            *Reduce.scratch(CHUNKS),
            *HeadSum.scratch(),
            *HeadSum.scratch(),
        ],
        3,
        (21, 22, 23),
    )


def place_kernel(
    all_ref, back_ref, ffn_ref, hid_ref, ghid_ref, tok_ref, gain_ref, mixer_ref, ffn_w, small_ref,
    out_ref, dtok_ref, bc_ref, kv_ref, x_w, z_w, q_w, dt_w, out_w, attn_w, gate_w, up_w, down_w,
    xtaps_ref, bctaps_ref, bias_ref, rate_ref, skip_ref, one_ref, two_ref,
):
    for c in range(2):
        for p in range(all_ref.shape[1]):
            for zh in range(2):
                rows = slice(p * 64, (p + 1) * 64)
                at, turned = (zh * 2 + c) * 128, (c * 2 + zh) * 128
                bc_ref[rows, at : at + 128] = all_ref[c, p, zh, 0, :, :128].astype(F32)
                kv_ref[rows, turned : turned + 128] = all_ref[c, p, zh, 0, :, 128:].astype(F32)
    for r in range(0, out_ref.shape[0], 32):
        rows = slice(r, r + 32)
        out_ref[rows, :] = (hid_ref[rows, :] + ffn_ref[rows, :].astype(F32)).astype(BF16)
        x = tok_ref[rows, :].astype(F32)
        scale = lax.rsqrt(jnp.mean(x * x, 1, keepdims=True) + EPSILON)
        n = x * scale
        scaled = back_ref[rows, :].astype(F32) * gain_ref[0:1, :]
        along = jnp.mean(n * scaled, 1, keepdims=True)
        dtok_ref[rows, :] = ghid_ref[rows, :] + scale * (scaled - n * along)

    @pl.when(pl.program_id(0) == 0)
    def _():
        at = WIDE
        for ref in (x_w, z_w, q_w):
            ref[...] = mixer_ref[:, at : at + ref.shape[1]]
            at += ref.shape[1]
        dt_w[...] = jnp.transpose(mixer_ref[:, at : at + 128])[:HEADS, :]
        at += WIDE
        for ref in (out_w, attn_w):
            ref[...] = mixer_ref[:, at : at + ref.shape[1]]
            at += ref.shape[1]
        at = 0
        for ref in (down_w, gate_w, up_w):
            ref[...] = ffn_w[:, at : at + ref.shape[1]]
            at += ref.shape[1]
        lane = lax.broadcasted_iota(jnp.int32, (1, 128), 1)
        lines = [jnp.zeros((1, 128), F32)] * 3
        for h in range(4):

            def row(k):
                piece = small_ref[h % 2, h // 2 * SMALL_AT + k // 8].astype(F32)
                return piece[k % 8 : k % 8 + 1, :]

            for k in range(CONV):
                for g in range(GROUPS):
                    cols = slice(h * INNER + g * 128, h * INNER + (g + 1) * 128)
                    xtaps_ref[k : k + 1, cols] = row(4 + GROUPS * k + g)
                bctaps_ref[k : k + 1, h * 128 : (h + 1) * 128] = row(28 + k)
                cols = pl.ds((4 * h + k) * 128, 128)
                one_ref[cols] = row(k).reshape(128)
                two_ref[cols] = row(32 + k).reshape(128)
            for k in range(3):
                shift = (h - k) * HEADS % 128
                moved = pltpu.roll(row(36), shift, 1) if shift else row(36)
                mine = (lane >= h * HEADS) & (lane < (h + 1) * HEADS)
                lines[k] = jnp.where(mine, moved, lines[k])
        for ref, line in zip((bias_ref, rate_ref, skip_ref), lines):
            ref[...] = line.reshape(128)[: 4 * HEADS]


def place(gathered, back, ffn, hidden_in, ghid, tokens, gain, mixer_w, ffn_w, small):
    steps = 2
    spans, rows, ff = PLANE * NZ // steps, ROWS // steps, ffn_w.shape[1] // 3
    half = steps // NZ
    s = jax.ShapeDtypeStruct

    def whole(shape):
        return pl.BlockSpec(shape, lambda i: (0,) * len(shape))

    token = pl.BlockSpec((rows, MODEL), lambda i: (i, 0))
    wide = pl.BlockSpec((64 * spans, 512), lambda i: (i, 0))
    kept = [
        (64, INNER), (64, INNER), (64, 256), (HEADS, 64), (64, INNER), (64, 256), (64, ff), (64, ff),
        (64, ff), (CONV, 4 * INNER), (CONV, BC), (4 * HEADS,), (4 * HEADS,), (4 * HEADS,), (MODEL,), (MODEL,),
    ]
    return pl.pallas_call(
        place_kernel,
        name="place",
        out_shape=(
            s((ROWS, MODEL), BF16), s((ROWS, MODEL), F32), s((MODEL, 512), F32),
            s((MODEL, 512), F32), *[s(shape, F32) for shape in kept],
        ),
        grid=(steps,),
        in_specs=[
            pl.BlockSpec((2, spans, 2, 1, 64, WIDE), lambda i: (0, i % half, 0, i // half, 0, 0)),
            token, token, token, token, token, whole((1, MODEL)), whole(mixer_w.shape),
            whole(ffn_w.shape), whole(small.shape),
        ],
        out_specs=(token, token, wide, wide, *[whole(shape) for shape in kept]),
        compiler_params=pltpu.CompilerParams(vmem_limit_bytes=VMEM_LIMIT),
    )(
        gathered.reshape(2, PLANE, 2, NZ, 64, WIDE), back, ffn, hidden_in, ghid, tokens, gain,
        mixer_w, ffn_w, small,
    )


def on_device(
    tokens, segment_ids, cotangent, norm1_gain, x_weight, z_weight, bc_weight, dt_weight,
    x_conv, bc_conv, dt_bias, decay_rate, skip_gain, out_weight, query_weight, kv_weight,
    attn_weight, norm2_gain, gate_weight, up_weight, down_weight,
):
    heads = decay_rate.shape[0]
    positions = block_index() * ROWS + jnp.arange(ROWS)
    half_dim = HEAD_DIM // 2
    frequency = ROPE_BASE ** (-(jnp.arange(half_dim).astype(F32) * 2.0 / HEAD_DIM))
    angles = positions.astype(F32)[:, None] * frequency[None, :]
    cosine, sine = jnp.cos(angles), jnp.sin(angles)
    cosine = jnp.concatenate([cosine, cosine], 1)
    sine = jnp.concatenate([-sine, sine], 1)
    dt_t, seg = dt_weight.T, segment_ids.reshape(1, ROWS)
    bias, rate, skip = (v.reshape(1, heads) for v in (dt_bias, decay_rate, skip_gain))
    gain_one, gain_two = norm1_gain.reshape(1, MODEL), norm2_gain.reshape(1, MODEL)

    (
        normed_t, cot_t, queries, x_pre, bc_pre, dt_raw, z_val, attended, lse, kv_all, edge_in,
        gated, core, x_act, bc_act, state_in, normed_near, cot_near, attended_low,
    ) = mixer_forward(
        tokens, cotangent, gain_one, query_weight, kv_weight, x_weight, bc_weight, dt_t, z_weight,
        cosine, sine, seg, x_conv, bc_conv, bias, rate, skip,
    )
    (
        hidden_in, two_t, grad_gate, grad_up, hidden, ffn_part, grad_hidden_in, mix_t, gains_two,
        grad_gated, grad_attended, two_near,
    ) = feed_forward(
        gated, attended_low, tokens, cotangent, gain_two, out_weight, attn_weight, gate_weight,
        up_weight, down_weight,
    )
    (
        grad_query, misc, grad_z, grad_x_pre, grad_dt, grad_x_conv, grad_bc_conv, grad_vectors,
        ffn_w, mix_near, mixed_near,
    ) = mixer_backward(
        queries, grad_attended, attended, lse, seg, kv_all, grad_gated, z_val, core, x_act,
        bc_act, x_pre, bc_pre, edge_in, dt_raw, state_in, bias, x_conv, bc_conv, rate,
        skip, grad_gate, grad_up, hidden, two_t, cot_t, cot_near, mix_t, cosine, sine, two_near,
        gated, attended_low,
    )
    mixer_w, gathered, small_sums, grad_normed, ffn_sum = finish(
        misc, grad_x_pre, grad_z, grad_query, grad_dt, gated, attended_low, normed_t, normed_near,
        mix_t, mix_near, ffn_part, tokens, x_weight, z_weight, query_weight, dt_t, grad_x_conv,
        grad_bc_conv, grad_vectors, gains_two, bc_weight, kv_weight, mixed_near,
    )
    (
        output, grad_tokens, bc_w, kv_w, x_w, z_w, q_w, dt_w, out_w, attn_w, gate_w, up_w, down_w,
        x_taps, bc_taps, bias_sum, rate_sum, skip_sum, gain_one_sum, gain_two_sum,
    ) = place(
        gathered, grad_normed, ffn_sum, hidden_in, grad_hidden_in, tokens, gain_one, mixer_w,
        ffn_w, small_sums,
    )
    return (
        output, grad_tokens, gain_one_sum, x_w, z_w, bc_w, dt_w.T, x_taps, bc_taps, bias_sum,
        rate_sum, skip_sum, out_w.T, q_w, kv_w, attn_w.T, gain_two_sum, gate_w, up_w, down_w.T,
    )


def solution(mesh):
    split = Mesh(mesh.devices.reshape(NZ, NX, NY, 2, 2), (*SEQ, "zh", "c"))
    head = ("zh", "c")
    rows, columns, both, turned = P(SEQ, None), P(None, head), P(SEQ, head), P(head, SEQ)
    return jax.shard_map(
        on_device,
        mesh=split,
        in_specs=(
            rows, P(SEQ), rows, P(), columns, columns, P(), columns, columns, P(), P(head),
            P(head), P(head), P(head, None), columns, P(), P(head, None), P(), columns, columns,
            P(head, None),
        ),
        out_specs=(
            rows, rows, P(), both, both, P(), both, P(), P(), P(), P(), P(), turned, both, P(),
            turned, P(), both, both, turned,
        ),
        check_vma=False,
    )
```
